32 devices in a mesh: bx: 4 (over x, core), by: 4 (over z), bz: 2 (over y).
Axes of the slice: x: 2, y: 2, z: 4, core: 2. Of those that a mesh axis runs over, the one named last changes fastest.
Arguments:
- forcing: float32 [64, 64, 512], P('bx', 'bz', 'by'), may hold values from -6 to 6
- start: float32 [64, 64, 512], P('bx', 'bz', 'by'), may hold values from -2 to 2
- element_class_index: int32 [16, 16, 128], P('bx', 'bz', 'by'), may hold values from 0 to 15
- class_coef: float32 [3, 16], replicated, may hold values from 0.3 to 3
Outputs:
- solution: float32 [64, 64, 512], P('bx', 'bz', 'by')
- residual: float32 [64, 64, 512], P('bx', 'bz', 'by')
The draws below stay inside these ranges and needn't reach their ends.
All inputs are finite; a program needn't handle non-finite values.
Results may differ from the reference program's by a relative error of at most 0.015.
Values may be sent and summed in bfloat16 or wider, within the bound.
No kernel may reach another device: no remote copies, remote signals or barrier semaphores. Data moves between devices by JAX's collectives and lax.ppermute only.
A program may use at most 64 MiB of HBM per device.

```python
import math
import jax
import jax.numpy as jnp
from jax import lax

COEF_CLASSES = 16
CYCLES = 2
ELEMENTS_X = 16
ELEMENTS_Z = 16
ELEMENTS_Y = 128
NX = 64
NZ = 64
NY = 512


def touch_ends(result, rng, smallest, largest):
    longest = result.shape.index(max(result.shape))
    spots = []
    for shift in (0, 1):
        where = [jax.random.randint(jax.random.fold_in(rng, axis), (), 0, length) for axis, length in enumerate(result.shape)]
        where[longest] = (where[longest] + shift) % result.shape[longest]
        spots.append(tuple(where))
    return result.at[spots[0]].set(smallest).at[spots[1]].set(largest)


def block_scale(key, shape, pieces, least, largest):
    level, own = 1.0, jax.random.fold_in(key, 6)
    for position, parts in pieces:
        draws = jnp.exp(jax.random.uniform(jax.random.fold_in(own, position), (parts,), jnp.float32, least / len(pieces), largest / len(pieces)))
        level = level * jnp.repeat(draws, shape[position] // parts).reshape([-1 if axis == position else 1 for axis in range(len(shape))])
    return level


def normal_values(stream_key, extent, width, most, shards=(), kind=jnp.bfloat16):
    entries = jax.random.normal(stream_key, extent, jnp.float32) * width
    if len(shards) > 0:
        entries = block_scale(stream_key, extent, shards, -0.22, 0.18) * entries
    return jnp.clip(entries, min=-most, max=most).astype(kind)


def setup_inputs(seed: int = 0) -> dict:
    key_of = jax.random.split(jax.random.key(seed), 5)
    return {
        "forcing": normal_values(key_of[0], (NX, NZ, NY), 1.0, 6.0, ((0, 4), (1, 2), (2, 4)), jnp.float32),
        "start": normal_values(key_of[1], (NX, NZ, NY), 0.3, 2.0, ((0, 4), (1, 2), (2, 4)), jnp.float32),
        "element_class_index": touch_ends(jax.random.randint(key_of[2], (ELEMENTS_X, ELEMENTS_Z, ELEMENTS_Y), 0, COEF_CLASSES), jax.random.fold_in(key_of[2], 1), 0, COEF_CLASSES - 1).astype(jnp.int32),
        "class_coef": jnp.clip(jnp.exp(jax.random.uniform(key_of[3], (3, COEF_CLASSES), jnp.float32, math.log(0.3), math.log(3.0))), 0.3, 3.0),
    }


FACE_PENALTY = 2.0
DAMPING = 0.6666666666666666

def face_factor(count):
    edges = jnp.arange(count + 1, dtype=jnp.int32)
    return jnp.where(edges % 4 == 0, FACE_PENALTY, 1.0).astype(jnp.float32)

def edge_weights(kappa_pad):
    inner_x = kappa_pad[:, 1:-1, 1:-1]
    weight_x = face_factor(inner_x.shape[0] - 2)[:, None, None] * ((inner_x[:-1] + inner_x[1:]) * 0.5)
    inner_z = kappa_pad[1:-1, :, 1:-1]
    weight_z = face_factor(inner_z.shape[1] - 2)[None, :, None] * ((inner_z[:, :-1] + inner_z[:, 1:]) * 0.5)
    inner_y = kappa_pad[1:-1, 1:-1, :]
    quadrature_weight_y = face_factor(inner_y.shape[2] - 2)[None, None, :] * ((inner_y[:, :, :-1] + inner_y[:, :, 1:]) * 0.5)
    return (weight_x, weight_z, quadrature_weight_y)

def operator_diagonal(weights, sigma_node):
    weight_x, weight_z, quadrature_weight_y = weights
    total = sigma_node + (weight_x[:-1] + weight_x[1:])
    total = total + (weight_z[:, :-1] + weight_z[:, 1:])
    return total + (quadrature_weight_y[:, :, :-1] + quadrature_weight_y[:, :, 1:])

def apply_operator(field_pad, weights, sigma_node):
    weight_x, weight_z, quadrature_weight_y = weights
    centre = field_pad[1:-1, 1:-1, 1:-1]
    total = sigma_node * centre
    total = total + weight_x[:-1] * (centre - field_pad[:-2, 1:-1, 1:-1]) + weight_x[1:] * (centre - field_pad[2:, 1:-1, 1:-1])
    total = total + weight_z[:, :-1] * (centre - field_pad[1:-1, :-2, 1:-1]) + weight_z[:, 1:] * (centre - field_pad[1:-1, 2:, 1:-1])
    total = total + quadrature_weight_y[:, :, :-1] * (centre - field_pad[1:-1, 1:-1, :-2]) + quadrature_weight_y[:, :, 1:] * (centre - field_pad[1:-1, 1:-1, 2:])
    return total

def node_field(element_values):
    return jnp.repeat(jnp.repeat(jnp.repeat(element_values, 4, 0), 4, 1), 4, 2)

def restrict_matrix():
    return jnp.array([[1.0, 2.0 / 3.0, 1.0 / 3.0, 0.0], [0.0, 1.0 / 3.0, 2.0 / 3.0, 1.0]], dtype=jnp.float32) * 0.5

def prolong_matrix():
    return jnp.array([[1.0, 0.0], [2.0 / 3.0, 1.0 / 3.0], [1.0 / 3.0, 2.0 / 3.0], [0.0, 1.0]], dtype=jnp.float32)

def restrict_field(field):
    count_x, count_z, count_y = (field.shape[0] // 4, field.shape[1] // 4, field.shape[2] // 4)
    blocks = field.reshape(count_x, 4, count_z, 4, count_y, 4)
    matrix = restrict_matrix()
    blocks = jnp.einsum('ai,pizjyk->pazjyk', matrix, blocks, precision=lax.Precision.HIGHEST)
    blocks = jnp.einsum('bj,pazjyk->pazbyk', matrix, blocks, precision=lax.Precision.HIGHEST)
    blocks = jnp.einsum('ck,pazbyk->pazbyc', matrix, blocks, precision=lax.Precision.HIGHEST)
    return blocks.reshape(2 * count_x, 2 * count_z, 2 * count_y)

def prolong_field(coarse):
    count_x, count_z, count_y = (coarse.shape[0] // 2, coarse.shape[1] // 2, coarse.shape[2] // 2)
    blocks = coarse.astype(jnp.float32).reshape(count_x, 2, count_z, 2, count_y, 2)
    matrix = prolong_matrix()
    blocks = jnp.einsum('ia,pazbyc->pizbyc', matrix, blocks, precision=lax.Precision.HIGHEST)
    blocks = jnp.einsum('jb,pizbyc->pizjyc', matrix, blocks, precision=lax.Precision.HIGHEST)
    blocks = jnp.einsum('kc,pizjyc->pizjyk', matrix, blocks, precision=lax.Precision.HIGHEST)
    return blocks.reshape(4 * count_x, 4 * count_z, 4 * count_y)

def sine_table(count):
    index_one = jnp.arange(count, dtype=jnp.int32) + 1
    product = (index_one[:, None] * index_one[None, :]).astype(jnp.float32)
    return (jnp.sin(product * (math.pi / (count + 1))) * math.sqrt(2.0 / (count + 1))).astype(jnp.bfloat16)

def spectrum_values(index_zero, count):
    return 2.0 - 2.0 * jnp.cos((index_zero + 1).astype(jnp.float32) * (math.pi / (count + 1)))

def transform(coarse, table, axis):
    moved = jnp.tensordot(table.astype(jnp.float32), coarse.astype(jnp.float32), axes=([1], [axis]), precision=lax.Precision.HIGHEST)
    return jnp.moveaxis(moved, 0, axis)

def reference(forcing, start, element_class_index, class_coef):
    kappa_node = node_field(class_coef[0][element_class_index])
    sigma_node = node_field(class_coef[1][element_class_index])
    beta_node = node_field(class_coef[2][element_class_index])
    weights = edge_weights(jnp.pad(kappa_node, 1))
    diagonal = operator_diagonal(weights, sigma_node)
    kappa_mean = jnp.mean(class_coef[0])
    sigma_mean = jnp.mean(class_coef[1])
    count_x, count_z, count_y = (2 * element_class_index.shape[0], 2 * element_class_index.shape[1], 2 * element_class_index.shape[2])
    table_x, table_z, table_y = (sine_table(count_x), sine_table(count_z), sine_table(count_y))
    eigen_x = spectrum_values(jnp.arange(count_x, dtype=jnp.int32), count_x)
    eigen_z = spectrum_values(jnp.arange(count_z, dtype=jnp.int32), count_z)
    eigen_y = spectrum_values(jnp.arange(count_y, dtype=jnp.int32), count_y)
    eigen_sum = kappa_mean * (eigen_x[:, None, None] + eigen_z[None, :, None] + eigen_y[None, None, :]) + sigma_mean

    def nonlinear_residual(solution):
        return forcing - apply_operator(jnp.pad(solution, 1), weights, sigma_node) - beta_node * solution * solution * solution
    solution = start
    for iteration in range(CYCLES):
        resid = nonlinear_residual(solution)
        smooth_one = DAMPING * resid / diagonal
        smooth_two = smooth_one + DAMPING * (resid - apply_operator(jnp.pad(smooth_one, 1), weights, sigma_node)) / diagonal
        coarse = restrict_field(resid).astype(jnp.bfloat16)
        coarse = transform(coarse, table_y, 2).astype(jnp.bfloat16)
        coarse = transform(coarse, table_z, 1).astype(jnp.bfloat16)
        coarse = (transform(coarse, table_x, 0) / eigen_sum).astype(jnp.bfloat16)
        coarse = transform(coarse, table_x, 0).astype(jnp.bfloat16)
        coarse = transform(coarse, table_z, 1).astype(jnp.bfloat16)
        coarse = transform(coarse, table_y, 2).astype(jnp.bfloat16)
        solution = solution + smooth_two + prolong_field(coarse)
    return (solution, nonlinear_residual(solution))
```

```python
import functools
import math

import jax
import jax.numpy as jnp
import numpy as np
from jax import lax
from jax.experimental import pallas as pl
from jax.experimental.pallas import tpu as pltpu
from jax.sharding import PartitionSpec as P

CYCLES = 2
DAMPING = 0.6666666666666666
F32 = jnp.float32
BF16 = jnp.bfloat16
AXES = ("bx", "by", "bz")
VMEM_LIMIT = 32 * 1024 * 1024


def up_to(value, multiple):
    return -(-value // multiple) * multiple


class Plan:
    def __init__(self, shape, nx, ny, nz):
        self.X, self.Z, self.Y = shape
        self.nx, self.ny, self.nz = nx, ny, nz
        self.n = nx * ny * nz
        self.cx, self.cz, self.cy = self.X // 2, self.Z // 2, self.Y // 2
        self.NX, self.NZ, self.NY = self.cx * nx, self.cz * nz, self.cy * ny
        self.modes = -(-self.NY // self.n)
        self.NYp = self.modes * self.n
        self.lanes = self.cx * self.cz
        rows = (2 * self.Z, 2 * self.Z, 2 * self.X, 2 * self.X, self.Z, 12)
        self.heights = [-(-r // self.n) for r in rows]
        self.offsets = [sum(self.heights[:i]) for i in range(6)]
        halo = sum(self.heights)
        self.go_halo = self.modes
        self.go = up_to(self.modes + halo, 8)
        self.back_halo = 2 * self.modes
        self.back = up_to(2 * self.modes + halo, 8)
        self.edge_lane = 6 * self.X
        self.extra = 2 * self.cz + 2 * self.cx
        assert self.lanes <= self.Y and self.extra <= self.lanes and self.edge_lane + 8 <= self.Y
        assert self.heights[5] == 1


def sine_table(count):
    index_one = np.arange(1, count + 1, dtype=np.int32)
    product = (index_one[:, None] * index_one[None, :]).astype(np.float32)
    value = np.sin(product * np.float32(math.pi / (count + 1)))
    return (value * np.float32(math.sqrt(2.0 / (count + 1)))).astype(BF16).astype(np.float32)


def spectrum_values(count):
    return 2.0 - 2.0 * np.cos(np.arange(1, count + 1) * (math.pi / (count + 1)))


RESTRICT = np.array([[3, 2, 1, 0], [0, 1, 2, 3]], np.float32)
PROLONG = np.array([[3, 0], [2, 1], [1, 2], [0, 3]], np.float32)


def tables(p):
    rx = np.kron(np.eye(p.X // 4), RESTRICT)
    rz = np.kron(np.eye(p.Z // 4), RESTRICT)
    ry = np.kron(np.eye(p.Y // 4), RESTRICT)
    px = np.kron(np.eye(p.X // 4), PROLONG)
    pz = np.kron(np.eye(p.Z // 4), PROLONG)
    py = np.kron(np.eye(p.Y // 4), PROLONG)
    sx, sz, sy = sine_table(p.NX), sine_table(p.NZ), sine_table(p.NY)
    out = {}
    out["rxz"] = np.kron(rx, rz)
    out["ry"] = ry
    syt = np.zeros((p.ny, p.NYp, p.cy), np.float32)
    syp = np.zeros((p.ny, p.cy + 16, p.NYp), np.float32)
    padded = np.zeros((p.NY + 16, p.NYp), np.float32)
    padded[8 : 8 + p.NY, : p.NY] = sy
    for b in range(p.ny):
        syt[b, : p.NY] = sy[:, b * p.cy : (b + 1) * p.cy]
        syp[b] = padded[b * p.cy : (b + 1) * p.cy + 16]
    out["syt"], out["syp"] = syt, syp
    wz = np.zeros((p.cx, p.NZ, p.nz, p.cx, p.cz), np.float32)
    for x in range(p.cx):
        wz[x, :, :, x, :] = sz.reshape(p.NZ, p.nz, p.cz)
    out["wz"] = wz.reshape(p.cx * p.NZ, p.nz * p.lanes)
    wx = np.einsum("bxk,mn->xbmkn", sx.reshape(p.nx, p.cx, p.NX), np.eye(p.modes))
    wx = wx.reshape(p.NX * p.modes, p.NX * p.modes)
    out["wx"], out["wxt"] = wx, wx.T
    szp = np.zeros((p.NZ, p.NZ + 2), np.float32)
    szp[:, 1:-1] = sz
    wzi = np.zeros((p.nz, p.cx, p.NZ, 2 * p.lanes), np.float32)
    for b in range(p.nz):
        for x in range(p.cx):
            wzi[b, x, :, x * p.cz : (x + 1) * p.cz] = sz[:, b * p.cz : (b + 1) * p.cz]
            wzi[b, x, :, p.lanes + x] = szp[:, b * p.cz]
            wzi[b, x, :, p.lanes + p.cx + x] = szp[:, (b + 1) * p.cz + 1]
    out["wzi"] = wzi.reshape(p.nz, p.cx * p.NZ, 2 * p.lanes)
    out["pyt"] = py.T
    pall = np.zeros((p.X * p.Z + 2 * p.Z + 2 * p.X, 2 * p.lanes), np.float32)
    at = p.X * p.Z
    pall[:at, : p.lanes] = np.kron(px, pz)
    col = p.lanes
    for _ in range(2):
        pall[at : at + p.Z, col : col + p.cz] = 3 * pz
        at, col = at + p.Z, col + p.cz
    for _ in range(2):
        pall[at : at + p.X, col : col + p.cx] = 3 * px
        at, col = at + p.X, col + p.cx
    out["pall"] = pall
    out["pzl"] = np.tile(pz, (1, p.cx))
    pyh = np.zeros((2, p.lanes, p.Y), np.float32)
    spread = np.repeat(px.T, p.cz, axis=0)
    for side in range(2):
        pyh[side, :, side : 2 * p.X : 2] = 3 * spread
    out["pyh"] = pyh.reshape(2 * p.lanes, p.Y)
    out = {key: jnp.asarray(value.astype(BF16)) for key, value in out.items()}
    lam = spectrum_values(p.NX)[None, :, None] + spectrum_values(p.NZ)[:, None, None]
    out["lamxz"] = jnp.asarray(np.broadcast_to(lam, (p.NZ, p.NX, p.modes)).reshape(p.NZ, -1).astype(np.float32))
    lamy = np.zeros(p.NYp)
    lamy[: p.NY] = spectrum_values(p.NY)
    lamy = np.broadcast_to(lamy.reshape(p.n, 1, 1, p.modes), (p.n, 1, p.NX, p.modes))
    out["lamy"] = jnp.asarray(lamy.reshape(p.n, 1, -1).astype(np.float32))
    return out


def iota(shape, dim):
    return lax.broadcasted_iota(jnp.int32, shape, dim)


def dot(a, b, dims=((1,), (0,))):
    return lax.dot_general(a, b, (dims, ((), ())), preferred_element_type=F32)


def halves(value):
    high = value.astype(BF16)
    return high, (value - high.astype(F32)).astype(BF16)


def dot_wide_right(table, value, dims=((1,), (0,))):
    high, low = halves(value)
    return dot(table, high, dims) + dot(table, low, dims)


def dot_wide_left(value, table, dims=((1,), (0,))):
    high, low = halves(value)
    return dot(high, table, dims) + dot(low, table, dims)


def roll(value, shift, axis):
    size = value.shape[axis]
    shift = shift % size
    return value if shift == 0 else pltpu.roll(value, shift, axis)


def lookup(classes, coef_ref, row):
    total = jnp.zeros_like(classes)
    for k in range(coef_ref.shape[1]):
        total = jnp.where(classes == k + 1.0, coef_ref[row, k], total)
    return total


def col_faces(get, p):
    lane = iota((p.Z, p.Y), 1) // 2
    total = jnp.zeros((p.Z, p.Y), F32)
    for i in range(p.X):
        total = jnp.where(lane == i, roll(get(i), 2 * i + 1, 1), total)
    return total


def swap_lanes(value):
    even = iota(value.shape, 1) % 2 == 0
    return jnp.where(even, roll(value, -1, 1), roll(value, 1, 1))


def shifted(value, axis, before, after):
    size = value.shape[axis]
    at = iota(value.shape, axis)
    low = jnp.where(at == 0, before, roll(value, 1, axis))
    high = jnp.where(at == size - 1, after, roll(value, -1, axis))
    return low, high


def plane_weights(kap, row_m, row_p, col_m, col_p):
    up, down = shifted(kap, 0, row_m, row_p)
    left, right = shifted(kap, 1, col_m, col_p)
    row, lane = iota(kap.shape, 0) % 4, iota(kap.shape, 1) % 4
    return (
        jnp.where(row == 0, kap + up, kap),
        jnp.where(row == 3, kap + down, kap),
        jnp.where(lane == 0, kap + left, kap),
        jnp.where(lane == 3, kap + right, kap),
    )


KAP, WZM, WZP, WYM, WYP, BASE, BETA = range(7)


class Brick:
    def __init__(self, p, cst_ref, kap_xm, kap_xp):
        self.p, self.cst, self.kap_xm, self.kap_xp = p, cst_ref, kap_xm, kap_xp

    def of(self, quantity, i):
        return self.cst[quantity, i // 4]

    def x_weights(self, i):
        kap = self.of(KAP, i)
        low = high = kap
        if i % 4 == 0:
            low = kap + (self.of(KAP, i - 1) if i else self.kap_xm)
        if i % 4 == 3:
            high = kap + (self.of(KAP, i + 1) if i + 1 < self.p.X else self.kap_xp)
        return low, high

    def diagonal(self, i):
        low, high = self.x_weights(i)
        return self.of(BASE, i) + (low + high)

    def neighbours(self, i, get, halo=None):
        p, v = self.p, get(i)
        low, high = self.x_weights(i)
        total = jnp.zeros_like(v)
        if i:
            total = total + low * get(i - 1)
        elif halo is not None:
            total = total + low * halo[0]
        if i + 1 < p.X:
            total = total + high * get(i + 1)
        elif halo is not None:
            total = total + high * halo[1]
        if halo is None:
            ends = (0.0, 0.0, 0.0, 0.0)
        else:
            yh = halo[4]
            ends = (halo[2][i : i + 1], halo[3][i : i + 1], yh[:, 2 * i : 2 * i + 1], yh[:, 2 * i + 1 : 2 * i + 2])
        up, down = shifted(v, 0, ends[0], ends[1])
        left, right = shifted(v, 1, ends[2], ends[3])
        total = total + self.of(WZM, i) * up + self.of(WZP, i) * down
        return total + self.of(WYM, i) * left + self.of(WYP, i) * right

    def from_halo(self, i, halo):
        p = self.p
        row, lane = iota((p.Z, p.Y), 0), iota((p.Z, p.Y), 1)
        yh = halo[4]
        total = jnp.where(row == 0, self.of(WZM, i) * halo[2][i : i + 1], 0.0)
        total = jnp.where(row == p.Z - 1, self.of(WZP, i) * halo[3][i : i + 1], total)
        total = total + jnp.where(lane == 0, self.of(WYM, i) * yh[:, 2 * i : 2 * i + 1], 0.0)
        total = total + jnp.where(lane == p.Y - 1, self.of(WYP, i) * yh[:, 2 * i + 1 : 2 * i + 2], 0.0)
        if i == 0:
            total = total + self.x_weights(i)[0] * halo[0]
        if i == p.X - 1:
            total = total + self.x_weights(i)[1] * halo[1]
        return total


def residual_plane(brick, i, get, halo, f):
    v = get(i)
    return f - brick.diagonal(i) * v + brick.neighbours(i, get, halo) - brick.of(BETA, i) * v * v * v


def put_rows(ref, stride, offset, n, rows):
    height = -(-rows.shape[0] // n)
    if rows.shape[0] < height * n:
        rows = jnp.concatenate([rows, jnp.zeros((height * n - rows.shape[0], rows.shape[1]), F32)], axis=0)
    for k in range(height):
        ref[pl.ds(offset + k, n, stride=stride), :] = rows[k * n : (k + 1) * n]


def get_rows(ref, stride, offset, n, count):
    height = -(-count // n)
    parts = [ref[pl.ds(offset + k, n, stride=stride), :] for k in range(height)]
    value = parts[0] if height == 1 else jnp.concatenate(parts, axis=0)
    return value[:count]


class Bounds:
    def __init__(self, p):
        self.uxm, self.uxp = (0, p.Z), (p.Z, p.Z)
        self.uzm, self.uzp = (2 * p.Z, p.X), (2 * p.Z + p.X, p.X)
        self.uy = (2 * p.Z + 2 * p.X, p.Z)
        self.count = 3 * p.Z + 2 * p.X


def read(ref, span):
    return ref[span[0] : span[0] + span[1], :]


def write_bounds(ref, b, values):
    for span, value in zip((b.uxm, b.uxp, b.uzm, b.uzp, b.uy), values):
        ref[span[0] : span[0] + span[1], :] = value


def read_bounds(ref, b):
    return tuple(read(ref, span) for span in (b.uxm, b.uxp, b.uzm, b.uzp, b.uy))


def start_cycle(p, brick, get, halo, f_ref, classes, rxz, ry, syt, s_ref, z1b_ref, go_ref, r_scr, z_scr, z2_scr, go_scr):
    X, Z, n = p.X, p.Z, p.n
    for i in range(X):
        r = residual_plane(brick, i, get, halo, f_ref[i])
        r_scr[i * Z : (i + 1) * Z, :] = r
        z_scr[i] = r * (DAMPING / brick.diagonal(i))
    z1 = lambda i: z_scr[i]
    coarse = dot_wide_right(rxz[...], r_scr[...])
    coarse = dot_wide_right(ry[...], coarse, ((1,), (1,))) * (1.0 / 216.0)
    part = dot(syt[lax.axis_index("by")], coarse.astype(BF16))
    for j in range(n):
        go_scr[j * p.go : j * p.go + p.modes, :] = part[j * p.modes : (j + 1) * p.modes]
    for i in range(X):
        v = z1(i)
        smooth = (2.0 - DAMPING) * v + (DAMPING / brick.diagonal(i)) * brick.neighbours(i, z1)
        z2_scr[i] = smooth
        s_ref[i] = get(i) + smooth
    z2 = lambda i: z2_scr[i]
    z1_y, z2_y = col_faces(z1, p), col_faces(z2, p)
    z1_zm, z1_zp = z_scr[:, 0, :], z_scr[:, Z - 1, :]
    write_bounds(z1b_ref, Bounds(p), (z1(0), z1(X - 1), z1_zm, z1_zp, z1_y))
    lane = iota((Z, p.Y), 1)
    sides = jnp.where(lane < 2 * X, z1_y, roll(z2_y, 2 * X, 1))
    edges = [z_scr[0, 0:1, :], z_scr[0, Z - 1 : Z, :], z_scr[X - 1, 0:1, :], z_scr[X - 1, Z - 1 : Z, :]]
    edges += [z1_y[0:1], z1_y[Z - 1 : Z]]
    if classes is None:
        sides = jnp.where(lane < 4 * X, sides, 0.0)
    else:
        cls, cls_y = classes
        sides = jnp.where(lane < 4 * X, sides, roll(cls_y, 4 * X, 1))
        sides = jnp.where(lane < 6 * X, sides, 0.0)
        edges += [cls(0)[0:1], cls(0)[Z - 1 : Z], cls(X - 1)[0:1], cls(X - 1)[Z - 1 : Z]]
        edges += [cls_y[0:1], cls_y[Z - 1 : Z]]
    pieces = (
        jnp.concatenate([z1(0), z2(0)], axis=0),
        jnp.concatenate([z1(X - 1), z2(X - 1)], axis=0),
        jnp.concatenate([z1_zm, z2_scr[:, 0, :]], axis=0),
        jnp.concatenate([z1_zp, z2_scr[:, Z - 1, :]], axis=0),
        sides,
        jnp.concatenate(edges, axis=0),
    )
    for piece, offset in zip(pieces, p.offsets):
        put_rows(go_scr, p.go, p.go_halo + offset, n, piece)
    used = p.go_halo + sum(p.heights)
    for k in range(used, p.go):
        go_scr[pl.ds(k, n, stride=p.go), :] = jnp.zeros((n, p.Y), F32)
    go_ref[...] = go_scr[...].astype(BF16)


def pack_kernel(p, index_ref, u_ref, cls_ref, xa_ref, xb_ref, za_ref, zb_ref, y_ref):
    X, Z, Y = p.X, p.Z, p.Y
    spread_z = (iota((Z, Z // 4), 0) // 4 == iota((Z, Z // 4), 1)).astype(BF16)
    spread_y = (iota((Y // 4, Y), 1) // 4 == iota((Y // 4, Y), 0)).astype(BF16)
    for a in range(X // 4):
        element = (index_ref[a] + 1).astype(F32).astype(BF16)
        cls_ref[a] = dot(dot(spread_z, element).astype(BF16), spread_y)
    u = lambda i: u_ref[i]
    cls = lambda i: cls_ref[i // 4]

    def face(axis, low, high, a_ref, b_ref):
        even = lax.axis_index(axis) % 2 == 0
        a_ref[...] = jnp.where(even, high, low)
        b_ref[...] = jnp.where(even, low, high)

    face(
        "bx",
        jnp.concatenate([u(0), cls(0)], axis=0),
        jnp.concatenate([u(X - 1), cls(X - 1)], axis=0),
        xa_ref,
        xb_ref,
    )
    rows = lambda z: jnp.concatenate([cls(i)[z : z + 1] for i in range(X)], axis=0)
    face(
        "bz",
        jnp.concatenate([u_ref[:, 0, :], rows(0)], axis=0),
        jnp.concatenate([u_ref[:, Z - 1, :], rows(Z - 1)], axis=0),
        za_ref,
        zb_ref,
    )
    y_ref[...] = jnp.concatenate([col_faces(u, p), col_faces(cls, p)], axis=0)


def received(axis, count, a_ref, b_ref):
    at = lax.axis_index(axis)
    even = at % 2 == 0
    a, b = a_ref[...], b_ref[...]
    low = jnp.where(even, b, a)
    high = jnp.where(even, a, b)
    return jnp.where(at > 0, low, 0.0), jnp.where(at < count - 1, high, 0.0)


def first_kernel(p, coef, u_ref, f_ref, cls_ref, xa, xb, za, zb, ya, yb, rxz, ry, syt,
                 go_ref, s_ref, z1b_ref, uhb_ref, clsb_ref, cst_ref, r_scr, z_scr, z2_scr, go_scr):
    X, Z, b = p.X, p.Z, Bounds(p)
    xm, xp = received("bx", p.nx, xa, xb)
    zm, zp = received("bz", p.nz, za, zb)
    ym, yp = received("by", p.ny, ya, yb)
    y = jnp.where(iota(ym.shape, 1) % 2 == 0, ym, yp)
    halo = (xm[:Z], xp[:Z], zm[:X], zp[:X], y[:Z])
    outside = (xm[Z:], xp[Z:], zm[X:], zp[X:], y[Z:])
    write_bounds(uhb_ref, b, halo)
    write_bounds(clsb_ref, b, outside)
    kap_h = tuple(lookup(value, coef, 0) for value in outside)
    for a in range(X // 4):
        kap = lookup(cls_ref[a], coef, 0)
        i = 4 * a
        wzm, wzp, wym, wyp = plane_weights(
            kap, kap_h[2][i : i + 1], kap_h[3][i : i + 1], kap_h[4][:, 2 * i : 2 * i + 1], kap_h[4][:, 2 * i + 1 : 2 * i + 2]
        )
        cst_ref[KAP, a] = kap
        cst_ref[WZM, a] = wzm
        cst_ref[WZP, a] = wzp
        cst_ref[WYM, a] = wym
        cst_ref[WYP, a] = wyp
        cst_ref[BASE, a] = lookup(cls_ref[a], coef, 1) + ((wzm + wzp) + (wym + wyp))
        cst_ref[BETA, a] = lookup(cls_ref[a], coef, 2)
    brick = Brick(p, cst_ref, kap_h[0], kap_h[1])
    cls = lambda i: cls_ref[i // 4]
    start_cycle(p, brick, lambda i: u_ref[i], halo, f_ref, (cls, col_faces(cls, p)), rxz, ry, syt,
                s_ref, z1b_ref, go_ref, r_scr, z_scr, z2_scr, go_scr)


def owner_kernel(p, coef, in_ref, wz, wx, wxt, wzi, lamxz, lamy, out_ref, in_scr, out_scr):
    n, m, nx, ny, nz = p.n, p.modes, p.nx, p.ny, p.nz
    me = (lax.axis_index("bx") * ny + lax.axis_index("by")) * nz + lax.axis_index("bz")
    in_scr[...] = in_ref[...].astype(F32)
    rows = []
    for bx in range(nx):
        lanes = []
        for bz in range(nz):
            total = None
            for by in range(ny):
                at = ((bx * ny + by) * nz + bz) * p.go
                piece = in_scr[at : at + m, :]
                total = piece if total is None else total + piece
            lanes.append(total)
        rows.append(jnp.concatenate(lanes, axis=1))
    data = jnp.concatenate(rows, axis=0)
    data = dot_wide_right(wz[...], data, ((1,), (1,)))
    data = jnp.concatenate([data[x * p.NZ : (x + 1) * p.NZ] for x in range(p.cx)], axis=1)
    data = dot_wide_left(data, wx[...])
    classes = coef.shape[1]
    kap_mean = sum(coef[0, k] for k in range(classes)) * (1.0 / classes)
    sig_mean = sum(coef[1, k] for k in range(classes)) * (1.0 / classes)
    data = data / (kap_mean * (lamxz[...] + lamy[me]) + sig_mean)
    data = dot_wide_left(data, wxt[...])
    width = nx * m
    data = jnp.concatenate([data[:, x * width : (x + 1) * width] for x in range(p.cx)], axis=0)
    high, low = halves(data)
    high, low = high.T, low.T
    lane = iota((m, p.Y), 1)
    for bz in range(nz):
        back = dot(high, wzi[bz]) + dot(low, wzi[bz])
        core = lambda bx: back[bx * m : (bx + 1) * m, : p.lanes]
        for bx in range(nx):
            ends = roll(back[bx * m : (bx + 1) * m, p.lanes :], 2 * p.cz, 1)
            below = roll(core(bx - 1), p.cz - p.lanes, 1) if bx else jnp.zeros((m, p.lanes), F32)
            above = roll(core(bx + 1), p.cz, 1) if bx + 1 < nx else jnp.zeros((m, p.lanes), F32)
            extra = jnp.where(lane < p.cz, below, jnp.where(lane < 2 * p.cz, above, ends))
            mine = core(bx)
            for by in range(ny):
                at = ((bx * ny + by) * nz + bz) * p.back
                out_scr[at : at + m, :] = mine
                out_scr[at + m : at + 2 * m, :] = extra

    device = iota((n, p.Y), 0)
    at_x, at_y, at_z = device // (ny * nz), (device // nz) % ny, device % nz

    def shift(value, dx, dy, dz):
        value = roll(value, -((dx * ny + dy) * nz + dz), 0)
        for at, step, count in ((at_x, dx, nx), (at_y, dy, ny), (at_z, dz, nz)):
            if step:
                value = jnp.where((at + step >= 0) & (at + step < count), value, 0.0)
        return value

    def take(k):
        return in_scr[pl.ds(p.go_halo + k, n, stride=p.go), :]

    def give(k, value):
        out_scr[pl.ds(p.back_halo + k, n, stride=p.back), :] = value

    for to, source, step in ((0, 1, (-1, 0, 0)), (1, 0, (1, 0, 0)), (2, 3, (0, 0, -1)), (3, 2, (0, 0, 1))):
        for k in range(p.heights[to]):
            give(p.offsets[to] + k, shift(take(p.offsets[source] + k), *step))
    lane = iota((n, p.Y), 1)
    even = lane % 2 == 0
    first, X2 = p.edge_lane, 2 * p.X
    for k in range(p.heights[4]):
        sides = take(p.offsets[4] + k)
        moved = jnp.where(lane < first + 2, roll(sides, first, 1), roll(sides, first + 2 - (X2 - 2), 1))
        moved = jnp.where(lane < first + 4, moved, roll(sides, first + 4 - 2 * X2, 1))
        moved = jnp.where(lane < first + 6, moved, roll(sides, first + 6 - (3 * X2 - 2), 1))
        which = (lane - first) % 4
        corner = jnp.where(
            which < 2,
            jnp.where(even, shift(moved, 1, -1, 0), shift(moved, 1, 1, 0)),
            jnp.where(even, shift(moved, -1, -1, 0), shift(moved, -1, 1, 0)),
        )
        plain = jnp.where(even, shift(sides, 0, -1, 0), shift(sides, 0, 1, 0))
        give(p.offsets[4] + k, jnp.where(lane < first, plain, jnp.where(lane < first + 8, corner, 0.0)))
    edges = take(p.offsets[5])
    kind = me % 6
    moved = jnp.where(even, shift(edges, 0, -1, -1), shift(edges, 0, 1, -1))
    for k, value in (
        (0, lambda: shift(edges, 1, 0, 1)),
        (1, lambda: shift(edges, 1, 0, -1)),
        (2, lambda: shift(edges, -1, 0, 1)),
        (3, lambda: shift(edges, -1, 0, -1)),
        (4, lambda: jnp.where(even, shift(edges, 0, -1, 1), shift(edges, 0, 1, 1))),
    ):
        moved = jnp.where(kind == k, value(), moved)
    give(p.offsets[5], moved)
    used = p.back_halo + sum(p.heights)
    for k in range(used, p.back):
        out_scr[pl.ds(k, n, stride=p.back), :] = jnp.zeros((n, p.Y), F32)
    out_ref[...] = out_scr[...].astype(BF16)


class Arrived:
    def __init__(self, p, ref):
        X, Z = p.X, p.Z
        rows = (2 * Z, 2 * Z, 2 * X, 2 * X, Z, 12)
        xm, xp, zm, zp, sides, edges = (
            get_rows(ref, p.back, p.back_halo + offset, p.n, count) for offset, count in zip(p.offsets, rows)
        )
        self.p, self.ref, self.sides, self.edges = p, ref, sides, edges
        self.z1 = (xm[:Z], xp[:Z], zm[:X], zp[:X], sides)
        self.z2 = (xm[Z:], xp[Z:], zm[X:], zp[X:], roll(sides, -2 * X, 1))

    def xz(self, kind, sx, sz):
        k = 6 * kind + (0 if sx else 2) + (0 if sz else 1)
        return self.edges[k : k + 1]

    def zy(self, kind, sz):
        k = 6 * kind + (4 if sz else 5)
        return self.edges[k : k + 1]

    def xy(self, kind, sx, sy):
        lane = self.p.edge_lane + 4 * kind + (0 if sx else 2) + sy
        return self.sides[:, lane : lane + 1]

    def xy_lanes(self, kind, plain):
        first, X2 = self.p.edge_lane + 4 * kind, 2 * self.p.X
        lane = iota(plain.shape, 1)
        value = jnp.where(lane < X2, plain, roll(self.sides, X2 - first, 1))
        return jnp.where(lane >= self.p.Y - 2, roll(self.sides, self.p.Y - 2 - first - 2, 1), value)


def coarse_rows(p, ref, syp, pyt, pall, pzl, pyh):
    n, m = p.n, p.modes
    core = jnp.concatenate([ref[j * p.back : j * p.back + m, :] for j in range(n)], axis=0)
    extra = jnp.concatenate([ref[j * p.back + m : j * p.back + 2 * m, :] for j in range(n)], axis=0)
    modes = jnp.concatenate([core, extra], axis=1).astype(BF16)
    values = dot(syp[lax.axis_index("by")], modes).astype(BF16)
    along = dot(values[8 : 8 + p.cy].T, pyt[...])
    nodes = dot_wide_right(pall[...], along) * (1.0 / 27.0)
    weights = pzl[...].astype(F32)
    ends = [weights * values.astype(F32)[k : k + 1, : p.lanes] for k in (7, 8 + p.cy)]
    side = dot_wide_left(jnp.concatenate(ends, axis=1), pyh[...]) * (1.0 / 27.0)
    return nodes, side


def column(row, count, side):
    shape = (count, row.shape[1])
    pick = iota(shape, 1) == 2 * iota(shape, 0) + side
    return jnp.sum(jnp.where(pick, row, 0.0), axis=1, keepdims=True)


def finish_cycle(p, coef, brick, now, first, s_ref, z1b_ref, uhb_ref, clsb_ref, nodes, side, u_ref):
    X, Z, b = p.X, p.Z, Bounds(p)
    for i in range(X):
        u_ref[i] = s_ref[i] + (DAMPING / brick.diagonal(i)) * brick.from_halo(i, now.z1) + nodes[i * Z : (i + 1) * Z]
    old, cls, own = read_bounds(uhb_ref, b), read_bounds(clsb_ref, b), read_bounds(z1b_ref, b)
    kap = lambda value: lookup(value, coef, 0)
    halo = []

    def new(k, weights, toward, others, correction):
        kap_here = kap(cls[k])
        diagonal = lookup(cls[k], coef, 1) + (kap_here + toward) + ((weights[0] + weights[1]) + (weights[2] + weights[3]))
        total = toward * own_faces[k]
        for part in others:
            total = total + part
        value = old[k] + now.z2[k] + (DAMPING / diagonal) * total + correction
        halo.append(jnp.where(cls[k] > 0.5, value, 0.0))

    own_faces = list(own[:4]) + [swap_lanes(own[4])]
    at = X * Z
    for k in range(2):
        kap_here = kap(cls[k])
        row_m, row_p = kap(first.xz(1, k, 0)), kap(first.xz(1, k, 1))
        col_m, col_p = kap(first.xy(1, k, 0)), kap(first.xy(1, k, 1))
        w = plane_weights(kap_here, row_m, row_p, col_m, col_p)
        row, lane = iota((Z, p.Y), 0), iota((Z, p.Y), 1)
        others = (
            jnp.where(row == 0, w[0] * now.xz(0, k, 0), 0.0),
            jnp.where(row == Z - 1, w[1] * now.xz(0, k, 1), 0.0),
            jnp.where(lane == 0, w[2] * now.xy(0, k, 0), 0.0),
            jnp.where(lane == p.Y - 1, w[3] * now.xy(0, k, 1), 0.0),
        )
        toward = kap_here + brick.of(KAP, 0 if k == 0 else X - 1)
        new(k, w, toward, others, nodes[at : at + Z])
        at += Z
    for k in range(2):
        kap_here = kap(cls[2 + k])
        row_m, row_p = kap(first.xz(1, 0, k)), kap(first.xz(1, 1, k))
        col_m, col_p = (kap(column(first.zy(1, k), X, side_y)) for side_y in range(2))
        w = plane_weights(kap_here, row_m, row_p, col_m, col_p)
        row, lane = iota((X, p.Y), 0), iota((X, p.Y), 1)
        others = (
            jnp.where(row == 0, w[0] * now.xz(0, 0, k), 0.0),
            jnp.where(row == X - 1, w[1] * now.xz(0, 1, k), 0.0),
            jnp.where(lane == 0, w[2] * column(now.zy(0, k), X, 0), 0.0),
            jnp.where(lane == p.Y - 1, w[3] * column(now.zy(0, k), X, 1), 0.0),
        )
        z = 0 if k == 0 else Z - 1
        mine = jnp.concatenate([brick.of(KAP, i)[z : z + 1] for i in range(X)], axis=0)
        new(2 + k, w, kap_here + mine, others, nodes[at : at + X])
        at += X
    wide = kap(first.xy_lanes(1, cls[4]))
    z1_wide = now.xy_lanes(0, now.z1[4])
    row_m, row_p = kap(first.zy(1, 0)), kap(first.zy(1, 1))
    up, down = shifted(wide, 0, row_m, row_p)
    left, right = roll(wide, 2, 1), roll(wide, -2, 1)
    row, lane = iota((Z, p.Y), 0), iota((Z, p.Y), 1)
    w = (
        jnp.where(row % 4 == 0, wide + up, wide),
        jnp.where(row % 4 == 3, wide + down, wide),
        jnp.where((lane // 2) % 4 == 0, wide + left, wide),
        jnp.where((lane // 2) % 4 == 3, wide + right, wide),
    )
    others = (
        jnp.where(row == 0, w[0] * now.zy(0, 0), 0.0),
        jnp.where(row == Z - 1, w[1] * now.zy(0, 1), 0.0),
        jnp.where(lane // 2 == 0, w[2] * roll(z1_wide, 2, 1), 0.0),
        jnp.where(lane // 2 == X - 1, w[3] * roll(z1_wide, -2, 1), 0.0),
    )
    mine = swap_lanes(col_faces(lambda i: brick.of(KAP, i), p))
    new(4, w, wide + mine, others, side)
    return tuple(halo)


def middle_kernel(p, coef, in_ref, f_ref, s_ref, z1b_ref, uhb_ref, clsb_ref, cst_ref,
                  syp, pyt, pall, pzl, pyh, rxz, ry, syt,
                  go_ref, s_out, z1b_out, uhb_out, in_scr, u_scr, r_scr, z_scr, z2_scr, go_scr):
    in_scr[...] = in_ref[...].astype(F32)
    b = Bounds(p)
    outside = read_bounds(clsb_ref, b)
    brick = Brick(p, cst_ref, lookup(outside[0], coef, 0), lookup(outside[1], coef, 0))
    now = Arrived(p, in_scr)
    nodes, side = coarse_rows(p, in_scr, syp, pyt, pall, pzl, pyh)
    halo = finish_cycle(p, coef, brick, now, now, s_ref, z1b_ref, uhb_ref, clsb_ref, nodes, side, u_scr)
    write_bounds(uhb_out, b, halo)
    start_cycle(p, brick, lambda i: u_scr[i], halo, f_ref, None, rxz, ry, syt,
                s_out, z1b_out, go_ref, r_scr, z_scr, z2_scr, go_scr)


def last_kernel(p, coef, in_ref, first_ref, f_ref, s_ref, z1b_ref, uhb_ref, clsb_ref, cst_ref,
                syp, pyt, pall, pzl, pyh, u_out, r_out, in_scr, first_scr):
    in_scr[...] = in_ref[...].astype(F32)
    first_scr[...] = first_ref[...].astype(F32)
    outside = read_bounds(clsb_ref, Bounds(p))
    brick = Brick(p, cst_ref, lookup(outside[0], coef, 0), lookup(outside[1], coef, 0))
    now, first = Arrived(p, in_scr), Arrived(p, first_scr)
    nodes, side = coarse_rows(p, in_scr, syp, pyt, pall, pzl, pyh)
    halo = finish_cycle(p, coef, brick, now, first, s_ref, z1b_ref, uhb_ref, clsb_ref, nodes, side, u_out)
    for i in range(p.X):
        r_out[i] = residual_plane(brick, i, lambda k: u_out[k], halo, f_ref[i])


def call(kernel, p, name, coef, inputs, outputs, scratch):
    smem = [pl.BlockSpec(memory_space=pltpu.SMEM)] if coef is not None else []
    args = ([coef] if coef is not None else []) + list(inputs)
    return pl.pallas_call(
        functools.partial(kernel, p),
        out_shape=[jax.ShapeDtypeStruct(shape, dtype) for shape, dtype in outputs],
        in_specs=smem + [pl.BlockSpec(memory_space=pltpu.VMEM)] * len(inputs),
        out_specs=[pl.BlockSpec(memory_space=pltpu.VMEM)] * len(outputs),
        scratch_shapes=[pltpu.VMEM(shape, F32) for shape in scratch],
        compiler_params=pltpu.CompilerParams(vmem_limit_bytes=VMEM_LIMIT),
        name=name,
    )(*args)


def swaps(axis, count, a, b):
    if count == 1:
        return a, b
    assert count % 2 == 0
    first = lax.ppermute(a, axis, [(i, i ^ 1) for i in range(count)])
    if count == 2:
        return first, first
    other = lambda i: (i + 1 if i % 2 else i - 1) % count
    return first, lax.ppermute(b, axis, [(i, other(i)) for i in range(count)])


def body(forcing, start, element_class_index, class_coef):
    p = Plan(start.shape, *(lax.axis_size(axis) for axis in AXES))
    t = tables(p)
    X, Z, Y, n = p.X, p.Z, p.Y, p.n
    bounds = Bounds(p).count
    block, flat, cst = (X, Z, Y), (X * Z, Y), (7, X // 4, Z, Y)
    cls, xa, xb, za, zb, yf = call(
        pack_kernel, p, "pack_faces", None, (element_class_index, start),
        [((X // 4, Z, Y), F32)] + [((2 * Z, Y), F32)] * 2 + [((2 * X, Y), F32)] * 2 + [((2 * Z, Y), F32)], [],
    )
    xa, xb = swaps("bx", p.nx, xa, xb)
    za, zb = swaps("bz", p.nz, za, zb)
    ya, yb = swaps("by", p.ny, yf, yf)
    go_shape, back_shape = (n * p.go, Y), (n * p.back, Y)
    starting = [flat, block, block, go_shape]
    restrict = (t["rxz"], t["ry"], t["syt"])
    prolong = (t["syp"], t["pyt"], t["pall"], t["pzl"], t["pyh"])
    go, s, z1b, uhb, clsb, coefs = call(
        first_kernel, p, "first_residual", class_coef,
        (start, forcing, cls, xa, xb, za, zb, ya, yb) + restrict,
        [(go_shape, BF16), (block, F32), ((bounds, Y), F32), ((bounds, Y), F32), ((bounds, Y), F32), (cst, F32)],
        starting,
    )
    first = None
    for cycle in range(CYCLES):
        came = lax.all_to_all(go, AXES, split_axis=0, concat_axis=0, tiled=True)
        (out,) = call(
            owner_kernel, p, "owned_modes", class_coef,
            (came, t["wz"], t["wx"], t["wxt"], t["wzi"], t["lamxz"], t["lamy"]),
            [(back_shape, BF16)], [go_shape, back_shape],
        )
        back = lax.all_to_all(out, AXES, split_axis=0, concat_axis=0, tiled=True)
        if cycle + 1 < CYCLES:
            assert first is None
            first = back
            go, s, z1b, uhb = call(
                middle_kernel, p, "next_residual", class_coef,
                (back, forcing, s, z1b, uhb, clsb, coefs) + prolong + restrict,
                [(go_shape, BF16), (block, F32), ((bounds, Y), F32), ((bounds, Y), F32)],
                [back_shape, block] + starting,
            )
        else:
            return tuple(call(
                last_kernel, p, "last_residual", class_coef,
                (back, first, forcing, s, z1b, uhb, clsb, coefs) + prolong,
                [(block, F32), (block, F32)], [back_shape, back_shape],
            ))


def solution(mesh):
    spec = P("bx", "bz", "by")
    return jax.shard_map(body, mesh=mesh, in_specs=(spec, spec, spec, P()), out_specs=(spec, spec), check_vma=False)
```

```python
import functools
import math

import jax
import jax.numpy as jnp
import numpy as np
from jax import lax
from jax.experimental import pallas as pl
from jax.experimental.pallas import tpu as pltpu
from jax.sharding import PartitionSpec as P

CYCLES = 2
DAMPING = 0.6666666666666666
F32 = jnp.float32
BF16 = jnp.bfloat16
AXES = ("bx", "by", "bz")
VMEM_LIMIT = 32 * 1024 * 1024


def up_to(value, multiple):
    return -(-value // multiple) * multiple


class Plan:
    def __init__(self, shape, nx, ny, nz):
        self.X, self.Z, self.Y = shape
        self.nx, self.ny, self.nz = nx, ny, nz
        self.n = nx * ny * nz
        self.cx, self.cz, self.cy = self.X // 2, self.Z // 2, self.Y // 2
        self.NX, self.NZ, self.NY = self.cx * nx, self.cz * nz, self.cy * ny
        self.modes = -(-self.NY // self.n)
        self.NYp = self.modes * self.n
        self.lanes = self.cx * self.cz
        rows = (2 * self.Z, 2 * self.Z, 2 * self.X, 2 * self.X, self.Z, 12)
        self.heights = [-(-r // self.n) for r in rows]
        self.offsets = [sum(self.heights[:i]) for i in range(6)]
        halo = sum(self.heights)
        self.go_halo = self.modes
        self.go = up_to(self.modes + halo, 8)
        self.back_halo = 2 * self.modes
        self.back = up_to(2 * self.modes + halo, 8)
        self.edge_lane = 6 * self.X
        self.extra = 2 * self.cz + 2 * self.cx
        assert self.lanes <= self.Y and self.extra <= self.lanes and self.edge_lane + 8 <= self.Y
        assert self.heights[5] == 1


def sine_table(count):
    index_one = np.arange(1, count + 1, dtype=np.int32)
    product = (index_one[:, None] * index_one[None, :]).astype(np.float32)
    value = np.sin(product * np.float32(math.pi / (count + 1)))
    return (value * np.float32(math.sqrt(2.0 / (count + 1)))).astype(BF16).astype(np.float32)


def spectrum_values(count):
    return 2.0 - 2.0 * np.cos(np.arange(1, count + 1) * (math.pi / (count + 1)))


RESTRICT = np.array([[3, 2, 1, 0], [0, 1, 2, 3]], np.float32)
PROLONG = np.array([[3, 0], [2, 1], [1, 2], [0, 3]], np.float32)


def tables(p):
    rx = np.kron(np.eye(p.X // 4), RESTRICT)
    rz = np.kron(np.eye(p.Z // 4), RESTRICT)
    ry = np.kron(np.eye(p.Y // 4), RESTRICT)
    px = np.kron(np.eye(p.X // 4), PROLONG)
    pz = np.kron(np.eye(p.Z // 4), PROLONG)
    py = np.kron(np.eye(p.Y // 4), PROLONG)
    sx, sz, sy = sine_table(p.NX), sine_table(p.NZ), sine_table(p.NY)
    out = {}
    out["rxz"] = np.kron(rx, rz)
    out["ry"] = ry
    padded = np.zeros((p.NY + 16, p.NYp), np.float32)
    padded[8 : 8 + p.NY, : p.NY] = sy
    out["sy"] = padded
    wz = np.zeros((p.cx, p.NZ, p.nz, p.cx, p.cz), np.float32)
    for x in range(p.cx):
        wz[x, :, :, x, :] = sz.reshape(p.NZ, p.nz, p.cz)
    out["wz"] = wz.reshape(p.cx * p.NZ, p.nz * p.lanes)
    wx = np.einsum("bxk,mn->xbmkn", sx.reshape(p.nx, p.cx, p.NX), np.eye(p.modes))
    wx = wx.reshape(p.NX * p.modes, p.NX * p.modes)
    out["wx"], out["wxt"] = wx, wx.T
    szp = np.zeros((p.NZ, p.NZ + 2), np.float32)
    szp[:, 1:-1] = sz
    wzi = np.zeros((p.nz, p.cx, p.NZ, 2 * p.lanes), np.float32)
    for b in range(p.nz):
        for x in range(p.cx):
            wzi[b, x, :, x * p.cz : (x + 1) * p.cz] = sz[:, b * p.cz : (b + 1) * p.cz]
            wzi[b, x, :, p.lanes + x] = szp[:, b * p.cz]
            wzi[b, x, :, p.lanes + p.cx + x] = szp[:, (b + 1) * p.cz + 1]
    out["wzi"] = wzi.reshape(p.nz, p.cx * p.NZ, 2 * p.lanes)
    out["pyt"] = py.T
    pall = np.zeros((p.X * p.Z + 2 * p.Z + 2 * p.X, 2 * p.lanes), np.float32)
    at = p.X * p.Z
    pall[:at, : p.lanes] = np.kron(px, pz)
    col = p.lanes
    for _ in range(2):
        pall[at : at + p.Z, col : col + p.cz] = 3 * pz
        at, col = at + p.Z, col + p.cz
    for _ in range(2):
        pall[at : at + p.X, col : col + p.cx] = 3 * px
        at, col = at + p.X, col + p.cx
    out["pall"] = np.concatenate([pall, np.tile(pz, (1, 2 * p.cx))])
    pyh = np.zeros((2, p.lanes, p.Y), np.float32)
    spread = np.repeat(px.T, p.cz, axis=0)
    for side in range(2):
        pyh[side, :, side : 2 * p.X : 2] = 3 * spread
    out["pyh"] = pyh.reshape(2 * p.lanes, p.Y)
    out = {key: jnp.asarray(value.astype(BF16)) for key, value in out.items()}
    lam = spectrum_values(p.NX)[None, :, None] + spectrum_values(p.NZ)[:, None, None]
    out["lamxz"] = jnp.asarray(np.broadcast_to(lam, (p.NZ, p.NX, p.modes)).reshape(p.NZ, -1).astype(np.float32))
    lamy = np.zeros(p.NYp)
    lamy[: p.NY] = spectrum_values(p.NY)
    lamy = np.broadcast_to(lamy.reshape(p.n, 1, 1, p.modes), (p.n, 1, p.NX, p.modes))
    out["lamy"] = jnp.asarray(lamy.reshape(p.n, 1, -1).astype(np.float32))
    return out


def iota(shape, dim):
    return lax.broadcasted_iota(jnp.int32, shape, dim)


def dot(a, b, dims=((1,), (0,))):
    return lax.dot_general(a, b, (dims, ((), ())), preferred_element_type=F32)


def halves(value):
    high = value.astype(BF16)
    return high, (value - high.astype(F32)).astype(BF16)


def dot_wide_right(table, value, dims=((1,), (0,))):
    high, low = halves(value)
    return dot(table, high, dims) + dot(table, low, dims)


def dot_wide_left(value, table, dims=((1,), (0,))):
    high, low = halves(value)
    return dot(high, table, dims) + dot(low, table, dims)


def roll(value, shift, axis):
    size = value.shape[axis]
    shift = shift % size
    return value if shift == 0 else pltpu.roll(value, shift, axis)


def lookup(classes, coef_ref, row):
    total = jnp.zeros_like(classes)
    for k in range(coef_ref.shape[1]):
        total = jnp.where(classes == k + 1.0, coef_ref[row, k], total)
    return total


def col_faces(get, p):
    lane = iota((p.Z, p.Y), 1) // 2
    total = jnp.zeros((p.Z, p.Y), F32)
    for i in range(p.X):
        total = jnp.where(lane == i, roll(get(i), 2 * i + 1, 1), total)
    return total


def swap_lanes(value):
    even = iota(value.shape, 1) % 2 == 0
    return jnp.where(even, roll(value, -1, 1), roll(value, 1, 1))


def shifted(value, axis, before, after):
    size = value.shape[axis]
    at = iota(value.shape, axis)
    low = jnp.where(at == 0, before, roll(value, 1, axis))
    high = jnp.where(at == size - 1, after, roll(value, -1, axis))
    return low, high


def plane_weights(kap, row_m, row_p, col_m, col_p):
    up, down = shifted(kap, 0, row_m, row_p)
    left, right = shifted(kap, 1, col_m, col_p)
    row, lane = iota(kap.shape, 0) % 4, iota(kap.shape, 1) % 4
    return (
        jnp.where(row == 0, kap + up, kap),
        jnp.where(row == 3, kap + down, kap),
        jnp.where(lane == 0, kap + left, kap),
        jnp.where(lane == 3, kap + right, kap),
    )


KAP, WZM, WZP, WYM, WYP, BASE, BETA = range(7)


class Brick:
    def __init__(self, p, cst_ref, kap_xm, kap_xp):
        self.p, self.cst, self.kap_xm, self.kap_xp = p, cst_ref, kap_xm, kap_xp

    def of(self, quantity, i):
        return self.cst[quantity, i // 4]

    def x_weights(self, i):
        kap = self.of(KAP, i)
        low = high = kap
        if i % 4 == 0:
            low = kap + (self.of(KAP, i - 1) if i else self.kap_xm)
        if i % 4 == 3:
            high = kap + (self.of(KAP, i + 1) if i + 1 < self.p.X else self.kap_xp)
        return low, high

    def diagonal(self, i):
        low, high = self.x_weights(i)
        return self.of(BASE, i) + (low + high)

    def neighbours(self, i, get, halo=None):
        p, v = self.p, get(i)
        low, high = self.x_weights(i)
        total = jnp.zeros_like(v)
        if i:
            total = total + low * get(i - 1)
        elif halo is not None:
            total = total + low * halo[0]
        if i + 1 < p.X:
            total = total + high * get(i + 1)
        elif halo is not None:
            total = total + high * halo[1]
        if halo is None:
            ends = (0.0, 0.0, 0.0, 0.0)
        else:
            yh = halo[4]
            ends = (halo[2][i : i + 1], halo[3][i : i + 1], yh[:, 2 * i : 2 * i + 1], yh[:, 2 * i + 1 : 2 * i + 2])
        up, down = shifted(v, 0, ends[0], ends[1])
        left, right = shifted(v, 1, ends[2], ends[3])
        total = total + self.of(WZM, i) * up + self.of(WZP, i) * down
        return total + self.of(WYM, i) * left + self.of(WYP, i) * right

    def from_halo(self, i, halo):
        p = self.p
        row, lane = iota((p.Z, p.Y), 0), iota((p.Z, p.Y), 1)
        yh = halo[4]
        total = jnp.where(row == 0, self.of(WZM, i) * halo[2][i : i + 1], 0.0)
        total = jnp.where(row == p.Z - 1, self.of(WZP, i) * halo[3][i : i + 1], total)
        total = total + jnp.where(lane == 0, self.of(WYM, i) * yh[:, 2 * i : 2 * i + 1], 0.0)
        total = total + jnp.where(lane == p.Y - 1, self.of(WYP, i) * yh[:, 2 * i + 1 : 2 * i + 2], 0.0)
        if i == 0:
            total = total + self.x_weights(i)[0] * halo[0]
        if i == p.X - 1:
            total = total + self.x_weights(i)[1] * halo[1]
        return total


def residual_plane(brick, i, get, halo, f):
    v = get(i)
    return f - brick.diagonal(i) * v + brick.neighbours(i, get, halo) - brick.of(BETA, i) * v * v * v


def put_rows(ref, stride, offset, n, rows):
    height = -(-rows.shape[0] // n)
    if rows.shape[0] < height * n:
        rows = jnp.concatenate([rows, jnp.zeros((height * n - rows.shape[0], rows.shape[1]), F32)], axis=0)
    for k in range(height):
        ref[pl.ds(offset + k, n, stride=stride), :] = rows[k * n : (k + 1) * n]


def get_rows(ref, stride, offset, n, count):
    height = -(-count // n)
    parts = [ref[pl.ds(offset + k, n, stride=stride), :] for k in range(height)]
    value = parts[0] if height == 1 else jnp.concatenate(parts, axis=0)
    return value[:count]


class Bounds:
    def __init__(self, p):
        self.uxm, self.uxp = (0, p.Z), (p.Z, p.Z)
        self.uzm, self.uzp = (2 * p.Z, p.X), (2 * p.Z + p.X, p.X)
        self.uy = (2 * p.Z + 2 * p.X, p.Z)
        self.count = 3 * p.Z + 2 * p.X


def read(ref, span):
    return ref[span[0] : span[0] + span[1], :]


def write_bounds(ref, b, values):
    for span, value in zip((b.uxm, b.uxp, b.uzm, b.uzp, b.uy), values):
        ref[span[0] : span[0] + span[1], :] = value


def read_bounds(ref, b):
    return tuple(read(ref, span) for span in (b.uxm, b.uxp, b.uzm, b.uzp, b.uy))


def start_cycle(p, brick, get, residual, classes, rxz, ry, sy, s_ref, z1b_ref, go_ref, r_scr, z_scr, z2_scr, go_scr):
    X, Z, n = p.X, p.Z, p.n
    for i in range(X):
        r = residual(i)
        r_scr[i * Z : (i + 1) * Z, :] = r
        z_scr[i] = r * (DAMPING / brick.diagonal(i))
    z1 = lambda i: z_scr[i]
    coarse = dot_wide_right(rxz[...], r_scr[...])
    coarse = dot_wide_right(ry[...], coarse, ((1,), (1,))) * (1.0 / 216.0)
    rows = sy[pl.ds(pl.multiple_of(lax.axis_index("by") * p.cy + 8, 8), p.cy), :]
    part = dot(rows.T, coarse.astype(BF16))
    for j in range(n):
        go_scr[j * p.go : j * p.go + p.modes, :] = part[j * p.modes : (j + 1) * p.modes]
    for i in range(X):
        v = z1(i)
        smooth = (2.0 - DAMPING) * v + (DAMPING / brick.diagonal(i)) * brick.neighbours(i, z1)
        z2_scr[i] = smooth
        s_ref[i] = get(i) + smooth
    z2 = lambda i: z2_scr[i]
    z1_y, z2_y = col_faces(z1, p), col_faces(z2, p)
    z1_zm, z1_zp = z_scr[:, 0, :], z_scr[:, Z - 1, :]
    write_bounds(z1b_ref, Bounds(p), (z1(0), z1(X - 1), z1_zm, z1_zp, z1_y))
    lane = iota((Z, p.Y), 1)
    sides = jnp.where(lane < 2 * X, z1_y, roll(z2_y, 2 * X, 1))
    edges = [z_scr[0, 0:1, :], z_scr[0, Z - 1 : Z, :], z_scr[X - 1, 0:1, :], z_scr[X - 1, Z - 1 : Z, :]]
    edges += [z1_y[0:1], z1_y[Z - 1 : Z]]
    if classes is None:
        sides = jnp.where(lane < 4 * X, sides, 0.0)
    else:
        cls, cls_y = classes
        sides = jnp.where(lane < 4 * X, sides, roll(cls_y, 4 * X, 1))
        sides = jnp.where(lane < 6 * X, sides, 0.0)
        edges += [cls(0)[0:1], cls(0)[Z - 1 : Z], cls(X - 1)[0:1], cls(X - 1)[Z - 1 : Z]]
        edges += [cls_y[0:1], cls_y[Z - 1 : Z]]
    pieces = (
        jnp.concatenate([z1(0), z2(0)], axis=0),
        jnp.concatenate([z1(X - 1), z2(X - 1)], axis=0),
        jnp.concatenate([z1_zm, z2_scr[:, 0, :]], axis=0),
        jnp.concatenate([z1_zp, z2_scr[:, Z - 1, :]], axis=0),
        sides,
        jnp.concatenate(edges, axis=0),
    )
    for piece, offset in zip(pieces, p.offsets):
        put_rows(go_scr, p.go, p.go_halo + offset, n, piece)
    used = p.go_halo + sum(p.heights)
    for k in range(used, p.go):
        go_scr[pl.ds(k, n, stride=p.go), :] = jnp.zeros((n, p.Y), F32)
    go_ref[...] = go_scr[...].astype(BF16)


def pack_kernel(p, index_hbm, u_hbm, cls_ref, xa_ref, xb_ref, za_ref, zb_ref, y_ref, index_ref, u_ref, sems):
    X, Z, Y = p.X, p.Z, p.Y
    pairs = ((index_hbm, index_ref), (u_hbm, u_ref))
    copies = [pltpu.make_async_copy(source, to, sems.at[k]) for k, (source, to) in enumerate(pairs)]
    for copy in copies:
        copy.start()
    copies[0].wait()
    spread_z = (iota((Z, Z // 4), 0) // 4 == iota((Z, Z // 4), 1)).astype(BF16)
    spread_y = (iota((Y // 4, Y), 1) // 4 == iota((Y // 4, Y), 0)).astype(BF16)
    for a in range(X // 4):
        element = (index_ref[a] + 1).astype(F32).astype(BF16)
        cls_ref[a] = dot(dot(spread_z, element).astype(BF16), spread_y)
    copies[1].wait()
    u = lambda i: u_ref[i]
    cls = lambda i: cls_ref[i // 4]

    def face(axis, low, high, a_ref, b_ref):
        even = lax.axis_index(axis) % 2 == 0
        a_ref[...] = jnp.where(even, high, low)
        b_ref[...] = jnp.where(even, low, high)

    face(
        "bx",
        jnp.concatenate([u(0), cls(0)], axis=0),
        jnp.concatenate([u(X - 1), cls(X - 1)], axis=0),
        xa_ref,
        xb_ref,
    )
    rows = lambda z: jnp.concatenate([cls(i)[z : z + 1] for i in range(X)], axis=0)
    face(
        "bz",
        jnp.concatenate([u_ref[:, 0, :], rows(0)], axis=0),
        jnp.concatenate([u_ref[:, Z - 1, :], rows(Z - 1)], axis=0),
        za_ref,
        zb_ref,
    )
    y_ref[...] = jnp.concatenate([col_faces(u, p), col_faces(cls, p)], axis=0)


def received(axis, count, a_ref, b_ref):
    at = lax.axis_index(axis)
    even = at % 2 == 0
    a, b = a_ref[...], b_ref[...]
    low = jnp.where(even, b, a)
    high = jnp.where(even, a, b)
    return jnp.where(at > 0, low, 0.0), jnp.where(at < count - 1, high, 0.0)


def prepare_kernel(p, coef, u_ref, f_ref, cls_ref, cst_ref, r_ref, u_out, clsy_ref):
    for a in range(p.X // 4):
        kap = lookup(cls_ref[a], coef, 0)
        wzm, wzp, wym, wyp = plane_weights(kap, 0.0, 0.0, 0.0, 0.0)
        cst_ref[KAP, a] = kap
        cst_ref[WZM, a] = wzm
        cst_ref[WZP, a] = wzp
        cst_ref[WYM, a] = wym
        cst_ref[WYP, a] = wyp
        cst_ref[BASE, a] = lookup(cls_ref[a], coef, 1) + ((wzm + wzp) + (wym + wyp))
        cst_ref[BETA, a] = lookup(cls_ref[a], coef, 2)
    brick = Brick(p, cst_ref, 0.0, 0.0)
    get = lambda i: u_ref[i]
    for i in range(p.X):
        r_ref[i] = residual_plane(brick, i, get, None, f_ref[i])
        u_out[i] = get(i)
    clsy_ref[...] = col_faces(lambda i: cls_ref[i // 4], p)


def first_kernel(p, coef, u_ref, r_ref, cls_ref, clsy_ref, cst0_ref, xa, xb, za, zb, ya, yb, rxz, ry, sy,
                 go_ref, s_ref, z1b_ref, uhb_ref, clsb_ref, cst_ref, r_scr, z_scr, z2_scr, go_scr):
    X, Z, Y, b = p.X, p.Z, p.Y, Bounds(p)
    xm, xp = received("bx", p.nx, xa, xb)
    zm, zp = received("bz", p.nz, za, zb)
    ym, yp = received("by", p.ny, ya, yb)
    y = jnp.where(iota(ym.shape, 1) % 2 == 0, ym, yp)
    halo = (xm[:Z], xp[:Z], zm[:X], zp[:X], y[:Z])
    outside = (xm[Z:], xp[Z:], zm[X:], zp[X:], y[Z:])
    write_bounds(uhb_ref, b, halo)
    write_bounds(clsb_ref, b, outside)
    kap_h = tuple(lookup(value, coef, 0) for value in outside)
    row, lane = iota((Z, Y), 0), iota((Z, Y), 1)
    more = []
    for a in range(X // 4):
        i = 4 * a
        ends = (
            (WZM, jnp.where(row == 0, kap_h[2][i : i + 1], 0.0)),
            (WZP, jnp.where(row == Z - 1, kap_h[3][i : i + 1], 0.0)),
            (WYM, jnp.where(lane == 0, kap_h[4][:, 2 * i : 2 * i + 1], 0.0)),
            (WYP, jnp.where(lane == Y - 1, kap_h[4][:, 2 * i + 1 : 2 * i + 2], 0.0)),
        )
        for k, end in ends:
            cst_ref[k, a] = cst0_ref[k, a] + end
        more.append((ends[0][1] + ends[1][1]) + (ends[2][1] + ends[3][1]))
        cst_ref[BASE, a] = cst0_ref[BASE, a] + more[a]
        cst_ref[KAP, a] = cst0_ref[KAP, a]
        cst_ref[BETA, a] = cst0_ref[BETA, a]
    brick = Brick(p, cst_ref, kap_h[0], kap_h[1])

    def residual(i):
        added = more[i // 4]
        if i == 0:
            added = added + kap_h[0]
        if i == X - 1:
            added = added + kap_h[1]
        return r_ref[i] - added * u_ref[i] + brick.from_halo(i, halo)

    cls = lambda i: cls_ref[i // 4]
    start_cycle(p, brick, lambda i: u_ref[i], residual, (cls, clsy_ref[...]), rxz, ry, sy,
                s_ref, z1b_ref, go_ref, r_scr, z_scr, z2_scr, go_scr)


def owner_kernel(p, coef, in_ref, wz, wx, wxt, wzi, lamxz, lamy, out_ref, in_scr, out_scr):
    n, m, nx, ny, nz = p.n, p.modes, p.nx, p.ny, p.nz
    me = (lax.axis_index("bx") * ny + lax.axis_index("by")) * nz + lax.axis_index("bz")
    in_scr[...] = in_ref[...].astype(F32)
    rows = []
    for bx in range(nx):
        lanes = []
        for bz in range(nz):
            total = None
            for by in range(ny):
                at = ((bx * ny + by) * nz + bz) * p.go
                piece = in_scr[at : at + m, :]
                total = piece if total is None else total + piece
            lanes.append(total)
        rows.append(jnp.concatenate(lanes, axis=1))
    data = jnp.concatenate(rows, axis=0)
    data = dot_wide_right(wz[...], data, ((1,), (1,)))
    data = jnp.concatenate([data[x * p.NZ : (x + 1) * p.NZ] for x in range(p.cx)], axis=1)
    data = dot_wide_left(data, wx[...])
    classes = coef.shape[1]
    kap_mean = sum(coef[0, k] for k in range(classes)) * (1.0 / classes)
    sig_mean = sum(coef[1, k] for k in range(classes)) * (1.0 / classes)
    data = data / (kap_mean * (lamxz[...] + lamy[me]) + sig_mean)
    data = dot_wide_left(data, wxt[...])
    width = nx * m
    data = jnp.concatenate([data[:, x * width : (x + 1) * width] for x in range(p.cx)], axis=0)
    high, low = halves(data)
    high, low = high.T, low.T
    lane = iota((m, p.Y), 1)
    for bz in range(nz):
        back = dot(high, wzi[bz]) + dot(low, wzi[bz])
        core = lambda bx: back[bx * m : (bx + 1) * m, : p.lanes]
        for bx in range(nx):
            ends = roll(back[bx * m : (bx + 1) * m, p.lanes :], 2 * p.cz, 1)
            below = roll(core(bx - 1), p.cz - p.lanes, 1) if bx else jnp.zeros((m, p.lanes), F32)
            above = roll(core(bx + 1), p.cz, 1) if bx + 1 < nx else jnp.zeros((m, p.lanes), F32)
            extra = jnp.where(lane < p.cz, below, jnp.where(lane < 2 * p.cz, above, ends))
            mine = core(bx)
            for by in range(ny):
                at = ((bx * ny + by) * nz + bz) * p.back
                out_scr[at : at + m, :] = mine
                out_scr[at + m : at + 2 * m, :] = extra

    device = iota((n, p.Y), 0)
    at_x, at_y, at_z = device // (ny * nz), (device // nz) % ny, device % nz

    def shift(value, dx, dy, dz):
        value = roll(value, -((dx * ny + dy) * nz + dz), 0)
        for at, step, count in ((at_x, dx, nx), (at_y, dy, ny), (at_z, dz, nz)):
            if step:
                value = jnp.where((at + step >= 0) & (at + step < count), value, 0.0)
        return value

    def take(k):
        return in_scr[pl.ds(p.go_halo + k, n, stride=p.go), :]

    def give(k, value):
        out_scr[pl.ds(p.back_halo + k, n, stride=p.back), :] = value

    for to, source, step in ((0, 1, (-1, 0, 0)), (1, 0, (1, 0, 0)), (2, 3, (0, 0, -1)), (3, 2, (0, 0, 1))):
        for k in range(p.heights[to]):
            give(p.offsets[to] + k, shift(take(p.offsets[source] + k), *step))
    lane = iota((n, p.Y), 1)
    even = lane % 2 == 0
    first, X2 = p.edge_lane, 2 * p.X
    for k in range(p.heights[4]):
        sides = take(p.offsets[4] + k)
        moved = jnp.where(lane < first + 2, roll(sides, first, 1), roll(sides, first + 2 - (X2 - 2), 1))
        moved = jnp.where(lane < first + 4, moved, roll(sides, first + 4 - 2 * X2, 1))
        moved = jnp.where(lane < first + 6, moved, roll(sides, first + 6 - (3 * X2 - 2), 1))
        which = (lane - first) % 4
        corner = jnp.where(
            which < 2,
            jnp.where(even, shift(moved, 1, -1, 0), shift(moved, 1, 1, 0)),
            jnp.where(even, shift(moved, -1, -1, 0), shift(moved, -1, 1, 0)),
        )
        plain = jnp.where(even, shift(sides, 0, -1, 0), shift(sides, 0, 1, 0))
        give(p.offsets[4] + k, jnp.where(lane < first, plain, jnp.where(lane < first + 8, corner, 0.0)))
    edges = take(p.offsets[5])
    kind = me % 6
    moved = jnp.where(even, shift(edges, 0, -1, -1), shift(edges, 0, 1, -1))
    for k, value in (
        (0, lambda: shift(edges, 1, 0, 1)),
        (1, lambda: shift(edges, 1, 0, -1)),
        (2, lambda: shift(edges, -1, 0, 1)),
        (3, lambda: shift(edges, -1, 0, -1)),
        (4, lambda: jnp.where(even, shift(edges, 0, -1, 1), shift(edges, 0, 1, 1))),
    ):
        moved = jnp.where(kind == k, value(), moved)
    give(p.offsets[5], moved)
    used = p.back_halo + sum(p.heights)
    for k in range(used, p.back):
        out_scr[pl.ds(k, n, stride=p.back), :] = jnp.zeros((n, p.Y), F32)
    out_ref[...] = out_scr[...].astype(BF16)


class Arrived:
    def __init__(self, p, ref):
        X, Z = p.X, p.Z
        rows = (2 * Z, 2 * Z, 2 * X, 2 * X, Z, 12)
        xm, xp, zm, zp, sides, edges = (
            get_rows(ref, p.back, p.back_halo + offset, p.n, count) for offset, count in zip(p.offsets, rows)
        )
        self.p, self.ref, self.sides, self.edges = p, ref, sides, edges
        self.z1 = (xm[:Z], xp[:Z], zm[:X], zp[:X], sides)
        self.z2 = (xm[Z:], xp[Z:], zm[X:], zp[X:], roll(sides, -2 * X, 1))

    def xz(self, kind, sx, sz):
        k = 6 * kind + (0 if sx else 2) + (0 if sz else 1)
        return self.edges[k : k + 1]

    def zy(self, kind, sz):
        k = 6 * kind + (4 if sz else 5)
        return self.edges[k : k + 1]

    def xy(self, kind, sx, sy):
        lane = self.p.edge_lane + 4 * kind + (0 if sx else 2) + sy
        return self.sides[:, lane : lane + 1]

    def xy_lanes(self, kind, plain):
        first, X2 = self.p.edge_lane + 4 * kind, 2 * self.p.X
        lane = iota(plain.shape, 1)
        value = jnp.where(lane < X2, plain, roll(self.sides, X2 - first, 1))
        return jnp.where(lane >= self.p.Y - 2, roll(self.sides, self.p.Y - 2 - first - 2, 1), value)


def coarse_rows(p, ref, sy, pyt, pall, pyh):
    n, m = p.n, p.modes
    core = jnp.concatenate([ref[j * p.back : j * p.back + m, :] for j in range(n)], axis=0)
    extra = jnp.concatenate([ref[j * p.back + m : j * p.back + 2 * m, :] for j in range(n)], axis=0)
    modes = jnp.concatenate([core, extra], axis=1).astype(BF16)
    rows = sy[pl.ds(pl.multiple_of(lax.axis_index("by") * p.cy, 8), p.cy + 16), :]
    values = dot(rows, modes).astype(BF16)
    along = dot(values[8 : 8 + p.cy].T, pyt[...])
    count = pall.shape[0] - p.Z
    nodes = dot_wide_right(pall[:count], along) * (1.0 / 27.0)
    weights = pall[count:, : p.lanes].astype(F32)
    ends = [weights * values.astype(F32)[k : k + 1, : p.lanes] for k in (7, 8 + p.cy)]
    side = dot_wide_left(jnp.concatenate(ends, axis=1), pyh[...]) * (1.0 / 27.0)
    return nodes, side


def column(row, count, side):
    shape = (count, row.shape[1])
    pick = iota(shape, 1) == 2 * iota(shape, 0) + side
    return jnp.sum(jnp.where(pick, row, 0.0), axis=1, keepdims=True)


def finish_cycle(p, coef, brick, now, first, s_ref, z1b_ref, uhb_ref, clsb_ref, nodes, side, u_ref):
    X, Z, b = p.X, p.Z, Bounds(p)
    for i in range(X):
        u_ref[i] = s_ref[i] + (DAMPING / brick.diagonal(i)) * brick.from_halo(i, now.z1) + nodes[i * Z : (i + 1) * Z]
    old, cls, own = read_bounds(uhb_ref, b), read_bounds(clsb_ref, b), read_bounds(z1b_ref, b)
    kap = lambda value: lookup(value, coef, 0)
    halo = []

    def new(k, weights, toward, others, correction):
        kap_here = kap(cls[k])
        diagonal = lookup(cls[k], coef, 1) + (kap_here + toward) + ((weights[0] + weights[1]) + (weights[2] + weights[3]))
        total = toward * own_faces[k]
        for part in others:
            total = total + part
        value = old[k] + now.z2[k] + (DAMPING / diagonal) * total + correction
        halo.append(jnp.where(cls[k] > 0.5, value, 0.0))

    own_faces = list(own[:4]) + [swap_lanes(own[4])]
    at = X * Z
    for k in range(2):
        kap_here = kap(cls[k])
        row_m, row_p = kap(first.xz(1, k, 0)), kap(first.xz(1, k, 1))
        col_m, col_p = kap(first.xy(1, k, 0)), kap(first.xy(1, k, 1))
        w = plane_weights(kap_here, row_m, row_p, col_m, col_p)
        row, lane = iota((Z, p.Y), 0), iota((Z, p.Y), 1)
        others = (
            jnp.where(row == 0, w[0] * now.xz(0, k, 0), 0.0),
            jnp.where(row == Z - 1, w[1] * now.xz(0, k, 1), 0.0),
            jnp.where(lane == 0, w[2] * now.xy(0, k, 0), 0.0),
            jnp.where(lane == p.Y - 1, w[3] * now.xy(0, k, 1), 0.0),
        )
        toward = kap_here + brick.of(KAP, 0 if k == 0 else X - 1)
        new(k, w, toward, others, nodes[at : at + Z])
        at += Z
    for k in range(2):
        kap_here = kap(cls[2 + k])
        row_m, row_p = kap(first.xz(1, 0, k)), kap(first.xz(1, 1, k))
        col_m, col_p = (kap(column(first.zy(1, k), X, side_y)) for side_y in range(2))
        w = plane_weights(kap_here, row_m, row_p, col_m, col_p)
        row, lane = iota((X, p.Y), 0), iota((X, p.Y), 1)
        others = (
            jnp.where(row == 0, w[0] * now.xz(0, 0, k), 0.0),
            jnp.where(row == X - 1, w[1] * now.xz(0, 1, k), 0.0),
            jnp.where(lane == 0, w[2] * column(now.zy(0, k), X, 0), 0.0),
            jnp.where(lane == p.Y - 1, w[3] * column(now.zy(0, k), X, 1), 0.0),
        )
        z = 0 if k == 0 else Z - 1
        mine = jnp.concatenate([brick.of(KAP, i)[z : z + 1] for i in range(X)], axis=0)
        new(2 + k, w, kap_here + mine, others, nodes[at : at + X])
        at += X
    wide = kap(first.xy_lanes(1, cls[4]))
    z1_wide = now.xy_lanes(0, now.z1[4])
    row_m, row_p = kap(first.zy(1, 0)), kap(first.zy(1, 1))
    up, down = shifted(wide, 0, row_m, row_p)
    left, right = roll(wide, 2, 1), roll(wide, -2, 1)
    row, lane = iota((Z, p.Y), 0), iota((Z, p.Y), 1)
    w = (
        jnp.where(row % 4 == 0, wide + up, wide),
        jnp.where(row % 4 == 3, wide + down, wide),
        jnp.where((lane // 2) % 4 == 0, wide + left, wide),
        jnp.where((lane // 2) % 4 == 3, wide + right, wide),
    )
    others = (
        jnp.where(row == 0, w[0] * now.zy(0, 0), 0.0),
        jnp.where(row == Z - 1, w[1] * now.zy(0, 1), 0.0),
        jnp.where(lane // 2 == 0, w[2] * roll(z1_wide, 2, 1), 0.0),
        jnp.where(lane // 2 == X - 1, w[3] * roll(z1_wide, -2, 1), 0.0),
    )
    mine = swap_lanes(col_faces(lambda i: brick.of(KAP, i), p))
    new(4, w, wide + mine, others, side)
    return tuple(halo)


def middle_kernel(p, coef, in_ref, f_ref, s_ref, z1b_ref, uhb_ref, clsb_ref, cst_ref,
                  sy, pyt, pall, pyh, rxz, ry,
                  go_ref, s_out, z1b_out, uhb_out, in_scr, u_scr, r_scr, z_scr, z2_scr, go_scr):
    in_scr[...] = in_ref[...].astype(F32)
    b = Bounds(p)
    outside = read_bounds(clsb_ref, b)
    brick = Brick(p, cst_ref, lookup(outside[0], coef, 0), lookup(outside[1], coef, 0))
    now = Arrived(p, in_scr)
    nodes, side = coarse_rows(p, in_scr, sy, pyt, pall, pyh)
    halo = finish_cycle(p, coef, brick, now, now, s_ref, z1b_ref, uhb_ref, clsb_ref, nodes, side, u_scr)
    write_bounds(uhb_out, b, halo)
    get = lambda i: u_scr[i]
    residual = lambda i: residual_plane(brick, i, get, halo, f_ref[i])
    start_cycle(p, brick, get, residual, None, rxz, ry, sy,
                s_out, z1b_out, go_ref, r_scr, z_scr, z2_scr, go_scr)


def last_kernel(p, coef, in_ref, first_ref, f_ref, s_ref, z1b_ref, uhb_ref, clsb_ref, cst_ref,
                sy, pyt, pall, pyh, u_out, r_out, in_scr, first_scr):
    in_scr[...] = in_ref[...].astype(F32)
    first_scr[...] = first_ref[...].astype(F32)
    outside = read_bounds(clsb_ref, Bounds(p))
    brick = Brick(p, cst_ref, lookup(outside[0], coef, 0), lookup(outside[1], coef, 0))
    now, first = Arrived(p, in_scr), Arrived(p, first_scr)
    nodes, side = coarse_rows(p, in_scr, sy, pyt, pall, pyh)
    halo = finish_cycle(p, coef, brick, now, first, s_ref, z1b_ref, uhb_ref, clsb_ref, nodes, side, u_out)
    for i in range(p.X):
        r_out[i] = residual_plane(brick, i, lambda k: u_out[k], halo, f_ref[i])


def call(kernel, p, name, coef, inputs, outputs, scratch, space=pltpu.VMEM, limit=VMEM_LIMIT, us=2):
    smem = [pl.BlockSpec(memory_space=pltpu.SMEM)] if coef is not None else []
    args = ([coef] if coef is not None else []) + list(inputs)
    return pl.pallas_call(
        functools.partial(kernel, p),
        out_shape=[jax.ShapeDtypeStruct(shape, dtype) for shape, dtype in outputs],
        in_specs=smem + [pl.BlockSpec(memory_space=space)] * len(inputs),
        out_specs=[pl.BlockSpec(memory_space=pltpu.VMEM)] * len(outputs),
        scratch_shapes=[pltpu.VMEM(shape, F32) if isinstance(shape, tuple) else shape for shape in scratch],
        compiler_params=pltpu.CompilerParams(vmem_limit_bytes=limit),
        cost_estimate=pl.CostEstimate(flops=0, bytes_accessed=us * 3_600_000, transcendentals=0),
        name=name,
    )(*args)


def swaps(axis, count, a, b):
    if count == 1:
        return a, b
    assert count % 2 == 0
    first = lax.ppermute(a, axis, [(i, i ^ 1) for i in range(count)])
    if count == 2:
        return first, first
    other = lambda i: (i + 1 if i % 2 else i - 1) % count
    return first, lax.ppermute(b, axis, [(i, other(i)) for i in range(count)])


def body(forcing, start, element_class_index, class_coef):
    p = Plan(start.shape, *(lax.axis_size(axis) for axis in AXES))
    t = tables(p)
    X, Z, Y, n = p.X, p.Z, p.Y, p.n
    bounds = Bounds(p).count
    block, flat, cst = (X, Z, Y), (X * Z, Y), (7, X // 4, Z, Y)
    cls, xa, xb, za, zb, yf = call(
        pack_kernel, p, "pack_faces", None, (element_class_index, start),
        [((X // 4, Z, Y), F32)] + [((2 * Z, Y), F32)] * 2 + [((2 * X, Y), F32)] * 2 + [((2 * Z, Y), F32)],
        [pltpu.VMEM(element_class_index.shape, jnp.int32), block, pltpu.SemaphoreType.DMA((2,))], pl.ANY, 62 * 1024 * 1024, 20,
    )
    xa, xb = swaps("bx", p.nx, xa, xb)
    za, zb = swaps("bz", p.nz, za, zb)
    ya, yb = swaps("by", p.ny, yf, yf)
    go_shape, back_shape = (n * p.go, Y), (n * p.back, Y)
    starting = [flat, block, block, go_shape]
    rxz, ry, sy = t["rxz"], t["ry"], t["sy"]
    cst0, r0, u0, clsy = call(
        prepare_kernel, p, "prepare", class_coef, (start, forcing, cls),
        [(cst, F32), (block, F32), (block, F32), ((Z, Y), F32)], [], us=6,
    )
    go, s, z1b, uhb, clsb, coefs = call(
        first_kernel, p, "first_residual", class_coef,
        (u0, r0, cls, clsy, cst0, xa, xb, za, zb, ya, yb, rxz, ry, sy),
        [(go_shape, BF16), (block, F32), ((bounds, Y), F32), ((bounds, Y), F32), ((bounds, Y), F32), (cst, F32)],
        starting,
    )
    prolong = (sy, t["pyt"], t["pall"], t["pyh"])
    first = None
    for cycle in range(CYCLES):
        came = lax.all_to_all(go, AXES, split_axis=0, concat_axis=0, tiled=True)
        (out,) = call(
            owner_kernel, p, "owned_modes", class_coef,
            (came, t["wz"], t["wx"], t["wxt"], t["wzi"], t["lamxz"], t["lamy"]),
            [(back_shape, BF16)], [go_shape, back_shape],
        )
        back = lax.all_to_all(out, AXES, split_axis=0, concat_axis=0, tiled=True)
        if cycle + 1 < CYCLES:
            assert first is None
            first = back
            go, s, z1b, uhb = call(
                middle_kernel, p, "next_residual", class_coef,
                (back, forcing, s, z1b, uhb, clsb, coefs) + prolong + (rxz, ry),
                [(go_shape, BF16), (block, F32), ((bounds, Y), F32), ((bounds, Y), F32)],
                [back_shape, block] + starting,
            )
        else:
            return tuple(call(
                last_kernel, p, "last_residual", class_coef,
                (back, first, forcing, s, z1b, uhb, clsb, coefs) + prolong,
                [(block, F32), (block, F32)], [back_shape, back_shape],
            ))


def solution(mesh):
    spec = P("bx", "bz", "by")
    return jax.shard_map(body, mesh=mesh, in_specs=(spec, spec, spec, P()), out_specs=(spec, spec), check_vma=False)
```

```python
import functools
import math

import jax
import jax.numpy as jnp
import numpy as np
from jax import lax
from jax.experimental import pallas as pl
from jax.experimental.pallas import tpu as pltpu
from jax.sharding import PartitionSpec as P

CYCLES = 2
DAMPING = 0.6666666666666666
F32 = jnp.float32
BF16 = jnp.bfloat16
AXES = ("bx", "by", "bz")
VMEM_LIMIT = 32 * 1024 * 1024


def up_to(value, multiple):
    return -(-value // multiple) * multiple


class Plan:
    def __init__(self, shape, nx, ny, nz):
        self.X, self.Z, self.Y = shape
        self.nx, self.ny, self.nz = nx, ny, nz
        self.n = nx * ny * nz
        self.cx, self.cz, self.cy = self.X // 2, self.Z // 2, self.Y // 2
        self.NX, self.NZ, self.NY = self.cx * nx, self.cz * nz, self.cy * ny
        self.modes = -(-self.NY // self.n)
        self.NYp = self.modes * self.n
        self.lanes = self.cx * self.cz
        rows = (2 * self.Z, 2 * self.Z, 2 * self.X, 2 * self.X, self.Z, 12)
        self.heights = [-(-r // self.n) for r in rows]
        self.offsets = [sum(self.heights[:i]) for i in range(6)]
        halo = sum(self.heights)
        self.go_halo = self.modes
        self.go = up_to(self.modes + halo, 8)
        self.back_halo = 2 * self.modes
        self.back = up_to(2 * self.modes + halo, 8)
        self.edge_lane = 6 * self.X
        self.extra = 2 * self.cz + 2 * self.cx
        self.staged = nx == 4 and nz == 2 and ny & (ny - 1) == 0 and self.NZ % LOW == 0
        assert self.lanes <= self.Y and self.extra <= self.lanes and self.edge_lane + 8 <= self.Y
        assert self.heights[5] == 1


def sine_table(count):
    index_one = np.arange(1, count + 1, dtype=np.int32)
    product = (index_one[:, None] * index_one[None, :]).astype(np.float32)
    value = np.sin(product * np.float32(math.pi / (count + 1)))
    return (value * np.float32(math.sqrt(2.0 / (count + 1)))).astype(BF16).astype(np.float32)


def spectrum_values(count):
    return 2.0 - 2.0 * np.cos(np.arange(1, count + 1) * (math.pi / (count + 1)))


RESTRICT = np.array([[3, 2, 1, 0], [0, 1, 2, 3]], np.float32)
PROLONG = np.array([[3, 0], [2, 1], [1, 2], [0, 3]], np.float32)


LOW = 8


def staged_tables(p, sx, sz, py):
    high, eye = p.NZ // LOW, np.eye(LOW)
    out = {}
    wzt = np.zeros((high, p.cx, LOW, p.nz, p.cx, p.cz), np.float32)
    for x in range(p.cx):
        wzt[:, x, :, :, x, :] = sz.reshape(high, LOW, p.nz, p.cz)
    out["wzt"] = wzt.reshape(p.cx * p.NZ, p.nz * p.lanes)
    out["kx"] = np.kron(sx, eye)
    sxp = np.zeros((p.NX + 2, p.NX), np.float32)
    sxp[1:-1] = sx
    out["kxi"] = np.kron(sxp, eye)
    szp = np.zeros((p.NZ + 2, p.NZ), np.float32)
    szp[1:-1] = sz
    zi = np.zeros((p.nz, p.lanes + p.extra, high, p.cx + 2, LOW), np.float32)
    for b in range(p.nz):
        mine = szp[b * p.cz + 1 : (b + 1) * p.cz + 1].reshape(p.cz, high, LOW)
        for x in range(p.cx):
            zi[b, x * p.cz : (x + 1) * p.cz, :, x + 1, :] = mine
            zi[b, p.lanes + 2 * p.cz + x, :, x + 1, :] = szp[b * p.cz].reshape(high, LOW)
            zi[b, p.lanes + 2 * p.cz + p.cx + x, :, x + 1, :] = szp[(b + 1) * p.cz + 1].reshape(high, LOW)
        zi[b, p.lanes : p.lanes + p.cz, :, 0, :] = mine
        zi[b, p.lanes + p.cz : p.lanes + 2 * p.cz, :, p.cx + 1, :] = mine
    out["zi"] = zi.reshape(p.nz, p.lanes + p.extra, -1)
    pye = np.zeros((p.cy + 16, p.Y), np.float32)
    pye[8 : 8 + p.cy] = py.T
    out["pye"] = pye
    return out


def tables(p):
    rx = np.kron(np.eye(p.X // 4), RESTRICT)
    rz = np.kron(np.eye(p.Z // 4), RESTRICT)
    ry = np.kron(np.eye(p.Y // 4), RESTRICT)
    px = np.kron(np.eye(p.X // 4), PROLONG)
    pz = np.kron(np.eye(p.Z // 4), PROLONG)
    py = np.kron(np.eye(p.Y // 4), PROLONG)
    sx, sz, sy = sine_table(p.NX), sine_table(p.NZ), sine_table(p.NY)
    out = {}
    out["rxz"] = np.kron(rx, rz)
    out["ry"] = ry
    padded = np.zeros((p.NY + 16, p.NYp), np.float32)
    padded[8 : 8 + p.NY, : p.NY] = sy
    out["sy"] = padded
    wz = np.zeros((p.cx, p.NZ, p.nz, p.cx, p.cz), np.float32)
    for x in range(p.cx):
        wz[x, :, :, x, :] = sz.reshape(p.NZ, p.nz, p.cz)
    out["wz"] = wz.reshape(p.cx * p.NZ, p.nz * p.lanes)
    wx = np.einsum("bxk,mn->xbmkn", sx.reshape(p.nx, p.cx, p.NX), np.eye(p.modes))
    wx = wx.reshape(p.NX * p.modes, p.NX * p.modes)
    out["wx"], out["wxt"] = wx, wx.T
    szp = np.zeros((p.NZ, p.NZ + 2), np.float32)
    szp[:, 1:-1] = sz
    wzi = np.zeros((p.nz, p.cx, p.NZ, 2 * p.lanes), np.float32)
    for b in range(p.nz):
        for x in range(p.cx):
            wzi[b, x, :, x * p.cz : (x + 1) * p.cz] = sz[:, b * p.cz : (b + 1) * p.cz]
            wzi[b, x, :, p.lanes + x] = szp[:, b * p.cz]
            wzi[b, x, :, p.lanes + p.cx + x] = szp[:, (b + 1) * p.cz + 1]
    out["wzi"] = wzi.reshape(p.nz, p.cx * p.NZ, 2 * p.lanes)
    out["pyt"] = py.T
    pall = np.zeros((p.X * p.Z + 2 * p.Z + 2 * p.X, 2 * p.lanes), np.float32)
    at = p.X * p.Z
    pall[:at, : p.lanes] = np.kron(px, pz)
    col = p.lanes
    for _ in range(2):
        pall[at : at + p.Z, col : col + p.cz] = 3 * pz
        at, col = at + p.Z, col + p.cz
    for _ in range(2):
        pall[at : at + p.X, col : col + p.cx] = 3 * px
        at, col = at + p.X, col + p.cx
    out["pall"] = np.concatenate([pall, np.tile(pz, (1, 2 * p.cx))])
    pyh = np.zeros((2, p.lanes, p.Y), np.float32)
    spread = np.repeat(px.T, p.cz, axis=0)
    for side in range(2):
        pyh[side, :, side : 2 * p.X : 2] = 3 * spread
    out["pyh"] = pyh.reshape(2 * p.lanes, p.Y)
    if p.staged:
        out.update(staged_tables(p, sx, sz, py))
    out = {key: jnp.asarray(value.astype(BF16)) for key, value in out.items()}
    if p.staged:
        lam = spectrum_values(p.NX)[None, :, None] + spectrum_values(p.NZ).reshape(-1, 1, LOW)
        out["lam_xz"] = jnp.asarray(lam.reshape(-1, 1).astype(np.float32))
        out["lam_y"] = jnp.asarray(spectrum_values(p.NY).reshape(1, -1).astype(np.float32))
        return out
    lam = spectrum_values(p.NX)[None, :, None] + spectrum_values(p.NZ)[:, None, None]
    out["lamxz"] = jnp.asarray(np.broadcast_to(lam, (p.NZ, p.NX, p.modes)).reshape(p.NZ, -1).astype(np.float32))
    lamy = np.zeros(p.NYp)
    lamy[: p.NY] = spectrum_values(p.NY)
    lamy = np.broadcast_to(lamy.reshape(p.n, 1, 1, p.modes), (p.n, 1, p.NX, p.modes))
    out["lamy"] = jnp.asarray(lamy.reshape(p.n, 1, -1).astype(np.float32))
    return out


def iota(shape, dim):
    return lax.broadcasted_iota(jnp.int32, shape, dim)


def dot(a, b, dims=((1,), (0,))):
    return lax.dot_general(a, b, (dims, ((), ())), preferred_element_type=F32)


def halves(value):
    high = value.astype(BF16)
    return high, (value - high.astype(F32)).astype(BF16)


def dot_wide_right(table, value, dims=((1,), (0,))):
    high, low = halves(value)
    return dot(table, high, dims) + dot(table, low, dims)


def dot_wide_left(value, table, dims=((1,), (0,))):
    high, low = halves(value)
    return dot(high, table, dims) + dot(low, table, dims)


def roll(value, shift, axis):
    size = value.shape[axis]
    shift = shift % size
    return value if shift == 0 else pltpu.roll(value, shift, axis)


def lookup(classes, coef_ref, row):
    total = jnp.zeros_like(classes)
    for k in range(coef_ref.shape[1]):
        total = jnp.where(classes == k + 1.0, coef_ref[row, k], total)
    return total


def col_faces(get, p):
    lane = iota((p.Z, p.Y), 1) // 2
    total = jnp.zeros((p.Z, p.Y), F32)
    for i in range(p.X):
        total = jnp.where(lane == i, roll(get(i), 2 * i + 1, 1), total)
    return total


def swap_lanes(value):
    even = iota(value.shape, 1) % 2 == 0
    return jnp.where(even, roll(value, -1, 1), roll(value, 1, 1))


def shifted(value, axis, before, after):
    size = value.shape[axis]
    at = iota(value.shape, axis)
    low = jnp.where(at == 0, before, roll(value, 1, axis))
    high = jnp.where(at == size - 1, after, roll(value, -1, axis))
    return low, high


def plane_weights(kap, row_m, row_p, col_m, col_p):
    up, down = shifted(kap, 0, row_m, row_p)
    left, right = shifted(kap, 1, col_m, col_p)
    row, lane = iota(kap.shape, 0) % 4, iota(kap.shape, 1) % 4
    return (
        jnp.where(row == 0, kap + up, kap),
        jnp.where(row == 3, kap + down, kap),
        jnp.where(lane == 0, kap + left, kap),
        jnp.where(lane == 3, kap + right, kap),
    )


KAP, WZM, WZP, WYM, WYP, BASE, BETA = range(7)


class Brick:
    def __init__(self, p, cst_ref, kap_xm, kap_xp):
        self.p, self.cst, self.kap_xm, self.kap_xp = p, cst_ref, kap_xm, kap_xp

    def of(self, quantity, i):
        return self.cst[quantity, i // 4]

    def x_weights(self, i):
        kap = self.of(KAP, i)
        low = high = kap
        if i % 4 == 0:
            low = kap + (self.of(KAP, i - 1) if i else self.kap_xm)
        if i % 4 == 3:
            high = kap + (self.of(KAP, i + 1) if i + 1 < self.p.X else self.kap_xp)
        return low, high

    def diagonal(self, i):
        low, high = self.x_weights(i)
        return self.of(BASE, i) + (low + high)

    def neighbours(self, i, get, halo=None):
        p, v = self.p, get(i)
        low, high = self.x_weights(i)
        total = jnp.zeros_like(v)
        if i:
            total = total + low * get(i - 1)
        elif halo is not None:
            total = total + low * halo[0]
        if i + 1 < p.X:
            total = total + high * get(i + 1)
        elif halo is not None:
            total = total + high * halo[1]
        if halo is None:
            ends = (0.0, 0.0, 0.0, 0.0)
        else:
            yh = halo[4]
            ends = (halo[2][i : i + 1], halo[3][i : i + 1], yh[:, 2 * i : 2 * i + 1], yh[:, 2 * i + 1 : 2 * i + 2])
        up, down = shifted(v, 0, ends[0], ends[1])
        left, right = shifted(v, 1, ends[2], ends[3])
        total = total + self.of(WZM, i) * up + self.of(WZP, i) * down
        return total + self.of(WYM, i) * left + self.of(WYP, i) * right

    def from_halo(self, i, halo):
        p = self.p
        row, lane = iota((p.Z, p.Y), 0), iota((p.Z, p.Y), 1)
        yh = halo[4]
        total = jnp.where(row == 0, self.of(WZM, i) * halo[2][i : i + 1], 0.0)
        total = jnp.where(row == p.Z - 1, self.of(WZP, i) * halo[3][i : i + 1], total)
        total = total + jnp.where(lane == 0, self.of(WYM, i) * yh[:, 2 * i : 2 * i + 1], 0.0)
        total = total + jnp.where(lane == p.Y - 1, self.of(WYP, i) * yh[:, 2 * i + 1 : 2 * i + 2], 0.0)
        if i == 0:
            total = total + self.x_weights(i)[0] * halo[0]
        if i == p.X - 1:
            total = total + self.x_weights(i)[1] * halo[1]
        return total


def residual_plane(brick, i, get, halo, f):
    v = get(i)
    return f - brick.diagonal(i) * v + brick.neighbours(i, get, halo) - brick.of(BETA, i) * v * v * v


def put_rows(ref, stride, offset, n, rows):
    height = -(-rows.shape[0] // n)
    if rows.shape[0] < height * n:
        rows = jnp.concatenate([rows, jnp.zeros((height * n - rows.shape[0], rows.shape[1]), F32)], axis=0)
    for k in range(height):
        ref[pl.ds(offset + k, n, stride=stride), :] = rows[k * n : (k + 1) * n]


def get_rows(ref, stride, offset, n, count):
    height = -(-count // n)
    parts = [ref[pl.ds(offset + k, n, stride=stride), :] for k in range(height)]
    value = parts[0] if height == 1 else jnp.concatenate(parts, axis=0)
    return value[:count]


class Bounds:
    def __init__(self, p):
        self.uxm, self.uxp = (0, p.Z), (p.Z, p.Z)
        self.uzm, self.uzp = (2 * p.Z, p.X), (2 * p.Z + p.X, p.X)
        self.uy = (2 * p.Z + 2 * p.X, p.Z)
        self.count = 3 * p.Z + 2 * p.X


def read(ref, span):
    return ref[span[0] : span[0] + span[1], :]


def write_bounds(ref, b, values):
    for span, value in zip((b.uxm, b.uxp, b.uzm, b.uzp, b.uy), values):
        ref[span[0] : span[0] + span[1], :] = value


def read_bounds(ref, b):
    return tuple(read(ref, span) for span in (b.uxm, b.uxp, b.uzm, b.uzp, b.uy))


def advance(p, brick, get, residual, rxz, ry, s_ref, r_scr, z_scr, z2_scr):
    X, Z = p.X, p.Z
    for i in range(X):
        r = residual(i)
        r_scr[i * Z : (i + 1) * Z, :] = r
        z_scr[i] = r * (DAMPING / brick.diagonal(i))
    z1 = lambda i: z_scr[i]
    coarse = dot_wide_right(rxz[...], r_scr[...])
    coarse = dot_wide_right(ry[...], coarse, ((1,), (1,))) * (1.0 / 216.0)
    for i in range(X):
        v = z1(i)
        smooth = (2.0 - DAMPING) * v + (DAMPING / brick.diagonal(i)) * brick.neighbours(i, z1)
        z2_scr[i] = smooth
        s_ref[i] = get(i) + smooth
    return coarse.astype(BF16)


def start_cycle(p, brick, get, residual, classes, rxz, ry, sy, s_ref, z1b_ref, go_ref, r_scr, z_scr, z2_scr, go_scr):
    X, Z, n = p.X, p.Z, p.n
    coarse = advance(p, brick, get, residual, rxz, ry, s_ref, r_scr, z_scr, z2_scr)
    z1 = lambda i: z_scr[i]
    rows = sy[pl.ds(pl.multiple_of(lax.axis_index("by") * p.cy + 8, 8), p.cy), :]
    part = dot(rows.T, coarse)
    for j in range(n):
        go_scr[j * p.go : j * p.go + p.modes, :] = part[j * p.modes : (j + 1) * p.modes]
    z2 = lambda i: z2_scr[i]
    z1_y, z2_y = col_faces(z1, p), col_faces(z2, p)
    z1_zm, z1_zp = z_scr[:, 0, :], z_scr[:, Z - 1, :]
    write_bounds(z1b_ref, Bounds(p), (z1(0), z1(X - 1), z1_zm, z1_zp, z1_y))
    lane = iota((Z, p.Y), 1)
    sides = jnp.where(lane < 2 * X, z1_y, roll(z2_y, 2 * X, 1))
    edges = [z_scr[0, 0:1, :], z_scr[0, Z - 1 : Z, :], z_scr[X - 1, 0:1, :], z_scr[X - 1, Z - 1 : Z, :]]
    edges += [z1_y[0:1], z1_y[Z - 1 : Z]]
    if classes is None:
        sides = jnp.where(lane < 4 * X, sides, 0.0)
    else:
        cls, cls_y = classes
        sides = jnp.where(lane < 4 * X, sides, roll(cls_y, 4 * X, 1))
        sides = jnp.where(lane < 6 * X, sides, 0.0)
        edges += [cls(0)[0:1], cls(0)[Z - 1 : Z], cls(X - 1)[0:1], cls(X - 1)[Z - 1 : Z]]
        edges += [cls_y[0:1], cls_y[Z - 1 : Z]]
    pieces = (
        jnp.concatenate([z1(0), z2(0)], axis=0),
        jnp.concatenate([z1(X - 1), z2(X - 1)], axis=0),
        jnp.concatenate([z1_zm, z2_scr[:, 0, :]], axis=0),
        jnp.concatenate([z1_zp, z2_scr[:, Z - 1, :]], axis=0),
        sides,
        jnp.concatenate(edges, axis=0),
    )
    for piece, offset in zip(pieces, p.offsets):
        put_rows(go_scr, p.go, p.go_halo + offset, n, piece)
    used = p.go_halo + sum(p.heights)
    for k in range(used, p.go):
        go_scr[pl.ds(k, n, stride=p.go), :] = jnp.zeros((n, p.Y), F32)
    go_ref[...] = go_scr[...].astype(BF16)


def pack_kernel(p, index_hbm, u_hbm, cls_ref, xa_ref, xb_ref, za_ref, zb_ref, y_ref, index_ref, u_ref, sems):
    X, Z, Y = p.X, p.Z, p.Y
    pairs = ((index_hbm, index_ref), (u_hbm, u_ref))
    copies = [pltpu.make_async_copy(source, to, sems.at[k]) for k, (source, to) in enumerate(pairs)]
    for copy in copies:
        copy.start()
    copies[0].wait()
    spread_z = (iota((Z, Z // 4), 0) // 4 == iota((Z, Z // 4), 1)).astype(BF16)
    spread_y = (iota((Y // 4, Y), 1) // 4 == iota((Y // 4, Y), 0)).astype(BF16)
    for a in range(X // 4):
        element = (index_ref[a] + 1).astype(F32).astype(BF16)
        cls_ref[a] = dot(dot(spread_z, element).astype(BF16), spread_y)
    copies[1].wait()
    u = lambda i: u_ref[i]
    cls = lambda i: cls_ref[i // 4]

    def face(axis, low, high, a_ref, b_ref):
        even = lax.axis_index(axis) % 2 == 0
        a_ref[...] = jnp.where(even, high, low)
        b_ref[...] = jnp.where(even, low, high)

    face(
        "bx",
        jnp.concatenate([u(0), cls(0)], axis=0),
        jnp.concatenate([u(X - 1), cls(X - 1)], axis=0),
        xa_ref,
        xb_ref,
    )
    rows = lambda z: jnp.concatenate([cls(i)[z : z + 1] for i in range(X)], axis=0)
    face(
        "bz",
        jnp.concatenate([u_ref[:, 0, :], rows(0)], axis=0),
        jnp.concatenate([u_ref[:, Z - 1, :], rows(Z - 1)], axis=0),
        za_ref,
        zb_ref,
    )
    y_ref[...] = jnp.concatenate([col_faces(u, p), col_faces(cls, p)], axis=0)


def received(axis, count, a_ref, b_ref):
    at = lax.axis_index(axis)
    even = at % 2 == 0
    a, b = a_ref[...], b_ref[...]
    low = jnp.where(even, b, a)
    high = jnp.where(even, a, b)
    return jnp.where(at > 0, low, 0.0), jnp.where(at < count - 1, high, 0.0)


def prepare_kernel(p, coef, u_ref, f_ref, cls_ref, cst_ref, r_ref, u_out, clsy_ref):
    for a in range(p.X // 4):
        kap = lookup(cls_ref[a], coef, 0)
        wzm, wzp, wym, wyp = plane_weights(kap, 0.0, 0.0, 0.0, 0.0)
        cst_ref[KAP, a] = kap
        cst_ref[WZM, a] = wzm
        cst_ref[WZP, a] = wzp
        cst_ref[WYM, a] = wym
        cst_ref[WYP, a] = wyp
        cst_ref[BASE, a] = lookup(cls_ref[a], coef, 1) + ((wzm + wzp) + (wym + wyp))
        cst_ref[BETA, a] = lookup(cls_ref[a], coef, 2)
    brick = Brick(p, cst_ref, 0.0, 0.0)
    get = lambda i: u_ref[i]
    for i in range(p.X):
        r_ref[i] = residual_plane(brick, i, get, None, f_ref[i])
        u_out[i] = get(i)
    clsy_ref[...] = col_faces(lambda i: cls_ref[i // 4], p)


def neighbours_in(p, coef, u_ref, r_ref, cst0_ref, xa, xb, za, zb, ya, yb, uhb_ref, clsb_ref, cst_ref):
    X, Z, Y, b = p.X, p.Z, p.Y, Bounds(p)
    xm, xp = received("bx", p.nx, xa, xb)
    zm, zp = received("bz", p.nz, za, zb)
    ym, yp = received("by", p.ny, ya, yb)
    y = jnp.where(iota(ym.shape, 1) % 2 == 0, ym, yp)
    halo = (xm[:Z], xp[:Z], zm[:X], zp[:X], y[:Z])
    outside = (xm[Z:], xp[Z:], zm[X:], zp[X:], y[Z:])
    write_bounds(uhb_ref, b, halo)
    write_bounds(clsb_ref, b, outside)
    kap_h = tuple(lookup(value, coef, 0) for value in outside)
    row, lane = iota((Z, Y), 0), iota((Z, Y), 1)
    more = []
    for a in range(X // 4):
        i = 4 * a
        ends = (
            (WZM, jnp.where(row == 0, kap_h[2][i : i + 1], 0.0)),
            (WZP, jnp.where(row == Z - 1, kap_h[3][i : i + 1], 0.0)),
            (WYM, jnp.where(lane == 0, kap_h[4][:, 2 * i : 2 * i + 1], 0.0)),
            (WYP, jnp.where(lane == Y - 1, kap_h[4][:, 2 * i + 1 : 2 * i + 2], 0.0)),
        )
        for k, end in ends:
            cst_ref[k, a] = cst0_ref[k, a] + end
        more.append((ends[0][1] + ends[1][1]) + (ends[2][1] + ends[3][1]))
        cst_ref[BASE, a] = cst0_ref[BASE, a] + more[a]
        cst_ref[KAP, a] = cst0_ref[KAP, a]
        cst_ref[BETA, a] = cst0_ref[BETA, a]
    brick = Brick(p, cst_ref, kap_h[0], kap_h[1])

    def residual(i):
        added = more[i // 4]
        if i == 0:
            added = added + kap_h[0]
        if i == X - 1:
            added = added + kap_h[1]
        return r_ref[i] - added * u_ref[i] + brick.from_halo(i, halo)

    return brick, residual


def first_kernel(p, coef, u_ref, r_ref, cls_ref, clsy_ref, cst0_ref, xa, xb, za, zb, ya, yb, rxz, ry, sy,
                 go_ref, s_ref, z1b_ref, uhb_ref, clsb_ref, cst_ref, r_scr, z_scr, z2_scr, go_scr):
    brick, residual = neighbours_in(p, coef, u_ref, r_ref, cst0_ref, xa, xb, za, zb, ya, yb, uhb_ref, clsb_ref, cst_ref)
    cls = lambda i: cls_ref[i // 4]
    start_cycle(p, brick, lambda i: u_ref[i], residual, (cls, clsy_ref[...]), rxz, ry, sy,
                s_ref, z1b_ref, go_ref, r_scr, z_scr, z2_scr, go_scr)


def owner_kernel(p, coef, in_ref, wz, wx, wxt, wzi, lamxz, lamy, out_ref, in_scr, out_scr):
    n, m, nx, ny, nz = p.n, p.modes, p.nx, p.ny, p.nz
    me = (lax.axis_index("bx") * ny + lax.axis_index("by")) * nz + lax.axis_index("bz")
    in_scr[...] = in_ref[...].astype(F32)
    rows = []
    for bx in range(nx):
        lanes = []
        for bz in range(nz):
            total = None
            for by in range(ny):
                at = ((bx * ny + by) * nz + bz) * p.go
                piece = in_scr[at : at + m, :]
                total = piece if total is None else total + piece
            lanes.append(total)
        rows.append(jnp.concatenate(lanes, axis=1))
    data = jnp.concatenate(rows, axis=0)
    data = dot_wide_right(wz[...], data, ((1,), (1,)))
    data = jnp.concatenate([data[x * p.NZ : (x + 1) * p.NZ] for x in range(p.cx)], axis=1)
    data = dot_wide_left(data, wx[...])
    classes = coef.shape[1]
    kap_mean = sum(coef[0, k] for k in range(classes)) * (1.0 / classes)
    sig_mean = sum(coef[1, k] for k in range(classes)) * (1.0 / classes)
    data = data / (kap_mean * (lamxz[...] + lamy[me]) + sig_mean)
    data = dot_wide_left(data, wxt[...])
    width = nx * m
    data = jnp.concatenate([data[:, x * width : (x + 1) * width] for x in range(p.cx)], axis=0)
    high, low = halves(data)
    high, low = high.T, low.T
    lane = iota((m, p.Y), 1)
    for bz in range(nz):
        back = dot(high, wzi[bz]) + dot(low, wzi[bz])
        core = lambda bx: back[bx * m : (bx + 1) * m, : p.lanes]
        for bx in range(nx):
            ends = roll(back[bx * m : (bx + 1) * m, p.lanes :], 2 * p.cz, 1)
            below = roll(core(bx - 1), p.cz - p.lanes, 1) if bx else jnp.zeros((m, p.lanes), F32)
            above = roll(core(bx + 1), p.cz, 1) if bx + 1 < nx else jnp.zeros((m, p.lanes), F32)
            extra = jnp.where(lane < p.cz, below, jnp.where(lane < 2 * p.cz, above, ends))
            mine = core(bx)
            for by in range(ny):
                at = ((bx * ny + by) * nz + bz) * p.back
                out_scr[at : at + m, :] = mine
                out_scr[at + m : at + 2 * m, :] = extra

    device = iota((n, p.Y), 0)
    at_x, at_y, at_z = device // (ny * nz), (device // nz) % ny, device % nz

    def shift(value, dx, dy, dz):
        value = roll(value, -((dx * ny + dy) * nz + dz), 0)
        for at, step, count in ((at_x, dx, nx), (at_y, dy, ny), (at_z, dz, nz)):
            if step:
                value = jnp.where((at + step >= 0) & (at + step < count), value, 0.0)
        return value

    def take(k):
        return in_scr[pl.ds(p.go_halo + k, n, stride=p.go), :]

    def give(k, value):
        out_scr[pl.ds(p.back_halo + k, n, stride=p.back), :] = value

    for to, source, step in ((0, 1, (-1, 0, 0)), (1, 0, (1, 0, 0)), (2, 3, (0, 0, -1)), (3, 2, (0, 0, 1))):
        for k in range(p.heights[to]):
            give(p.offsets[to] + k, shift(take(p.offsets[source] + k), *step))
    lane = iota((n, p.Y), 1)
    even = lane % 2 == 0
    first, X2 = p.edge_lane, 2 * p.X
    for k in range(p.heights[4]):
        sides = take(p.offsets[4] + k)
        moved = jnp.where(lane < first + 2, roll(sides, first, 1), roll(sides, first + 2 - (X2 - 2), 1))
        moved = jnp.where(lane < first + 4, moved, roll(sides, first + 4 - 2 * X2, 1))
        moved = jnp.where(lane < first + 6, moved, roll(sides, first + 6 - (3 * X2 - 2), 1))
        which = (lane - first) % 4
        corner = jnp.where(
            which < 2,
            jnp.where(even, shift(moved, 1, -1, 0), shift(moved, 1, 1, 0)),
            jnp.where(even, shift(moved, -1, -1, 0), shift(moved, -1, 1, 0)),
        )
        plain = jnp.where(even, shift(sides, 0, -1, 0), shift(sides, 0, 1, 0))
        give(p.offsets[4] + k, jnp.where(lane < first, plain, jnp.where(lane < first + 8, corner, 0.0)))
    edges = take(p.offsets[5])
    kind = me % 6
    moved = jnp.where(even, shift(edges, 0, -1, -1), shift(edges, 0, 1, -1))
    for k, value in (
        (0, lambda: shift(edges, 1, 0, 1)),
        (1, lambda: shift(edges, 1, 0, -1)),
        (2, lambda: shift(edges, -1, 0, 1)),
        (3, lambda: shift(edges, -1, 0, -1)),
        (4, lambda: jnp.where(even, shift(edges, 0, -1, 1), shift(edges, 0, 1, 1))),
    ):
        moved = jnp.where(kind == k, value(), moved)
    give(p.offsets[5], moved)
    used = p.back_halo + sum(p.heights)
    for k in range(used, p.back):
        out_scr[pl.ds(k, n, stride=p.back), :] = jnp.zeros((n, p.Y), F32)
    out_ref[...] = out_scr[...].astype(BF16)


class Arrived:
    def __init__(self, p, ref):
        X, Z = p.X, p.Z
        rows = (2 * Z, 2 * Z, 2 * X, 2 * X, Z, 12)
        xm, xp, zm, zp, sides, edges = (
            get_rows(ref, p.back, p.back_halo + offset, p.n, count) for offset, count in zip(p.offsets, rows)
        )
        self.p, self.ref, self.sides, self.edges = p, ref, sides, edges
        self.z1 = (xm[:Z], xp[:Z], zm[:X], zp[:X], sides)
        self.z2 = (xm[Z:], xp[Z:], zm[X:], zp[X:], roll(sides, -2 * X, 1))

    def xz(self, kind, sx, sz):
        k = 6 * kind + (0 if sx else 2) + (0 if sz else 1)
        return self.edges[k : k + 1]

    def zy(self, kind, sz):
        k = 6 * kind + (4 if sz else 5)
        return self.edges[k : k + 1]

    def xy(self, kind, sx, sy):
        lane = self.p.edge_lane + 4 * kind + (0 if sx else 2) + sy
        return self.sides[:, lane : lane + 1]

    def xy_lanes(self, kind, plain):
        first, X2 = self.p.edge_lane + 4 * kind, 2 * self.p.X
        lane = iota(plain.shape, 1)
        value = jnp.where(lane < X2, plain, roll(self.sides, X2 - first, 1))
        return jnp.where(lane >= self.p.Y - 2, roll(self.sides, self.p.Y - 2 - first - 2, 1), value)


def coarse_rows(p, ref, sy, pyt, pall, pyh):
    n, m = p.n, p.modes
    core = jnp.concatenate([ref[j * p.back : j * p.back + m, :] for j in range(n)], axis=0)
    extra = jnp.concatenate([ref[j * p.back + m : j * p.back + 2 * m, :] for j in range(n)], axis=0)
    modes = jnp.concatenate([core, extra], axis=1).astype(BF16)
    rows = sy[pl.ds(pl.multiple_of(lax.axis_index("by") * p.cy, 8), p.cy + 16), :]
    values = dot(rows, modes).astype(BF16)
    along = dot(values[8 : 8 + p.cy].T, pyt[...])
    count = pall.shape[0] - p.Z
    nodes = dot_wide_right(pall[:count], along) * (1.0 / 27.0)
    weights = pall[count:, : p.lanes].astype(F32)
    ends = [weights * values.astype(F32)[k : k + 1, : p.lanes] for k in (7, 8 + p.cy)]
    side = dot_wide_left(jnp.concatenate(ends, axis=1), pyh[...]) * (1.0 / 27.0)
    return nodes, side


def column(row, count, side):
    shape = (count, row.shape[1])
    pick = iota(shape, 1) == 2 * iota(shape, 0) + side
    return jnp.sum(jnp.where(pick, row, 0.0), axis=1, keepdims=True)


def finish_cycle(p, coef, brick, now, first, s_ref, z1b_ref, uhb_ref, clsb_ref, nodes, side, u_ref):
    X, Z, b = p.X, p.Z, Bounds(p)
    for i in range(X):
        u_ref[i] = s_ref[i] + (DAMPING / brick.diagonal(i)) * brick.from_halo(i, now.z1) + nodes[i * Z : (i + 1) * Z]
    old, cls, own = read_bounds(uhb_ref, b), read_bounds(clsb_ref, b), read_bounds(z1b_ref, b)
    kap = lambda value: lookup(value, coef, 0)
    halo = []

    def new(k, weights, toward, others, correction):
        kap_here = kap(cls[k])
        diagonal = lookup(cls[k], coef, 1) + (kap_here + toward) + ((weights[0] + weights[1]) + (weights[2] + weights[3]))
        total = toward * own_faces[k]
        for part in others:
            total = total + part
        value = old[k] + now.z2[k] + (DAMPING / diagonal) * total + correction
        halo.append(jnp.where(cls[k] > 0.5, value, 0.0))

    own_faces = list(own[:4]) + [swap_lanes(own[4])]
    at = X * Z
    for k in range(2):
        kap_here = kap(cls[k])
        row_m, row_p = kap(first.xz(1, k, 0)), kap(first.xz(1, k, 1))
        col_m, col_p = kap(first.xy(1, k, 0)), kap(first.xy(1, k, 1))
        w = plane_weights(kap_here, row_m, row_p, col_m, col_p)
        row, lane = iota((Z, p.Y), 0), iota((Z, p.Y), 1)
        others = (
            jnp.where(row == 0, w[0] * now.xz(0, k, 0), 0.0),
            jnp.where(row == Z - 1, w[1] * now.xz(0, k, 1), 0.0),
            jnp.where(lane == 0, w[2] * now.xy(0, k, 0), 0.0),
            jnp.where(lane == p.Y - 1, w[3] * now.xy(0, k, 1), 0.0),
        )
        toward = kap_here + brick.of(KAP, 0 if k == 0 else X - 1)
        new(k, w, toward, others, nodes[at : at + Z])
        at += Z
    for k in range(2):
        kap_here = kap(cls[2 + k])
        row_m, row_p = kap(first.xz(1, 0, k)), kap(first.xz(1, 1, k))
        col_m, col_p = (kap(column(first.zy(1, k), X, side_y)) for side_y in range(2))
        w = plane_weights(kap_here, row_m, row_p, col_m, col_p)
        row, lane = iota((X, p.Y), 0), iota((X, p.Y), 1)
        others = (
            jnp.where(row == 0, w[0] * now.xz(0, 0, k), 0.0),
            jnp.where(row == X - 1, w[1] * now.xz(0, 1, k), 0.0),
            jnp.where(lane == 0, w[2] * column(now.zy(0, k), X, 0), 0.0),
            jnp.where(lane == p.Y - 1, w[3] * column(now.zy(0, k), X, 1), 0.0),
        )
        z = 0 if k == 0 else Z - 1
        mine = jnp.concatenate([brick.of(KAP, i)[z : z + 1] for i in range(X)], axis=0)
        new(2 + k, w, kap_here + mine, others, nodes[at : at + X])
        at += X
    wide = kap(first.xy_lanes(1, cls[4]))
    z1_wide = now.xy_lanes(0, now.z1[4])
    row_m, row_p = kap(first.zy(1, 0)), kap(first.zy(1, 1))
    up, down = shifted(wide, 0, row_m, row_p)
    left, right = roll(wide, 2, 1), roll(wide, -2, 1)
    row, lane = iota((Z, p.Y), 0), iota((Z, p.Y), 1)
    w = (
        jnp.where(row % 4 == 0, wide + up, wide),
        jnp.where(row % 4 == 3, wide + down, wide),
        jnp.where((lane // 2) % 4 == 0, wide + left, wide),
        jnp.where((lane // 2) % 4 == 3, wide + right, wide),
    )
    others = (
        jnp.where(row == 0, w[0] * now.zy(0, 0), 0.0),
        jnp.where(row == Z - 1, w[1] * now.zy(0, 1), 0.0),
        jnp.where(lane // 2 == 0, w[2] * roll(z1_wide, 2, 1), 0.0),
        jnp.where(lane // 2 == X - 1, w[3] * roll(z1_wide, -2, 1), 0.0),
    )
    mine = swap_lanes(col_faces(lambda i: brick.of(KAP, i), p))
    new(4, w, wide + mine, others, side)
    return tuple(halo)


def middle_kernel(p, coef, in_ref, f_ref, s_ref, z1b_ref, uhb_ref, clsb_ref, cst_ref,
                  sy, pyt, pall, pyh, rxz, ry,
                  go_ref, s_out, z1b_out, uhb_out, in_scr, u_scr, r_scr, z_scr, z2_scr, go_scr):
    in_scr[...] = in_ref[...].astype(F32)
    b = Bounds(p)
    outside = read_bounds(clsb_ref, b)
    brick = Brick(p, cst_ref, lookup(outside[0], coef, 0), lookup(outside[1], coef, 0))
    now = Arrived(p, in_scr)
    nodes, side = coarse_rows(p, in_scr, sy, pyt, pall, pyh)
    halo = finish_cycle(p, coef, brick, now, now, s_ref, z1b_ref, uhb_ref, clsb_ref, nodes, side, u_scr)
    write_bounds(uhb_out, b, halo)
    get = lambda i: u_scr[i]
    residual = lambda i: residual_plane(brick, i, get, halo, f_ref[i])
    start_cycle(p, brick, get, residual, None, rxz, ry, sy,
                s_out, z1b_out, go_ref, r_scr, z_scr, z2_scr, go_scr)


def last_kernel(p, coef, in_ref, first_ref, f_ref, s_ref, z1b_ref, uhb_ref, clsb_ref, cst_ref,
                sy, pyt, pall, pyh, u_out, r_out, in_scr, first_scr):
    in_scr[...] = in_ref[...].astype(F32)
    first_scr[...] = first_ref[...].astype(F32)
    outside = read_bounds(clsb_ref, Bounds(p))
    brick = Brick(p, cst_ref, lookup(outside[0], coef, 0), lookup(outside[1], coef, 0))
    now, first = Arrived(p, in_scr), Arrived(p, first_scr)
    nodes, side = coarse_rows(p, in_scr, sy, pyt, pall, pyh)
    halo = finish_cycle(p, coef, brick, now, first, s_ref, z1b_ref, uhb_ref, clsb_ref, nodes, side, u_out)
    for i in range(p.X):
        r_out[i] = residual_plane(brick, i, lambda k: u_out[k], halo, f_ref[i])


class Sends:
    def __init__(self, p):
        X, Z = p.X, p.Z
        self.first = p.cy + Z
        self.x_face, self.z_face = p.NY, p.NY
        self.x_rows = p.NY + 3 * Z
        self.z_rows = p.NY + 2 * X + 16
        self.xz_rows = p.NY + 16
        self.second = 2 * p.cx * p.NZ * p.NY // p.Y
        self.last = self.second + 3 * Z + 16
        self.faces = 4 * Z + 4 * X


def pick(condition, a, b):
    return jnp.where(condition, a, b)


def send_first(p, coarse, z_scr, z2_scr, z1b_ref, a_ref, faces_ref):
    X, Z = p.X, p.Z
    z1, z2 = (lambda i: z_scr[i]), (lambda i: z2_scr[i])
    z1_y, z2_y = col_faces(z1, p), col_faces(z2, p)
    z_rows = (z_scr[:, 0, :], z_scr[:, Z - 1, :], z2_scr[:, 0, :], z2_scr[:, Z - 1, :])
    write_bounds(z1b_ref, Bounds(p), (z1(0), z1(X - 1), z_rows[0], z_rows[1], z1_y))
    a_ref[0 : p.cy, :] = coarse
    lane = iota((Z, p.Y), 1)
    a_ref[p.cy :, :] = jnp.where(lane < 2 * X, z1_y, roll(z2_y, 2 * X, 1)).astype(BF16)
    for k, plane in enumerate((z1(0), z1(X - 1), z2(0), z2(X - 1))):
        faces_ref[k * Z : (k + 1) * Z, :] = plane.astype(BF16)
    for k, rows in enumerate(z_rows):
        faces_ref[4 * Z + k * X : 4 * Z + (k + 1) * X, :] = rows.astype(BF16)


def face_x(p, faces_ref, high):
    X, Z = p.X, p.Z
    return tuple(pick(high, faces_ref[(k + 1) * Z : (k + 2) * Z, :], faces_ref[k * Z : (k + 1) * Z, :]) for k in (0, 2))


def face_z(p, faces_ref, high):
    X, at = p.X, 4 * p.Z
    return tuple(
        pick(high, faces_ref[at + (k + 1) * X : at + (k + 2) * X, :], faces_ref[at + k * X : at + (k + 1) * X, :]) for k in (0, 2)
    )


def pad_rows(rows, count):
    rows = [row.astype(F32) for row in rows]
    return jnp.concatenate(rows + [jnp.zeros((count - len(rows), rows[0].shape[1]), F32)], axis=0).astype(BF16)


def y_block(p, sides, cls_y):
    lane = iota(sides.shape, 1)
    return jnp.where(lane < 2 * p.X, sides, roll(cls_y, 2 * p.X, 1))


def after_first(p, *refs):
    ny = p.ny
    buffers, (faces_ref, clsb_ref, cls_ref, sy, x_ref, z_ref, xz_ref, sides_ref, all_scr) = refs[:ny], refs[ny:]
    X, Z, sends, b = p.X, p.Z, Sends(p), Bounds(p)
    bx, by, bz = (lax.axis_index(axis) for axis in AXES)
    low = high = jnp.zeros((Z, p.Y), F32)
    for d in range(ny):
        other = by ^ d
        all_scr[pl.ds(pl.multiple_of(other * p.cy, 16), p.cy), :] = buffers[d][0 : p.cy, :]
        if d:
            value = buffers[d][p.cy :, :].astype(F32)
            low = pick(other == by - 1, value, low)
            high = pick(other == by + 1, value, high)
    sides = jnp.where(iota((Z, p.Y), 1) % 2 == 0, low, high)
    sides_ref[...] = sides
    modes = dot(sy[8 : 8 + p.NY, :], all_scr[...]).astype(BF16)
    cls_y = read(clsb_ref, b.uy)
    odd, up = bx % 2 == 1, bz == 0
    for ref in (x_ref, z_ref, xz_ref):
        ref[0 : p.NY, :] = modes
    at = p.NY
    z1, z2 = face_x(p, faces_ref, odd)
    x_ref[at : at + Z, :] = z1
    x_ref[at + Z : at + 2 * Z, :] = z2
    x_ref[at + 2 * Z : at + 3 * Z, :] = y_block(p, sides, cls_y).astype(BF16)
    z1, z2 = face_z(p, faces_ref, up)
    z_ref[at : at + X, :] = z1
    z_ref[at + X : at + 2 * X, :] = z2
    z_ref[at + 2 * X : at + 2 * X + 16, :] = pad_rows(
        [pick(up, value[Z - 1 : Z], value[0:1]) for value in (sides, cls_y)], 16
    )
    z1 = z1.astype(F32)
    cls = pick(odd, cls_ref[X // 4 - 1], cls_ref[0])
    xz_ref[at : at + 16, :] = pad_rows(
        [pick(odd, z1[X - 1 : X], z1[0:1]), pick(up, cls[Z - 1 : Z], cls[0:1])], 16
    )


def after_second(p, own_ref, x_in, z_in, xz_in, faces_ref, clsb_ref, sides_ref, wzt, out_ref):
    X, Z, Y, sends, b = p.X, p.Z, p.Y, Sends(p), Bounds(p)
    bx, bz = lax.axis_index("bx"), lax.axis_index("bz")
    odd, up = bx % 2 == 1, bz == 0
    at = 0
    for one, two in ((own_ref, z_in), (x_in, xz_in)):
        one, two = one[0 : p.NY, :], two[0 : p.NY, :]
        data = jnp.concatenate([pick(up, one, two), pick(up, two, one)], axis=1)
        data = dot(wzt[...], data, ((1,), (1,))).astype(BF16)
        for k in range(p.NY // Y):
            rows = data.shape[0]
            out_ref[at : at + rows, :] = data[:, k * Y : (k + 1) * Y]
            at += rows
    z1, z2 = face_x(p, faces_ref, jnp.logical_not(odd))
    out_ref[at : at + Z, :] = z1
    out_ref[at + Z : at + 2 * Z, :] = z2
    out_ref[at + 2 * Z : at + 3 * Z, :] = y_block(p, sides_ref[...], read(clsb_ref, b.uy)).astype(BF16)
    beyond = z_in[p.NY : p.NY + X, :].astype(F32)
    classes = pick(up, read(clsb_ref, b.uzp), read(clsb_ref, b.uzm))
    out_ref[at + 3 * Z : at + 3 * Z + 16, :] = pad_rows(
        [pick(odd, value[0:1], value[X - 1 : X]) for value in (beyond, classes)], 16
    )


class Exchanged:
    def __init__(self, p, sides_ref, x_in, z_in, xz_in, last_in):
        X, Z = p.X, p.Z
        self.p = p
        bx, bz = lax.axis_index("bx"), lax.axis_index("bz")
        odd, self.up = bx % 2 == 1, bz == 0
        some = (bx > 0) & (bx < p.nx - 1)
        across = lambda ref, at, count: pick(some, ref[at : at + count, :].astype(F32), 0.0)
        beside = lambda at, count: last_in[at : at + count, :].astype(F32)
        both = lambda one, two: (pick(odd, one, two), pick(odd, two, one))
        start = Sends(p).second
        one = [beside(start + k * Z, Z) for k in range(3)]
        two = [across(x_in, p.NY + k * Z, Z) for k in range(3)]
        z1, z2, self.blocks = (both(one[k], two[k]) for k in range(3))
        one, two = beside(start + 3 * Z, 8), across(xz_in, p.NY, 8)
        self.corners = both(one, two)
        zs = [z_in[p.NY + k * X : p.NY + (k + 1) * X, :].astype(F32) for k in range(2)]
        ends = [(pick(self.up, 0.0, value), pick(self.up, value, 0.0)) for value in zs]
        self.rows = z_in[p.NY + 2 * X : p.NY + 2 * X + 8, :].astype(F32)
        sides = sides_ref[...]
        self.z1 = z1 + ends[0] + (sides,)
        self.z2 = z2 + ends[1] + (roll(sides, -2 * X, 1),)

    def there(self, sz, value):
        return pick(self.up, value, 0.0) if sz else pick(self.up, 0.0, value)

    def xz(self, kind, sx, sz):
        return self.there(sz, self.corners[sx][kind : kind + 1])

    def zy(self, kind, sz):
        return self.there(sz, self.rows[kind : kind + 1])

    def xy(self, kind, sx, sy):
        X2 = 2 * self.p.X
        lane = kind * X2 + (0 if sx else X2 - 2) + sy
        return self.blocks[sx][:, lane : lane + 1]

    def xy_lanes(self, kind, plain):
        X2, Y = 2 * self.p.X, self.p.Y
        lane = iota(plain.shape, 1)
        value = jnp.where(lane < X2, plain, roll(self.blocks[1], X2 * (1 - kind), 1))
        return jnp.where(lane >= Y - 2, roll(self.blocks[0], Y - X2 * (1 + kind), 1), value)


def coarse_staged(p, own_ref, last_in, lines_scr, inverse, kx, kxi, zi, sy, pye, pall, pyh):
    Y, NY = p.Y, p.NY
    bx, by, bz = (lax.axis_index(axis) for axis in AXES)
    rows = p.cx * p.NZ
    at = 0
    for index in ((bx, bx ^ 1), (bx ^ 3, bx ^ 2)):
        for k in range(NY // Y):
            for ref, block in zip((own_ref, last_in), index):
                lines_scr[block, :, k * Y : (k + 1) * Y] = ref[at : at + rows, :]
            at += rows
    step = p.cx * LOW
    back = kxi[pl.ds(pl.multiple_of(bx * step, 16), step + 2 * LOW), :]
    parts = []
    for h in range(p.NZ // LOW):
        lines = jnp.concatenate([lines_scr[x, h * step : (h + 1) * step, :] for x in range(p.nx)], axis=0)
        count = p.NX * LOW
        modes = (dot(kx[...], lines) * inverse[h * count : (h + 1) * count, :]).astype(BF16)
        parts.append(dot(back, modes).astype(BF16))
    values = dot(zi[bz], jnp.concatenate(parts, axis=0)).astype(BF16)
    table = sy[pl.ds(pl.multiple_of(by * p.cy, 16), p.cy + 16), :]
    values = dot(values, table, ((1,), (1,))).astype(BF16)
    count = pall.shape[0] - p.Z
    nodes = dot_wide_right(pall[:count, : p.lanes + p.extra], dot(values, pye[...])) * (1.0 / 27.0)
    ends = values[: p.lanes].astype(F32)
    spread = ends[:, 7:8] * pyh[: p.lanes].astype(F32) + ends[:, 8 + p.cy : 9 + p.cy] * pyh[p.lanes :].astype(F32)
    side = dot_wide_right(pall[count:, : p.lanes], spread) * (1.0 / 27.0)
    return nodes, side


def inverse_kernel(p, coef, lam_xz, lam_y, out_ref):
    classes = coef.shape[1]
    kap_mean = sum(coef[0, k] for k in range(classes)) * (1.0 / classes)
    sig_mean = sum(coef[1, k] for k in range(classes)) * (1.0 / classes)
    step = p.NX * LOW
    for h in range(p.NZ // LOW):
        lam = lam_xz[h * step : (h + 1) * step, :] + lam_y[...]
        out_ref[h * step : (h + 1) * step, :] = 1.0 / (kap_mean * lam + sig_mean)


def first_staged(p, coef, u_ref, r_ref, cls_ref, cst0_ref, xa, xb, za, zb, ya, yb, rxz, ry,
                 a_ref, faces_ref, s_ref, z1b_ref, uhb_ref, clsb_ref, cst_ref, r_scr, z_scr, z2_scr):
    brick, residual = neighbours_in(p, coef, u_ref, r_ref, cst0_ref, xa, xb, za, zb, ya, yb, uhb_ref, clsb_ref, cst_ref)
    coarse = advance(p, brick, lambda i: u_ref[i], residual, rxz, ry, s_ref, r_scr, z_scr, z2_scr)
    send_first(p, coarse, z_scr, z2_scr, z1b_ref, a_ref, faces_ref)


def middle_staged(p, coef, f_ref, s_ref, z1b_ref, uhb_ref, clsb_ref, cst_ref, sides, x_in, z_in, xz_in, own, last_in,
                  inverse, kx, kxi, zi, sy, pye, pall, pyh, rxz, ry,
                  a_ref, faces_ref, s_out, z1b_out, uhb_out, lines_scr, u_scr, r_scr, z_scr, z2_scr):
    b = Bounds(p)
    brick = Brick(p, cst_ref, lookup(read(clsb_ref, b.uxm), coef, 0), lookup(read(clsb_ref, b.uxp), coef, 0))
    now = Exchanged(p, sides, x_in, z_in, xz_in, last_in)
    nodes, side = coarse_staged(p, own, last_in, lines_scr, inverse, kx, kxi, zi, sy, pye, pall, pyh)
    halo = finish_cycle(p, coef, brick, now, now, s_ref, z1b_ref, uhb_ref, clsb_ref, nodes, side, u_scr)
    write_bounds(uhb_out, b, halo)
    get = lambda i: u_scr[i]
    residual = lambda i: residual_plane(brick, i, get, halo, f_ref[i])
    coarse = advance(p, brick, get, residual, rxz, ry, s_out, r_scr, z_scr, z2_scr)
    send_first(p, coarse, z_scr, z2_scr, z1b_out, a_ref, faces_ref)


def last_staged(p, coef, f_ref, s_ref, z1b_ref, uhb_ref, clsb_ref, cst_ref, sides, x_in, z_in, xz_in, own, last_in,
                inverse, kx, kxi, zi, sy, pye, pall, pyh, u_out, r_out, lines_scr):
    b = Bounds(p)
    brick = Brick(p, cst_ref, lookup(read(clsb_ref, b.uxm), coef, 0), lookup(read(clsb_ref, b.uxp), coef, 0))
    now = Exchanged(p, sides, x_in, z_in, xz_in, last_in)
    nodes, side = coarse_staged(p, own, last_in, lines_scr, inverse, kx, kxi, zi, sy, pye, pall, pyh)
    halo = finish_cycle(p, coef, brick, now, now, s_ref, z1b_ref, uhb_ref, clsb_ref, nodes, side, u_out)
    for i in range(p.X):
        r_out[i] = residual_plane(brick, i, lambda k: u_out[k], halo, f_ref[i])


def call(kernel, p, name, coef, inputs, outputs, scratch, space=pltpu.VMEM, limit=VMEM_LIMIT, us=2):
    smem = [pl.BlockSpec(memory_space=pltpu.SMEM)] if coef is not None else []
    args = ([coef] if coef is not None else []) + list(inputs)
    return pl.pallas_call(
        functools.partial(kernel, p),
        out_shape=[jax.ShapeDtypeStruct(shape, dtype) for shape, dtype in outputs],
        in_specs=smem + [pl.BlockSpec(memory_space=space)] * len(inputs),
        out_specs=[pl.BlockSpec(memory_space=pltpu.VMEM)] * len(outputs),
        scratch_shapes=[pltpu.VMEM(shape, F32) if isinstance(shape, tuple) else shape for shape in scratch],
        compiler_params=pltpu.CompilerParams(vmem_limit_bytes=limit),
        cost_estimate=pl.CostEstimate(flops=0, bytes_accessed=us * 3_600_000, transcendentals=0),
        name=name,
    )(*args)


def swaps(axis, count, a, b):
    if count == 1:
        return a, b
    assert count % 2 == 0
    first = lax.ppermute(a, axis, [(i, i ^ 1) for i in range(count)])
    if count == 2:
        return first, first
    other = lambda i: (i + 1 if i % 2 else i - 1) % count
    return first, lax.ppermute(b, axis, [(i, other(i)) for i in range(count)])


def body(forcing, start, element_class_index, class_coef):
    p = Plan(start.shape, *(lax.axis_size(axis) for axis in AXES))
    t = tables(p)
    X, Z, Y, n = p.X, p.Z, p.Y, p.n
    bounds = Bounds(p).count
    block, flat, cst = (X, Z, Y), (X * Z, Y), (7, X // 4, Z, Y)
    cls, xa, xb, za, zb, yf = call(
        pack_kernel, p, "pack_faces", None, (element_class_index, start),
        [((X // 4, Z, Y), F32)] + [((2 * Z, Y), F32)] * 2 + [((2 * X, Y), F32)] * 2 + [((2 * Z, Y), F32)],
        [pltpu.VMEM(element_class_index.shape, jnp.int32), block, pltpu.SemaphoreType.DMA((2,))], pl.ANY, 62 * 1024 * 1024, 20,
    )
    xa, xb = swaps("bx", p.nx, xa, xb)
    za, zb = swaps("bz", p.nz, za, zb)
    ya, yb = swaps("by", p.ny, yf, yf)
    go_shape, back_shape = (n * p.go, Y), (n * p.back, Y)
    starting = [flat, block, block, go_shape]
    rxz, ry, sy = t["rxz"], t["ry"], t["sy"]
    cst0, r0, u0, clsy = call(
        prepare_kernel, p, "prepare", class_coef, (start, forcing, cls),
        [(cst, F32), (block, F32), (block, F32), ((Z, Y), F32)], [], us=6,
    )
    if p.staged:
        return staged_cycles(p, t, class_coef, forcing, cls, u0, r0, cst0, (xa, xb, za, zb, ya, yb))
    go, s, z1b, uhb, clsb, coefs = call(
        first_kernel, p, "first_residual", class_coef,
        (u0, r0, cls, clsy, cst0, xa, xb, za, zb, ya, yb, rxz, ry, sy),
        [(go_shape, BF16), (block, F32), ((bounds, Y), F32), ((bounds, Y), F32), ((bounds, Y), F32), (cst, F32)],
        starting,
    )
    prolong = (sy, t["pyt"], t["pall"], t["pyh"])
    first = None
    for cycle in range(CYCLES):
        came = lax.all_to_all(go, AXES, split_axis=0, concat_axis=0, tiled=True)
        (out,) = call(
            owner_kernel, p, "owned_modes", class_coef,
            (came, t["wz"], t["wx"], t["wxt"], t["wzi"], t["lamxz"], t["lamy"]),
            [(back_shape, BF16)], [go_shape, back_shape],
        )
        back = lax.all_to_all(out, AXES, split_axis=0, concat_axis=0, tiled=True)
        if cycle + 1 < CYCLES:
            assert first is None
            first = back
            go, s, z1b, uhb = call(
                middle_kernel, p, "next_residual", class_coef,
                (back, forcing, s, z1b, uhb, clsb, coefs) + prolong + (rxz, ry),
                [(go_shape, BF16), (block, F32), ((bounds, Y), F32), ((bounds, Y), F32)],
                [back_shape, block] + starting,
            )
        else:
            return tuple(call(
                last_kernel, p, "last_residual", class_coef,
                (back, first, forcing, s, z1b, uhb, clsb, coefs) + prolong,
                [(block, F32), (block, F32)], [back_shape, back_shape],
            ))


def staged_cycles(p, t, class_coef, forcing, cls, u0, r0, cst0, faces_in):
    X, Z, Y = p.X, p.Z, p.Y
    sends, bounds = Sends(p), (Bounds(p).count, Y)
    block, flat = (X, Z, Y), (X * Z, Y)
    out = [((sends.first, Y), BF16), ((sends.faces, Y), BF16), (block, F32), (bounds, F32), (bounds, F32)]
    scratch = [flat, block, block]
    (inverse,) = call(
        inverse_kernel, p, "inverse_spectrum", class_coef, (t["lam_xz"], t["lam_y"]), [((p.NZ * p.NX, p.NY), F32)], []
    )
    a, faces, s, z1b, uhb, clsb, coefs = call(
        first_staged, p, "first_residual", class_coef, (u0, r0, cls, cst0) + faces_in + (t["rxz"], t["ry"]),
        out + [(bounds, F32), (cst0.shape, F32)], scratch,
    )
    lines = pltpu.VMEM((p.nx, p.cx * p.NZ, p.NY), BF16)
    back = tuple(t[key] for key in ("kx", "kxi", "zi", "sy", "pye", "pall", "pyh"))
    pairs = lambda count, d: [(i, i ^ d) for i in range(count)]
    for cycle in range(CYCLES):
        came = [a] + [lax.ppermute(a, "by", pairs(p.ny, d)) for d in range(1, p.ny)]
        x, z, xz, sides = call(
            after_first, p, "y_modes", None, (*came, faces, clsb, cls, t["sy"]),
            [((rows, Y), BF16) for rows in (sends.x_rows, sends.z_rows, sends.xz_rows)] + [((Z, Y), F32)],
            [pltpu.VMEM((p.NY, Y), BF16)],
        )
        plane, across = p.nx * p.nz, (p.nx - 1) * p.nz
        x_in = lax.ppermute(x, ("bx", "bz"), pairs(plane, across))
        z_in = lax.ppermute(z, ("bx", "bz"), pairs(plane, 1))
        xz_in = lax.ppermute(xz, ("bx", "bz"), pairs(plane, across + 1))
        (own,) = call(
            after_second, p, "z_modes", None, (x, x_in, z_in, xz_in, faces, clsb, sides, t["wzt"]),
            [((sends.last, Y), BF16)], [],
        )
        last_in = lax.ppermute(own, "bx", pairs(p.nx, 1))
        inputs = (forcing, s, z1b, uhb, clsb, coefs, sides, x_in, z_in, xz_in, own, last_in, inverse) + back
        if cycle + 1 < CYCLES:
            a, faces, s, z1b, uhb = call(
                middle_staged, p, "next_residual", class_coef, inputs + (t["rxz"], t["ry"]), out, [lines, block] + scratch
            )
        else:
            return tuple(call(last_staged, p, "last_residual", class_coef, inputs, [(block, F32), (block, F32)], [lines]))


def solution(mesh):
    spec = P("bx", "bz", "by")
    return jax.shard_map(body, mesh=mesh, in_specs=(spec, spec, spec, P()), out_specs=(spec, spec), check_vma=False)
```

```python
import functools
import math

import jax
import jax.numpy as jnp
import numpy as np
from jax import lax
from jax.experimental import pallas as pl
from jax.experimental.pallas import tpu as pltpu
from jax.sharding import PartitionSpec as P

CYCLES = 2
DAMPING = 0.6666666666666666
F32 = jnp.float32
BF16 = jnp.bfloat16
AXES = ("bx", "by", "bz")
VMEM_LIMIT = 32 * 1024 * 1024


def up_to(value, multiple):
    return -(-value // multiple) * multiple


class Plan:
    def __init__(self, shape, nx, ny, nz):
        self.X, self.Z, self.Y = shape
        self.nx, self.ny, self.nz = nx, ny, nz
        self.n = nx * ny * nz
        self.cx, self.cz, self.cy = self.X // 2, self.Z // 2, self.Y // 2
        self.NX, self.NZ, self.NY = self.cx * nx, self.cz * nz, self.cy * ny
        self.modes = -(-self.NY // self.n)
        self.NYp = self.modes * self.n
        self.lanes = self.cx * self.cz
        rows = (2 * self.Z, 2 * self.Z, 2 * self.X, 2 * self.X, self.Z, 12)
        self.heights = [-(-r // self.n) for r in rows]
        self.offsets = [sum(self.heights[:i]) for i in range(6)]
        halo = sum(self.heights)
        self.go_halo = self.modes
        self.go = up_to(self.modes + halo, 8)
        self.back_halo = 2 * self.modes
        self.back = up_to(2 * self.modes + halo, 8)
        self.edge_lane = 6 * self.X
        self.extra = 2 * self.cz + 2 * self.cx
        self.staged = nx == 4 and nz == 2 and ny & (ny - 1) == 0 and self.NZ % LOW == 0
        assert self.lanes <= self.Y and self.extra <= self.lanes and self.edge_lane + 8 <= self.Y
        assert self.heights[5] == 1


def sine_table(count):
    index_one = np.arange(1, count + 1, dtype=np.int32)
    product = (index_one[:, None] * index_one[None, :]).astype(np.float32)
    value = np.sin(product * np.float32(math.pi / (count + 1)))
    return (value * np.float32(math.sqrt(2.0 / (count + 1)))).astype(BF16).astype(np.float32)


def spectrum_values(count):
    return 2.0 - 2.0 * np.cos(np.arange(1, count + 1) * (math.pi / (count + 1)))


RESTRICT = np.array([[3, 2, 1, 0], [0, 1, 2, 3]], np.float32)
PROLONG = np.array([[3, 0], [2, 1], [1, 2], [0, 3]], np.float32)


LOW = 8


def staged_tables(p, sx, sz, py):
    high, eye = p.NZ // LOW, np.eye(LOW)
    out = {}
    wzt = np.zeros((high, p.cx, LOW, p.nz, p.cx, p.cz), np.float32)
    for x in range(p.cx):
        wzt[:, x, :, :, x, :] = sz.reshape(high, LOW, p.nz, p.cz)
    out["wzt"] = wzt.reshape(p.cx * p.NZ, p.nz * p.lanes)
    blocks = sx.reshape(p.NX, p.nx, p.cx)
    order = lambda b: [b, b ^ 3, b ^ 1, b ^ 2]
    out["kx"] = np.stack([np.kron(blocks[:, order(b)].reshape(p.NX, p.NX), eye) for b in range(p.nx)])
    sxp = np.zeros((p.NX + 2, p.NX), np.float32)
    sxp[1:-1] = sx
    out["kxi"] = np.kron(sxp, eye)
    szp = np.zeros((p.NZ + 2, p.NZ), np.float32)
    szp[1:-1] = sz
    zi = np.zeros((p.nz, p.lanes + p.extra, high, p.cx + 2, LOW), np.float32)
    for b in range(p.nz):
        mine = szp[b * p.cz + 1 : (b + 1) * p.cz + 1].reshape(p.cz, high, LOW)
        for x in range(p.cx):
            zi[b, x * p.cz : (x + 1) * p.cz, :, x + 1, :] = mine
            zi[b, p.lanes + 2 * p.cz + x, :, x + 1, :] = szp[b * p.cz].reshape(high, LOW)
            zi[b, p.lanes + 2 * p.cz + p.cx + x, :, x + 1, :] = szp[(b + 1) * p.cz + 1].reshape(high, LOW)
        zi[b, p.lanes : p.lanes + p.cz, :, 0, :] = mine
        zi[b, p.lanes + p.cz : p.lanes + 2 * p.cz, :, p.cx + 1, :] = mine
    out["zi"] = zi.reshape(p.nz, p.lanes + p.extra, -1)
    pye = np.zeros((p.cy + 16, 2 * p.Y), np.float32)
    pye[8 : 8 + p.cy, : p.Y] = py.T
    pye[7, p.Y] = pye[8 + p.cy, p.Y + 1] = 1
    out["pye"] = pye
    return out


def tables(p):
    rx = np.kron(np.eye(p.X // 4), RESTRICT)
    rz = np.kron(np.eye(p.Z // 4), RESTRICT)
    ry = np.kron(np.eye(p.Y // 4), RESTRICT)
    px = np.kron(np.eye(p.X // 4), PROLONG)
    pz = np.kron(np.eye(p.Z // 4), PROLONG)
    py = np.kron(np.eye(p.Y // 4), PROLONG)
    sx, sz, sy = sine_table(p.NX), sine_table(p.NZ), sine_table(p.NY)
    out = {}
    out["rxz"] = np.kron(rx, rz)
    out["ry"] = ry
    padded = np.zeros((p.NY + 16, p.NYp), np.float32)
    padded[8 : 8 + p.NY, : p.NY] = sy
    out["sy"] = padded
    wz = np.zeros((p.cx, p.NZ, p.nz, p.cx, p.cz), np.float32)
    for x in range(p.cx):
        wz[x, :, :, x, :] = sz.reshape(p.NZ, p.nz, p.cz)
    out["wz"] = wz.reshape(p.cx * p.NZ, p.nz * p.lanes)
    wx = np.einsum("bxk,mn->xbmkn", sx.reshape(p.nx, p.cx, p.NX), np.eye(p.modes))
    wx = wx.reshape(p.NX * p.modes, p.NX * p.modes)
    out["wx"], out["wxt"] = wx, wx.T
    szp = np.zeros((p.NZ, p.NZ + 2), np.float32)
    szp[:, 1:-1] = sz
    wzi = np.zeros((p.nz, p.cx, p.NZ, 2 * p.lanes), np.float32)
    for b in range(p.nz):
        for x in range(p.cx):
            wzi[b, x, :, x * p.cz : (x + 1) * p.cz] = sz[:, b * p.cz : (b + 1) * p.cz]
            wzi[b, x, :, p.lanes + x] = szp[:, b * p.cz]
            wzi[b, x, :, p.lanes + p.cx + x] = szp[:, (b + 1) * p.cz + 1]
    out["wzi"] = wzi.reshape(p.nz, p.cx * p.NZ, 2 * p.lanes)
    out["pyt"] = py.T
    pall = np.zeros((p.X * p.Z + 2 * p.Z + 2 * p.X, 2 * p.lanes), np.float32)
    at = p.X * p.Z
    pall[:at, : p.lanes] = np.kron(px, pz)
    col = p.lanes
    for _ in range(2):
        pall[at : at + p.Z, col : col + p.cz] = 3 * pz
        at, col = at + p.Z, col + p.cz
    for _ in range(2):
        pall[at : at + p.X, col : col + p.cx] = 3 * px
        at, col = at + p.X, col + p.cx
    out["pall"] = np.concatenate([pall, np.tile(pz, (1, 2 * p.cx))])
    pyh = np.zeros((2, p.lanes, p.Y), np.float32)
    spread = np.repeat(px.T, p.cz, axis=0)
    for side in range(2):
        pyh[side, :, side : 2 * p.X : 2] = 3 * spread
    out["pyh"] = pyh.reshape(2 * p.lanes, p.Y)
    if p.staged:
        out.update(staged_tables(p, sx, sz, py))
    out = {key: jnp.asarray(value.astype(BF16)) for key, value in out.items()}
    if p.staged:
        lam = spectrum_values(p.NX)[None, :, None] + spectrum_values(p.NZ).reshape(-1, 1, LOW)
        out["lam_xz"] = jnp.asarray(lam.reshape(-1, 1).astype(np.float32))
        out["lam_y"] = jnp.asarray(spectrum_values(p.NY).reshape(1, -1).astype(np.float32))
        return out
    lam = spectrum_values(p.NX)[None, :, None] + spectrum_values(p.NZ)[:, None, None]
    out["lamxz"] = jnp.asarray(np.broadcast_to(lam, (p.NZ, p.NX, p.modes)).reshape(p.NZ, -1).astype(np.float32))
    lamy = np.zeros(p.NYp)
    lamy[: p.NY] = spectrum_values(p.NY)
    lamy = np.broadcast_to(lamy.reshape(p.n, 1, 1, p.modes), (p.n, 1, p.NX, p.modes))
    out["lamy"] = jnp.asarray(lamy.reshape(p.n, 1, -1).astype(np.float32))
    return out


def iota(shape, dim):
    return lax.broadcasted_iota(jnp.int32, shape, dim)


def dot(a, b, dims=((1,), (0,))):
    return lax.dot_general(a, b, (dims, ((), ())), preferred_element_type=F32)


def halves(value):
    high = value.astype(BF16)
    return high, (value - high.astype(F32)).astype(BF16)


def dot_wide_right(table, value, dims=((1,), (0,))):
    high, low = halves(value)
    return dot(table, high, dims) + dot(table, low, dims)


def dot_wide_left(value, table, dims=((1,), (0,))):
    high, low = halves(value)
    return dot(high, table, dims) + dot(low, table, dims)


def roll(value, shift, axis):
    size = value.shape[axis]
    shift = shift % size
    return value if shift == 0 else pltpu.roll(value, shift, axis)


def lookup(classes, coef_ref, row):
    total = jnp.zeros_like(classes)
    for k in range(coef_ref.shape[1]):
        total = jnp.where(classes == k + 1.0, coef_ref[row, k], total)
    return total


def col_faces(get, p):
    lane = iota((p.Z, p.Y), 1) // 2
    total = jnp.zeros((p.Z, p.Y), F32)
    for i in range(p.X):
        total = jnp.where(lane == i, roll(get(i), 2 * i + 1, 1), total)
    return total


def swap_lanes(value):
    even = iota(value.shape, 1) % 2 == 0
    return jnp.where(even, roll(value, -1, 1), roll(value, 1, 1))


def shifted(value, axis, before, after):
    size = value.shape[axis]
    at = iota(value.shape, axis)
    low = jnp.where(at == 0, before, roll(value, 1, axis))
    high = jnp.where(at == size - 1, after, roll(value, -1, axis))
    return low, high


def plane_weights(kap, row_m, row_p, col_m, col_p):
    up, down = shifted(kap, 0, row_m, row_p)
    left, right = shifted(kap, 1, col_m, col_p)
    row, lane = iota(kap.shape, 0) % 4, iota(kap.shape, 1) % 4
    return (
        jnp.where(row == 0, kap + up, kap),
        jnp.where(row == 3, kap + down, kap),
        jnp.where(lane == 0, kap + left, kap),
        jnp.where(lane == 3, kap + right, kap),
    )


KAP, WZM, WZP, WYM, WYP, BASE, BETA = range(7)


class Brick:
    def __init__(self, p, cst_ref, kap_xm, kap_xp):
        self.p, self.cst, self.kap_xm, self.kap_xp = p, cst_ref, kap_xm, kap_xp

    def of(self, quantity, i):
        return self.cst[quantity, i // 4]

    def x_weights(self, i):
        kap = self.of(KAP, i)
        low = high = kap
        if i % 4 == 0:
            low = kap + (self.of(KAP, i - 1) if i else self.kap_xm)
        if i % 4 == 3:
            high = kap + (self.of(KAP, i + 1) if i + 1 < self.p.X else self.kap_xp)
        return low, high

    def diagonal(self, i):
        low, high = self.x_weights(i)
        return self.of(BASE, i) + (low + high)

    def neighbours(self, i, get, halo=None):
        p, v = self.p, get(i)
        low, high = self.x_weights(i)
        total = jnp.zeros_like(v)
        if i:
            total = total + low * get(i - 1)
        elif halo is not None:
            total = total + low * halo[0]
        if i + 1 < p.X:
            total = total + high * get(i + 1)
        elif halo is not None:
            total = total + high * halo[1]
        if halo is None:
            ends = (0.0, 0.0, 0.0, 0.0)
        else:
            yh = halo[4]
            ends = (halo[2][i : i + 1], halo[3][i : i + 1], yh[:, 2 * i : 2 * i + 1], yh[:, 2 * i + 1 : 2 * i + 2])
        up, down = shifted(v, 0, ends[0], ends[1])
        left, right = shifted(v, 1, ends[2], ends[3])
        total = total + self.of(WZM, i) * up + self.of(WZP, i) * down
        return total + self.of(WYM, i) * left + self.of(WYP, i) * right

    def from_halo(self, i, halo):
        p = self.p
        row, lane = iota((p.Z, p.Y), 0), iota((p.Z, p.Y), 1)
        yh = halo[4]
        total = jnp.where(row == 0, self.of(WZM, i) * halo[2][i : i + 1], 0.0)
        total = jnp.where(row == p.Z - 1, self.of(WZP, i) * halo[3][i : i + 1], total)
        total = total + jnp.where(lane == 0, self.of(WYM, i) * yh[:, 2 * i : 2 * i + 1], 0.0)
        total = total + jnp.where(lane == p.Y - 1, self.of(WYP, i) * yh[:, 2 * i + 1 : 2 * i + 2], 0.0)
        if i == 0:
            total = total + self.x_weights(i)[0] * halo[0]
        if i == p.X - 1:
            total = total + self.x_weights(i)[1] * halo[1]
        return total


def residual_plane(brick, i, get, halo, f):
    v = get(i)
    return f - brick.diagonal(i) * v + brick.neighbours(i, get, halo) - brick.of(BETA, i) * v * v * v


def put_rows(ref, stride, offset, n, rows):
    height = -(-rows.shape[0] // n)
    if rows.shape[0] < height * n:
        rows = jnp.concatenate([rows, jnp.zeros((height * n - rows.shape[0], rows.shape[1]), F32)], axis=0)
    for k in range(height):
        ref[pl.ds(offset + k, n, stride=stride), :] = rows[k * n : (k + 1) * n]


def get_rows(ref, stride, offset, n, count):
    height = -(-count // n)
    parts = [ref[pl.ds(offset + k, n, stride=stride), :] for k in range(height)]
    value = parts[0] if height == 1 else jnp.concatenate(parts, axis=0)
    return value[:count]


class Bounds:
    def __init__(self, p):
        self.uxm, self.uxp = (0, p.Z), (p.Z, p.Z)
        self.uzm, self.uzp = (2 * p.Z, p.X), (2 * p.Z + p.X, p.X)
        self.uy = (2 * p.Z + 2 * p.X, p.Z)
        self.count = 3 * p.Z + 2 * p.X


def read(ref, span):
    return ref[span[0] : span[0] + span[1], :]


def write_bounds(ref, b, values):
    for span, value in zip((b.uxm, b.uxp, b.uzm, b.uzp, b.uy), values):
        ref[span[0] : span[0] + span[1], :] = value


def read_bounds(ref, b):
    return tuple(read(ref, span) for span in (b.uxm, b.uxp, b.uzm, b.uzp, b.uy))


def advance(p, brick, get, residual, rxz, ry, s_ref, r_scr, z_scr, z2_scr):
    X, Z = p.X, p.Z
    for i in range(X):
        r = residual(i)
        r_scr[i * Z : (i + 1) * Z, :] = r
        z_scr[i] = r * (DAMPING / brick.diagonal(i))
    z1 = lambda i: z_scr[i]
    coarse = dot_wide_right(rxz[...], r_scr[...])
    coarse = dot_wide_right(ry[...], coarse, ((1,), (1,))) * (1.0 / 216.0)
    for i in range(X):
        v = z1(i)
        smooth = (2.0 - DAMPING) * v + (DAMPING / brick.diagonal(i)) * brick.neighbours(i, z1)
        z2_scr[i] = smooth
        s_ref[i] = get(i) + smooth
    return coarse.astype(BF16)


def start_cycle(p, brick, get, residual, classes, rxz, ry, sy, s_ref, z1b_ref, go_ref, r_scr, z_scr, z2_scr, go_scr):
    X, Z, n = p.X, p.Z, p.n
    coarse = advance(p, brick, get, residual, rxz, ry, s_ref, r_scr, z_scr, z2_scr)
    z1 = lambda i: z_scr[i]
    rows = sy[pl.ds(pl.multiple_of(lax.axis_index("by") * p.cy + 8, 8), p.cy), :]
    part = dot(rows.T, coarse)
    for j in range(n):
        go_scr[j * p.go : j * p.go + p.modes, :] = part[j * p.modes : (j + 1) * p.modes]
    z2 = lambda i: z2_scr[i]
    z1_y, z2_y = col_faces(z1, p), col_faces(z2, p)
    z1_zm, z1_zp = z_scr[:, 0, :], z_scr[:, Z - 1, :]
    write_bounds(z1b_ref, Bounds(p), (z1(0), z1(X - 1), z1_zm, z1_zp, z1_y))
    lane = iota((Z, p.Y), 1)
    sides = jnp.where(lane < 2 * X, z1_y, roll(z2_y, 2 * X, 1))
    edges = [z_scr[0, 0:1, :], z_scr[0, Z - 1 : Z, :], z_scr[X - 1, 0:1, :], z_scr[X - 1, Z - 1 : Z, :]]
    edges += [z1_y[0:1], z1_y[Z - 1 : Z]]
    if classes is None:
        sides = jnp.where(lane < 4 * X, sides, 0.0)
    else:
        cls, cls_y = classes
        sides = jnp.where(lane < 4 * X, sides, roll(cls_y, 4 * X, 1))
        sides = jnp.where(lane < 6 * X, sides, 0.0)
        edges += [cls(0)[0:1], cls(0)[Z - 1 : Z], cls(X - 1)[0:1], cls(X - 1)[Z - 1 : Z]]
        edges += [cls_y[0:1], cls_y[Z - 1 : Z]]
    pieces = (
        jnp.concatenate([z1(0), z2(0)], axis=0),
        jnp.concatenate([z1(X - 1), z2(X - 1)], axis=0),
        jnp.concatenate([z1_zm, z2_scr[:, 0, :]], axis=0),
        jnp.concatenate([z1_zp, z2_scr[:, Z - 1, :]], axis=0),
        sides,
        jnp.concatenate(edges, axis=0),
    )
    for piece, offset in zip(pieces, p.offsets):
        put_rows(go_scr, p.go, p.go_halo + offset, n, piece)
    used = p.go_halo + sum(p.heights)
    for k in range(used, p.go):
        go_scr[pl.ds(k, n, stride=p.go), :] = jnp.zeros((n, p.Y), F32)
    go_ref[...] = go_scr[...].astype(BF16)


def sides_kernel(p, u_ref, y_ref):
    y_ref[...] = col_faces(lambda i: u_ref[i], p)


def pack_kernel(p, index_ref, u_ref, uy_ref, cls_ref, xa_ref, xb_ref, za_ref, zb_ref, y_ref):
    X, Z, Y = p.X, p.Z, p.Y
    spread_z = (iota((Z, Z // 4), 0) // 4 == iota((Z, Z // 4), 1)).astype(BF16)
    spread_y = (iota((Y // 4, Y), 1) // 4 == iota((Y // 4, Y), 0)).astype(BF16)
    for a in range(X // 4):
        element = (index_ref[a] + 1).astype(F32).astype(BF16)
        cls_ref[a] = dot(dot(spread_z, element).astype(BF16), spread_y)
    cls = lambda i: cls_ref[i // 4]

    def face(axis, low, high, a_ref, b_ref, at):
        even = lax.axis_index(axis) % 2 == 0
        count = low.shape[0]
        a_ref[at : at + count, :] = jnp.where(even, high, low)
        b_ref[at : at + count, :] = jnp.where(even, low, high)

    face("bx", u_ref[0], u_ref[X - 1], xa_ref, xb_ref, 0)
    face("bx", cls(0), cls(X - 1), xa_ref, xb_ref, Z)
    rows = lambda z: jnp.concatenate([cls(i)[z : z + 1] for i in range(X)], axis=0)
    face("bz", u_ref[:, 0, :], u_ref[:, Z - 1, :], za_ref, zb_ref, 0)
    face("bz", rows(0), rows(Z - 1), za_ref, zb_ref, X)
    y_ref[0:Z, :] = uy_ref[...]
    y_ref[Z : 2 * Z, :] = col_faces(cls, p)


def received(axis, count, a_ref, b_ref):
    at = lax.axis_index(axis)
    even = at % 2 == 0
    a, b = a_ref[...], b_ref[...]
    low = jnp.where(even, b, a)
    high = jnp.where(even, a, b)
    return jnp.where(at > 0, low, 0.0), jnp.where(at < count - 1, high, 0.0)


def prepare_kernel(p, coef, u_ref, f_ref, cls_ref, cst_ref, r_ref):
    for a in range(p.X // 4):
        kap = lookup(cls_ref[a], coef, 0)
        wzm, wzp, wym, wyp = plane_weights(kap, 0.0, 0.0, 0.0, 0.0)
        cst_ref[KAP, a] = kap
        cst_ref[WZM, a] = wzm
        cst_ref[WZP, a] = wzp
        cst_ref[WYM, a] = wym
        cst_ref[WYP, a] = wyp
        cst_ref[BASE, a] = lookup(cls_ref[a], coef, 1) + ((wzm + wzp) + (wym + wyp))
        cst_ref[BETA, a] = lookup(cls_ref[a], coef, 2)
    brick = Brick(p, cst_ref, 0.0, 0.0)
    get = lambda i: u_ref[i]
    for i in range(p.X):
        r_ref[i] = residual_plane(brick, i, get, None, f_ref[i])


def neighbours_in(p, coef, u_ref, r_ref, cst0_ref, xa, xb, za, zb, ya, yb, uhb_ref, clsb_ref, cst_ref):
    X, Z, Y, b = p.X, p.Z, p.Y, Bounds(p)
    xm, xp = received("bx", p.nx, xa, xb)
    zm, zp = received("bz", p.nz, za, zb)
    ym, yp = received("by", p.ny, ya, yb)
    y = jnp.where(iota(ym.shape, 1) % 2 == 0, ym, yp)
    halo = (xm[:Z], xp[:Z], zm[:X], zp[:X], y[:Z])
    outside = (xm[Z:], xp[Z:], zm[X:], zp[X:], y[Z:])
    write_bounds(uhb_ref, b, halo)
    write_bounds(clsb_ref, b, outside)
    kap_h = tuple(lookup(value, coef, 0) for value in outside)
    row, lane = iota((Z, Y), 0), iota((Z, Y), 1)
    more = []
    for a in range(X // 4):
        i = 4 * a
        ends = (
            (WZM, jnp.where(row == 0, kap_h[2][i : i + 1], 0.0)),
            (WZP, jnp.where(row == Z - 1, kap_h[3][i : i + 1], 0.0)),
            (WYM, jnp.where(lane == 0, kap_h[4][:, 2 * i : 2 * i + 1], 0.0)),
            (WYP, jnp.where(lane == Y - 1, kap_h[4][:, 2 * i + 1 : 2 * i + 2], 0.0)),
        )
        for k, end in ends:
            cst_ref[k, a] = cst0_ref[k, a] + end
        more.append((ends[0][1] + ends[1][1]) + (ends[2][1] + ends[3][1]))
        cst_ref[BASE, a] = cst0_ref[BASE, a] + more[a]
        cst_ref[KAP, a] = cst0_ref[KAP, a]
        cst_ref[BETA, a] = cst0_ref[BETA, a]
    brick = Brick(p, cst_ref, kap_h[0], kap_h[1])

    def residual(i):
        added = more[i // 4]
        if i == 0:
            added = added + kap_h[0]
        if i == X - 1:
            added = added + kap_h[1]
        return r_ref[i] - added * u_ref[i] + brick.from_halo(i, halo)

    return brick, residual


def first_kernel(p, coef, u_ref, r_ref, cls_ref, cst0_ref, xa, xb, za, zb, ya, yb, rxz, ry, sy,
                 go_ref, s_ref, z1b_ref, uhb_ref, clsb_ref, cst_ref, r_scr, z_scr, z2_scr, go_scr):
    brick, residual = neighbours_in(p, coef, u_ref, r_ref, cst0_ref, xa, xb, za, zb, ya, yb, uhb_ref, clsb_ref, cst_ref)
    cls = lambda i: cls_ref[i // 4]
    start_cycle(p, brick, lambda i: u_ref[i], residual, (cls, col_faces(cls, p)), rxz, ry, sy,
                s_ref, z1b_ref, go_ref, r_scr, z_scr, z2_scr, go_scr)


def owner_kernel(p, coef, in_ref, wz, wx, wxt, wzi, lamxz, lamy, out_ref, in_scr, out_scr):
    n, m, nx, ny, nz = p.n, p.modes, p.nx, p.ny, p.nz
    me = (lax.axis_index("bx") * ny + lax.axis_index("by")) * nz + lax.axis_index("bz")
    in_scr[...] = in_ref[...].astype(F32)
    rows = []
    for bx in range(nx):
        lanes = []
        for bz in range(nz):
            total = None
            for by in range(ny):
                at = ((bx * ny + by) * nz + bz) * p.go
                piece = in_scr[at : at + m, :]
                total = piece if total is None else total + piece
            lanes.append(total)
        rows.append(jnp.concatenate(lanes, axis=1))
    data = jnp.concatenate(rows, axis=0)
    data = dot_wide_right(wz[...], data, ((1,), (1,)))
    data = jnp.concatenate([data[x * p.NZ : (x + 1) * p.NZ] for x in range(p.cx)], axis=1)
    data = dot_wide_left(data, wx[...])
    classes = coef.shape[1]
    kap_mean = sum(coef[0, k] for k in range(classes)) * (1.0 / classes)
    sig_mean = sum(coef[1, k] for k in range(classes)) * (1.0 / classes)
    data = data / (kap_mean * (lamxz[...] + lamy[me]) + sig_mean)
    data = dot_wide_left(data, wxt[...])
    width = nx * m
    data = jnp.concatenate([data[:, x * width : (x + 1) * width] for x in range(p.cx)], axis=0)
    high, low = halves(data)
    high, low = high.T, low.T
    lane = iota((m, p.Y), 1)
    for bz in range(nz):
        back = dot(high, wzi[bz]) + dot(low, wzi[bz])
        core = lambda bx: back[bx * m : (bx + 1) * m, : p.lanes]
        for bx in range(nx):
            ends = roll(back[bx * m : (bx + 1) * m, p.lanes :], 2 * p.cz, 1)
            below = roll(core(bx - 1), p.cz - p.lanes, 1) if bx else jnp.zeros((m, p.lanes), F32)
            above = roll(core(bx + 1), p.cz, 1) if bx + 1 < nx else jnp.zeros((m, p.lanes), F32)
            extra = jnp.where(lane < p.cz, below, jnp.where(lane < 2 * p.cz, above, ends))
            mine = core(bx)
            for by in range(ny):
                at = ((bx * ny + by) * nz + bz) * p.back
                out_scr[at : at + m, :] = mine
                out_scr[at + m : at + 2 * m, :] = extra

    device = iota((n, p.Y), 0)
    at_x, at_y, at_z = device // (ny * nz), (device // nz) % ny, device % nz

    def shift(value, dx, dy, dz):
        value = roll(value, -((dx * ny + dy) * nz + dz), 0)
        for at, step, count in ((at_x, dx, nx), (at_y, dy, ny), (at_z, dz, nz)):
            if step:
                value = jnp.where((at + step >= 0) & (at + step < count), value, 0.0)
        return value

    def take(k):
        return in_scr[pl.ds(p.go_halo + k, n, stride=p.go), :]

    def give(k, value):
        out_scr[pl.ds(p.back_halo + k, n, stride=p.back), :] = value

    for to, source, step in ((0, 1, (-1, 0, 0)), (1, 0, (1, 0, 0)), (2, 3, (0, 0, -1)), (3, 2, (0, 0, 1))):
        for k in range(p.heights[to]):
            give(p.offsets[to] + k, shift(take(p.offsets[source] + k), *step))
    lane = iota((n, p.Y), 1)
    even = lane % 2 == 0
    first, X2 = p.edge_lane, 2 * p.X
    for k in range(p.heights[4]):
        sides = take(p.offsets[4] + k)
        moved = jnp.where(lane < first + 2, roll(sides, first, 1), roll(sides, first + 2 - (X2 - 2), 1))
        moved = jnp.where(lane < first + 4, moved, roll(sides, first + 4 - 2 * X2, 1))
        moved = jnp.where(lane < first + 6, moved, roll(sides, first + 6 - (3 * X2 - 2), 1))
        which = (lane - first) % 4
        corner = jnp.where(
            which < 2,
            jnp.where(even, shift(moved, 1, -1, 0), shift(moved, 1, 1, 0)),
            jnp.where(even, shift(moved, -1, -1, 0), shift(moved, -1, 1, 0)),
        )
        plain = jnp.where(even, shift(sides, 0, -1, 0), shift(sides, 0, 1, 0))
        give(p.offsets[4] + k, jnp.where(lane < first, plain, jnp.where(lane < first + 8, corner, 0.0)))
    edges = take(p.offsets[5])
    kind = me % 6
    moved = jnp.where(even, shift(edges, 0, -1, -1), shift(edges, 0, 1, -1))
    for k, value in (
        (0, lambda: shift(edges, 1, 0, 1)),
        (1, lambda: shift(edges, 1, 0, -1)),
        (2, lambda: shift(edges, -1, 0, 1)),
        (3, lambda: shift(edges, -1, 0, -1)),
        (4, lambda: jnp.where(even, shift(edges, 0, -1, 1), shift(edges, 0, 1, 1))),
    ):
        moved = jnp.where(kind == k, value(), moved)
    give(p.offsets[5], moved)
    used = p.back_halo + sum(p.heights)
    for k in range(used, p.back):
        out_scr[pl.ds(k, n, stride=p.back), :] = jnp.zeros((n, p.Y), F32)
    out_ref[...] = out_scr[...].astype(BF16)


class Arrived:
    def __init__(self, p, ref):
        X, Z = p.X, p.Z
        rows = (2 * Z, 2 * Z, 2 * X, 2 * X, Z, 12)
        xm, xp, zm, zp, sides, edges = (
            get_rows(ref, p.back, p.back_halo + offset, p.n, count) for offset, count in zip(p.offsets, rows)
        )
        self.p, self.ref, self.sides, self.edges = p, ref, sides, edges
        self.z1 = (xm[:Z], xp[:Z], zm[:X], zp[:X], sides)
        self.z2 = (xm[Z:], xp[Z:], zm[X:], zp[X:], roll(sides, -2 * X, 1))

    def xz(self, kind, sx, sz):
        k = 6 * kind + (0 if sx else 2) + (0 if sz else 1)
        return self.edges[k : k + 1]

    def zy(self, kind, sz):
        k = 6 * kind + (4 if sz else 5)
        return self.edges[k : k + 1]

    def xy(self, kind, sx, sy):
        lane = self.p.edge_lane + 4 * kind + (0 if sx else 2) + sy
        return self.sides[:, lane : lane + 1]

    def xy_lanes(self, kind, plain):
        first, X2 = self.p.edge_lane + 4 * kind, 2 * self.p.X
        lane = iota(plain.shape, 1)
        value = jnp.where(lane < X2, plain, roll(self.sides, X2 - first, 1))
        return jnp.where(lane >= self.p.Y - 2, roll(self.sides, self.p.Y - 2 - first - 2, 1), value)


def coarse_rows(p, ref, sy, pyt, pall, pyh):
    n, m = p.n, p.modes
    core = jnp.concatenate([ref[j * p.back : j * p.back + m, :] for j in range(n)], axis=0)
    extra = jnp.concatenate([ref[j * p.back + m : j * p.back + 2 * m, :] for j in range(n)], axis=0)
    modes = jnp.concatenate([core, extra], axis=1).astype(BF16)
    rows = sy[pl.ds(pl.multiple_of(lax.axis_index("by") * p.cy, 8), p.cy + 16), :]
    values = dot(rows, modes).astype(BF16)
    along = dot(values[8 : 8 + p.cy].T, pyt[...])
    count = pall.shape[0] - p.Z
    nodes = dot_wide_right(pall[:count], along) * (1.0 / 27.0)
    weights = pall[count:, : p.lanes].astype(F32)
    ends = [weights * values.astype(F32)[k : k + 1, : p.lanes] for k in (7, 8 + p.cy)]
    side = dot_wide_left(jnp.concatenate(ends, axis=1), pyh[...]) * (1.0 / 27.0)
    return nodes, side


def column(row, count, side):
    shape = (count, row.shape[1])
    pick = iota(shape, 1) == 2 * iota(shape, 0) + side
    return jnp.sum(jnp.where(pick, row, 0.0), axis=1, keepdims=True)


def finish_cycle(p, coef, brick, now, first, s_ref, z1b_ref, uhb_ref, clsb_ref, nodes, side, u_ref):
    X, Z, b = p.X, p.Z, Bounds(p)
    for i in range(X):
        u_ref[i] = s_ref[i] + (DAMPING / brick.diagonal(i)) * brick.from_halo(i, now.z1) + nodes[i * Z : (i + 1) * Z]
    old, cls, own = read_bounds(uhb_ref, b), read_bounds(clsb_ref, b), read_bounds(z1b_ref, b)
    kap = lambda value: lookup(value, coef, 0)
    halo = []

    def new(k, weights, toward, others, correction):
        kap_here = kap(cls[k])
        diagonal = lookup(cls[k], coef, 1) + (kap_here + toward) + ((weights[0] + weights[1]) + (weights[2] + weights[3]))
        total = toward * own_faces[k]
        for part in others:
            total = total + part
        value = old[k] + now.z2[k] + (DAMPING / diagonal) * total + correction
        halo.append(jnp.where(cls[k] > 0.5, value, 0.0))

    own_faces = list(own[:4]) + [swap_lanes(own[4])]
    at = X * Z
    for k in range(2):
        kap_here = kap(cls[k])
        row_m, row_p = kap(first.xz(1, k, 0)), kap(first.xz(1, k, 1))
        col_m, col_p = kap(first.xy(1, k, 0)), kap(first.xy(1, k, 1))
        w = plane_weights(kap_here, row_m, row_p, col_m, col_p)
        row, lane = iota((Z, p.Y), 0), iota((Z, p.Y), 1)
        others = (
            jnp.where(row == 0, w[0] * now.xz(0, k, 0), 0.0),
            jnp.where(row == Z - 1, w[1] * now.xz(0, k, 1), 0.0),
            jnp.where(lane == 0, w[2] * now.xy(0, k, 0), 0.0),
            jnp.where(lane == p.Y - 1, w[3] * now.xy(0, k, 1), 0.0),
        )
        toward = kap_here + brick.of(KAP, 0 if k == 0 else X - 1)
        new(k, w, toward, others, nodes[at : at + Z])
        at += Z
    for k in range(2):
        kap_here = kap(cls[2 + k])
        row_m, row_p = kap(first.xz(1, 0, k)), kap(first.xz(1, 1, k))
        col_m, col_p = (kap(column(first.zy(1, k), X, side_y)) for side_y in range(2))
        w = plane_weights(kap_here, row_m, row_p, col_m, col_p)
        row, lane = iota((X, p.Y), 0), iota((X, p.Y), 1)
        others = (
            jnp.where(row == 0, w[0] * now.xz(0, 0, k), 0.0),
            jnp.where(row == X - 1, w[1] * now.xz(0, 1, k), 0.0),
            jnp.where(lane == 0, w[2] * column(now.zy(0, k), X, 0), 0.0),
            jnp.where(lane == p.Y - 1, w[3] * column(now.zy(0, k), X, 1), 0.0),
        )
        z = 0 if k == 0 else Z - 1
        mine = jnp.concatenate([brick.of(KAP, i)[z : z + 1] for i in range(X)], axis=0)
        new(2 + k, w, kap_here + mine, others, nodes[at : at + X])
        at += X
    wide = kap(first.xy_lanes(1, cls[4]))
    z1_wide = now.xy_lanes(0, now.z1[4])
    row_m, row_p = kap(first.zy(1, 0)), kap(first.zy(1, 1))
    up, down = shifted(wide, 0, row_m, row_p)
    left, right = roll(wide, 2, 1), roll(wide, -2, 1)
    row, lane = iota((Z, p.Y), 0), iota((Z, p.Y), 1)
    w = (
        jnp.where(row % 4 == 0, wide + up, wide),
        jnp.where(row % 4 == 3, wide + down, wide),
        jnp.where((lane // 2) % 4 == 0, wide + left, wide),
        jnp.where((lane // 2) % 4 == 3, wide + right, wide),
    )
    others = (
        jnp.where(row == 0, w[0] * now.zy(0, 0), 0.0),
        jnp.where(row == Z - 1, w[1] * now.zy(0, 1), 0.0),
        jnp.where(lane // 2 == 0, w[2] * roll(z1_wide, 2, 1), 0.0),
        jnp.where(lane // 2 == X - 1, w[3] * roll(z1_wide, -2, 1), 0.0),
    )
    mine = swap_lanes(col_faces(lambda i: brick.of(KAP, i), p))
    new(4, w, wide + mine, others, side)
    return tuple(halo)


def middle_kernel(p, coef, in_ref, f_ref, s_ref, z1b_ref, uhb_ref, clsb_ref, cst_ref,
                  sy, pyt, pall, pyh, rxz, ry,
                  go_ref, s_out, z1b_out, uhb_out, in_scr, u_scr, r_scr, z_scr, z2_scr, go_scr):
    in_scr[...] = in_ref[...].astype(F32)
    b = Bounds(p)
    outside = read_bounds(clsb_ref, b)
    brick = Brick(p, cst_ref, lookup(outside[0], coef, 0), lookup(outside[1], coef, 0))
    now = Arrived(p, in_scr)
    nodes, side = coarse_rows(p, in_scr, sy, pyt, pall, pyh)
    halo = finish_cycle(p, coef, brick, now, now, s_ref, z1b_ref, uhb_ref, clsb_ref, nodes, side, u_scr)
    write_bounds(uhb_out, b, halo)
    get = lambda i: u_scr[i]
    residual = lambda i: residual_plane(brick, i, get, halo, f_ref[i])
    start_cycle(p, brick, get, residual, None, rxz, ry, sy,
                s_out, z1b_out, go_ref, r_scr, z_scr, z2_scr, go_scr)


def last_kernel(p, coef, in_ref, first_ref, f_ref, s_ref, z1b_ref, uhb_ref, clsb_ref, cst_ref,
                sy, pyt, pall, pyh, u_out, r_out, in_scr, first_scr):
    in_scr[...] = in_ref[...].astype(F32)
    first_scr[...] = first_ref[...].astype(F32)
    outside = read_bounds(clsb_ref, Bounds(p))
    brick = Brick(p, cst_ref, lookup(outside[0], coef, 0), lookup(outside[1], coef, 0))
    now, first = Arrived(p, in_scr), Arrived(p, first_scr)
    nodes, side = coarse_rows(p, in_scr, sy, pyt, pall, pyh)
    halo = finish_cycle(p, coef, brick, now, first, s_ref, z1b_ref, uhb_ref, clsb_ref, nodes, side, u_out)
    for i in range(p.X):
        r_out[i] = residual_plane(brick, i, lambda k: u_out[k], halo, f_ref[i])


class Sends:
    def __init__(self, p):
        X, Z = p.X, p.Z
        self.first = p.cy + Z
        self.x_face, self.z_face = p.NY, p.NY
        self.x_rows = p.NY + 3 * Z
        self.z_rows = p.NY + 2 * X + 16
        self.xz_rows = p.NY + 16
        self.second = 2 * p.cx * p.NZ * p.NY // p.Y
        self.last = self.second + 3 * Z + 16
        self.faces = 4 * Z + 4 * X


def pick(condition, a, b):
    return jnp.where(condition, a, b)


def send_first(p, coarse, z_scr, z2_scr, z1b_ref, a_ref, faces_ref):
    X, Z = p.X, p.Z
    z1, z2 = (lambda i: z_scr[i]), (lambda i: z2_scr[i])
    z1_y, z2_y = col_faces(z1, p), col_faces(z2, p)
    z_rows = (z_scr[:, 0, :], z_scr[:, Z - 1, :], z2_scr[:, 0, :], z2_scr[:, Z - 1, :])
    write_bounds(z1b_ref, Bounds(p), (z1(0), z1(X - 1), z_rows[0], z_rows[1], z1_y))
    a_ref[0 : p.cy, :] = coarse
    lane = iota((Z, p.Y), 1)
    a_ref[p.cy :, :] = jnp.where(lane < 2 * X, z1_y, roll(z2_y, 2 * X, 1)).astype(BF16)
    for k, plane in enumerate((z1(0), z1(X - 1), z2(0), z2(X - 1))):
        faces_ref[k * Z : (k + 1) * Z, :] = plane.astype(BF16)
    for k, rows in enumerate(z_rows):
        faces_ref[4 * Z + k * X : 4 * Z + (k + 1) * X, :] = rows.astype(BF16)


def face_x(p, faces_ref, high):
    X, Z = p.X, p.Z
    return tuple(pick(high, faces_ref[(k + 1) * Z : (k + 2) * Z, :], faces_ref[k * Z : (k + 1) * Z, :]) for k in (0, 2))


def face_z(p, faces_ref, high):
    X, at = p.X, 4 * p.Z
    return tuple(
        pick(high, faces_ref[at + (k + 1) * X : at + (k + 2) * X, :], faces_ref[at + k * X : at + (k + 1) * X, :]) for k in (0, 2)
    )


def pad_rows(rows, count):
    rows = [row.astype(F32) for row in rows]
    return jnp.concatenate(rows + [jnp.zeros((count - len(rows), rows[0].shape[1]), F32)], axis=0).astype(BF16)


def y_block(p, sides, cls_y):
    lane = iota(sides.shape, 1)
    return jnp.where(lane < 2 * p.X, sides, roll(cls_y, 2 * p.X, 1))


def after_first(p, *refs):
    ny = p.ny
    buffers, (faces_ref, clsb_ref, cls_ref, sy, x_ref, z_ref, xz_ref, sides_ref, all_scr) = refs[:ny], refs[ny:]
    X, Z, sends, b = p.X, p.Z, Sends(p), Bounds(p)
    bx, by, bz = (lax.axis_index(axis) for axis in AXES)
    low = high = jnp.zeros((Z, p.Y), F32)
    for d in range(ny):
        other = by ^ d
        all_scr[pl.ds(pl.multiple_of(other * p.cy, 16), p.cy), :] = buffers[d][0 : p.cy, :]
        if d:
            value = buffers[d][p.cy :, :].astype(F32)
            low = pick(other == by - 1, value, low)
            high = pick(other == by + 1, value, high)
    sides = jnp.where(iota((Z, p.Y), 1) % 2 == 0, low, high)
    sides_ref[...] = sides
    modes = dot(sy[8 : 8 + p.NY, :], all_scr[...]).astype(BF16)
    cls_y = read(clsb_ref, b.uy)
    odd, up = bx % 2 == 1, bz == 0
    for ref in (x_ref, z_ref, xz_ref):
        ref[0 : p.NY, :] = modes
    at = p.NY
    z1, z2 = face_x(p, faces_ref, odd)
    x_ref[at : at + Z, :] = z1
    x_ref[at + Z : at + 2 * Z, :] = z2
    x_ref[at + 2 * Z : at + 3 * Z, :] = y_block(p, sides, cls_y).astype(BF16)
    z1, z2 = face_z(p, faces_ref, up)
    z_ref[at : at + X, :] = z1
    z_ref[at + X : at + 2 * X, :] = z2
    z_ref[at + 2 * X : at + 2 * X + 16, :] = pad_rows(
        [pick(up, value[Z - 1 : Z], value[0:1]) for value in (sides, cls_y)], 16
    )
    z1 = z1.astype(F32)
    cls = pick(odd, cls_ref[X // 4 - 1], cls_ref[0])
    xz_ref[at : at + 16, :] = pad_rows(
        [pick(odd, z1[X - 1 : X], z1[0:1]), pick(up, cls[Z - 1 : Z], cls[0:1])], 16
    )


def after_second(p, own_ref, x_in, z_in, xz_in, faces_ref, clsb_ref, sides_ref, wzt, out_ref):
    X, Z, Y, sends, b = p.X, p.Z, p.Y, Sends(p), Bounds(p)
    bx, bz = lax.axis_index("bx"), lax.axis_index("bz")
    odd, up = bx % 2 == 1, bz == 0
    at = 0
    for one, two in ((own_ref, z_in), (x_in, xz_in)):
        one, two = one[0 : p.NY, :], two[0 : p.NY, :]
        data = jnp.concatenate([pick(up, one, two), pick(up, two, one)], axis=1)
        data = dot(wzt[...], data, ((1,), (1,))).astype(BF16)
        for k in range(p.NY // Y):
            rows = data.shape[0]
            out_ref[at : at + rows, :] = data[:, k * Y : (k + 1) * Y]
            at += rows
    z1, z2 = face_x(p, faces_ref, jnp.logical_not(odd))
    out_ref[at : at + Z, :] = z1
    out_ref[at + Z : at + 2 * Z, :] = z2
    out_ref[at + 2 * Z : at + 3 * Z, :] = y_block(p, sides_ref[...], read(clsb_ref, b.uy)).astype(BF16)
    beyond = z_in[p.NY : p.NY + X, :].astype(F32)
    classes = pick(up, read(clsb_ref, b.uzp), read(clsb_ref, b.uzm))
    out_ref[at + 3 * Z : at + 3 * Z + 16, :] = pad_rows(
        [pick(odd, value[0:1], value[X - 1 : X]) for value in (beyond, classes)], 16
    )


class Beyond:
    def __init__(self, p):
        X, Z = p.X, p.Z
        self.cross = 0
        self.core = Z
        self.z = 6 * Z
        self.y = 6 * Z + 4 * X
        self.kap = 10 * Z + 4 * X
        self.count = self.kap + Bounds(p).count


def rows_at(ref, at, count):
    return ref[at : at + count, :]


def beyond_kernel(p, coef, s_ref, z1b_ref, uhb_ref, clsb_ref, cls_ref, cst_ref, sides_ref, x_in, z_in, xz_in, s_out, out_ref):
    X, Z, Y, b, to = p.X, p.Z, p.Y, Bounds(p), Beyond(p)
    bx, bz = lax.axis_index("bx"), lax.axis_index("bz")
    odd, up = bx % 2 == 1, bz == 0
    some = (bx > 0) & (bx < p.nx - 1)
    kaps, sigs = lookup(clsb_ref[...], coef, 0), lookup(clsb_ref[...], coef, 1)
    out_ref[to.kap :, :] = kaps
    part = lambda value, span: value[span[0] : span[0] + span[1]]
    x_part = lambda value, high: pick(high, part(value, b.uxp), part(value, b.uxm))
    z_part = lambda value: pick(up, part(value, b.uzp), part(value, b.uzm))
    z1b, uhb = z1b_ref[...], uhb_ref[...]
    across = lambda at, count: pick(some, x_in[p.NY + at : p.NY + at + count, :].astype(F32), 0.0)
    x_z1, x_z2, block = across(0, Z), across(Z, Z), across(2 * Z, Z)
    corner = pick(some, xz_in[p.NY : p.NY + 16, :].astype(F32), 0.0)
    corner_z1, corner_kap = corner[0:1], lookup(corner[1:2], coef, 0)
    z_z1, z_z2 = (z_in[p.NY + k * X : p.NY + (k + 1) * X, :].astype(F32) for k in range(2))
    z_rows = z_in[p.NY + 2 * X : p.NY + 2 * X + 16, :].astype(F32)
    zy_z1, zy_kap = z_rows[0:1], lookup(z_rows[1:2], coef, 0)
    block_kap = lookup(block, coef, 0)
    sides = sides_ref[...]
    brick = Brick(p, cst_ref, part(kaps, b.uxm), part(kaps, b.uxp))
    halo = (pick(odd, 0.0, x_z1), pick(odd, x_z1, 0.0), pick(up, 0.0, z_z1), pick(up, z_z1, 0.0), sides)
    for i in range(X):
        s_out[i] = s_ref[i] + (DAMPING / brick.diagonal(i)) * brick.from_halo(i, halo)
    row, lane = iota((Z, Y), 0), iota((Z, Y), 1)
    face = lambda high: pick(high, brick.of(KAP, X - 1), brick.of(KAP, 0))

    k, sigma = x_part(kaps, odd), x_part(sigs, odd)
    toward = k + face(odd)
    X2 = 2 * X
    ends = lambda value, first: [pick(odd, value[:, first + c : first + c + 1], value[:, first + X2 - 2 + c : first + X2 - 1 + c]) for c in (0, 1)]
    col_kap, col_z1 = ends(block_kap, X2), ends(block, 0)
    w = plane_weights(k, pick(up, 0.0, corner_kap), pick(up, corner_kap, 0.0), col_kap[0], col_kap[1])
    total = toward * x_part(z1b, odd)
    total = total + jnp.where(row == pick(up, Z - 1, 0), pick(up, w[1], w[0]) * corner_z1, 0.0)
    total = total + jnp.where(lane == 0, w[2] * col_z1[0], 0.0) + jnp.where(lane == Y - 1, w[3] * col_z1[1], 0.0)
    diagonal = sigma + (k + toward) + ((w[0] + w[1]) + (w[2] + w[3]))
    value = x_part(uhb, odd) + x_z2 + (DAMPING / diagonal) * total
    out_ref[to.cross : to.cross + Z, :] = jnp.where(k > 0.0, value, 0.0)

    other = jnp.logical_not(odd)
    k, sigma = x_part(kaps, other), x_part(sigs, other)
    toward = k + face(other)
    for j, value in enumerate((k, toward, sigma + (k + toward), x_part(z1b, other), x_part(uhb, other))):
        out_ref[to.core + j * Z : to.core + (j + 1) * Z, :] = value

    k, sigma = z_part(kaps), z_part(sigs)
    own = jnp.concatenate([pick(up, cst_ref[KAP, i // 4, Z - 1 : Z, :], cst_ref[KAP, i // 4, 0:1, :]) for i in range(X)], axis=0)
    toward = k + own
    col_kap, col_z1 = ([column(value, X, c) for c in (0, 1)] for value in (zy_kap, zy_z1))
    w = plane_weights(k, pick(odd, 0.0, corner_kap), pick(odd, corner_kap, 0.0), col_kap[0], col_kap[1])
    zrow, zlane = iota((X, Y), 0), iota((X, Y), 1)
    total = toward * z_part(z1b)
    total = total + jnp.where(zrow == pick(odd, X - 1, 0), pick(odd, w[1], w[0]) * corner_z1, 0.0)
    total = total + jnp.where(zlane == 0, w[2] * col_z1[0], 0.0) + jnp.where(zlane == Y - 1, w[3] * col_z1[1], 0.0)
    diagonal = sigma + (k + toward) + ((w[0] + w[1]) + (w[2] + w[3]))
    for j, value in enumerate((z_part(uhb) + z_z2, total, diagonal, k)):
        out_ref[to.z + j * X : to.z + (j + 1) * X, :] = value

    k, sigma = part(kaps, b.uy), part(sigs, b.uy)
    toward = k + swap_lanes(col_faces(lambda i: brick.of(KAP, i), p))
    reach = lambda value, shift: pick(odd, roll(value, X2 + shift, 1), roll(value, Y - X2 + shift, 1))
    begin = pick(odd, X2, Y - 2)
    far = (lane >= begin) & (lane < begin + 2)
    wide = jnp.where(far, reach(block_kap, -X2), jnp.where(lane < X2, k, 0.0))
    wide_z1 = jnp.where(far, reach(block, 0), 0.0)
    above, below = shifted(wide, 0, pick(up, 0.0, zy_kap), pick(up, zy_kap, 0.0))
    left, right = roll(wide, 2, 1), roll(wide, -2, 1)
    place = lane // 2
    w = (
        jnp.where(row % 4 == 0, wide + above, wide),
        jnp.where(row % 4 == 3, wide + below, wide),
        jnp.where(place % 4 == 0, wide + left, wide),
        jnp.where(place % 4 == 3, wide + right, wide),
    )
    total = toward * swap_lanes(part(z1b, b.uy))
    total = total + jnp.where(row == pick(up, Z - 1, 0), pick(up, w[1], w[0]) * zy_z1, 0.0)
    total = total + jnp.where(place == 0, w[2] * roll(wide_z1, 2, 1), 0.0)
    total = total + jnp.where(place == X - 1, w[3] * roll(wide_z1, -2, 1), 0.0)
    diagonal = sigma + (k + toward) + ((w[0] + w[1]) + (w[2] + w[3]))
    for j, value in enumerate((part(uhb, b.uy) + roll(sides, -X2, 1), total, diagonal, k)):
        out_ref[to.y + j * Z : to.y + (j + 1) * Z, :] = value


def finish_staged(p, coef, brick, s_ref, beyond_ref, last_in, nodes, side, u_ref):
    X, Z, Y, to = p.X, p.Z, p.Y, Beyond(p)
    bx, bz = lax.axis_index("bx"), lax.axis_index("bz")
    odd, up = bx % 2 == 1, bz == 0
    start, X2 = Sends(p).second, 2 * X
    z1, z2, block = (last_in[start + k * Z : start + (k + 1) * Z, :].astype(F32) for k in range(3))
    corner = last_in[start + 3 * Z : start + 3 * Z + 16, :].astype(F32)
    corner_z1, corner_kap = corner[0:1], lookup(corner[1:2], coef, 0)
    block_kap = lookup(block, coef, 0)
    for i in range(X):
        value = s_ref[i] + nodes[i * Z : (i + 1) * Z]
        if i in (0, X - 1):
            weight = brick.x_weights(i)[0 if i == 0 else 1]
            here = odd if i == 0 else jnp.logical_not(odd)
            value = value + (DAMPING / brick.diagonal(i)) * (weight * pick(here, z1, 0.0))
        u_ref[i] = value
    row, lane = iota((Z, Y), 0), iota((Z, Y), 1)

    k, toward, diagonal, own, old = (rows_at(beyond_ref, to.core + j * Z, Z) for j in range(5))
    ends = lambda value, first: [pick(odd, value[:, first + X2 - 2 + c : first + X2 - 1 + c], value[:, first + c : first + c + 1]) for c in (0, 1)]
    col_kap, col_z1 = ends(block_kap, X2), ends(block, 0)
    w = plane_weights(k, pick(up, 0.0, corner_kap), pick(up, corner_kap, 0.0), col_kap[0], col_kap[1])
    total = toward * own
    total = total + jnp.where(row == pick(up, Z - 1, 0), pick(up, w[1], w[0]) * corner_z1, 0.0)
    total = total + jnp.where(lane == 0, w[2] * col_z1[0], 0.0) + jnp.where(lane == Y - 1, w[3] * col_z1[1], 0.0)
    diagonal = diagonal + ((w[0] + w[1]) + (w[2] + w[3]))
    core = jnp.where(k > 0.0, old + z2 + (DAMPING / diagonal) * total, 0.0)
    cross = rows_at(beyond_ref, to.cross, Z)
    at = X * Z
    below, above = nodes[at : at + Z], nodes[at + Z : at + 2 * Z]
    some = (bx > 0) & (bx < p.nx - 1)
    core = jnp.where(k > 0.0, core + pick(odd, below, above), 0.0)
    cross = pick(some, cross + pick(odd, above, below), 0.0)
    at += 2 * Z

    value, total, diagonal, k = (rows_at(beyond_ref, to.z + j * X, X) for j in range(4))
    edge = iota((X, Y), 0) == pick(odd, 0, X - 1)
    total = total + jnp.where(edge, (k + corner_kap) * corner_z1, 0.0)
    diagonal = diagonal + jnp.where(edge, corner_kap, 0.0)
    value = value + (DAMPING / diagonal) * total + pick(up, nodes[at + X : at + 2 * X], nodes[at : at + X])
    z = jnp.where(k > 0.0, value, 0.0)

    value, total, diagonal, k = (rows_at(beyond_ref, to.y + j * Z, Z) for j in range(4))
    begin = pick(odd, 0, X2 - 2)
    edge = (lane >= begin) & (lane < begin + 2)
    reach = lambda value, shift: pick(odd, roll(value, 2 - X2 + shift, 1), roll(value, X2 - 2 + shift, 1))
    edge_kap = reach(block_kap, -X2)
    total = total + jnp.where(edge, (k + edge_kap) * reach(block, 0), 0.0)
    diagonal = diagonal + jnp.where(edge, edge_kap, 0.0)
    y = jnp.where(k > 0.0, value + (DAMPING / diagonal) * total + side, 0.0)
    return pick(odd, core, cross), pick(odd, cross, core), pick(up, 0.0, z), pick(up, z, 0.0), y


def coarse_staged(p, own_ref, last_in, inverse, kx, kxi, zi, along_y, pall, pyh):
    Y, NY = p.Y, p.NY
    bx, bz = lax.axis_index("bx"), lax.axis_index("bz")
    rows, step, count = p.cx * p.NZ, p.cx * LOW, p.NX * LOW
    back = kxi[pl.ds(pl.multiple_of(bx * step, 16), step + 2 * LOW), :]
    table = kx[bx]
    parts = []
    for h in range(p.NZ // LOW):
        lines = []
        for ref in (own_ref, last_in):
            for block in range(2):
                at = [(block * (NY // Y) + k) * rows + h * step for k in range(NY // Y)]
                lines.append(jnp.concatenate([ref[i : i + step, :] for i in at], axis=1))
        modes = dot(table, jnp.concatenate(lines, axis=0)) * inverse[h * count : (h + 1) * count, :]
        parts.append(dot(back, modes.astype(BF16)).astype(BF16))
    values = dot(zi[bz], jnp.concatenate(parts, axis=0)).astype(BF16)
    values = dot(values, along_y[: p.NY, :]) + dot(values, along_y[p.NY :, :])
    count = pall.shape[0] - p.Z
    nodes = dot_wide_right(pall[:count, : p.lanes + p.extra], values[:, :Y]) * (1.0 / 27.0)
    ends = values[: p.lanes, Y:]
    spread = ends[:, 0:1] * pyh[: p.lanes].astype(F32) + ends[:, 1:2] * pyh[p.lanes :].astype(F32)
    side = dot_wide_right(pall[count:, : p.lanes], spread) * (1.0 / 27.0)
    return nodes, side


def inverse_kernel(p, coef, lam_xz, lam_y, sy, pye, out_ref, along_ref):
    classes = coef.shape[1]
    kap_mean = sum(coef[0, k] for k in range(classes)) * (1.0 / classes)
    sig_mean = sum(coef[1, k] for k in range(classes)) * (1.0 / classes)
    step = p.NX * LOW
    for h in range(p.NZ // LOW):
        lam = lam_xz[h * step : (h + 1) * step, :] + lam_y[...]
        out_ref[h * step : (h + 1) * step, :] = 1.0 / (kap_mean * lam + sig_mean)
    rows = sy[pl.ds(pl.multiple_of(lax.axis_index("by") * p.cy, 16), p.cy + 16), :]
    high, low = halves(dot(rows.T, pye[...]))
    along_ref[: p.NY, :] = high
    along_ref[p.NY :, :] = low


def first_staged(p, coef, u_ref, r_ref, cls_ref, cst0_ref, xa, xb, za, zb, ya, yb, rxz, ry,
                 a_ref, faces_ref, s_ref, z1b_ref, uhb_ref, clsb_ref, cst_ref, r_scr, z_scr, z2_scr):
    brick, residual = neighbours_in(p, coef, u_ref, r_ref, cst0_ref, xa, xb, za, zb, ya, yb, uhb_ref, clsb_ref, cst_ref)
    coarse = advance(p, brick, lambda i: u_ref[i], residual, rxz, ry, s_ref, r_scr, z_scr, z2_scr)
    send_first(p, coarse, z_scr, z2_scr, z1b_ref, a_ref, faces_ref)


def correct(p, coef, s_ref, beyond_ref, cst_ref, own, last_in, inverse, kx, kxi, zi, along_y, pall, pyh, u_ref):
    b, at = Bounds(p), Beyond(p).kap
    brick = Brick(p, cst_ref, rows_at(beyond_ref, at + b.uxm[0], p.Z), rows_at(beyond_ref, at + b.uxp[0], p.Z))
    nodes, side = coarse_staged(p, own, last_in, inverse, kx, kxi, zi, along_y, pall, pyh)
    return brick, finish_staged(p, coef, brick, s_ref, beyond_ref, last_in, nodes, side, u_ref)


def middle_staged(p, coef, f_ref, s_ref, beyond_ref, cst_ref, own, last_in, inverse, kx, kxi, zi, along_y, pall, pyh, rxz, ry,
                  a_ref, faces_ref, s_out, z1b_out, uhb_out, u_scr, r_scr, z_scr, z2_scr):
    brick, halo = correct(p, coef, s_ref, beyond_ref, cst_ref, own, last_in, inverse, kx, kxi, zi, along_y, pall, pyh, u_scr)
    write_bounds(uhb_out, Bounds(p), halo)
    get = lambda i: u_scr[i]
    residual = lambda i: residual_plane(brick, i, get, halo, f_ref[i])
    coarse = advance(p, brick, get, residual, rxz, ry, s_out, r_scr, z_scr, z2_scr)
    send_first(p, coarse, z_scr, z2_scr, z1b_out, a_ref, faces_ref)


def last_staged(p, coef, f_ref, s_ref, beyond_ref, cst_ref, own, last_in, inverse, kx, kxi, zi, along_y, pall, pyh,
                u_out, r_out, u_scr, r_scr, sems):
    brick, halo = correct(p, coef, s_ref, beyond_ref, cst_ref, own, last_in, inverse, kx, kxi, zi, along_y, pall, pyh, u_scr)
    copies = [pltpu.make_async_copy(u_scr, u_out, sems.at[0])]
    copies[0].start()
    chunk = p.X // 4
    for k in range(4):
        for i in range(k * chunk, (k + 1) * chunk):
            r_scr[i] = residual_plane(brick, i, lambda j: u_scr[j], halo, f_ref[i])
        part = pl.ds(k * chunk, chunk)
        copies.append(pltpu.make_async_copy(r_scr.at[part], r_out.at[part], sems.at[k + 1]))
        copies[-1].start()
    for copy in copies:
        copy.wait()


def call(kernel, p, name, coef, inputs, outputs, scratch, us=2, out_space=pltpu.VMEM):
    smem = [pl.BlockSpec(memory_space=pltpu.SMEM)] if coef is not None else []
    args = ([coef] if coef is not None else []) + list(inputs)
    return pl.pallas_call(
        functools.partial(kernel, p),
        out_shape=[jax.ShapeDtypeStruct(shape, dtype) for shape, dtype in outputs],
        in_specs=smem + [pl.BlockSpec(memory_space=pltpu.VMEM)] * len(inputs),
        out_specs=[pl.BlockSpec(memory_space=out_space)] * len(outputs),
        scratch_shapes=[pltpu.VMEM(shape, F32) if isinstance(shape, tuple) else shape for shape in scratch],
        compiler_params=pltpu.CompilerParams(vmem_limit_bytes=VMEM_LIMIT),
        cost_estimate=pl.CostEstimate(flops=0, bytes_accessed=us * 3_600_000, transcendentals=0),
        name=name,
    )(*args)


def swaps(axis, count, a, b, near=None):
    if count == 1:
        return a, b
    assert count % 2 == 0
    first = lax.ppermute(a, axis, [(i, i ^ 1) for i in range(count)])
    if count == 2:
        return first, first
    other = lambda i: (i + 1 if i % 2 else i - 1) % count
    if near is None:
        return first, lax.ppermute(b, axis, [(i, other(i)) for i in range(count)])
    name, size = near
    pairs = []
    for k in range(size):
        for i in range(count):
            to = (k ^ 1, i) if i in (0, count - 1) else (k, other(i))
            pairs.append((k * count + i, to[0] * count + to[1]))
    return first, lax.ppermute(b, (name, axis), pairs)


def body(forcing, start, element_class_index, class_coef):
    p = Plan(start.shape, *(lax.axis_size(axis) for axis in AXES))
    t = tables(p)
    X, Z, Y, n = p.X, p.Z, p.Y, p.n
    bounds = Bounds(p).count
    block, flat, cst = (X, Z, Y), (X * Z, Y), (7, X // 4, Z, Y)
    (uy,) = call(sides_kernel, p, "start_sides", None, (start,), [((Z, Y), F32)], [], us=20)
    cls, xa, xb, za, zb, yf = call(
        pack_kernel, p, "pack_faces", None, (element_class_index, start, uy),
        [((X // 4, Z, Y), F32)] + [((2 * Z, Y), F32)] * 2 + [((2 * X, Y), F32)] * 2 + [((2 * Z, Y), F32)], [], us=20,
    )
    xa, xb = swaps("bx", p.nx, xa, xb)
    za, zb = swaps("bz", p.nz, za, zb)
    ya, yb = swaps("by", p.ny, yf, yf, ("bx", p.nx) if p.nx % 2 == 0 else None)
    go_shape, back_shape = (n * p.go, Y), (n * p.back, Y)
    starting = [flat, block, block, go_shape]
    rxz, ry, sy = t["rxz"], t["ry"], t["sy"]
    cst0, r0 = call(prepare_kernel, p, "prepare", class_coef, (start, forcing, cls), [(cst, F32), (block, F32)], [], us=6)
    if p.staged:
        return staged_cycles(p, t, class_coef, forcing, cls, start, r0, cst0, (xa, xb, za, zb, ya, yb))
    go, s, z1b, uhb, clsb, coefs = call(
        first_kernel, p, "first_residual", class_coef,
        (start, r0, cls, cst0, xa, xb, za, zb, ya, yb, rxz, ry, sy),
        [(go_shape, BF16), (block, F32), ((bounds, Y), F32), ((bounds, Y), F32), ((bounds, Y), F32), (cst, F32)],
        starting,
    )
    prolong = (sy, t["pyt"], t["pall"], t["pyh"])
    first = None
    for cycle in range(CYCLES):
        came = lax.all_to_all(go, AXES, split_axis=0, concat_axis=0, tiled=True)
        (out,) = call(
            owner_kernel, p, "owned_modes", class_coef,
            (came, t["wz"], t["wx"], t["wxt"], t["wzi"], t["lamxz"], t["lamy"]),
            [(back_shape, BF16)], [go_shape, back_shape],
        )
        back = lax.all_to_all(out, AXES, split_axis=0, concat_axis=0, tiled=True)
        if cycle + 1 < CYCLES:
            assert first is None
            first = back
            go, s, z1b, uhb = call(
                middle_kernel, p, "next_residual", class_coef,
                (back, forcing, s, z1b, uhb, clsb, coefs) + prolong + (rxz, ry),
                [(go_shape, BF16), (block, F32), ((bounds, Y), F32), ((bounds, Y), F32)],
                [back_shape, block] + starting,
            )
        else:
            return tuple(call(
                last_kernel, p, "last_residual", class_coef,
                (back, first, forcing, s, z1b, uhb, clsb, coefs) + prolong,
                [(block, F32), (block, F32)], [back_shape, back_shape],
            ))


def staged_cycles(p, t, class_coef, forcing, cls, u0, r0, cst0, faces_in):
    X, Z, Y = p.X, p.Z, p.Y
    sends, bounds = Sends(p), (Bounds(p).count, Y)
    block, flat = (X, Z, Y), (X * Z, Y)
    out = [((sends.first, Y), BF16), ((sends.faces, Y), BF16), (block, F32), (bounds, F32), (bounds, F32)]
    scratch = [flat, block, block]
    inverse, along_y = call(
        inverse_kernel, p, "inverse_spectrum", class_coef, (t["lam_xz"], t["lam_y"], t["sy"], t["pye"]),
        [((p.NZ * p.NX, p.NY), F32), ((2 * p.NY, 2 * Y), BF16)], [],
    )
    a, faces, s, z1b, uhb, clsb, coefs = call(
        first_staged, p, "first_residual", class_coef, (u0, r0, cls, cst0) + faces_in + (t["rxz"], t["ry"]),
        out + [(bounds, F32), (cst0.shape, F32)], scratch,
    )
    pairs = lambda count, d: [(i, i ^ d) for i in range(count)]
    for cycle in range(CYCLES):
        came = [a] + [lax.ppermute(a, "by", pairs(p.ny, d)) for d in range(1, p.ny)]
        x, z, xz, sides = call(
            after_first, p, "y_modes", None, (*came, faces, clsb, cls, t["sy"]),
            [((rows, Y), BF16) for rows in (sends.x_rows, sends.z_rows, sends.xz_rows)] + [((Z, Y), F32)],
            [pltpu.VMEM((p.NY, Y), BF16)],
        )
        plane, across = p.nx * p.nz, (p.nx - 1) * p.nz
        x_in = lax.ppermute(x, ("bx", "bz"), pairs(plane, across))
        z_in = lax.ppermute(z, ("bx", "bz"), pairs(plane, 1))
        xz_in = lax.ppermute(xz, ("bx", "bz"), pairs(plane, across + 1))
        if cycle == 0:
            x_in, inverse, along_y = lax.optimization_barrier((x_in, inverse, along_y))
            back = (inverse, t["kx"], t["kxi"], t["zi"], along_y, t["pall"], t["pyh"])
        (own,) = call(
            after_second, p, "z_modes", None, (x, x_in, z_in, xz_in, faces, clsb, sides, t["wzt"]),
            [((sends.last, Y), BF16)], [],
        )
        last_in = lax.ppermute(own, "bx", pairs(p.nx, 1))
        s, beyond = call(
            beyond_kernel, p, "beyond", class_coef, (s, z1b, uhb, clsb, cls, coefs, sides, x_in, z_in, xz_in),
            [(block, F32), ((Beyond(p).count, Y), F32)], [],
        )
        inputs = (forcing, s, beyond, coefs, own, last_in) + back
        if cycle + 1 < CYCLES:
            a, faces, s, z1b, uhb = call(
                middle_staged, p, "next_residual", class_coef, inputs + (t["rxz"], t["ry"]), out, [block] + scratch
            )
        else:
            return tuple(call(
                last_staged, p, "last_residual", class_coef, inputs, [(block, F32), (block, F32)],
                [block, block, pltpu.SemaphoreType.DMA((5,))], out_space=pl.ANY,
            ))


def solution(mesh):
    spec = P("bx", "bz", "by")
    return jax.shard_map(body, mesh=mesh, in_specs=(spec, spec, spec, P()), out_specs=(spec, spec), check_vma=False)
```

```python
import functools
import math

import jax
import jax.numpy as jnp
import numpy as np
from jax import lax
from jax.experimental import pallas as pl
from jax.experimental.pallas import tpu as pltpu
from jax.sharding import PartitionSpec as P

CYCLES = 2
DAMPING = 0.6666666666666666
F32 = jnp.float32
BF16 = jnp.bfloat16
AXES = ("bx", "by", "bz")
VMEM_LIMIT = 32 * 1024 * 1024


def up_to(value, multiple):
    return -(-value // multiple) * multiple


class Plan:
    def __init__(self, shape, nx, ny, nz):
        self.X, self.Z, self.Y = shape
        self.nx, self.ny, self.nz = nx, ny, nz
        self.n = nx * ny * nz
        self.cx, self.cz, self.cy = self.X // 2, self.Z // 2, self.Y // 2
        self.NX, self.NZ, self.NY = self.cx * nx, self.cz * nz, self.cy * ny
        self.modes = -(-self.NY // self.n)
        self.NYp = self.modes * self.n
        self.lanes = self.cx * self.cz
        rows = (2 * self.Z, 2 * self.Z, 2 * self.X, 2 * self.X, self.Z, 12)
        self.heights = [-(-r // self.n) for r in rows]
        self.offsets = [sum(self.heights[:i]) for i in range(6)]
        halo = sum(self.heights)
        self.go_halo = self.modes
        self.go = up_to(self.modes + halo, 8)
        self.back_halo = 2 * self.modes
        self.back = up_to(2 * self.modes + halo, 8)
        self.edge_lane = 6 * self.X
        self.extra = 2 * self.cz + 2 * self.cx
        self.staged = nx == 4 and nz == 2 and ny & (ny - 1) == 0 and self.NZ % LOW == 0
        assert self.lanes <= self.Y and self.extra <= self.lanes and self.edge_lane + 8 <= self.Y
        assert self.heights[5] == 1


def sine_table(count):
    index_one = np.arange(1, count + 1, dtype=np.int32)
    product = (index_one[:, None] * index_one[None, :]).astype(np.float32)
    value = np.sin(product * np.float32(math.pi / (count + 1)))
    return (value * np.float32(math.sqrt(2.0 / (count + 1)))).astype(BF16).astype(np.float32)


def spectrum_values(count):
    return 2.0 - 2.0 * np.cos(np.arange(1, count + 1) * (math.pi / (count + 1)))


RESTRICT = np.array([[3, 2, 1, 0], [0, 1, 2, 3]], np.float32)
PROLONG = np.array([[3, 0], [2, 1], [1, 2], [0, 3]], np.float32)


LOW = 8


def staged_tables(p, sx, sz, py):
    high, eye = p.NZ // LOW, np.eye(LOW)
    out = {}
    wzt = np.zeros((high, p.cx, LOW, p.nz, p.cx, p.cz), np.float32)
    for x in range(p.cx):
        wzt[:, x, :, :, x, :] = sz.reshape(high, LOW, p.nz, p.cz)
    out["wzt"] = wzt.reshape(p.cx * p.NZ, p.nz * p.lanes)
    blocks = sx.reshape(p.NX, p.nx, p.cx)
    order = lambda b: [b, b ^ 3, b ^ 1, b ^ 2]
    out["kx"] = np.stack([np.kron(blocks[:, order(b)].reshape(p.NX, p.NX), eye) for b in range(p.nx)])
    sxp = np.zeros((p.NX + 2, p.NX), np.float32)
    sxp[1:-1] = sx
    out["kxi"] = np.kron(sxp, eye)
    szp = np.zeros((p.NZ + 2, p.NZ), np.float32)
    szp[1:-1] = sz
    zi = np.zeros((p.nz, p.lanes + p.extra, high, p.cx + 2, LOW), np.float32)
    for b in range(p.nz):
        mine = szp[b * p.cz + 1 : (b + 1) * p.cz + 1].reshape(p.cz, high, LOW)
        for x in range(p.cx):
            zi[b, x * p.cz : (x + 1) * p.cz, :, x + 1, :] = mine
            zi[b, p.lanes + 2 * p.cz + x, :, x + 1, :] = szp[b * p.cz].reshape(high, LOW)
            zi[b, p.lanes + 2 * p.cz + p.cx + x, :, x + 1, :] = szp[(b + 1) * p.cz + 1].reshape(high, LOW)
        zi[b, p.lanes : p.lanes + p.cz, :, 0, :] = mine
        zi[b, p.lanes + p.cz : p.lanes + 2 * p.cz, :, p.cx + 1, :] = mine
    out["zi"] = zi.reshape(p.nz, p.lanes + p.extra, -1)
    pye = np.zeros((p.cy + 16, 2 * p.Y), np.float32)
    pye[8 : 8 + p.cy, : p.Y] = py.T
    pye[7, p.Y] = pye[8 + p.cy, p.Y + 1] = 1
    out["pye"] = pye
    return out


def tables(p):
    rx = np.kron(np.eye(p.X // 4), RESTRICT)
    rz = np.kron(np.eye(p.Z // 4), RESTRICT)
    ry = np.kron(np.eye(p.Y // 4), RESTRICT)
    px = np.kron(np.eye(p.X // 4), PROLONG)
    pz = np.kron(np.eye(p.Z // 4), PROLONG)
    py = np.kron(np.eye(p.Y // 4), PROLONG)
    sx, sz, sy = sine_table(p.NX), sine_table(p.NZ), sine_table(p.NY)
    out = {}
    out["rxz"] = np.kron(rx, rz)
    out["ry"] = ry
    padded = np.zeros((p.NY + 16, p.NYp), np.float32)
    padded[8 : 8 + p.NY, : p.NY] = sy
    out["sy"] = padded
    wz = np.zeros((p.cx, p.NZ, p.nz, p.cx, p.cz), np.float32)
    for x in range(p.cx):
        wz[x, :, :, x, :] = sz.reshape(p.NZ, p.nz, p.cz)
    out["wz"] = wz.reshape(p.cx * p.NZ, p.nz * p.lanes)
    wx = np.einsum("bxk,mn->xbmkn", sx.reshape(p.nx, p.cx, p.NX), np.eye(p.modes))
    wx = wx.reshape(p.NX * p.modes, p.NX * p.modes)
    out["wx"], out["wxt"] = wx, wx.T
    szp = np.zeros((p.NZ, p.NZ + 2), np.float32)
    szp[:, 1:-1] = sz
    wzi = np.zeros((p.nz, p.cx, p.NZ, 2 * p.lanes), np.float32)
    for b in range(p.nz):
        for x in range(p.cx):
            wzi[b, x, :, x * p.cz : (x + 1) * p.cz] = sz[:, b * p.cz : (b + 1) * p.cz]
            wzi[b, x, :, p.lanes + x] = szp[:, b * p.cz]
            wzi[b, x, :, p.lanes + p.cx + x] = szp[:, (b + 1) * p.cz + 1]
    out["wzi"] = wzi.reshape(p.nz, p.cx * p.NZ, 2 * p.lanes)
    out["pyt"] = py.T
    pall = np.zeros((p.X * p.Z + 2 * p.Z + 2 * p.X, 2 * p.lanes), np.float32)
    at = p.X * p.Z
    pall[:at, : p.lanes] = np.kron(px, pz)
    col = p.lanes
    for _ in range(2):
        pall[at : at + p.Z, col : col + p.cz] = 3 * pz
        at, col = at + p.Z, col + p.cz
    for _ in range(2):
        pall[at : at + p.X, col : col + p.cx] = 3 * px
        at, col = at + p.X, col + p.cx
    out["pall"] = np.concatenate([pall, np.tile(pz, (1, 2 * p.cx))])
    pyh = np.zeros((2, p.lanes, p.Y), np.float32)
    spread = np.repeat(px.T, p.cz, axis=0)
    for side in range(2):
        pyh[side, :, side : 2 * p.X : 2] = 3 * spread
    out["pyh"] = pyh.reshape(2 * p.lanes, p.Y)
    if p.staged:
        out.update(staged_tables(p, sx, sz, py))
    out = {key: jnp.asarray(value.astype(BF16)) for key, value in out.items()}
    if p.staged:
        lam = spectrum_values(p.NX)[None, :, None] + spectrum_values(p.NZ).reshape(-1, 1, LOW)
        out["lam_xz"] = jnp.asarray(lam.reshape(-1, 1).astype(np.float32))
        out["lam_y"] = jnp.asarray(spectrum_values(p.NY).reshape(1, -1).astype(np.float32))
        return out
    lam = spectrum_values(p.NX)[None, :, None] + spectrum_values(p.NZ)[:, None, None]
    out["lamxz"] = jnp.asarray(np.broadcast_to(lam, (p.NZ, p.NX, p.modes)).reshape(p.NZ, -1).astype(np.float32))
    lamy = np.zeros(p.NYp)
    lamy[: p.NY] = spectrum_values(p.NY)
    lamy = np.broadcast_to(lamy.reshape(p.n, 1, 1, p.modes), (p.n, 1, p.NX, p.modes))
    out["lamy"] = jnp.asarray(lamy.reshape(p.n, 1, -1).astype(np.float32))
    return out


def iota(shape, dim):
    return lax.broadcasted_iota(jnp.int32, shape, dim)


def dot(a, b, dims=((1,), (0,))):
    return lax.dot_general(a, b, (dims, ((), ())), preferred_element_type=F32)


def halves(value):
    high = value.astype(BF16)
    return high, (value - high.astype(F32)).astype(BF16)


def dot_wide_right(table, value, dims=((1,), (0,))):
    axis = 1 - dims[1][0]
    count = value.shape[axis]
    both = dot(table, jnp.concatenate(halves(value), axis=axis), dims)
    return both[:, :count] + both[:, count:]


def dot_wide_left(value, table, dims=((1,), (0,))):
    high, low = halves(value)
    return dot(high, table, dims) + dot(low, table, dims)


def roll(value, shift, axis):
    size = value.shape[axis]
    shift = shift % size
    return value if shift == 0 else pltpu.roll(value, shift, axis)


def lookup(classes, coef_ref, row):
    total = jnp.zeros_like(classes)
    for k in range(coef_ref.shape[1]):
        total = jnp.where(classes == k + 1.0, coef_ref[row, k], total)
    return total


def col_faces(get, p):
    lane = iota((p.Z, p.Y), 1) // 2
    total = jnp.zeros((p.Z, p.Y), F32)
    for i in range(p.X):
        total = jnp.where(lane == i, roll(get(i), 2 * i + 1, 1), total)
    return total


def swap_lanes(value):
    even = iota(value.shape, 1) % 2 == 0
    return jnp.where(even, roll(value, -1, 1), roll(value, 1, 1))


def shifted(value, axis, before, after):
    size = value.shape[axis]
    at = iota(value.shape, axis)
    low = jnp.where(at == 0, before, roll(value, 1, axis))
    high = jnp.where(at == size - 1, after, roll(value, -1, axis))
    return low, high


def plane_weights(kap, row_m, row_p, col_m, col_p):
    up, down = shifted(kap, 0, row_m, row_p)
    left, right = shifted(kap, 1, col_m, col_p)
    row, lane = iota(kap.shape, 0) % 4, iota(kap.shape, 1) % 4
    return (
        jnp.where(row == 0, kap + up, kap),
        jnp.where(row == 3, kap + down, kap),
        jnp.where(lane == 0, kap + left, kap),
        jnp.where(lane == 3, kap + right, kap),
    )


KAP, WZM, WZP, WYM, WYP, BASE, BETA, DAMP = range(8)
QUANTITIES = DAMP + 3


class Brick:
    def __init__(self, p, cst_ref, kap_xm, kap_xp):
        self.p, self.cst, self.kap_xm, self.kap_xp = p, cst_ref, kap_xm, kap_xp

    def of(self, quantity, i):
        return self.cst[quantity, i // 4]

    def x_weights(self, i):
        kap = self.of(KAP, i)
        low = high = kap
        if i % 4 == 0:
            low = kap + (self.of(KAP, i - 1) if i else self.kap_xm)
        if i % 4 == 3:
            high = kap + (self.of(KAP, i + 1) if i + 1 < self.p.X else self.kap_xp)
        return low, high

    def diagonal(self, i):
        low, high = self.x_weights(i)
        return self.of(BASE, i) + (low + high)

    def damp(self, i):
        return self.cst[DAMP + (0 if i % 4 == 0 else 2 if i % 4 == 3 else 1), i // 4]

    def neighbours(self, i, get, halo=None):
        p, v = self.p, get(i)
        low, high = self.x_weights(i)
        total = jnp.zeros_like(v)
        if i:
            total = total + low * get(i - 1)
        elif halo is not None:
            total = total + low * halo[0]
        if i + 1 < p.X:
            total = total + high * get(i + 1)
        elif halo is not None:
            total = total + high * halo[1]
        if halo is None:
            ends = (0.0, 0.0, 0.0, 0.0)
        else:
            side = self.y_ends(halo[4], i)
            ends = (halo[2][i : i + 1], halo[3][i : i + 1], side, side)
        up, down = shifted(v, 0, ends[0], ends[1])
        left, right = shifted(v, 1, ends[2], ends[3])
        total = total + self.of(WZM, i) * up + self.of(WZP, i) * down
        return total + self.of(WYM, i) * left + self.of(WYP, i) * right

    def y_ends(self, yh, i):
        return roll(swap_lanes(yh), self.p.Y - 1 - 2 * i, 1)

    def from_halo(self, i, halo):
        p = self.p
        row, lane = iota((p.Z, p.Y), 0), iota((p.Z, p.Y), 1)
        side = self.y_ends(halo[4], i)
        total = jnp.where(row == 0, self.of(WZM, i) * halo[2][i : i + 1], 0.0)
        total = jnp.where(row == p.Z - 1, self.of(WZP, i) * halo[3][i : i + 1], total)
        total = total + jnp.where(lane == 0, self.of(WYM, i) * side, 0.0)
        total = total + jnp.where(lane == p.Y - 1, self.of(WYP, i) * side, 0.0)
        if i == 0:
            total = total + self.x_weights(i)[0] * halo[0]
        if i == p.X - 1:
            total = total + self.x_weights(i)[1] * halo[1]
        return total


def residual_plane(brick, i, get, halo, f):
    v = get(i)
    return f - brick.diagonal(i) * v + brick.neighbours(i, get, halo) - brick.of(BETA, i) * v * v * v


def put_rows(ref, stride, offset, n, rows):
    height = -(-rows.shape[0] // n)
    if rows.shape[0] < height * n:
        rows = jnp.concatenate([rows, jnp.zeros((height * n - rows.shape[0], rows.shape[1]), F32)], axis=0)
    for k in range(height):
        ref[pl.ds(offset + k, n, stride=stride), :] = rows[k * n : (k + 1) * n]


def get_rows(ref, stride, offset, n, count):
    height = -(-count // n)
    parts = [ref[pl.ds(offset + k, n, stride=stride), :] for k in range(height)]
    value = parts[0] if height == 1 else jnp.concatenate(parts, axis=0)
    return value[:count]


class Bounds:
    def __init__(self, p):
        self.uxm, self.uxp = (0, p.Z), (p.Z, p.Z)
        self.uzm, self.uzp = (2 * p.Z, p.X), (2 * p.Z + p.X, p.X)
        self.uy = (2 * p.Z + 2 * p.X, p.Z)
        self.count = 3 * p.Z + 2 * p.X


def read(ref, span):
    return ref[span[0] : span[0] + span[1], :]


def write_bounds(ref, b, values):
    for span, value in zip((b.uxm, b.uxp, b.uzm, b.uzp, b.uy), values):
        ref[span[0] : span[0] + span[1], :] = value


def read_bounds(ref, b):
    return tuple(read(ref, span) for span in (b.uxm, b.uxp, b.uzm, b.uzp, b.uy))


def advance(p, brick, get, residual, rxz, ry, s_ref, r_scr, z_scr, z2_scr):
    X, Z = p.X, p.Z
    for i in range(X):
        r = residual(i)
        r_scr[i * Z : (i + 1) * Z, :] = r
        z_scr[i] = r * brick.damp(i)
    z1 = lambda i: z_scr[i]
    coarse = dot_wide_right(rxz[...], r_scr[...])
    coarse = dot_wide_right(ry[...], coarse, ((1,), (1,))) * (1.0 / 216.0)
    for i in range(X):
        v = z1(i)
        smooth = (2.0 - DAMPING) * v + brick.damp(i) * brick.neighbours(i, z1)
        z2_scr[i] = smooth
        s_ref[i] = get(i) + smooth
    return coarse.astype(BF16)


def start_cycle(p, brick, get, residual, classes, rxz, ry, sy, s_ref, z1b_ref, go_ref, r_scr, z_scr, z2_scr, go_scr):
    X, Z, n = p.X, p.Z, p.n
    coarse = advance(p, brick, get, residual, rxz, ry, s_ref, r_scr, z_scr, z2_scr)
    z1 = lambda i: z_scr[i]
    rows = sy[pl.ds(pl.multiple_of(lax.axis_index("by") * p.cy + 8, 8), p.cy), :]
    part = dot(rows.T, coarse)
    for j in range(n):
        go_scr[j * p.go : j * p.go + p.modes, :] = part[j * p.modes : (j + 1) * p.modes]
    z2 = lambda i: z2_scr[i]
    z1_y, z2_y = col_faces(z1, p), col_faces(z2, p)
    z1_zm, z1_zp = z_scr[:, 0, :], z_scr[:, Z - 1, :]
    write_bounds(z1b_ref, Bounds(p), (z1(0), z1(X - 1), z1_zm, z1_zp, z1_y))
    lane = iota((Z, p.Y), 1)
    sides = jnp.where(lane < 2 * X, z1_y, roll(z2_y, 2 * X, 1))
    edges = [z_scr[0, 0:1, :], z_scr[0, Z - 1 : Z, :], z_scr[X - 1, 0:1, :], z_scr[X - 1, Z - 1 : Z, :]]
    edges += [z1_y[0:1], z1_y[Z - 1 : Z]]
    if classes is None:
        sides = jnp.where(lane < 4 * X, sides, 0.0)
    else:
        cls, cls_y = classes
        sides = jnp.where(lane < 4 * X, sides, roll(cls_y, 4 * X, 1))
        sides = jnp.where(lane < 6 * X, sides, 0.0)
        edges += [cls(0)[0:1], cls(0)[Z - 1 : Z], cls(X - 1)[0:1], cls(X - 1)[Z - 1 : Z]]
        edges += [cls_y[0:1], cls_y[Z - 1 : Z]]
    pieces = (
        jnp.concatenate([z1(0), z2(0)], axis=0),
        jnp.concatenate([z1(X - 1), z2(X - 1)], axis=0),
        jnp.concatenate([z1_zm, z2_scr[:, 0, :]], axis=0),
        jnp.concatenate([z1_zp, z2_scr[:, Z - 1, :]], axis=0),
        sides,
        jnp.concatenate(edges, axis=0),
    )
    for piece, offset in zip(pieces, p.offsets):
        put_rows(go_scr, p.go, p.go_halo + offset, n, piece)
    used = p.go_halo + sum(p.heights)
    for k in range(used, p.go):
        go_scr[pl.ds(k, n, stride=p.go), :] = jnp.zeros((n, p.Y), F32)
    go_ref[...] = go_scr[...].astype(BF16)


def sides_kernel(p, u_ref, y_ref):
    y_ref[...] = col_faces(lambda i: u_ref[i], p)


def pack_kernel(p, index_ref, u_ref, uy_ref, cls_ref, xa_ref, xb_ref, za_ref, zb_ref, y_ref):
    X, Z, Y = p.X, p.Z, p.Y
    spread_z = (iota((Z, Z // 4), 0) // 4 == iota((Z, Z // 4), 1)).astype(BF16)
    spread_y = (iota((Y // 4, Y), 1) // 4 == iota((Y // 4, Y), 0)).astype(BF16)
    for a in range(X // 4):
        element = (index_ref[a] + 1).astype(F32).astype(BF16)
        cls_ref[a] = dot(dot(spread_z, element).astype(BF16), spread_y)
    cls = lambda i: cls_ref[i // 4]

    def face(axis, low, high, a_ref, b_ref, at):
        even = lax.axis_index(axis) % 2 == 0
        count = low.shape[0]
        a_ref[at : at + count, :] = jnp.where(even, high, low)
        b_ref[at : at + count, :] = jnp.where(even, low, high)

    face("bx", u_ref[0], u_ref[X - 1], xa_ref, xb_ref, 0)
    face("bx", cls(0), cls(X - 1), xa_ref, xb_ref, Z)
    rows = lambda z: jnp.concatenate([cls(i)[z : z + 1] for i in range(X)], axis=0)
    face("bz", u_ref[:, 0, :], u_ref[:, Z - 1, :], za_ref, zb_ref, 0)
    face("bz", rows(0), rows(Z - 1), za_ref, zb_ref, X)
    y_ref[0:Z, :] = uy_ref[...]
    y_ref[Z : 2 * Z, :] = col_faces(cls, p)


def received(axis, count, a_ref, b_ref):
    at = lax.axis_index(axis)
    even = at % 2 == 0
    a, b = a_ref[...], b_ref[...]
    low = jnp.where(even, b, a)
    high = jnp.where(even, a, b)
    return jnp.where(at > 0, low, 0.0), jnp.where(at < count - 1, high, 0.0)


def prepare_kernel(p, coef, u_ref, f_ref, cls_ref, cst_ref, r_ref):
    for a in range(p.X // 4):
        kap = lookup(cls_ref[a], coef, 0)
        wzm, wzp, wym, wyp = plane_weights(kap, 0.0, 0.0, 0.0, 0.0)
        cst_ref[KAP, a] = kap
        cst_ref[WZM, a] = wzm
        cst_ref[WZP, a] = wzp
        cst_ref[WYM, a] = wym
        cst_ref[WYP, a] = wyp
        cst_ref[BASE, a] = lookup(cls_ref[a], coef, 1) + ((wzm + wzp) + (wym + wyp))
        cst_ref[BETA, a] = lookup(cls_ref[a], coef, 2)
    brick = Brick(p, cst_ref, 0.0, 0.0)
    get = lambda i: u_ref[i]
    for i in range(p.X):
        r_ref[i] = residual_plane(brick, i, get, None, f_ref[i])


def neighbours_in(p, coef, u_ref, r_ref, cst0_ref, xa, xb, za, zb, ya, yb, uhb_ref, clsb_ref, cst_ref):
    X, Z, Y, b = p.X, p.Z, p.Y, Bounds(p)
    xm, xp = received("bx", p.nx, xa, xb)
    zm, zp = received("bz", p.nz, za, zb)
    ym, yp = received("by", p.ny, ya, yb)
    y = jnp.where(iota(ym.shape, 1) % 2 == 0, ym, yp)
    halo = (xm[:Z], xp[:Z], zm[:X], zp[:X], y[:Z])
    outside = (xm[Z:], xp[Z:], zm[X:], zp[X:], y[Z:])
    write_bounds(uhb_ref, b, halo)
    write_bounds(clsb_ref, b, outside)
    kap_h = tuple(lookup(value, coef, 0) for value in outside)
    row, lane = iota((Z, Y), 0), iota((Z, Y), 1)
    more = []
    for a in range(X // 4):
        i = 4 * a
        ends = (
            (WZM, jnp.where(row == 0, kap_h[2][i : i + 1], 0.0)),
            (WZP, jnp.where(row == Z - 1, kap_h[3][i : i + 1], 0.0)),
            (WYM, jnp.where(lane == 0, kap_h[4][:, 2 * i : 2 * i + 1], 0.0)),
            (WYP, jnp.where(lane == Y - 1, kap_h[4][:, 2 * i + 1 : 2 * i + 2], 0.0)),
        )
        for k, end in ends:
            cst_ref[k, a] = cst0_ref[k, a] + end
        more.append((ends[0][1] + ends[1][1]) + (ends[2][1] + ends[3][1]))
        cst_ref[BASE, a] = cst0_ref[BASE, a] + more[a]
        cst_ref[KAP, a] = cst0_ref[KAP, a]
        cst_ref[BETA, a] = cst0_ref[BETA, a]
    brick = Brick(p, cst_ref, kap_h[0], kap_h[1])
    for a in range(X // 4):
        for k, i in enumerate((4 * a, 4 * a + 1, 4 * a + 3)):
            cst_ref[DAMP + k, a] = DAMPING / brick.diagonal(i)

    def residual(i):
        added = more[i // 4]
        if i == 0:
            added = added + kap_h[0]
        if i == X - 1:
            added = added + kap_h[1]
        return r_ref[i] - added * u_ref[i] + brick.from_halo(i, halo)

    return brick, residual


def first_kernel(p, coef, u_ref, r_ref, cls_ref, cst0_ref, xa, xb, za, zb, ya, yb, rxz, ry, sy,
                 go_ref, s_ref, z1b_ref, uhb_ref, clsb_ref, cst_ref, r_scr, z_scr, z2_scr, go_scr):
    brick, residual = neighbours_in(p, coef, u_ref, r_ref, cst0_ref, xa, xb, za, zb, ya, yb, uhb_ref, clsb_ref, cst_ref)
    cls = lambda i: cls_ref[i // 4]
    start_cycle(p, brick, lambda i: u_ref[i], residual, (cls, col_faces(cls, p)), rxz, ry, sy,
                s_ref, z1b_ref, go_ref, r_scr, z_scr, z2_scr, go_scr)


def owner_kernel(p, coef, in_ref, wz, wx, wxt, wzi, lamxz, lamy, out_ref, in_scr, out_scr):
    n, m, nx, ny, nz = p.n, p.modes, p.nx, p.ny, p.nz
    me = (lax.axis_index("bx") * ny + lax.axis_index("by")) * nz + lax.axis_index("bz")
    in_scr[...] = in_ref[...].astype(F32)
    rows = []
    for bx in range(nx):
        lanes = []
        for bz in range(nz):
            total = None
            for by in range(ny):
                at = ((bx * ny + by) * nz + bz) * p.go
                piece = in_scr[at : at + m, :]
                total = piece if total is None else total + piece
            lanes.append(total)
        rows.append(jnp.concatenate(lanes, axis=1))
    data = jnp.concatenate(rows, axis=0)
    data = dot_wide_right(wz[...], data, ((1,), (1,)))
    data = jnp.concatenate([data[x * p.NZ : (x + 1) * p.NZ] for x in range(p.cx)], axis=1)
    data = dot_wide_left(data, wx[...])
    classes = coef.shape[1]
    kap_mean = sum(coef[0, k] for k in range(classes)) * (1.0 / classes)
    sig_mean = sum(coef[1, k] for k in range(classes)) * (1.0 / classes)
    data = data / (kap_mean * (lamxz[...] + lamy[me]) + sig_mean)
    data = dot_wide_left(data, wxt[...])
    width = nx * m
    data = jnp.concatenate([data[:, x * width : (x + 1) * width] for x in range(p.cx)], axis=0)
    high, low = halves(data)
    high, low = high.T, low.T
    lane = iota((m, p.Y), 1)
    for bz in range(nz):
        back = dot(high, wzi[bz]) + dot(low, wzi[bz])
        core = lambda bx: back[bx * m : (bx + 1) * m, : p.lanes]
        for bx in range(nx):
            ends = roll(back[bx * m : (bx + 1) * m, p.lanes :], 2 * p.cz, 1)
            below = roll(core(bx - 1), p.cz - p.lanes, 1) if bx else jnp.zeros((m, p.lanes), F32)
            above = roll(core(bx + 1), p.cz, 1) if bx + 1 < nx else jnp.zeros((m, p.lanes), F32)
            extra = jnp.where(lane < p.cz, below, jnp.where(lane < 2 * p.cz, above, ends))
            mine = core(bx)
            for by in range(ny):
                at = ((bx * ny + by) * nz + bz) * p.back
                out_scr[at : at + m, :] = mine
                out_scr[at + m : at + 2 * m, :] = extra

    device = iota((n, p.Y), 0)
    at_x, at_y, at_z = device // (ny * nz), (device // nz) % ny, device % nz

    def shift(value, dx, dy, dz):
        value = roll(value, -((dx * ny + dy) * nz + dz), 0)
        for at, step, count in ((at_x, dx, nx), (at_y, dy, ny), (at_z, dz, nz)):
            if step:
                value = jnp.where((at + step >= 0) & (at + step < count), value, 0.0)
        return value

    def take(k):
        return in_scr[pl.ds(p.go_halo + k, n, stride=p.go), :]

    def give(k, value):
        out_scr[pl.ds(p.back_halo + k, n, stride=p.back), :] = value

    for to, source, step in ((0, 1, (-1, 0, 0)), (1, 0, (1, 0, 0)), (2, 3, (0, 0, -1)), (3, 2, (0, 0, 1))):
        for k in range(p.heights[to]):
            give(p.offsets[to] + k, shift(take(p.offsets[source] + k), *step))
    lane = iota((n, p.Y), 1)
    even = lane % 2 == 0
    first, X2 = p.edge_lane, 2 * p.X
    for k in range(p.heights[4]):
        sides = take(p.offsets[4] + k)
        moved = jnp.where(lane < first + 2, roll(sides, first, 1), roll(sides, first + 2 - (X2 - 2), 1))
        moved = jnp.where(lane < first + 4, moved, roll(sides, first + 4 - 2 * X2, 1))
        moved = jnp.where(lane < first + 6, moved, roll(sides, first + 6 - (3 * X2 - 2), 1))
        which = (lane - first) % 4
        corner = jnp.where(
            which < 2,
            jnp.where(even, shift(moved, 1, -1, 0), shift(moved, 1, 1, 0)),
            jnp.where(even, shift(moved, -1, -1, 0), shift(moved, -1, 1, 0)),
        )
        plain = jnp.where(even, shift(sides, 0, -1, 0), shift(sides, 0, 1, 0))
        give(p.offsets[4] + k, jnp.where(lane < first, plain, jnp.where(lane < first + 8, corner, 0.0)))
    edges = take(p.offsets[5])
    kind = me % 6
    moved = jnp.where(even, shift(edges, 0, -1, -1), shift(edges, 0, 1, -1))
    for k, value in (
        (0, lambda: shift(edges, 1, 0, 1)),
        (1, lambda: shift(edges, 1, 0, -1)),
        (2, lambda: shift(edges, -1, 0, 1)),
        (3, lambda: shift(edges, -1, 0, -1)),
        (4, lambda: jnp.where(even, shift(edges, 0, -1, 1), shift(edges, 0, 1, 1))),
    ):
        moved = jnp.where(kind == k, value(), moved)
    give(p.offsets[5], moved)
    used = p.back_halo + sum(p.heights)
    for k in range(used, p.back):
        out_scr[pl.ds(k, n, stride=p.back), :] = jnp.zeros((n, p.Y), F32)
    out_ref[...] = out_scr[...].astype(BF16)


class Arrived:
    def __init__(self, p, ref):
        X, Z = p.X, p.Z
        rows = (2 * Z, 2 * Z, 2 * X, 2 * X, Z, 12)
        xm, xp, zm, zp, sides, edges = (
            get_rows(ref, p.back, p.back_halo + offset, p.n, count) for offset, count in zip(p.offsets, rows)
        )
        self.p, self.ref, self.sides, self.edges = p, ref, sides, edges
        self.z1 = (xm[:Z], xp[:Z], zm[:X], zp[:X], sides)
        self.z2 = (xm[Z:], xp[Z:], zm[X:], zp[X:], roll(sides, -2 * X, 1))

    def xz(self, kind, sx, sz):
        k = 6 * kind + (0 if sx else 2) + (0 if sz else 1)
        return self.edges[k : k + 1]

    def zy(self, kind, sz):
        k = 6 * kind + (4 if sz else 5)
        return self.edges[k : k + 1]

    def xy(self, kind, sx, sy):
        lane = self.p.edge_lane + 4 * kind + (0 if sx else 2) + sy
        return self.sides[:, lane : lane + 1]

    def xy_lanes(self, kind, plain):
        first, X2 = self.p.edge_lane + 4 * kind, 2 * self.p.X
        lane = iota(plain.shape, 1)
        value = jnp.where(lane < X2, plain, roll(self.sides, X2 - first, 1))
        return jnp.where(lane >= self.p.Y - 2, roll(self.sides, self.p.Y - 2 - first - 2, 1), value)


def coarse_rows(p, ref, sy, pyt, pall, pyh):
    n, m = p.n, p.modes
    core = jnp.concatenate([ref[j * p.back : j * p.back + m, :] for j in range(n)], axis=0)
    extra = jnp.concatenate([ref[j * p.back + m : j * p.back + 2 * m, :] for j in range(n)], axis=0)
    modes = jnp.concatenate([core, extra], axis=1).astype(BF16)
    rows = sy[pl.ds(pl.multiple_of(lax.axis_index("by") * p.cy, 8), p.cy + 16), :]
    values = dot(rows, modes).astype(BF16)
    along = dot(values[8 : 8 + p.cy].T, pyt[...])
    count = pall.shape[0] - p.Z
    nodes = dot_wide_right(pall[:count], along) * (1.0 / 27.0)
    weights = pall[count:, : p.lanes].astype(F32)
    ends = [weights * values.astype(F32)[k : k + 1, : p.lanes] for k in (7, 8 + p.cy)]
    side = dot_wide_left(jnp.concatenate(ends, axis=1), pyh[...]) * (1.0 / 27.0)
    return nodes, side


def column(row, count, side):
    shape = (count, row.shape[1])
    pick = iota(shape, 1) == 2 * iota(shape, 0) + side
    return jnp.sum(jnp.where(pick, row, 0.0), axis=1, keepdims=True)


def finish_cycle(p, coef, brick, now, first, s_ref, z1b_ref, uhb_ref, clsb_ref, nodes, side, u_ref):
    X, Z, b = p.X, p.Z, Bounds(p)
    for i in range(X):
        u_ref[i] = s_ref[i] + brick.damp(i) * brick.from_halo(i, now.z1) + nodes[i * Z : (i + 1) * Z]
    old, cls, own = read_bounds(uhb_ref, b), read_bounds(clsb_ref, b), read_bounds(z1b_ref, b)
    kap = lambda value: lookup(value, coef, 0)
    halo = []

    def new(k, weights, toward, others, correction):
        kap_here = kap(cls[k])
        diagonal = lookup(cls[k], coef, 1) + (kap_here + toward) + ((weights[0] + weights[1]) + (weights[2] + weights[3]))
        total = toward * own_faces[k]
        for part in others:
            total = total + part
        value = old[k] + now.z2[k] + (DAMPING / diagonal) * total + correction
        halo.append(jnp.where(cls[k] > 0.5, value, 0.0))

    own_faces = list(own[:4]) + [swap_lanes(own[4])]
    at = X * Z
    for k in range(2):
        kap_here = kap(cls[k])
        row_m, row_p = kap(first.xz(1, k, 0)), kap(first.xz(1, k, 1))
        col_m, col_p = kap(first.xy(1, k, 0)), kap(first.xy(1, k, 1))
        w = plane_weights(kap_here, row_m, row_p, col_m, col_p)
        row, lane = iota((Z, p.Y), 0), iota((Z, p.Y), 1)
        others = (
            jnp.where(row == 0, w[0] * now.xz(0, k, 0), 0.0),
            jnp.where(row == Z - 1, w[1] * now.xz(0, k, 1), 0.0),
            jnp.where(lane == 0, w[2] * now.xy(0, k, 0), 0.0),
            jnp.where(lane == p.Y - 1, w[3] * now.xy(0, k, 1), 0.0),
        )
        toward = kap_here + brick.of(KAP, 0 if k == 0 else X - 1)
        new(k, w, toward, others, nodes[at : at + Z])
        at += Z
    for k in range(2):
        kap_here = kap(cls[2 + k])
        row_m, row_p = kap(first.xz(1, 0, k)), kap(first.xz(1, 1, k))
        col_m, col_p = (kap(column(first.zy(1, k), X, side_y)) for side_y in range(2))
        w = plane_weights(kap_here, row_m, row_p, col_m, col_p)
        row, lane = iota((X, p.Y), 0), iota((X, p.Y), 1)
        others = (
            jnp.where(row == 0, w[0] * now.xz(0, 0, k), 0.0),
            jnp.where(row == X - 1, w[1] * now.xz(0, 1, k), 0.0),
            jnp.where(lane == 0, w[2] * column(now.zy(0, k), X, 0), 0.0),
            jnp.where(lane == p.Y - 1, w[3] * column(now.zy(0, k), X, 1), 0.0),
        )
        z = 0 if k == 0 else Z - 1
        mine = jnp.concatenate([brick.of(KAP, i)[z : z + 1] for i in range(X)], axis=0)
        new(2 + k, w, kap_here + mine, others, nodes[at : at + X])
        at += X
    wide = kap(first.xy_lanes(1, cls[4]))
    z1_wide = now.xy_lanes(0, now.z1[4])
    row_m, row_p = kap(first.zy(1, 0)), kap(first.zy(1, 1))
    up, down = shifted(wide, 0, row_m, row_p)
    left, right = roll(wide, 2, 1), roll(wide, -2, 1)
    row, lane = iota((Z, p.Y), 0), iota((Z, p.Y), 1)
    w = (
        jnp.where(row % 4 == 0, wide + up, wide),
        jnp.where(row % 4 == 3, wide + down, wide),
        jnp.where((lane // 2) % 4 == 0, wide + left, wide),
        jnp.where((lane // 2) % 4 == 3, wide + right, wide),
    )
    others = (
        jnp.where(row == 0, w[0] * now.zy(0, 0), 0.0),
        jnp.where(row == Z - 1, w[1] * now.zy(0, 1), 0.0),
        jnp.where(lane // 2 == 0, w[2] * roll(z1_wide, 2, 1), 0.0),
        jnp.where(lane // 2 == X - 1, w[3] * roll(z1_wide, -2, 1), 0.0),
    )
    mine = swap_lanes(col_faces(lambda i: brick.of(KAP, i), p))
    new(4, w, wide + mine, others, side)
    return tuple(halo)


def middle_kernel(p, coef, in_ref, f_ref, s_ref, z1b_ref, uhb_ref, clsb_ref, cst_ref,
                  sy, pyt, pall, pyh, rxz, ry,
                  go_ref, s_out, z1b_out, uhb_out, in_scr, u_scr, r_scr, z_scr, z2_scr, go_scr):
    in_scr[...] = in_ref[...].astype(F32)
    b = Bounds(p)
    outside = read_bounds(clsb_ref, b)
    brick = Brick(p, cst_ref, lookup(outside[0], coef, 0), lookup(outside[1], coef, 0))
    now = Arrived(p, in_scr)
    nodes, side = coarse_rows(p, in_scr, sy, pyt, pall, pyh)
    halo = finish_cycle(p, coef, brick, now, now, s_ref, z1b_ref, uhb_ref, clsb_ref, nodes, side, u_scr)
    write_bounds(uhb_out, b, halo)
    get = lambda i: u_scr[i]
    residual = lambda i: residual_plane(brick, i, get, halo, f_ref[i])
    start_cycle(p, brick, get, residual, None, rxz, ry, sy,
                s_out, z1b_out, go_ref, r_scr, z_scr, z2_scr, go_scr)


def last_kernel(p, coef, in_ref, first_ref, f_ref, s_ref, z1b_ref, uhb_ref, clsb_ref, cst_ref,
                sy, pyt, pall, pyh, u_out, r_out, in_scr, first_scr):
    in_scr[...] = in_ref[...].astype(F32)
    first_scr[...] = first_ref[...].astype(F32)
    outside = read_bounds(clsb_ref, Bounds(p))
    brick = Brick(p, cst_ref, lookup(outside[0], coef, 0), lookup(outside[1], coef, 0))
    now, first = Arrived(p, in_scr), Arrived(p, first_scr)
    nodes, side = coarse_rows(p, in_scr, sy, pyt, pall, pyh)
    halo = finish_cycle(p, coef, brick, now, first, s_ref, z1b_ref, uhb_ref, clsb_ref, nodes, side, u_out)
    for i in range(p.X):
        r_out[i] = residual_plane(brick, i, lambda k: u_out[k], halo, f_ref[i])


class Sends:
    def __init__(self, p):
        X, Z = p.X, p.Z
        self.first = p.cy + Z
        self.x_face, self.z_face = p.NY, p.NY
        self.x_rows = p.NY + 3 * Z
        self.z_rows = p.NY + 2 * X + 16
        self.xz_rows = p.NY + 16
        self.second = 2 * p.cx * p.NZ * p.NY // p.Y
        self.last = self.second + 3 * Z + 16
        self.faces = 4 * Z + 4 * X


def pick(condition, a, b):
    return jnp.where(condition, a, b)


def send_first(p, coarse, z_scr, z2_scr, z1b_ref, a_ref, faces_ref):
    X, Z = p.X, p.Z
    z1, z2 = (lambda i: z_scr[i]), (lambda i: z2_scr[i])
    z1_y, z2_y = col_faces(z1, p), col_faces(z2, p)
    z_rows = (z_scr[:, 0, :], z_scr[:, Z - 1, :], z2_scr[:, 0, :], z2_scr[:, Z - 1, :])
    write_bounds(z1b_ref, Bounds(p), (z1(0), z1(X - 1), z_rows[0], z_rows[1], z1_y))
    a_ref[0 : p.cy, :] = coarse
    lane = iota((Z, p.Y), 1)
    a_ref[p.cy :, :] = jnp.where(lane < 2 * X, z1_y, roll(z2_y, 2 * X, 1)).astype(BF16)
    for k, plane in enumerate((z1(0), z1(X - 1), z2(0), z2(X - 1))):
        faces_ref[k * Z : (k + 1) * Z, :] = plane.astype(BF16)
    for k, rows in enumerate(z_rows):
        faces_ref[4 * Z + k * X : 4 * Z + (k + 1) * X, :] = rows.astype(BF16)


def face_x(p, faces_ref, high):
    X, Z = p.X, p.Z
    return tuple(pick(high, faces_ref[(k + 1) * Z : (k + 2) * Z, :], faces_ref[k * Z : (k + 1) * Z, :]) for k in (0, 2))


def face_z(p, faces_ref, high):
    X, at = p.X, 4 * p.Z
    return tuple(
        pick(high, faces_ref[at + (k + 1) * X : at + (k + 2) * X, :], faces_ref[at + k * X : at + (k + 1) * X, :]) for k in (0, 2)
    )


def pad_rows(rows, count):
    rows = [row.astype(F32) for row in rows]
    return jnp.concatenate(rows + [jnp.zeros((count - len(rows), rows[0].shape[1]), F32)], axis=0).astype(BF16)


def y_block(p, sides, cls_y):
    lane = iota(sides.shape, 1)
    return jnp.where(lane < 2 * p.X, sides, roll(cls_y, 2 * p.X, 1))


def after_first(p, *refs):
    ny = p.ny
    buffers, (faces_ref, clsb_ref, cls_ref, sy, x_ref, z_ref, xz_ref, sides_ref, all_scr) = refs[:ny], refs[ny:]
    X, Z, sends, b = p.X, p.Z, Sends(p), Bounds(p)
    bx, by, bz = (lax.axis_index(axis) for axis in AXES)
    low = high = jnp.zeros((Z, p.Y), F32)
    for d in range(ny):
        other = by ^ d
        all_scr[pl.ds(pl.multiple_of(other * p.cy, 16), p.cy), :] = buffers[d][0 : p.cy, :]
        if d:
            value = buffers[d][p.cy :, :].astype(F32)
            low = pick(other == by - 1, value, low)
            high = pick(other == by + 1, value, high)
    sides = jnp.where(iota((Z, p.Y), 1) % 2 == 0, low, high)
    sides_ref[...] = sides
    modes = dot(sy[8 : 8 + p.NY, :], all_scr[...]).astype(BF16)
    cls_y = read(clsb_ref, b.uy)
    odd, up = bx % 2 == 1, bz == 0
    for ref in (x_ref, z_ref, xz_ref):
        ref[0 : p.NY, :] = modes
    at = p.NY
    z1, z2 = face_x(p, faces_ref, odd)
    x_ref[at : at + Z, :] = z1
    x_ref[at + Z : at + 2 * Z, :] = z2
    x_ref[at + 2 * Z : at + 3 * Z, :] = y_block(p, sides, cls_y).astype(BF16)
    z1, z2 = face_z(p, faces_ref, up)
    z_ref[at : at + X, :] = z1
    z_ref[at + X : at + 2 * X, :] = z2
    z_ref[at + 2 * X : at + 2 * X + 16, :] = pad_rows(
        [pick(up, value[Z - 1 : Z], value[0:1]) for value in (sides, cls_y)], 16
    )
    z1 = z1.astype(F32)
    cls = pick(odd, cls_ref[X // 4 - 1], cls_ref[0])
    xz_ref[at : at + 16, :] = pad_rows(
        [pick(odd, z1[X - 1 : X], z1[0:1]), pick(up, cls[Z - 1 : Z], cls[0:1])], 16
    )


def after_second(p, own_ref, x_in, z_in, xz_in, faces_ref, clsb_ref, sides_ref, wzt, out_ref):
    X, Z, Y, sends, b = p.X, p.Z, p.Y, Sends(p), Bounds(p)
    bx, bz = lax.axis_index("bx"), lax.axis_index("bz")
    odd, up = bx % 2 == 1, bz == 0
    at = 0
    for one, two in ((own_ref, z_in), (x_in, xz_in)):
        one, two = one[0 : p.NY, :], two[0 : p.NY, :]
        data = jnp.concatenate([pick(up, one, two), pick(up, two, one)], axis=1)
        data = dot(wzt[...], data, ((1,), (1,))).astype(BF16)
        for k in range(p.NY // Y):
            rows = data.shape[0]
            out_ref[at : at + rows, :] = data[:, k * Y : (k + 1) * Y]
            at += rows
    z1, z2 = face_x(p, faces_ref, jnp.logical_not(odd))
    out_ref[at : at + Z, :] = z1
    out_ref[at + Z : at + 2 * Z, :] = z2
    out_ref[at + 2 * Z : at + 3 * Z, :] = y_block(p, sides_ref[...], read(clsb_ref, b.uy)).astype(BF16)
    beyond = z_in[p.NY : p.NY + X, :].astype(F32)
    classes = pick(up, read(clsb_ref, b.uzp), read(clsb_ref, b.uzm))
    out_ref[at + 3 * Z : at + 3 * Z + 16, :] = pad_rows(
        [pick(odd, value[0:1], value[X - 1 : X]) for value in (beyond, classes)], 16
    )


class Beyond:
    def __init__(self, p):
        X, Z = p.X, p.Z
        self.cross = 0
        self.core = Z
        self.z = 6 * Z
        self.y = 6 * Z + 4 * X
        self.kap = 10 * Z + 4 * X
        self.count = self.kap + Bounds(p).count


def rows_at(ref, at, count):
    return ref[at : at + count, :]


def beyond_kernel(p, coef, s_ref, z1b_ref, uhb_ref, clsb_ref, cls_ref, cst_ref, sides_ref, x_in, z_in, xz_in, s_out, out_ref):
    X, Z, Y, b, to = p.X, p.Z, p.Y, Bounds(p), Beyond(p)
    bx, bz = lax.axis_index("bx"), lax.axis_index("bz")
    odd, up = bx % 2 == 1, bz == 0
    some = (bx > 0) & (bx < p.nx - 1)
    kaps, sigs = lookup(clsb_ref[...], coef, 0), lookup(clsb_ref[...], coef, 1)
    out_ref[to.kap :, :] = kaps
    part = lambda value, span: value[span[0] : span[0] + span[1]]
    x_part = lambda value, high: pick(high, part(value, b.uxp), part(value, b.uxm))
    z_part = lambda value: pick(up, part(value, b.uzp), part(value, b.uzm))
    z1b, uhb = z1b_ref[...], uhb_ref[...]
    across = lambda at, count: pick(some, x_in[p.NY + at : p.NY + at + count, :].astype(F32), 0.0)
    x_z1, x_z2, block = across(0, Z), across(Z, Z), across(2 * Z, Z)
    corner = pick(some, xz_in[p.NY : p.NY + 16, :].astype(F32), 0.0)
    corner_z1, corner_kap = corner[0:1], lookup(corner[1:2], coef, 0)
    z_z1, z_z2 = (z_in[p.NY + k * X : p.NY + (k + 1) * X, :].astype(F32) for k in range(2))
    z_rows = z_in[p.NY + 2 * X : p.NY + 2 * X + 16, :].astype(F32)
    zy_z1, zy_kap = z_rows[0:1], lookup(z_rows[1:2], coef, 0)
    block_kap = lookup(block, coef, 0)
    sides = sides_ref[...]
    brick = Brick(p, cst_ref, part(kaps, b.uxm), part(kaps, b.uxp))
    halo = (pick(odd, 0.0, x_z1), pick(odd, x_z1, 0.0), pick(up, 0.0, z_z1), pick(up, z_z1, 0.0), sides)
    for i in range(X):
        s_out[i] = s_ref[i] + brick.damp(i) * brick.from_halo(i, halo)
    row, lane = iota((Z, Y), 0), iota((Z, Y), 1)
    face = lambda high: pick(high, brick.of(KAP, X - 1), brick.of(KAP, 0))

    k, sigma = x_part(kaps, odd), x_part(sigs, odd)
    toward = k + face(odd)
    X2 = 2 * X
    ends = lambda value, first: [pick(odd, value[:, first + c : first + c + 1], value[:, first + X2 - 2 + c : first + X2 - 1 + c]) for c in (0, 1)]
    col_kap, col_z1 = ends(block_kap, X2), ends(block, 0)
    w = plane_weights(k, pick(up, 0.0, corner_kap), pick(up, corner_kap, 0.0), col_kap[0], col_kap[1])
    total = toward * x_part(z1b, odd)
    total = total + jnp.where(row == pick(up, Z - 1, 0), pick(up, w[1], w[0]) * corner_z1, 0.0)
    total = total + jnp.where(lane == 0, w[2] * col_z1[0], 0.0) + jnp.where(lane == Y - 1, w[3] * col_z1[1], 0.0)
    diagonal = sigma + (k + toward) + ((w[0] + w[1]) + (w[2] + w[3]))
    value = x_part(uhb, odd) + x_z2 + (DAMPING / diagonal) * total
    out_ref[to.cross : to.cross + Z, :] = jnp.where(k > 0.0, value, 0.0)

    other = jnp.logical_not(odd)
    k, sigma = x_part(kaps, other), x_part(sigs, other)
    toward = k + face(other)
    for j, value in enumerate((k, toward, sigma + (k + toward), x_part(z1b, other), x_part(uhb, other))):
        out_ref[to.core + j * Z : to.core + (j + 1) * Z, :] = value

    k, sigma = z_part(kaps), z_part(sigs)
    own = jnp.concatenate([pick(up, cst_ref[KAP, i // 4, Z - 1 : Z, :], cst_ref[KAP, i // 4, 0:1, :]) for i in range(X)], axis=0)
    toward = k + own
    col_kap, col_z1 = ([column(value, X, c) for c in (0, 1)] for value in (zy_kap, zy_z1))
    w = plane_weights(k, pick(odd, 0.0, corner_kap), pick(odd, corner_kap, 0.0), col_kap[0], col_kap[1])
    zrow, zlane = iota((X, Y), 0), iota((X, Y), 1)
    total = toward * z_part(z1b)
    total = total + jnp.where(zrow == pick(odd, X - 1, 0), pick(odd, w[1], w[0]) * corner_z1, 0.0)
    total = total + jnp.where(zlane == 0, w[2] * col_z1[0], 0.0) + jnp.where(zlane == Y - 1, w[3] * col_z1[1], 0.0)
    diagonal = sigma + (k + toward) + ((w[0] + w[1]) + (w[2] + w[3]))
    for j, value in enumerate((z_part(uhb) + z_z2, total, diagonal, k)):
        out_ref[to.z + j * X : to.z + (j + 1) * X, :] = value

    k, sigma = part(kaps, b.uy), part(sigs, b.uy)
    toward = k + swap_lanes(col_faces(lambda i: brick.of(KAP, i), p))
    reach = lambda value, shift: pick(odd, roll(value, X2 + shift, 1), roll(value, Y - X2 + shift, 1))
    begin = pick(odd, X2, Y - 2)
    far = (lane >= begin) & (lane < begin + 2)
    wide = jnp.where(far, reach(block_kap, -X2), jnp.where(lane < X2, k, 0.0))
    wide_z1 = jnp.where(far, reach(block, 0), 0.0)
    above, below = shifted(wide, 0, pick(up, 0.0, zy_kap), pick(up, zy_kap, 0.0))
    left, right = roll(wide, 2, 1), roll(wide, -2, 1)
    place = lane // 2
    w = (
        jnp.where(row % 4 == 0, wide + above, wide),
        jnp.where(row % 4 == 3, wide + below, wide),
        jnp.where(place % 4 == 0, wide + left, wide),
        jnp.where(place % 4 == 3, wide + right, wide),
    )
    total = toward * swap_lanes(part(z1b, b.uy))
    total = total + jnp.where(row == pick(up, Z - 1, 0), pick(up, w[1], w[0]) * zy_z1, 0.0)
    total = total + jnp.where(place == 0, w[2] * roll(wide_z1, 2, 1), 0.0)
    total = total + jnp.where(place == X - 1, w[3] * roll(wide_z1, -2, 1), 0.0)
    diagonal = sigma + (k + toward) + ((w[0] + w[1]) + (w[2] + w[3]))
    for j, value in enumerate((part(uhb, b.uy) + roll(sides, -X2, 1), total, diagonal, k)):
        out_ref[to.y + j * Z : to.y + (j + 1) * Z, :] = value


def last_halo(p, coef, beyond_ref, last_in):
    X, Z, Y, to = p.X, p.Z, p.Y, Beyond(p)
    bx, bz = lax.axis_index("bx"), lax.axis_index("bz")
    odd, up = bx % 2 == 1, bz == 0
    start, X2 = Sends(p).second, 2 * X
    z1, z2, block = (last_in[start + k * Z : start + (k + 1) * Z, :].astype(F32) for k in range(3))
    corner = last_in[start + 3 * Z : start + 3 * Z + 16, :].astype(F32)
    corner_z1, corner_kap = corner[0:1], lookup(corner[1:2], coef, 0)
    block_kap = lookup(block, coef, 0)
    row, lane = iota((Z, Y), 0), iota((Z, Y), 1)

    k, toward, diagonal, own, old = (rows_at(beyond_ref, to.core + j * Z, Z) for j in range(5))
    ends = lambda value, first: [pick(odd, value[:, first + X2 - 2 + c : first + X2 - 1 + c], value[:, first + c : first + c + 1]) for c in (0, 1)]
    col_kap, col_z1 = ends(block_kap, X2), ends(block, 0)
    w = plane_weights(k, pick(up, 0.0, corner_kap), pick(up, corner_kap, 0.0), col_kap[0], col_kap[1])
    total = toward * own
    total = total + jnp.where(row == pick(up, Z - 1, 0), pick(up, w[1], w[0]) * corner_z1, 0.0)
    total = total + jnp.where(lane == 0, w[2] * col_z1[0], 0.0) + jnp.where(lane == Y - 1, w[3] * col_z1[1], 0.0)
    diagonal = diagonal + ((w[0] + w[1]) + (w[2] + w[3]))
    core = (k, old + z2 + (DAMPING / diagonal) * total)
    value, total, diagonal, k = (rows_at(beyond_ref, to.z + j * X, X) for j in range(4))
    edge = iota((X, Y), 0) == pick(odd, 0, X - 1)
    total = total + jnp.where(edge, (k + corner_kap) * corner_z1, 0.0)
    diagonal = diagonal + jnp.where(edge, corner_kap, 0.0)
    z = (k, value + (DAMPING / diagonal) * total)

    value, total, diagonal, k = (rows_at(beyond_ref, to.y + j * Z, Z) for j in range(4))
    begin = pick(odd, 0, X2 - 2)
    edge = (lane >= begin) & (lane < begin + 2)
    reach = lambda value, shift: pick(odd, roll(value, 2 - X2 + shift, 1), roll(value, X2 - 2 + shift, 1))
    edge_kap = reach(block_kap, -X2)
    total = total + jnp.where(edge, (k + edge_kap) * reach(block, 0), 0.0)
    diagonal = diagonal + jnp.where(edge, edge_kap, 0.0)
    return z1, core, z, (k, value + (DAMPING / diagonal) * total)


def finish_staged(p, brick, s_ref, beyond_ref, parts, nodes, side, u_ref):
    X, Z, to = p.X, p.Z, Beyond(p)
    bx, bz = lax.axis_index("bx"), lax.axis_index("bz")
    odd, up = bx % 2 == 1, bz == 0
    some = (bx > 0) & (bx < p.nx - 1)
    z1, core, z, y = parts
    for i in range(X):
        value = s_ref[i] + nodes[i * Z : (i + 1) * Z]
        if i in (0, X - 1):
            weight = brick.x_weights(i)[0 if i == 0 else 1]
            here = odd if i == 0 else jnp.logical_not(odd)
            value = value + brick.damp(i) * (weight * pick(here, z1, 0.0))
        u_ref[i] = value
    at = X * Z
    below, above = nodes[at : at + Z], nodes[at + Z : at + 2 * Z]
    core = jnp.where(core[0] > 0.0, core[1] + pick(odd, below, above), 0.0)
    cross = pick(some, rows_at(beyond_ref, to.cross, Z) + pick(odd, above, below), 0.0)
    at += 2 * Z
    z = jnp.where(z[0] > 0.0, z[1] + pick(up, nodes[at + X : at + 2 * X], nodes[at : at + X]), 0.0)
    y = jnp.where(y[0] > 0.0, y[1] + side, 0.0)
    return pick(odd, core, cross), pick(odd, cross, core), pick(up, 0.0, z), pick(up, z, 0.0), y


def coarse_staged(p, own_ref, last_in, inverse, kx, kxi, zi, along_y, pall, pyh):
    Y, NY = p.Y, p.NY
    bx, bz = lax.axis_index("bx"), lax.axis_index("bz")
    rows, step, count = p.cx * p.NZ, p.cx * LOW, p.NX * LOW
    back = kxi[pl.ds(pl.multiple_of(bx * step, 16), step + 2 * LOW), :]
    table = kx[bx]
    parts = []
    for h in range(p.NZ // LOW):
        lines = []
        for ref in (own_ref, last_in):
            for block in range(2):
                at = [(block * (NY // Y) + k) * rows + h * step for k in range(NY // Y)]
                lines.append(jnp.concatenate([ref[i : i + step, :] for i in at], axis=1))
        parts.append(dot(table, jnp.concatenate(lines, axis=0)))
    parts = [(value * inverse[h * count : (h + 1) * count, :]).astype(BF16) for h, value in enumerate(parts)]
    values = dot(back, jnp.concatenate(parts, axis=1)).astype(BF16)
    values = jnp.concatenate([values[:, h * NY : (h + 1) * NY] for h in range(len(parts))], axis=0)
    values = dot(zi[bz], values).astype(BF16)
    values = dot(jnp.concatenate([values, values], axis=1), along_y[...])
    count = pall.shape[0] - p.Z
    nodes = dot_wide_right(pall[:count, : p.lanes + p.extra], values[:, :Y]) * (1.0 / 27.0)
    ends = values[: p.lanes, Y:]
    spread = ends[:, 0:1] * pyh[: p.lanes].astype(F32) + ends[:, 1:2] * pyh[p.lanes :].astype(F32)
    side = dot_wide_right(pall[count:, : p.lanes], spread) * (1.0 / 27.0)
    return nodes, side


def inverse_kernel(p, coef, lam_xz, lam_y, sy, pye, out_ref, along_ref):
    classes = coef.shape[1]
    kap_mean = sum(coef[0, k] for k in range(classes)) * (1.0 / classes)
    sig_mean = sum(coef[1, k] for k in range(classes)) * (1.0 / classes)
    step = p.NX * LOW
    for h in range(p.NZ // LOW):
        lam = lam_xz[h * step : (h + 1) * step, :] + lam_y[...]
        out_ref[h * step : (h + 1) * step, :] = 1.0 / (kap_mean * lam + sig_mean)
    rows = sy[pl.ds(pl.multiple_of(lax.axis_index("by") * p.cy, 16), p.cy + 16), :]
    high, low = halves(dot(rows.T, pye[...]))
    along_ref[: p.NY, :] = high
    along_ref[p.NY :, :] = low


def first_staged(p, coef, u_ref, r_ref, cls_ref, cst0_ref, xa, xb, za, zb, ya, yb, rxz, ry,
                 a_ref, faces_ref, s_ref, z1b_ref, uhb_ref, clsb_ref, cst_ref, r_scr, z_scr, z2_scr):
    brick, residual = neighbours_in(p, coef, u_ref, r_ref, cst0_ref, xa, xb, za, zb, ya, yb, uhb_ref, clsb_ref, cst_ref)
    coarse = advance(p, brick, lambda i: u_ref[i], residual, rxz, ry, s_ref, r_scr, z_scr, z2_scr)
    send_first(p, coarse, z_scr, z2_scr, z1b_ref, a_ref, faces_ref)


def correct(p, coef, s_ref, beyond_ref, cst_ref, own, last_in, inverse, kx, kxi, zi, along_y, pall, pyh, u_ref):
    b, at = Bounds(p), Beyond(p).kap
    brick = Brick(p, cst_ref, rows_at(beyond_ref, at + b.uxm[0], p.Z), rows_at(beyond_ref, at + b.uxp[0], p.Z))
    parts = last_halo(p, coef, beyond_ref, last_in)
    nodes, side = coarse_staged(p, own, last_in, inverse, kx, kxi, zi, along_y, pall, pyh)
    return brick, finish_staged(p, brick, s_ref, beyond_ref, parts, nodes, side, u_ref)


def middle_staged(p, coef, f_ref, s_ref, beyond_ref, cst_ref, own, last_in, inverse, kx, kxi, zi, along_y, pall, pyh, rxz, ry,
                  a_ref, faces_ref, s_out, z1b_out, uhb_out, u_scr, r_scr, z_scr, z2_scr):
    brick, halo = correct(p, coef, s_ref, beyond_ref, cst_ref, own, last_in, inverse, kx, kxi, zi, along_y, pall, pyh, u_scr)
    write_bounds(uhb_out, Bounds(p), halo)
    get = lambda i: u_scr[i]
    residual = lambda i: residual_plane(brick, i, get, halo, f_ref[i])
    coarse = advance(p, brick, get, residual, rxz, ry, s_out, r_scr, z_scr, z2_scr)
    send_first(p, coarse, z_scr, z2_scr, z1b_out, a_ref, faces_ref)


def last_staged(p, coef, f_ref, s_ref, beyond_ref, cst_ref, own, last_in, inverse, kx, kxi, zi, along_y, pall, pyh,
                u_out, r_out, u_scr, r_scr, sems):
    brick, halo = correct(p, coef, s_ref, beyond_ref, cst_ref, own, last_in, inverse, kx, kxi, zi, along_y, pall, pyh, u_scr)
    copies = [pltpu.make_async_copy(u_scr, u_out, sems.at[0])]
    copies[0].start()
    chunk = p.X // 4
    for k in range(4):
        for i in range(k * chunk, (k + 1) * chunk):
            r_scr[i] = residual_plane(brick, i, lambda j: u_scr[j], halo, f_ref[i])
        part = pl.ds(k * chunk, chunk)
        copies.append(pltpu.make_async_copy(r_scr.at[part], r_out.at[part], sems.at[k + 1]))
        copies[-1].start()
    for copy in copies:
        copy.wait()


def call(kernel, p, name, coef, inputs, outputs, scratch, us=2, out_space=pltpu.VMEM):
    smem = [pl.BlockSpec(memory_space=pltpu.SMEM)] if coef is not None else []
    args = ([coef] if coef is not None else []) + list(inputs)
    return pl.pallas_call(
        functools.partial(kernel, p),
        out_shape=[jax.ShapeDtypeStruct(shape, dtype) for shape, dtype in outputs],
        in_specs=smem + [pl.BlockSpec(memory_space=pltpu.VMEM)] * len(inputs),
        out_specs=[pl.BlockSpec(memory_space=out_space)] * len(outputs),
        scratch_shapes=[pltpu.VMEM(shape, F32) if isinstance(shape, tuple) else shape for shape in scratch],
        compiler_params=pltpu.CompilerParams(vmem_limit_bytes=VMEM_LIMIT),
        cost_estimate=pl.CostEstimate(flops=0, bytes_accessed=us * 3_600_000, transcendentals=0),
        name=name,
    )(*args)


def swaps(axis, count, a, b, near=None):
    if count == 1:
        return a, b
    assert count % 2 == 0
    first = lax.ppermute(a, axis, [(i, i ^ 1) for i in range(count)])
    if count == 2:
        return first, first
    other = lambda i: (i + 1 if i % 2 else i - 1) % count
    if near is None:
        return first, lax.ppermute(b, axis, [(i, other(i)) for i in range(count)])
    name, size = near
    pairs = []
    for k in range(size):
        for i in range(count):
            to = (k ^ 1, i) if i in (0, count - 1) else (k, other(i))
            pairs.append((k * count + i, to[0] * count + to[1]))
    return first, lax.ppermute(b, (name, axis), pairs)


def body(forcing, start, element_class_index, class_coef):
    p = Plan(start.shape, *(lax.axis_size(axis) for axis in AXES))
    t = tables(p)
    X, Z, Y, n = p.X, p.Z, p.Y, p.n
    bounds = Bounds(p).count
    block, flat, cst = (X, Z, Y), (X * Z, Y), (DAMP, X // 4, Z, Y)
    (uy,) = call(sides_kernel, p, "start_sides", None, (start,), [((Z, Y), F32)], [], us=20)
    cls, xa, xb, za, zb, yf = call(
        pack_kernel, p, "pack_faces", None, (element_class_index, start, uy),
        [((X // 4, Z, Y), F32)] + [((2 * Z, Y), F32)] * 2 + [((2 * X, Y), F32)] * 2 + [((2 * Z, Y), F32)], [], us=20,
    )
    xa, xb = swaps("bx", p.nx, xa, xb)
    za, zb = swaps("bz", p.nz, za, zb)
    ya, yb = swaps("by", p.ny, yf, yf, ("bx", p.nx) if p.nx % 2 == 0 else None)
    go_shape, back_shape = (n * p.go, Y), (n * p.back, Y)
    starting = [flat, block, block, go_shape]
    rxz, ry, sy = t["rxz"], t["ry"], t["sy"]
    cst0, r0 = call(prepare_kernel, p, "prepare", class_coef, (start, forcing, cls), [(cst, F32), (block, F32)], [], us=6)
    if p.staged:
        return staged_cycles(p, t, class_coef, forcing, cls, start, r0, cst0, (xa, xb, za, zb, ya, yb))
    go, s, z1b, uhb, clsb, coefs = call(
        first_kernel, p, "first_residual", class_coef,
        (start, r0, cls, cst0, xa, xb, za, zb, ya, yb, rxz, ry, sy),
        [(go_shape, BF16), (block, F32), ((bounds, Y), F32), ((bounds, Y), F32), ((bounds, Y), F32), ((QUANTITIES,) + cst[1:], F32)],
        starting,
    )
    prolong = (sy, t["pyt"], t["pall"], t["pyh"])
    first = None
    for cycle in range(CYCLES):
        came = lax.all_to_all(go, AXES, split_axis=0, concat_axis=0, tiled=True)
        (out,) = call(
            owner_kernel, p, "owned_modes", class_coef,
            (came, t["wz"], t["wx"], t["wxt"], t["wzi"], t["lamxz"], t["lamy"]),
            [(back_shape, BF16)], [go_shape, back_shape],
        )
        back = lax.all_to_all(out, AXES, split_axis=0, concat_axis=0, tiled=True)
        if cycle + 1 < CYCLES:
            assert first is None
            first = back
            go, s, z1b, uhb = call(
                middle_kernel, p, "next_residual", class_coef,
                (back, forcing, s, z1b, uhb, clsb, coefs) + prolong + (rxz, ry),
                [(go_shape, BF16), (block, F32), ((bounds, Y), F32), ((bounds, Y), F32)],
                [back_shape, block] + starting,
            )
        else:
            return tuple(call(
                last_kernel, p, "last_residual", class_coef,
                (back, first, forcing, s, z1b, uhb, clsb, coefs) + prolong,
                [(block, F32), (block, F32)], [back_shape, back_shape],
            ))


def staged_cycles(p, t, class_coef, forcing, cls, u0, r0, cst0, faces_in):
    X, Z, Y = p.X, p.Z, p.Y
    sends, bounds = Sends(p), (Bounds(p).count, Y)
    block, flat = (X, Z, Y), (X * Z, Y)
    out = [((sends.first, Y), BF16), ((sends.faces, Y), BF16), (block, F32), (bounds, F32), (bounds, F32)]
    scratch = [flat, block, block]
    inverse, along_y = call(
        inverse_kernel, p, "inverse_spectrum", class_coef, (t["lam_xz"], t["lam_y"], t["sy"], t["pye"]),
        [((p.NZ * p.NX, p.NY), F32), ((2 * p.NY, 2 * Y), BF16)], [],
    )
    a, faces, s, z1b, uhb, clsb, coefs = call(
        first_staged, p, "first_residual", class_coef, (u0, r0, cls, cst0) + faces_in + (t["rxz"], t["ry"]),
        out + [(bounds, F32), ((QUANTITIES,) + cst0.shape[1:], F32)], scratch,
    )
    pairs = lambda count, d: [(i, i ^ d) for i in range(count)]
    for cycle in range(CYCLES):
        came = [a] + [lax.ppermute(a, "by", pairs(p.ny, d)) for d in range(1, p.ny)]
        x, z, xz, sides = call(
            after_first, p, "y_modes", None, (*came, faces, clsb, cls, t["sy"]),
            [((rows, Y), BF16) for rows in (sends.x_rows, sends.z_rows, sends.xz_rows)] + [((Z, Y), F32)],
            [pltpu.VMEM((p.NY, Y), BF16)],
        )
        plane, across = p.nx * p.nz, (p.nx - 1) * p.nz
        x_in = lax.ppermute(x, ("bx", "bz"), pairs(plane, across))
        z_in = lax.ppermute(z, ("bx", "bz"), pairs(plane, 1))
        xz_in = lax.ppermute(xz, ("bx", "bz"), pairs(plane, across + 1))
        if cycle == 0:
            x_in, inverse, along_y = lax.optimization_barrier((x_in, inverse, along_y))
            back = (inverse, t["kx"], t["kxi"], t["zi"], along_y, t["pall"], t["pyh"])
        (own,) = call(
            after_second, p, "z_modes", None, (x, x_in, z_in, xz_in, faces, clsb, sides, t["wzt"]),
            [((sends.last, Y), BF16)], [],
        )
        last_in = lax.ppermute(own, "bx", pairs(p.nx, 1))
        s, beyond = call(
            beyond_kernel, p, "beyond", class_coef, (s, z1b, uhb, clsb, cls, coefs, sides, x_in, z_in, xz_in),
            [(block, F32), ((Beyond(p).count, Y), F32)], [],
        )
        inputs = (forcing, s, beyond, coefs, own, last_in) + back
        if cycle + 1 < CYCLES:
            a, faces, s, z1b, uhb = call(
                middle_staged, p, "next_residual", class_coef, inputs + (t["rxz"], t["ry"]), out, [block] + scratch
            )
        else:
            return tuple(call(
                last_staged, p, "last_residual", class_coef, inputs, [(block, F32), (block, F32)],
                [block, block, pltpu.SemaphoreType.DMA((5,))], out_space=pl.ANY,
            ))


def solution(mesh):
    spec = P("bx", "bz", "by")
    return jax.shard_map(body, mesh=mesh, in_specs=(spec, spec, spec, P()), out_specs=(spec, spec), check_vma=False)
```

```python
import functools
import math

import jax
import jax.numpy as jnp
import numpy as np
from jax import lax
from jax.experimental import pallas as pl
from jax.experimental.pallas import tpu as pltpu
from jax.sharding import PartitionSpec as P

CYCLES = 2
DAMPING = 0.6666666666666666
F32 = jnp.float32
BF16 = jnp.bfloat16
AXES = ("bx", "by", "bz")
VMEM_LIMIT = 32 * 1024 * 1024


def up_to(value, multiple):
    return -(-value // multiple) * multiple


class Plan:
    def __init__(self, shape, nx, ny, nz):
        self.X, self.Z, self.Y = shape
        self.nx, self.ny, self.nz = nx, ny, nz
        self.n = nx * ny * nz
        self.cx, self.cz, self.cy = self.X // 2, self.Z // 2, self.Y // 2
        self.NX, self.NZ, self.NY = self.cx * nx, self.cz * nz, self.cy * ny
        self.modes = -(-self.NY // self.n)
        self.NYp = self.modes * self.n
        self.lanes = self.cx * self.cz
        rows = (2 * self.Z, 2 * self.Z, 2 * self.X, 2 * self.X, self.Z, 12)
        self.heights = [-(-r // self.n) for r in rows]
        self.offsets = [sum(self.heights[:i]) for i in range(6)]
        halo = sum(self.heights)
        self.go_halo = self.modes
        self.go = up_to(self.modes + halo, 8)
        self.back_halo = 2 * self.modes
        self.back = up_to(2 * self.modes + halo, 8)
        self.edge_lane = 6 * self.X
        self.extra = 2 * self.cz + 2 * self.cx
        self.staged = nx == 4 and nz == 2 and ny & (ny - 1) == 0 and self.NZ % LOW == 0 and 8 * self.X <= self.Y
        assert self.lanes <= self.Y and self.extra <= self.lanes and self.edge_lane + 8 <= self.Y
        assert self.heights[5] == 1


def sine_table(count):
    index_one = np.arange(1, count + 1, dtype=np.int32)
    product = (index_one[:, None] * index_one[None, :]).astype(np.float32)
    value = np.sin(product * np.float32(math.pi / (count + 1)))
    return (value * np.float32(math.sqrt(2.0 / (count + 1)))).astype(BF16).astype(np.float32)


def spectrum_values(count):
    return 2.0 - 2.0 * np.cos(np.arange(1, count + 1) * (math.pi / (count + 1)))


RESTRICT = np.array([[3, 2, 1, 0], [0, 1, 2, 3]], np.float32)
PROLONG = np.array([[3, 0], [2, 1], [1, 2], [0, 3]], np.float32)


LOW = 8


def staged_tables(p, sx, sz, py):
    high, eye = p.NZ // LOW, np.eye(LOW)
    out = {}
    wzt = np.zeros((high, p.cx, LOW, p.nz, p.cx, p.cz), np.float32)
    for x in range(p.cx):
        wzt[:, x, :, :, x, :] = sz.reshape(high, LOW, p.nz, p.cz)
    out["wzt"] = wzt.reshape(p.cx * p.NZ, p.nz * p.lanes)
    blocks = sx.reshape(p.NX, p.nx, p.cx)
    order = lambda b: [b, b ^ 3, b ^ 1, b ^ 2]
    out["kx"] = np.stack([np.kron(blocks[:, order(b)].reshape(p.NX, p.NX), eye) for b in range(p.nx)])
    sxp = np.zeros((p.NX + 2, p.NX), np.float32)
    sxp[1:-1] = sx
    out["kxi"] = np.kron(sxp, eye)
    szp = np.zeros((p.NZ + 2, p.NZ), np.float32)
    szp[1:-1] = sz
    zi = np.zeros((p.nz, p.lanes + p.extra, high, p.cx + 2, LOW), np.float32)
    for b in range(p.nz):
        mine = szp[b * p.cz + 1 : (b + 1) * p.cz + 1].reshape(p.cz, high, LOW)
        for x in range(p.cx):
            zi[b, x * p.cz : (x + 1) * p.cz, :, x + 1, :] = mine
            zi[b, p.lanes + 2 * p.cz + x, :, x + 1, :] = szp[b * p.cz].reshape(high, LOW)
            zi[b, p.lanes + 2 * p.cz + p.cx + x, :, x + 1, :] = szp[(b + 1) * p.cz + 1].reshape(high, LOW)
        zi[b, p.lanes : p.lanes + p.cz, :, 0, :] = mine
        zi[b, p.lanes + p.cz : p.lanes + 2 * p.cz, :, p.cx + 1, :] = mine
    out["zi"] = zi.reshape(p.nz, p.lanes + p.extra, -1)
    pye = np.zeros((p.cy + 16, 2 * p.Y), np.float32)
    pye[8 : 8 + p.cy, : p.Y] = py.T
    pye[7, p.Y] = pye[8 + p.cy, p.Y + 1] = 1
    out["pye"] = pye
    return out


def tables(p):
    rx = np.kron(np.eye(p.X // 4), RESTRICT)
    rz = np.kron(np.eye(p.Z // 4), RESTRICT)
    ry = np.kron(np.eye(p.Y // 4), RESTRICT)
    px = np.kron(np.eye(p.X // 4), PROLONG)
    pz = np.kron(np.eye(p.Z // 4), PROLONG)
    py = np.kron(np.eye(p.Y // 4), PROLONG)
    sx, sz, sy = sine_table(p.NX), sine_table(p.NZ), sine_table(p.NY)
    out = {}
    out["rxz"] = np.kron(rx, rz)
    out["ry"] = ry
    padded = np.zeros((p.NY + 16, p.NYp), np.float32)
    padded[8 : 8 + p.NY, : p.NY] = sy
    out["sy"] = padded
    wz = np.zeros((p.cx, p.NZ, p.nz, p.cx, p.cz), np.float32)
    for x in range(p.cx):
        wz[x, :, :, x, :] = sz.reshape(p.NZ, p.nz, p.cz)
    out["wz"] = wz.reshape(p.cx * p.NZ, p.nz * p.lanes)
    wx = np.einsum("bxk,mn->xbmkn", sx.reshape(p.nx, p.cx, p.NX), np.eye(p.modes))
    wx = wx.reshape(p.NX * p.modes, p.NX * p.modes)
    out["wx"], out["wxt"] = wx, wx.T
    szp = np.zeros((p.NZ, p.NZ + 2), np.float32)
    szp[:, 1:-1] = sz
    wzi = np.zeros((p.nz, p.cx, p.NZ, 2 * p.lanes), np.float32)
    for b in range(p.nz):
        for x in range(p.cx):
            wzi[b, x, :, x * p.cz : (x + 1) * p.cz] = sz[:, b * p.cz : (b + 1) * p.cz]
            wzi[b, x, :, p.lanes + x] = szp[:, b * p.cz]
            wzi[b, x, :, p.lanes + p.cx + x] = szp[:, (b + 1) * p.cz + 1]
    out["wzi"] = wzi.reshape(p.nz, p.cx * p.NZ, 2 * p.lanes)
    out["pyt"] = py.T
    pall = np.zeros((p.X * p.Z + 2 * p.Z + 2 * p.X, 2 * p.lanes), np.float32)
    at = p.X * p.Z
    pall[:at, : p.lanes] = np.kron(px, pz)
    col = p.lanes
    for _ in range(2):
        pall[at : at + p.Z, col : col + p.cz] = 3 * pz
        at, col = at + p.Z, col + p.cz
    for _ in range(2):
        pall[at : at + p.X, col : col + p.cx] = 3 * px
        at, col = at + p.X, col + p.cx
    out["pall"] = np.concatenate([pall, np.tile(pz, (1, 2 * p.cx))])
    pyh = np.zeros((2, p.lanes, p.Y), np.float32)
    spread = np.repeat(px.T, p.cz, axis=0)
    for side in range(2):
        pyh[side, :, side : 2 * p.X : 2] = 3 * spread
    out["pyh"] = pyh.reshape(2 * p.lanes, p.Y)
    if p.staged:
        out.update(staged_tables(p, sx, sz, py))
    out = {key: jnp.asarray(value.astype(BF16)) for key, value in out.items()}
    if p.staged:
        lam = spectrum_values(p.NX)[None, :, None] + spectrum_values(p.NZ).reshape(-1, 1, LOW)
        out["lam_xz"] = jnp.asarray(lam.reshape(-1, 1).astype(np.float32))
        out["lam_y"] = jnp.asarray(spectrum_values(p.NY).reshape(1, -1).astype(np.float32))
        return out
    lam = spectrum_values(p.NX)[None, :, None] + spectrum_values(p.NZ)[:, None, None]
    out["lamxz"] = jnp.asarray(np.broadcast_to(lam, (p.NZ, p.NX, p.modes)).reshape(p.NZ, -1).astype(np.float32))
    lamy = np.zeros(p.NYp)
    lamy[: p.NY] = spectrum_values(p.NY)
    lamy = np.broadcast_to(lamy.reshape(p.n, 1, 1, p.modes), (p.n, 1, p.NX, p.modes))
    out["lamy"] = jnp.asarray(lamy.reshape(p.n, 1, -1).astype(np.float32))
    return out


def iota(shape, dim):
    return lax.broadcasted_iota(jnp.int32, shape, dim)


def dot(a, b, dims=((1,), (0,))):
    return lax.dot_general(a, b, (dims, ((), ())), preferred_element_type=F32)


def halves(value):
    high = value.astype(BF16)
    return high, (value - high.astype(F32)).astype(BF16)


def dot_wide_right(table, value, dims=((1,), (0,))):
    axis = 1 - dims[1][0]
    count = value.shape[axis]
    both = dot(table, jnp.concatenate(halves(value), axis=axis), dims)
    return both[:, :count] + both[:, count:]


def dot_wide_left(value, table, dims=((1,), (0,))):
    high, low = halves(value)
    return dot(high, table, dims) + dot(low, table, dims)


def roll(value, shift, axis):
    size = value.shape[axis]
    shift = shift % size
    return value if shift == 0 else pltpu.roll(value, shift, axis)


def lookup(classes, coef_ref, row):
    total = jnp.zeros_like(classes)
    for k in range(coef_ref.shape[1]):
        total = jnp.where(classes == k + 1.0, coef_ref[row, k], total)
    return total


def col_faces(get, p):
    lane = iota((p.Z, p.Y), 1) // 2
    total = jnp.zeros((p.Z, p.Y), F32)
    for i in range(p.X):
        total = jnp.where(lane == i, roll(get(i), 2 * i + 1, 1), total)
    return total


def swap_lanes(value):
    even = iota(value.shape, 1) % 2 == 0
    return jnp.where(even, roll(value, -1, 1), roll(value, 1, 1))


def shifted(value, axis, before, after):
    size = value.shape[axis]
    at = iota(value.shape, axis)
    low = jnp.where(at == 0, before, roll(value, 1, axis))
    high = jnp.where(at == size - 1, after, roll(value, -1, axis))
    return low, high


def plane_weights(kap, row_m, row_p, col_m, col_p):
    up, down = shifted(kap, 0, row_m, row_p)
    left, right = shifted(kap, 1, col_m, col_p)
    row, lane = iota(kap.shape, 0) % 4, iota(kap.shape, 1) % 4
    return (
        jnp.where(row == 0, kap + up, kap),
        jnp.where(row == 3, kap + down, kap),
        jnp.where(lane == 0, kap + left, kap),
        jnp.where(lane == 3, kap + right, kap),
    )


KAP, WZM, WZP, WYM, WYP, BASE, BETA, DAMP = range(8)
QUANTITIES = DAMP + 3


class Brick:
    def __init__(self, p, cst_ref, kap_xm, kap_xp):
        self.p, self.cst, self.kap_xm, self.kap_xp = p, cst_ref, kap_xm, kap_xp

    def of(self, quantity, i):
        return self.cst[quantity, i // 4]

    def x_weights(self, i):
        kap = self.of(KAP, i)
        low = high = kap
        if i % 4 == 0:
            low = kap + (self.of(KAP, i - 1) if i else self.kap_xm)
        if i % 4 == 3:
            high = kap + (self.of(KAP, i + 1) if i + 1 < self.p.X else self.kap_xp)
        return low, high

    def diagonal(self, i):
        low, high = self.x_weights(i)
        return self.of(BASE, i) + (low + high)

    def damp(self, i):
        return self.cst[DAMP + (0 if i % 4 == 0 else 2 if i % 4 == 3 else 1), i // 4]

    def neighbours(self, i, get, halo=None):
        p, v = self.p, get(i)
        low, high = self.x_weights(i)
        total = jnp.zeros_like(v)
        if i:
            total = total + low * get(i - 1)
        elif halo is not None:
            total = total + low * halo[0]
        if i + 1 < p.X:
            total = total + high * get(i + 1)
        elif halo is not None:
            total = total + high * halo[1]
        if halo is None:
            ends = (0.0, 0.0, 0.0, 0.0)
        else:
            side = self.y_ends(halo[4], i)
            ends = (halo[2][i : i + 1], halo[3][i : i + 1], side, side)
        up, down = shifted(v, 0, ends[0], ends[1])
        left, right = shifted(v, 1, ends[2], ends[3])
        total = total + self.of(WZM, i) * up + self.of(WZP, i) * down
        return total + self.of(WYM, i) * left + self.of(WYP, i) * right

    def y_ends(self, yh, i):
        return roll(swap_lanes(yh), self.p.Y - 1 - 2 * i, 1)

    def from_halo(self, i, halo):
        p = self.p
        row, lane = iota((p.Z, p.Y), 0), iota((p.Z, p.Y), 1)
        side = self.y_ends(halo[4], i)
        total = jnp.where(row == 0, self.of(WZM, i) * halo[2][i : i + 1], 0.0)
        total = jnp.where(row == p.Z - 1, self.of(WZP, i) * halo[3][i : i + 1], total)
        total = total + jnp.where(lane == 0, self.of(WYM, i) * side, 0.0)
        total = total + jnp.where(lane == p.Y - 1, self.of(WYP, i) * side, 0.0)
        if i == 0:
            total = total + self.x_weights(i)[0] * halo[0]
        if i == p.X - 1:
            total = total + self.x_weights(i)[1] * halo[1]
        return total


def residual_plane(brick, i, get, halo, f):
    v = get(i)
    return f - brick.diagonal(i) * v + brick.neighbours(i, get, halo) - brick.of(BETA, i) * v * v * v


def put_rows(ref, stride, offset, n, rows):
    height = -(-rows.shape[0] // n)
    if rows.shape[0] < height * n:
        rows = jnp.concatenate([rows, jnp.zeros((height * n - rows.shape[0], rows.shape[1]), F32)], axis=0)
    for k in range(height):
        ref[pl.ds(offset + k, n, stride=stride), :] = rows[k * n : (k + 1) * n]


def get_rows(ref, stride, offset, n, count):
    height = -(-count // n)
    parts = [ref[pl.ds(offset + k, n, stride=stride), :] for k in range(height)]
    value = parts[0] if height == 1 else jnp.concatenate(parts, axis=0)
    return value[:count]


class Bounds:
    def __init__(self, p):
        self.uxm, self.uxp = (0, p.Z), (p.Z, p.Z)
        self.uzm, self.uzp = (2 * p.Z, p.X), (2 * p.Z + p.X, p.X)
        self.uy = (2 * p.Z + 2 * p.X, p.Z)
        self.count = 3 * p.Z + 2 * p.X


def read(ref, span):
    return ref[span[0] : span[0] + span[1], :]


def write_bounds(ref, b, values):
    for span, value in zip((b.uxm, b.uxp, b.uzm, b.uzp, b.uy), values):
        ref[span[0] : span[0] + span[1], :] = value


def read_bounds(ref, b):
    return tuple(read(ref, span) for span in (b.uxm, b.uxp, b.uzm, b.uzp, b.uy))


def advance(p, brick, get, residual, rxz, ry, s_ref, r_scr, z_scr, z2_scr):
    X, Z = p.X, p.Z
    for i in range(X):
        r = residual(i)
        r_scr[i * Z : (i + 1) * Z, :] = r
        z_scr[i] = r * brick.damp(i)
    z1 = lambda i: z_scr[i]
    coarse = dot_wide_right(rxz[...], r_scr[...])
    coarse = dot_wide_right(ry[...], coarse, ((1,), (1,))) * (1.0 / 216.0)
    for i in range(X):
        v = z1(i)
        smooth = (2.0 - DAMPING) * v + brick.damp(i) * brick.neighbours(i, z1)
        z2_scr[i] = smooth
        s_ref[i] = get(i) + smooth
    return coarse.astype(BF16)


def start_cycle(p, brick, get, residual, classes, rxz, ry, sy, s_ref, z1b_ref, go_ref, r_scr, z_scr, z2_scr, go_scr):
    X, Z, n = p.X, p.Z, p.n
    coarse = advance(p, brick, get, residual, rxz, ry, s_ref, r_scr, z_scr, z2_scr)
    z1 = lambda i: z_scr[i]
    rows = sy[pl.ds(pl.multiple_of(lax.axis_index("by") * p.cy + 8, 8), p.cy), :]
    part = dot(rows.T, coarse)
    for j in range(n):
        go_scr[j * p.go : j * p.go + p.modes, :] = part[j * p.modes : (j + 1) * p.modes]
    z2 = lambda i: z2_scr[i]
    z1_y, z2_y = col_faces(z1, p), col_faces(z2, p)
    z1_zm, z1_zp = z_scr[:, 0, :], z_scr[:, Z - 1, :]
    write_bounds(z1b_ref, Bounds(p), (z1(0), z1(X - 1), z1_zm, z1_zp, z1_y))
    lane = iota((Z, p.Y), 1)
    sides = jnp.where(lane < 2 * X, z1_y, roll(z2_y, 2 * X, 1))
    edges = [z_scr[0, 0:1, :], z_scr[0, Z - 1 : Z, :], z_scr[X - 1, 0:1, :], z_scr[X - 1, Z - 1 : Z, :]]
    edges += [z1_y[0:1], z1_y[Z - 1 : Z]]
    if classes is None:
        sides = jnp.where(lane < 4 * X, sides, 0.0)
    else:
        cls, cls_y = classes
        sides = jnp.where(lane < 4 * X, sides, roll(cls_y, 4 * X, 1))
        sides = jnp.where(lane < 6 * X, sides, 0.0)
        edges += [cls(0)[0:1], cls(0)[Z - 1 : Z], cls(X - 1)[0:1], cls(X - 1)[Z - 1 : Z]]
        edges += [cls_y[0:1], cls_y[Z - 1 : Z]]
    pieces = (
        jnp.concatenate([z1(0), z2(0)], axis=0),
        jnp.concatenate([z1(X - 1), z2(X - 1)], axis=0),
        jnp.concatenate([z1_zm, z2_scr[:, 0, :]], axis=0),
        jnp.concatenate([z1_zp, z2_scr[:, Z - 1, :]], axis=0),
        sides,
        jnp.concatenate(edges, axis=0),
    )
    for piece, offset in zip(pieces, p.offsets):
        put_rows(go_scr, p.go, p.go_halo + offset, n, piece)
    used = p.go_halo + sum(p.heights)
    for k in range(used, p.go):
        go_scr[pl.ds(k, n, stride=p.go), :] = jnp.zeros((n, p.Y), F32)
    go_ref[...] = go_scr[...].astype(BF16)


def sides_kernel(p, u_ref, y_ref):
    y_ref[...] = col_faces(lambda i: u_ref[i], p)


def pack_kernel(p, index_ref, u_ref, uy_ref, cls_ref, xa_ref, xb_ref, za_ref, zb_ref, y_ref):
    X, Z, Y = p.X, p.Z, p.Y
    spread_z = (iota((Z, Z // 4), 0) // 4 == iota((Z, Z // 4), 1)).astype(BF16)
    spread_y = (iota((Y // 4, Y), 1) // 4 == iota((Y // 4, Y), 0)).astype(BF16)
    for a in range(X // 4):
        element = (index_ref[a] + 1).astype(F32).astype(BF16)
        cls_ref[a] = dot(dot(spread_z, element).astype(BF16), spread_y)
    cls = lambda i: cls_ref[i // 4]

    def face(axis, low, high, a_ref, b_ref, at):
        even = lax.axis_index(axis) % 2 == 0
        count = low.shape[0]
        a_ref[at : at + count, :] = jnp.where(even, high, low)
        b_ref[at : at + count, :] = jnp.where(even, low, high)

    face("bx", u_ref[0], u_ref[X - 1], xa_ref, xb_ref, 0)
    face("bx", cls(0), cls(X - 1), xa_ref, xb_ref, Z)
    rows = lambda z: jnp.concatenate([cls(i)[z : z + 1] for i in range(X)], axis=0)
    face("bz", u_ref[:, 0, :], u_ref[:, Z - 1, :], za_ref, zb_ref, 0)
    face("bz", rows(0), rows(Z - 1), za_ref, zb_ref, X)
    if X < Z:
        za_ref[2 * X :, :] = zb_ref[2 * X :, :] = jnp.zeros((2 * (Z - X), Y), F32)
    y_ref[0:Z, :] = uy_ref[...]
    y_ref[Z : 2 * Z, :] = col_faces(cls, p)


def received(axis, count, a_ref, b_ref):
    at = lax.axis_index(axis)
    even = at % 2 == 0
    a, b = a_ref[...], b_ref[...]
    low = jnp.where(even, b, a)
    high = jnp.where(even, a, b)
    return jnp.where(at > 0, low, 0.0), jnp.where(at < count - 1, high, 0.0)


def prepare_kernel(p, coef, u_ref, f_ref, cls_ref, cst_ref, r_ref):
    for a in range(p.X // 4):
        kap = lookup(cls_ref[a], coef, 0)
        wzm, wzp, wym, wyp = plane_weights(kap, 0.0, 0.0, 0.0, 0.0)
        cst_ref[KAP, a] = kap
        cst_ref[WZM, a] = wzm
        cst_ref[WZP, a] = wzp
        cst_ref[WYM, a] = wym
        cst_ref[WYP, a] = wyp
        cst_ref[BASE, a] = lookup(cls_ref[a], coef, 1) + ((wzm + wzp) + (wym + wyp))
        cst_ref[BETA, a] = lookup(cls_ref[a], coef, 2)
    brick = Brick(p, cst_ref, 0.0, 0.0)
    get = lambda i: u_ref[i]
    for i in range(p.X):
        r_ref[i] = residual_plane(brick, i, get, None, f_ref[i])


def neighbours_in(p, coef, u_ref, r_ref, cst0_ref, xa, xb, za, zb, ya, yb, uhb_ref, clsb_ref, cst_ref):
    X, Z, Y, b = p.X, p.Z, p.Y, Bounds(p)
    xm, xp = received("bx", p.nx, xa, xb)
    zm, zp = (value[: 2 * X] for value in received("bz", p.nz, za, zb))
    ym, yp = received("by", p.ny, ya, yb)
    y = jnp.where(iota(ym.shape, 1) % 2 == 0, ym, yp)
    halo = (xm[:Z], xp[:Z], zm[:X], zp[:X], y[:Z])
    outside = (xm[Z:], xp[Z:], zm[X:], zp[X:], y[Z:])
    write_bounds(uhb_ref, b, halo)
    write_bounds(clsb_ref, b, outside)
    kap_h = tuple(lookup(value, coef, 0) for value in outside)
    row, lane = iota((Z, Y), 0), iota((Z, Y), 1)
    more = []
    for a in range(X // 4):
        i = 4 * a
        ends = (
            (WZM, jnp.where(row == 0, kap_h[2][i : i + 1], 0.0)),
            (WZP, jnp.where(row == Z - 1, kap_h[3][i : i + 1], 0.0)),
            (WYM, jnp.where(lane == 0, kap_h[4][:, 2 * i : 2 * i + 1], 0.0)),
            (WYP, jnp.where(lane == Y - 1, kap_h[4][:, 2 * i + 1 : 2 * i + 2], 0.0)),
        )
        for k, end in ends:
            cst_ref[k, a] = cst0_ref[k, a] + end
        more.append((ends[0][1] + ends[1][1]) + (ends[2][1] + ends[3][1]))
        cst_ref[BASE, a] = cst0_ref[BASE, a] + more[a]
        cst_ref[KAP, a] = cst0_ref[KAP, a]
        cst_ref[BETA, a] = cst0_ref[BETA, a]
    brick = Brick(p, cst_ref, kap_h[0], kap_h[1])
    for a in range(X // 4):
        for k, i in enumerate((4 * a, 4 * a + 1, 4 * a + 3)):
            cst_ref[DAMP + k, a] = DAMPING / brick.diagonal(i)

    def residual(i):
        added = more[i // 4]
        if i == 0:
            added = added + kap_h[0]
        if i == X - 1:
            added = added + kap_h[1]
        return r_ref[i] - added * u_ref[i] + brick.from_halo(i, halo)

    return brick, residual


def first_kernel(p, coef, u_ref, r_ref, cls_ref, cst0_ref, xa, xb, za, zb, ya, yb, rxz, ry, sy,
                 go_ref, s_ref, z1b_ref, uhb_ref, clsb_ref, cst_ref, r_scr, z_scr, z2_scr, go_scr):
    brick, residual = neighbours_in(p, coef, u_ref, r_ref, cst0_ref, xa, xb, za, zb, ya, yb, uhb_ref, clsb_ref, cst_ref)
    cls = lambda i: cls_ref[i // 4]
    start_cycle(p, brick, lambda i: u_ref[i], residual, (cls, col_faces(cls, p)), rxz, ry, sy,
                s_ref, z1b_ref, go_ref, r_scr, z_scr, z2_scr, go_scr)


def owner_kernel(p, coef, in_ref, wz, wx, wxt, wzi, lamxz, lamy, out_ref, in_scr, out_scr):
    n, m, nx, ny, nz = p.n, p.modes, p.nx, p.ny, p.nz
    me = (lax.axis_index("bx") * ny + lax.axis_index("by")) * nz + lax.axis_index("bz")
    in_scr[...] = in_ref[...].astype(F32)
    rows = []
    for bx in range(nx):
        lanes = []
        for bz in range(nz):
            total = None
            for by in range(ny):
                at = ((bx * ny + by) * nz + bz) * p.go
                piece = in_scr[at : at + m, :]
                total = piece if total is None else total + piece
            lanes.append(total)
        rows.append(jnp.concatenate(lanes, axis=1))
    data = jnp.concatenate(rows, axis=0)
    data = dot_wide_right(wz[...], data, ((1,), (1,)))
    data = jnp.concatenate([data[x * p.NZ : (x + 1) * p.NZ] for x in range(p.cx)], axis=1)
    data = dot_wide_left(data, wx[...])
    classes = coef.shape[1]
    kap_mean = sum(coef[0, k] for k in range(classes)) * (1.0 / classes)
    sig_mean = sum(coef[1, k] for k in range(classes)) * (1.0 / classes)
    data = data / (kap_mean * (lamxz[...] + lamy[me]) + sig_mean)
    data = dot_wide_left(data, wxt[...])
    width = nx * m
    data = jnp.concatenate([data[:, x * width : (x + 1) * width] for x in range(p.cx)], axis=0)
    high, low = halves(data)
    high, low = high.T, low.T
    lane = iota((m, p.Y), 1)
    for bz in range(nz):
        back = dot(high, wzi[bz]) + dot(low, wzi[bz])
        core = lambda bx: back[bx * m : (bx + 1) * m, : p.lanes]
        for bx in range(nx):
            ends = roll(back[bx * m : (bx + 1) * m, p.lanes :], 2 * p.cz, 1)
            below = roll(core(bx - 1), p.cz - p.lanes, 1) if bx else jnp.zeros((m, p.lanes), F32)
            above = roll(core(bx + 1), p.cz, 1) if bx + 1 < nx else jnp.zeros((m, p.lanes), F32)
            extra = jnp.where(lane < p.cz, below, jnp.where(lane < 2 * p.cz, above, ends))
            mine = core(bx)
            for by in range(ny):
                at = ((bx * ny + by) * nz + bz) * p.back
                out_scr[at : at + m, :] = mine
                out_scr[at + m : at + 2 * m, :] = extra

    device = iota((n, p.Y), 0)
    at_x, at_y, at_z = device // (ny * nz), (device // nz) % ny, device % nz

    def shift(value, dx, dy, dz):
        value = roll(value, -((dx * ny + dy) * nz + dz), 0)
        for at, step, count in ((at_x, dx, nx), (at_y, dy, ny), (at_z, dz, nz)):
            if step:
                value = jnp.where((at + step >= 0) & (at + step < count), value, 0.0)
        return value

    def take(k):
        return in_scr[pl.ds(p.go_halo + k, n, stride=p.go), :]

    def give(k, value):
        out_scr[pl.ds(p.back_halo + k, n, stride=p.back), :] = value

    for to, source, step in ((0, 1, (-1, 0, 0)), (1, 0, (1, 0, 0)), (2, 3, (0, 0, -1)), (3, 2, (0, 0, 1))):
        for k in range(p.heights[to]):
            give(p.offsets[to] + k, shift(take(p.offsets[source] + k), *step))
    lane = iota((n, p.Y), 1)
    even = lane % 2 == 0
    first, X2 = p.edge_lane, 2 * p.X
    for k in range(p.heights[4]):
        sides = take(p.offsets[4] + k)
        moved = jnp.where(lane < first + 2, roll(sides, first, 1), roll(sides, first + 2 - (X2 - 2), 1))
        moved = jnp.where(lane < first + 4, moved, roll(sides, first + 4 - 2 * X2, 1))
        moved = jnp.where(lane < first + 6, moved, roll(sides, first + 6 - (3 * X2 - 2), 1))
        which = (lane - first) % 4
        corner = jnp.where(
            which < 2,
            jnp.where(even, shift(moved, 1, -1, 0), shift(moved, 1, 1, 0)),
            jnp.where(even, shift(moved, -1, -1, 0), shift(moved, -1, 1, 0)),
        )
        plain = jnp.where(even, shift(sides, 0, -1, 0), shift(sides, 0, 1, 0))
        give(p.offsets[4] + k, jnp.where(lane < first, plain, jnp.where(lane < first + 8, corner, 0.0)))
    edges = take(p.offsets[5])
    kind = me % 6
    moved = jnp.where(even, shift(edges, 0, -1, -1), shift(edges, 0, 1, -1))
    for k, value in (
        (0, lambda: shift(edges, 1, 0, 1)),
        (1, lambda: shift(edges, 1, 0, -1)),
        (2, lambda: shift(edges, -1, 0, 1)),
        (3, lambda: shift(edges, -1, 0, -1)),
        (4, lambda: jnp.where(even, shift(edges, 0, -1, 1), shift(edges, 0, 1, 1))),
    ):
        moved = jnp.where(kind == k, value(), moved)
    give(p.offsets[5], moved)
    used = p.back_halo + sum(p.heights)
    for k in range(used, p.back):
        out_scr[pl.ds(k, n, stride=p.back), :] = jnp.zeros((n, p.Y), F32)
    out_ref[...] = out_scr[...].astype(BF16)


class Arrived:
    def __init__(self, p, ref):
        X, Z = p.X, p.Z
        rows = (2 * Z, 2 * Z, 2 * X, 2 * X, Z, 12)
        xm, xp, zm, zp, sides, edges = (
            get_rows(ref, p.back, p.back_halo + offset, p.n, count) for offset, count in zip(p.offsets, rows)
        )
        self.p, self.ref, self.sides, self.edges = p, ref, sides, edges
        self.z1 = (xm[:Z], xp[:Z], zm[:X], zp[:X], sides)
        self.z2 = (xm[Z:], xp[Z:], zm[X:], zp[X:], roll(sides, -2 * X, 1))

    def xz(self, kind, sx, sz):
        k = 6 * kind + (0 if sx else 2) + (0 if sz else 1)
        return self.edges[k : k + 1]

    def zy(self, kind, sz):
        k = 6 * kind + (4 if sz else 5)
        return self.edges[k : k + 1]

    def xy(self, kind, sx, sy):
        lane = self.p.edge_lane + 4 * kind + (0 if sx else 2) + sy
        return self.sides[:, lane : lane + 1]

    def xy_lanes(self, kind, plain):
        first, X2 = self.p.edge_lane + 4 * kind, 2 * self.p.X
        lane = iota(plain.shape, 1)
        value = jnp.where(lane < X2, plain, roll(self.sides, X2 - first, 1))
        return jnp.where(lane >= self.p.Y - 2, roll(self.sides, self.p.Y - 2 - first - 2, 1), value)


def coarse_rows(p, ref, sy, pyt, pall, pyh):
    n, m = p.n, p.modes
    core = jnp.concatenate([ref[j * p.back : j * p.back + m, :] for j in range(n)], axis=0)
    extra = jnp.concatenate([ref[j * p.back + m : j * p.back + 2 * m, :] for j in range(n)], axis=0)
    modes = jnp.concatenate([core, extra], axis=1).astype(BF16)
    rows = sy[pl.ds(pl.multiple_of(lax.axis_index("by") * p.cy, 8), p.cy + 16), :]
    values = dot(rows, modes).astype(BF16)
    along = dot(values[8 : 8 + p.cy].T, pyt[...])
    count = pall.shape[0] - p.Z
    nodes = dot_wide_right(pall[:count], along) * (1.0 / 27.0)
    weights = pall[count:, : p.lanes].astype(F32)
    ends = [weights * values.astype(F32)[k : k + 1, : p.lanes] for k in (7, 8 + p.cy)]
    side = dot_wide_left(jnp.concatenate(ends, axis=1), pyh[...]) * (1.0 / 27.0)
    return nodes, side


def column(row, count, side):
    shape = (count, row.shape[1])
    pick = iota(shape, 1) == 2 * iota(shape, 0) + side
    return jnp.sum(jnp.where(pick, row, 0.0), axis=1, keepdims=True)


def finish_cycle(p, coef, brick, now, first, s_ref, z1b_ref, uhb_ref, clsb_ref, nodes, side, u_ref):
    X, Z, b = p.X, p.Z, Bounds(p)
    for i in range(X):
        u_ref[i] = s_ref[i] + brick.damp(i) * brick.from_halo(i, now.z1) + nodes[i * Z : (i + 1) * Z]
    old, cls, own = read_bounds(uhb_ref, b), read_bounds(clsb_ref, b), read_bounds(z1b_ref, b)
    kap = lambda value: lookup(value, coef, 0)
    halo = []

    def new(k, weights, toward, others, correction):
        kap_here = kap(cls[k])
        diagonal = lookup(cls[k], coef, 1) + (kap_here + toward) + ((weights[0] + weights[1]) + (weights[2] + weights[3]))
        total = toward * own_faces[k]
        for part in others:
            total = total + part
        value = old[k] + now.z2[k] + (DAMPING / diagonal) * total + correction
        halo.append(jnp.where(cls[k] > 0.5, value, 0.0))

    own_faces = list(own[:4]) + [swap_lanes(own[4])]
    at = X * Z
    for k in range(2):
        kap_here = kap(cls[k])
        row_m, row_p = kap(first.xz(1, k, 0)), kap(first.xz(1, k, 1))
        col_m, col_p = kap(first.xy(1, k, 0)), kap(first.xy(1, k, 1))
        w = plane_weights(kap_here, row_m, row_p, col_m, col_p)
        row, lane = iota((Z, p.Y), 0), iota((Z, p.Y), 1)
        others = (
            jnp.where(row == 0, w[0] * now.xz(0, k, 0), 0.0),
            jnp.where(row == Z - 1, w[1] * now.xz(0, k, 1), 0.0),
            jnp.where(lane == 0, w[2] * now.xy(0, k, 0), 0.0),
            jnp.where(lane == p.Y - 1, w[3] * now.xy(0, k, 1), 0.0),
        )
        toward = kap_here + brick.of(KAP, 0 if k == 0 else X - 1)
        new(k, w, toward, others, nodes[at : at + Z])
        at += Z
    for k in range(2):
        kap_here = kap(cls[2 + k])
        row_m, row_p = kap(first.xz(1, 0, k)), kap(first.xz(1, 1, k))
        col_m, col_p = (kap(column(first.zy(1, k), X, side_y)) for side_y in range(2))
        w = plane_weights(kap_here, row_m, row_p, col_m, col_p)
        row, lane = iota((X, p.Y), 0), iota((X, p.Y), 1)
        others = (
            jnp.where(row == 0, w[0] * now.xz(0, 0, k), 0.0),
            jnp.where(row == X - 1, w[1] * now.xz(0, 1, k), 0.0),
            jnp.where(lane == 0, w[2] * column(now.zy(0, k), X, 0), 0.0),
            jnp.where(lane == p.Y - 1, w[3] * column(now.zy(0, k), X, 1), 0.0),
        )
        z = 0 if k == 0 else Z - 1
        mine = jnp.concatenate([brick.of(KAP, i)[z : z + 1] for i in range(X)], axis=0)
        new(2 + k, w, kap_here + mine, others, nodes[at : at + X])
        at += X
    wide = kap(first.xy_lanes(1, cls[4]))
    z1_wide = now.xy_lanes(0, now.z1[4])
    row_m, row_p = kap(first.zy(1, 0)), kap(first.zy(1, 1))
    up, down = shifted(wide, 0, row_m, row_p)
    left, right = roll(wide, 2, 1), roll(wide, -2, 1)
    row, lane = iota((Z, p.Y), 0), iota((Z, p.Y), 1)
    w = (
        jnp.where(row % 4 == 0, wide + up, wide),
        jnp.where(row % 4 == 3, wide + down, wide),
        jnp.where((lane // 2) % 4 == 0, wide + left, wide),
        jnp.where((lane // 2) % 4 == 3, wide + right, wide),
    )
    others = (
        jnp.where(row == 0, w[0] * now.zy(0, 0), 0.0),
        jnp.where(row == Z - 1, w[1] * now.zy(0, 1), 0.0),
        jnp.where(lane // 2 == 0, w[2] * roll(z1_wide, 2, 1), 0.0),
        jnp.where(lane // 2 == X - 1, w[3] * roll(z1_wide, -2, 1), 0.0),
    )
    mine = swap_lanes(col_faces(lambda i: brick.of(KAP, i), p))
    new(4, w, wide + mine, others, side)
    return tuple(halo)


def middle_kernel(p, coef, in_ref, f_ref, s_ref, z1b_ref, uhb_ref, clsb_ref, cst_ref,
                  sy, pyt, pall, pyh, rxz, ry,
                  go_ref, s_out, z1b_out, uhb_out, in_scr, u_scr, r_scr, z_scr, z2_scr, go_scr):
    in_scr[...] = in_ref[...].astype(F32)
    b = Bounds(p)
    outside = read_bounds(clsb_ref, b)
    brick = Brick(p, cst_ref, lookup(outside[0], coef, 0), lookup(outside[1], coef, 0))
    now = Arrived(p, in_scr)
    nodes, side = coarse_rows(p, in_scr, sy, pyt, pall, pyh)
    halo = finish_cycle(p, coef, brick, now, now, s_ref, z1b_ref, uhb_ref, clsb_ref, nodes, side, u_scr)
    write_bounds(uhb_out, b, halo)
    get = lambda i: u_scr[i]
    residual = lambda i: residual_plane(brick, i, get, halo, f_ref[i])
    start_cycle(p, brick, get, residual, None, rxz, ry, sy,
                s_out, z1b_out, go_ref, r_scr, z_scr, z2_scr, go_scr)


def last_kernel(p, coef, in_ref, first_ref, f_ref, s_ref, z1b_ref, uhb_ref, clsb_ref, cst_ref,
                sy, pyt, pall, pyh, u_out, r_out, in_scr, first_scr):
    in_scr[...] = in_ref[...].astype(F32)
    first_scr[...] = first_ref[...].astype(F32)
    outside = read_bounds(clsb_ref, Bounds(p))
    brick = Brick(p, cst_ref, lookup(outside[0], coef, 0), lookup(outside[1], coef, 0))
    now, first = Arrived(p, in_scr), Arrived(p, first_scr)
    nodes, side = coarse_rows(p, in_scr, sy, pyt, pall, pyh)
    halo = finish_cycle(p, coef, brick, now, first, s_ref, z1b_ref, uhb_ref, clsb_ref, nodes, side, u_out)
    for i in range(p.X):
        r_out[i] = residual_plane(brick, i, lambda k: u_out[k], halo, f_ref[i])


class Sends:
    def __init__(self, p):
        X, Z = p.X, p.Z
        self.first = p.cy + Z // 2
        self.x_face, self.z_face = p.NY, p.NY
        self.x_rows = p.NY + 2 * Z + Z // 2
        self.z_rows = p.NY + 2 * X + 16
        self.xz_rows = p.NY + 16
        self.second = 2 * p.cx * p.NZ * p.NY // p.Y
        self.corner = self.second + 2 * Z + Z // 2
        self.last = self.corner + 16
        self.faces = 4 * Z + 4 * X


def pick(condition, a, b):
    return jnp.where(condition, a, b)


def fold(value):
    count, lanes = value.shape
    low, high = value[: count // 2], value[count // 2 :]
    return jnp.where(iota(low.shape, 1) < lanes // 2, low, roll(high, lanes // 2, 1)).astype(BF16)


def unfold(value):
    value = value.astype(F32)
    return jnp.concatenate([value, roll(value, value.shape[1] // 2, 1)], axis=0)


def send_first(p, coarse, z_scr, z2_scr, z1b_ref, a_ref, faces_ref):
    X, Z = p.X, p.Z
    z1, z2 = (lambda i: z_scr[i]), (lambda i: z2_scr[i])
    z1_y, z2_y = col_faces(z1, p), col_faces(z2, p)
    z_rows = (z_scr[:, 0, :], z_scr[:, Z - 1, :], z2_scr[:, 0, :], z2_scr[:, Z - 1, :])
    write_bounds(z1b_ref, Bounds(p), (z1(0), z1(X - 1), z_rows[0], z_rows[1], z1_y))
    a_ref[0 : p.cy, :] = coarse
    lane = iota((Z, p.Y), 1)
    a_ref[p.cy :, :] = fold(jnp.where(lane < 2 * X, z1_y, roll(z2_y, 2 * X, 1)))
    for k, plane in enumerate((z1(0), z1(X - 1), z2(0), z2(X - 1))):
        faces_ref[k * Z : (k + 1) * Z, :] = plane.astype(BF16)
    for k, rows in enumerate(z_rows):
        faces_ref[4 * Z + k * X : 4 * Z + (k + 1) * X, :] = rows.astype(BF16)


def face_x(p, faces_ref, high):
    X, Z = p.X, p.Z
    return tuple(pick(high, faces_ref[(k + 1) * Z : (k + 2) * Z, :], faces_ref[k * Z : (k + 1) * Z, :]) for k in (0, 2))


def face_z(p, faces_ref, high):
    X, at = p.X, 4 * p.Z
    return tuple(
        pick(high, faces_ref[at + (k + 1) * X : at + (k + 2) * X, :], faces_ref[at + k * X : at + (k + 1) * X, :]) for k in (0, 2)
    )


def pad_rows(rows, count):
    rows = [row.astype(F32) for row in rows]
    return jnp.concatenate(rows + [jnp.zeros((count - len(rows), rows[0].shape[1]), F32)], axis=0).astype(BF16)


def y_block(p, sides, cls_y):
    lane = iota(sides.shape, 1)
    return jnp.where(lane < 2 * p.X, sides, roll(cls_y, 2 * p.X, 1))


def distances(count):
    return tuple(range(1, count))


def after_first(p, *refs):
    ny = p.ny
    buffers, (faces_ref, clsb_ref, cls_ref, sy, x_ref, z_ref, xz_ref, sides_ref, all_scr) = refs[:ny], refs[ny:]
    X, Z, sends, b = p.X, p.Z, Sends(p), Bounds(p)
    bx, by, bz = (lax.axis_index(axis) for axis in AXES)
    low = high = jnp.zeros((Z, p.Y), F32)
    for d, buffer in zip((0,) + distances(ny), buffers):
        other = by ^ d
        all_scr[pl.ds(pl.multiple_of(other * p.cy, 16), p.cy), :] = buffer[0 : p.cy, :]
        if d and d & (d + 1) == 0:
            value = unfold(buffer[p.cy :, :])
            low = pick(other == by - 1, value, low)
            high = pick(other == by + 1, value, high)
    sides = jnp.where(iota((Z, p.Y), 1) % 2 == 0, low, high)
    sides_ref[...] = sides
    modes = dot(sy[8 : 8 + p.NY, :], all_scr[...]).astype(BF16)
    cls_y = read(clsb_ref, b.uy)
    odd, up = bx % 2 == 1, bz == 0
    for ref in (x_ref, z_ref, xz_ref):
        ref[0 : p.NY, :] = modes
    at = p.NY
    z1, z2 = face_x(p, faces_ref, odd)
    x_ref[at : at + Z, :] = z1
    x_ref[at + Z : at + 2 * Z, :] = z2
    x_ref[at + 2 * Z :, :] = fold(y_block(p, sides, cls_y))
    z1, z2 = face_z(p, faces_ref, up)
    z_ref[at : at + X, :] = z1
    z_ref[at + X : at + 2 * X, :] = z2
    z_ref[at + 2 * X : at + 2 * X + 16, :] = pad_rows(
        [pick(up, value[Z - 1 : Z], value[0:1]) for value in (sides, cls_y)], 16
    )
    z1 = z1.astype(F32)
    cls = pick(odd, cls_ref[X // 4 - 1], cls_ref[0])
    xz_ref[at : at + 16, :] = pad_rows(
        [pick(odd, z1[X - 1 : X], z1[0:1]), pick(up, cls[Z - 1 : Z], cls[0:1])], 16
    )


def after_second(p, own_ref, x_in, z_in, xz_in, faces_ref, clsb_ref, sides_ref, wzt, out_ref):
    X, Z, Y, sends, b = p.X, p.Z, p.Y, Sends(p), Bounds(p)
    bx, bz = lax.axis_index("bx"), lax.axis_index("bz")
    odd, up = bx % 2 == 1, bz == 0
    at = 0
    for one, two in ((own_ref, z_in), (x_in, xz_in)):
        one, two = one[0 : p.NY, :], two[0 : p.NY, :]
        data = jnp.concatenate([pick(up, one, two), pick(up, two, one)], axis=1)
        data = dot(wzt[...], data, ((1,), (1,))).astype(BF16)
        for k in range(p.NY // Y):
            rows = data.shape[0]
            out_ref[at : at + rows, :] = data[:, k * Y : (k + 1) * Y]
            at += rows
    z1, z2 = face_x(p, faces_ref, jnp.logical_not(odd))
    out_ref[at : at + Z, :] = z1
    out_ref[at + Z : at + 2 * Z, :] = z2
    out_ref[at + 2 * Z : sends.corner, :] = fold(y_block(p, sides_ref[...], read(clsb_ref, b.uy)))
    beyond = z_in[p.NY : p.NY + X, :].astype(F32)
    classes = pick(up, read(clsb_ref, b.uzp), read(clsb_ref, b.uzm))
    out_ref[sends.corner :, :] = pad_rows(
        [pick(odd, value[0:1], value[X - 1 : X]) for value in (beyond, classes)], 16
    )


class Beyond:
    def __init__(self, p):
        X, Z = p.X, p.Z
        self.cross = 0
        self.core = Z
        self.z = 6 * Z
        self.y = 6 * Z + 4 * X
        self.kap = 10 * Z + 4 * X
        self.count = self.kap + Bounds(p).count


def rows_at(ref, at, count):
    return ref[at : at + count, :]


def beyond_kernel(p, coef, s_ref, z1b_ref, uhb_ref, clsb_ref, cls_ref, cst_ref, sides_ref, x_in, z_in, xz_in, s_out, out_ref):
    X, Z, Y, b, to = p.X, p.Z, p.Y, Bounds(p), Beyond(p)
    bx, bz = lax.axis_index("bx"), lax.axis_index("bz")
    odd, up = bx % 2 == 1, bz == 0
    some = (bx > 0) & (bx < p.nx - 1)
    kaps, sigs = lookup(clsb_ref[...], coef, 0), lookup(clsb_ref[...], coef, 1)
    out_ref[to.kap :, :] = kaps
    part = lambda value, span: value[span[0] : span[0] + span[1]]
    x_part = lambda value, high: pick(high, part(value, b.uxp), part(value, b.uxm))
    z_part = lambda value: pick(up, part(value, b.uzp), part(value, b.uzm))
    z1b, uhb = z1b_ref[...], uhb_ref[...]
    across = lambda at, count: pick(some, x_in[p.NY + at : p.NY + at + count, :].astype(F32), 0.0)
    x_z1, x_z2, block = across(0, Z), across(Z, Z), unfold(across(2 * Z, Z // 2))
    corner = pick(some, xz_in[p.NY : p.NY + 16, :].astype(F32), 0.0)
    corner_z1, corner_kap = corner[0:1], lookup(corner[1:2], coef, 0)
    z_z1, z_z2 = (z_in[p.NY + k * X : p.NY + (k + 1) * X, :].astype(F32) for k in range(2))
    z_rows = z_in[p.NY + 2 * X : p.NY + 2 * X + 16, :].astype(F32)
    zy_z1, zy_kap = z_rows[0:1], lookup(z_rows[1:2], coef, 0)
    block_kap = lookup(block, coef, 0)
    sides = sides_ref[...]
    brick = Brick(p, cst_ref, part(kaps, b.uxm), part(kaps, b.uxp))
    halo = (pick(odd, 0.0, x_z1), pick(odd, x_z1, 0.0), pick(up, 0.0, z_z1), pick(up, z_z1, 0.0), sides)
    for i in range(X):
        s_out[i] = s_ref[i] + brick.damp(i) * brick.from_halo(i, halo)
    row, lane = iota((Z, Y), 0), iota((Z, Y), 1)
    face = lambda high: pick(high, brick.of(KAP, X - 1), brick.of(KAP, 0))

    k, sigma = x_part(kaps, odd), x_part(sigs, odd)
    toward = k + face(odd)
    X2 = 2 * X
    ends = lambda value, first: [pick(odd, value[:, first + c : first + c + 1], value[:, first + X2 - 2 + c : first + X2 - 1 + c]) for c in (0, 1)]
    col_kap, col_z1 = ends(block_kap, X2), ends(block, 0)
    w = plane_weights(k, pick(up, 0.0, corner_kap), pick(up, corner_kap, 0.0), col_kap[0], col_kap[1])
    total = toward * x_part(z1b, odd)
    total = total + jnp.where(row == pick(up, Z - 1, 0), pick(up, w[1], w[0]) * corner_z1, 0.0)
    total = total + jnp.where(lane == 0, w[2] * col_z1[0], 0.0) + jnp.where(lane == Y - 1, w[3] * col_z1[1], 0.0)
    diagonal = sigma + (k + toward) + ((w[0] + w[1]) + (w[2] + w[3]))
    value = x_part(uhb, odd) + x_z2 + (DAMPING / diagonal) * total
    out_ref[to.cross : to.cross + Z, :] = jnp.where(k > 0.0, value, 0.0)

    other = jnp.logical_not(odd)
    k, sigma = x_part(kaps, other), x_part(sigs, other)
    toward = k + face(other)
    for j, value in enumerate((k, toward, sigma + (k + toward), x_part(z1b, other), x_part(uhb, other))):
        out_ref[to.core + j * Z : to.core + (j + 1) * Z, :] = value

    k, sigma = z_part(kaps), z_part(sigs)
    own = jnp.concatenate([pick(up, cst_ref[KAP, i // 4, Z - 1 : Z, :], cst_ref[KAP, i // 4, 0:1, :]) for i in range(X)], axis=0)
    toward = k + own
    col_kap, col_z1 = ([column(value, X, c) for c in (0, 1)] for value in (zy_kap, zy_z1))
    w = plane_weights(k, pick(odd, 0.0, corner_kap), pick(odd, corner_kap, 0.0), col_kap[0], col_kap[1])
    zrow, zlane = iota((X, Y), 0), iota((X, Y), 1)
    total = toward * z_part(z1b)
    total = total + jnp.where(zrow == pick(odd, X - 1, 0), pick(odd, w[1], w[0]) * corner_z1, 0.0)
    total = total + jnp.where(zlane == 0, w[2] * col_z1[0], 0.0) + jnp.where(zlane == Y - 1, w[3] * col_z1[1], 0.0)
    diagonal = sigma + (k + toward) + ((w[0] + w[1]) + (w[2] + w[3]))
    for j, value in enumerate((z_part(uhb) + z_z2, total, diagonal, k)):
        out_ref[to.z + j * X : to.z + (j + 1) * X, :] = value

    k, sigma = part(kaps, b.uy), part(sigs, b.uy)
    toward = k + swap_lanes(col_faces(lambda i: brick.of(KAP, i), p))
    reach = lambda value, shift: pick(odd, roll(value, X2 + shift, 1), roll(value, Y - X2 + shift, 1))
    begin = pick(odd, X2, Y - 2)
    far = (lane >= begin) & (lane < begin + 2)
    wide = jnp.where(far, reach(block_kap, -X2), jnp.where(lane < X2, k, 0.0))
    wide_z1 = jnp.where(far, reach(block, 0), 0.0)
    above, below = shifted(wide, 0, pick(up, 0.0, zy_kap), pick(up, zy_kap, 0.0))
    left, right = roll(wide, 2, 1), roll(wide, -2, 1)
    place = lane // 2
    w = (
        jnp.where(row % 4 == 0, wide + above, wide),
        jnp.where(row % 4 == 3, wide + below, wide),
        jnp.where(place % 4 == 0, wide + left, wide),
        jnp.where(place % 4 == 3, wide + right, wide),
    )
    total = toward * swap_lanes(part(z1b, b.uy))
    total = total + jnp.where(row == pick(up, Z - 1, 0), pick(up, w[1], w[0]) * zy_z1, 0.0)
    total = total + jnp.where(place == 0, w[2] * roll(wide_z1, 2, 1), 0.0)
    total = total + jnp.where(place == X - 1, w[3] * roll(wide_z1, -2, 1), 0.0)
    diagonal = sigma + (k + toward) + ((w[0] + w[1]) + (w[2] + w[3]))
    for j, value in enumerate((part(uhb, b.uy) + roll(sides, -X2, 1), total, diagonal, k)):
        out_ref[to.y + j * Z : to.y + (j + 1) * Z, :] = value


def last_halo(p, coef, beyond_ref, last_in):
    X, Z, Y, to = p.X, p.Z, p.Y, Beyond(p)
    bx, bz = lax.axis_index("bx"), lax.axis_index("bz")
    odd, up = bx % 2 == 1, bz == 0
    start, end, X2 = Sends(p).second, Sends(p).corner, 2 * X
    z1, z2 = (last_in[start + k * Z : start + (k + 1) * Z, :].astype(F32) for k in range(2))
    block = unfold(last_in[start + 2 * Z : end, :])
    corner = last_in[end : end + 16, :].astype(F32)
    corner_z1, corner_kap = corner[0:1], lookup(corner[1:2], coef, 0)
    block_kap = lookup(block, coef, 0)
    row, lane = iota((Z, Y), 0), iota((Z, Y), 1)

    k, toward, diagonal, own, old = (rows_at(beyond_ref, to.core + j * Z, Z) for j in range(5))
    ends = lambda value, first: [pick(odd, value[:, first + X2 - 2 + c : first + X2 - 1 + c], value[:, first + c : first + c + 1]) for c in (0, 1)]
    col_kap, col_z1 = ends(block_kap, X2), ends(block, 0)
    w = plane_weights(k, pick(up, 0.0, corner_kap), pick(up, corner_kap, 0.0), col_kap[0], col_kap[1])
    total = toward * own
    total = total + jnp.where(row == pick(up, Z - 1, 0), pick(up, w[1], w[0]) * corner_z1, 0.0)
    total = total + jnp.where(lane == 0, w[2] * col_z1[0], 0.0) + jnp.where(lane == Y - 1, w[3] * col_z1[1], 0.0)
    diagonal = diagonal + ((w[0] + w[1]) + (w[2] + w[3]))
    core = (k, old + z2 + (DAMPING / diagonal) * total)
    value, total, diagonal, k = (rows_at(beyond_ref, to.z + j * X, X) for j in range(4))
    edge = iota((X, Y), 0) == pick(odd, 0, X - 1)
    total = total + jnp.where(edge, (k + corner_kap) * corner_z1, 0.0)
    diagonal = diagonal + jnp.where(edge, corner_kap, 0.0)
    z = (k, value + (DAMPING / diagonal) * total)

    value, total, diagonal, k = (rows_at(beyond_ref, to.y + j * Z, Z) for j in range(4))
    begin = pick(odd, 0, X2 - 2)
    edge = (lane >= begin) & (lane < begin + 2)
    reach = lambda value, shift: pick(odd, roll(value, 2 - X2 + shift, 1), roll(value, X2 - 2 + shift, 1))
    edge_kap = reach(block_kap, -X2)
    total = total + jnp.where(edge, (k + edge_kap) * reach(block, 0), 0.0)
    diagonal = diagonal + jnp.where(edge, edge_kap, 0.0)
    return z1, core, z, (k, value + (DAMPING / diagonal) * total)


def finish_staged(p, brick, s_ref, beyond_ref, parts, nodes, side, u_ref):
    X, Z, to = p.X, p.Z, Beyond(p)
    bx, bz = lax.axis_index("bx"), lax.axis_index("bz")
    odd, up = bx % 2 == 1, bz == 0
    some = (bx > 0) & (bx < p.nx - 1)
    z1, core, z, y = parts
    for i in range(X):
        value = s_ref[i] + nodes[i * Z : (i + 1) * Z]
        if i in (0, X - 1):
            weight = brick.x_weights(i)[0 if i == 0 else 1]
            here = odd if i == 0 else jnp.logical_not(odd)
            value = value + brick.damp(i) * (weight * pick(here, z1, 0.0))
        u_ref[i] = value
    at = X * Z
    below, above = nodes[at : at + Z], nodes[at + Z : at + 2 * Z]
    core = jnp.where(core[0] > 0.0, core[1] + pick(odd, below, above), 0.0)
    cross = pick(some, rows_at(beyond_ref, to.cross, Z) + pick(odd, above, below), 0.0)
    at += 2 * Z
    z = jnp.where(z[0] > 0.0, z[1] + pick(up, nodes[at + X : at + 2 * X], nodes[at : at + X]), 0.0)
    y = jnp.where(y[0] > 0.0, y[1] + side, 0.0)
    return pick(odd, core, cross), pick(odd, cross, core), pick(up, 0.0, z), pick(up, z, 0.0), y


def coarse_staged(p, own_ref, last_in, inverse, kx, kxi, zi, along_y, pall, pyh):
    Y, NY = p.Y, p.NY
    bx, bz = lax.axis_index("bx"), lax.axis_index("bz")
    rows, step, count = p.cx * p.NZ, p.cx * LOW, p.NX * LOW
    back = kxi[pl.ds(pl.multiple_of(bx * step, 16), step + 2 * LOW), :]
    table = kx[bx]
    parts = []
    for h in range(p.NZ // LOW):
        lines = []
        for ref in (own_ref, last_in):
            for block in range(2):
                at = [(block * (NY // Y) + k) * rows + h * step for k in range(NY // Y)]
                lines.append(jnp.concatenate([ref[i : i + step, :] for i in at], axis=1))
        parts.append(dot(table, jnp.concatenate(lines, axis=0)))
    parts = [(value * inverse[h * count : (h + 1) * count, :]).astype(BF16) for h, value in enumerate(parts)]
    values = dot(back, jnp.concatenate(parts, axis=1)).astype(BF16)
    values = jnp.concatenate([values[:, h * NY : (h + 1) * NY] for h in range(len(parts))], axis=0)
    values = dot(zi[bz], values).astype(BF16)
    values = dot(jnp.concatenate([values, values], axis=1), along_y[...])
    count = pall.shape[0] - p.Z
    nodes = dot_wide_right(pall[:count, : p.lanes + p.extra], values[:, :Y]) * (1.0 / 27.0)
    ends = values[: p.lanes, Y:]
    spread = ends[:, 0:1] * pyh[: p.lanes].astype(F32) + ends[:, 1:2] * pyh[p.lanes :].astype(F32)
    side = dot_wide_right(pall[count:, : p.lanes], spread) * (1.0 / 27.0)
    return nodes, side


def inverse_kernel(p, coef, lam_xz, lam_y, sy, pye, out_ref, along_ref):
    classes = coef.shape[1]
    kap_mean = sum(coef[0, k] for k in range(classes)) * (1.0 / classes)
    sig_mean = sum(coef[1, k] for k in range(classes)) * (1.0 / classes)
    step = p.NX * LOW
    for h in range(p.NZ // LOW):
        lam = lam_xz[h * step : (h + 1) * step, :] + lam_y[...]
        out_ref[h * step : (h + 1) * step, :] = 1.0 / (kap_mean * lam + sig_mean)
    rows = sy[pl.ds(pl.multiple_of(lax.axis_index("by") * p.cy, 16), p.cy + 16), :]
    high, low = halves(dot(rows.T, pye[...]))
    along_ref[: p.NY, :] = high
    along_ref[p.NY :, :] = low


def first_staged(p, coef, u_ref, r_ref, cls_ref, cst0_ref, xa, xb, za, zb, ya, yb, rxz, ry,
                 a_ref, faces_ref, s_ref, z1b_ref, uhb_ref, clsb_ref, cst_ref, r_scr, z_scr, z2_scr):
    brick, residual = neighbours_in(p, coef, u_ref, r_ref, cst0_ref, xa, xb, za, zb, ya, yb, uhb_ref, clsb_ref, cst_ref)
    coarse = advance(p, brick, lambda i: u_ref[i], residual, rxz, ry, s_ref, r_scr, z_scr, z2_scr)
    send_first(p, coarse, z_scr, z2_scr, z1b_ref, a_ref, faces_ref)


def correct(p, coef, s_ref, beyond_ref, cst_ref, own, last_in, inverse, kx, kxi, zi, along_y, pall, pyh, u_ref):
    b, at = Bounds(p), Beyond(p).kap
    brick = Brick(p, cst_ref, rows_at(beyond_ref, at + b.uxm[0], p.Z), rows_at(beyond_ref, at + b.uxp[0], p.Z))
    parts = last_halo(p, coef, beyond_ref, last_in)
    nodes, side = coarse_staged(p, own, last_in, inverse, kx, kxi, zi, along_y, pall, pyh)
    return brick, finish_staged(p, brick, s_ref, beyond_ref, parts, nodes, side, u_ref)


def middle_staged(p, coef, f_ref, s_ref, beyond_ref, cst_ref, own, last_in, inverse, kx, kxi, zi, along_y, pall, pyh, rxz, ry,
                  a_ref, faces_ref, s_out, z1b_out, uhb_out, u_scr, r_scr, z_scr, z2_scr):
    brick, halo = correct(p, coef, s_ref, beyond_ref, cst_ref, own, last_in, inverse, kx, kxi, zi, along_y, pall, pyh, u_scr)
    write_bounds(uhb_out, Bounds(p), halo)
    get = lambda i: u_scr[i]
    residual = lambda i: residual_plane(brick, i, get, halo, f_ref[i])
    coarse = advance(p, brick, get, residual, rxz, ry, s_out, r_scr, z_scr, z2_scr)
    send_first(p, coarse, z_scr, z2_scr, z1b_out, a_ref, faces_ref)


def last_staged(p, coef, f_ref, s_ref, beyond_ref, cst_ref, own, last_in, inverse, kx, kxi, zi, along_y, pall, pyh,
                u_out, r_out, u_scr, r_scr, sems):
    brick, halo = correct(p, coef, s_ref, beyond_ref, cst_ref, own, last_in, inverse, kx, kxi, zi, along_y, pall, pyh, u_scr)
    copies = [pltpu.make_async_copy(u_scr, u_out, sems.at[0])]
    copies[0].start()
    chunk = p.X // 4
    for k in range(4):
        for i in range(k * chunk, (k + 1) * chunk):
            r_scr[i] = residual_plane(brick, i, lambda j: u_scr[j], halo, f_ref[i])
        part = pl.ds(k * chunk, chunk)
        copies.append(pltpu.make_async_copy(r_scr.at[part], r_out.at[part], sems.at[k + 1]))
        copies[-1].start()
    for copy in copies:
        copy.wait()


def call(kernel, p, name, coef, inputs, outputs, scratch, us=2, out_space=pltpu.VMEM):
    smem = [pl.BlockSpec(memory_space=pltpu.SMEM)] if coef is not None else []
    args = ([coef] if coef is not None else []) + list(inputs)
    return pl.pallas_call(
        functools.partial(kernel, p),
        out_shape=[jax.ShapeDtypeStruct(shape, dtype) for shape, dtype in outputs],
        in_specs=smem + [pl.BlockSpec(memory_space=pltpu.VMEM)] * len(inputs),
        out_specs=[pl.BlockSpec(memory_space=out_space)] * len(outputs),
        scratch_shapes=[pltpu.VMEM(shape, F32) if isinstance(shape, tuple) else shape for shape in scratch],
        compiler_params=pltpu.CompilerParams(vmem_limit_bytes=VMEM_LIMIT),
        cost_estimate=pl.CostEstimate(flops=0, bytes_accessed=us * 3_600_000, transcendentals=0),
        name=name,
    )(*args)


def swaps(axis, count, a, b, near=None):
    if count == 1:
        return a, b
    assert count % 2 == 0
    first = lax.ppermute(a, axis, [(i, i ^ 1) for i in range(count)])
    if count == 2:
        return first, first
    other = lambda i: (i + 1 if i % 2 else i - 1) % count
    if near is None:
        return first, lax.ppermute(b, axis, [(i, other(i)) for i in range(count)])
    name, size = near
    pairs = []
    for k in range(size):
        for i in range(count):
            to = (k ^ 1, i) if i in (0, count - 1) else (k, other(i))
            pairs.append((k * count + i, to[0] * count + to[1]))
    return first, lax.ppermute(b, (name, axis), pairs)


def body(forcing, start, element_class_index, class_coef):
    p = Plan(start.shape, *(lax.axis_size(axis) for axis in AXES))
    t = tables(p)
    X, Z, Y, n = p.X, p.Z, p.Y, p.n
    bounds = Bounds(p).count
    block, flat, cst = (X, Z, Y), (X * Z, Y), (DAMP, X // 4, Z, Y)
    (uy,) = call(sides_kernel, p, "start_sides", None, (start,), [((Z, Y), F32)], [], us=20)
    cls, xa, xb, za, zb, yf = call(
        pack_kernel, p, "pack_faces", None, (element_class_index, start, uy),
        [((X // 4, Z, Y), F32)] + [((2 * Z, Y), F32)] * 2 + [((2 * max(X, Z), Y), F32)] * 2 + [((2 * Z, Y), F32)], [], us=20,
    )
    xa, xb = swaps("bx", p.nx, xa, xb)
    za, zb = swaps("bz", p.nz, za, zb)
    ya, yb = swaps("by", p.ny, yf, yf, ("bx", p.nx) if p.nx % 2 == 0 else None)
    go_shape, back_shape = (n * p.go, Y), (n * p.back, Y)
    starting = [flat, block, block, go_shape]
    rxz, ry, sy = t["rxz"], t["ry"], t["sy"]
    cst0, r0 = call(prepare_kernel, p, "prepare", class_coef, (start, forcing, cls), [(cst, F32), (block, F32)], [], us=6)
    if p.staged:
        return staged_cycles(p, t, class_coef, forcing, cls, start, r0, cst0, (xa, xb, za, zb, ya, yb))
    go, s, z1b, uhb, clsb, coefs = call(
        first_kernel, p, "first_residual", class_coef,
        (start, r0, cls, cst0, xa, xb, za, zb, ya, yb, rxz, ry, sy),
        [(go_shape, BF16), (block, F32), ((bounds, Y), F32), ((bounds, Y), F32), ((bounds, Y), F32), ((QUANTITIES,) + cst[1:], F32)],
        starting,
    )
    prolong = (sy, t["pyt"], t["pall"], t["pyh"])
    first = None
    for cycle in range(CYCLES):
        came = lax.all_to_all(go, AXES, split_axis=0, concat_axis=0, tiled=True)
        (out,) = call(
            owner_kernel, p, "owned_modes", class_coef,
            (came, t["wz"], t["wx"], t["wxt"], t["wzi"], t["lamxz"], t["lamy"]),
            [(back_shape, BF16)], [go_shape, back_shape],
        )
        back = lax.all_to_all(out, AXES, split_axis=0, concat_axis=0, tiled=True)
        if cycle + 1 < CYCLES:
            assert first is None
            first = back
            go, s, z1b, uhb = call(
                middle_kernel, p, "next_residual", class_coef,
                (back, forcing, s, z1b, uhb, clsb, coefs) + prolong + (rxz, ry),
                [(go_shape, BF16), (block, F32), ((bounds, Y), F32), ((bounds, Y), F32)],
                [back_shape, block] + starting,
            )
        else:
            return tuple(call(
                last_kernel, p, "last_residual", class_coef,
                (back, first, forcing, s, z1b, uhb, clsb, coefs) + prolong,
                [(block, F32), (block, F32)], [back_shape, back_shape],
            ))


def staged_cycles(p, t, class_coef, forcing, cls, u0, r0, cst0, faces_in):
    X, Z, Y = p.X, p.Z, p.Y
    sends, bounds = Sends(p), (Bounds(p).count, Y)
    block, flat = (X, Z, Y), (X * Z, Y)
    out = [((sends.first, Y), BF16), ((sends.faces, Y), BF16), (block, F32), (bounds, F32), (bounds, F32)]
    scratch = [flat, block, block]
    inverse, along_y = call(
        inverse_kernel, p, "inverse_spectrum", class_coef, (t["lam_xz"], t["lam_y"], t["sy"], t["pye"]),
        [((p.NZ * p.NX, p.NY), F32), ((2 * p.NY, 2 * Y), BF16)], [],
    )
    a, faces, s, z1b, uhb, clsb, coefs = call(
        first_staged, p, "first_residual", class_coef, (u0, r0, cls, cst0) + faces_in + (t["rxz"], t["ry"]),
        out + [(bounds, F32), ((QUANTITIES,) + cst0.shape[1:], F32)], scratch,
    )
    pairs = lambda count, d: [(i, i ^ d) for i in range(count)]
    for cycle in range(CYCLES):
        came = [a] + [lax.ppermute(a, "by", pairs(p.ny, d)) for d in distances(p.ny)]
        x, z, xz, sides = call(
            after_first, p, "y_modes", None, (*came, faces, clsb, cls, t["sy"]),
            [((rows, Y), BF16) for rows in (sends.x_rows, sends.z_rows, sends.xz_rows)] + [((Z, Y), F32)],
            [pltpu.VMEM((p.NY, Y), BF16)],
        )
        plane, across = p.nx * p.nz, (p.nx - 1) * p.nz
        x_in = lax.ppermute(x, ("bx", "bz"), pairs(plane, across))
        z_in = lax.ppermute(z, ("bx", "bz"), pairs(plane, 1))
        xz_in = lax.ppermute(xz, ("bx", "bz"), pairs(plane, across + 1))
        if cycle == 0:
            x_in, inverse, along_y = lax.optimization_barrier((x_in, inverse, along_y))
            back = (inverse, t["kx"], t["kxi"], t["zi"], along_y, t["pall"], t["pyh"])
        (own,) = call(
            after_second, p, "z_modes", None, (x, x_in, z_in, xz_in, faces, clsb, sides, t["wzt"]),
            [((sends.last, Y), BF16)], [],
        )
        last_in = lax.ppermute(own, "bx", pairs(p.nx, 1))
        s, beyond = call(
            beyond_kernel, p, "beyond", class_coef, (s, z1b, uhb, clsb, cls, coefs, sides, x_in, z_in, xz_in),
            [(block, F32), ((Beyond(p).count, Y), F32)], [],
        )
        inputs = (forcing, s, beyond, coefs, own, last_in) + back
        if cycle + 1 < CYCLES:
            a, faces, s, z1b, uhb = call(
                middle_staged, p, "next_residual", class_coef, inputs + (t["rxz"], t["ry"]), out, [block] + scratch
            )
        else:
            return tuple(call(
                last_staged, p, "last_residual", class_coef, inputs, [(block, F32), (block, F32)],
                [block, block, pltpu.SemaphoreType.DMA((5,))], out_space=pl.ANY,
            ))


def solution(mesh):
    spec = P("bx", "bz", "by")
    return jax.shard_map(body, mesh=mesh, in_specs=(spec, spec, spec, P()), out_specs=(spec, spec), check_vma=False)
```

```python
import functools
import math

import jax
import jax.numpy as jnp
import numpy as np
from jax import lax
from jax.experimental import pallas as pl
from jax.experimental.pallas import tpu as pltpu
from jax.sharding import PartitionSpec as P

CYCLES = 2
DAMPING = 0.6666666666666666
F32 = jnp.float32
BF16 = jnp.bfloat16
AXES = ("bx", "by", "bz")
VMEM_LIMIT = 32 * 1024 * 1024


def up_to(value, multiple):
    return -(-value // multiple) * multiple


class Plan:
    def __init__(self, shape, nx, ny, nz):
        self.X, self.Z, self.Y = shape
        self.nx, self.ny, self.nz = nx, ny, nz
        self.n = nx * ny * nz
        self.cx, self.cz, self.cy = self.X // 2, self.Z // 2, self.Y // 2
        self.NX, self.NZ, self.NY = self.cx * nx, self.cz * nz, self.cy * ny
        self.modes = -(-self.NY // self.n)
        self.NYp = self.modes * self.n
        self.lanes = self.cx * self.cz
        rows = (2 * self.Z, 2 * self.Z, 2 * self.X, 2 * self.X, self.Z, 12)
        self.heights = [-(-r // self.n) for r in rows]
        self.offsets = [sum(self.heights[:i]) for i in range(6)]
        halo = sum(self.heights)
        self.go_halo = self.modes
        self.go = up_to(self.modes + halo, 8)
        self.back_halo = 2 * self.modes
        self.back = up_to(2 * self.modes + halo, 8)
        self.edge_lane = 6 * self.X
        self.extra = 2 * self.cz + 2 * self.cx
        self.staged = nx == 4 and nz == 2 and ny & (ny - 1) == 0 and self.NZ % LOW == 0 and 8 * self.X <= self.Y
        assert self.lanes <= self.Y and self.extra <= self.lanes and self.edge_lane + 8 <= self.Y
        assert self.heights[5] == 1


def sine_table(count):
    index_one = np.arange(1, count + 1, dtype=np.int32)
    product = (index_one[:, None] * index_one[None, :]).astype(np.float32)
    value = np.sin(product * np.float32(math.pi / (count + 1)))
    return (value * np.float32(math.sqrt(2.0 / (count + 1)))).astype(BF16).astype(np.float32)


def spectrum_values(count):
    return 2.0 - 2.0 * np.cos(np.arange(1, count + 1) * (math.pi / (count + 1)))


RESTRICT = np.array([[3, 2, 1, 0], [0, 1, 2, 3]], np.float32)
PROLONG = np.array([[3, 0], [2, 1], [1, 2], [0, 3]], np.float32)


LOW = 8


def staged_tables(p, sx, sz, py):
    high, eye = p.NZ // LOW, np.eye(LOW)
    out = {}
    wzt = np.zeros((high, p.cx, LOW, p.nz, p.cx, p.cz), np.float32)
    for x in range(p.cx):
        wzt[:, x, :, :, x, :] = sz.reshape(high, LOW, p.nz, p.cz)
    out["wzt"] = wzt.reshape(p.cx * p.NZ, p.nz * p.lanes)
    blocks = sx.reshape(p.NX, p.nx, p.cx)
    order = lambda b: [b, b ^ 3, b ^ 1, b ^ 2]
    out["kx"] = np.stack([np.kron(blocks[:, order(b)].reshape(p.NX, p.NX), eye) for b in range(p.nx)])
    sxp = np.zeros((p.NX + 2, p.NX), np.float32)
    sxp[1:-1] = sx
    out["kxi"] = np.kron(sxp, eye)
    szp = np.zeros((p.NZ + 2, p.NZ), np.float32)
    szp[1:-1] = sz
    zi = np.zeros((p.nz, p.lanes + p.extra, high, p.cx + 2, LOW), np.float32)
    for b in range(p.nz):
        mine = szp[b * p.cz + 1 : (b + 1) * p.cz + 1].reshape(p.cz, high, LOW)
        for x in range(p.cx):
            zi[b, x * p.cz : (x + 1) * p.cz, :, x + 1, :] = mine
            zi[b, p.lanes + 2 * p.cz + x, :, x + 1, :] = szp[b * p.cz].reshape(high, LOW)
            zi[b, p.lanes + 2 * p.cz + p.cx + x, :, x + 1, :] = szp[(b + 1) * p.cz + 1].reshape(high, LOW)
        zi[b, p.lanes : p.lanes + p.cz, :, 0, :] = mine
        zi[b, p.lanes + p.cz : p.lanes + 2 * p.cz, :, p.cx + 1, :] = mine
    out["zi"] = zi.reshape(p.nz, p.lanes + p.extra, -1)
    pye = np.zeros((p.cy + 16, 2 * p.Y), np.float32)
    pye[8 : 8 + p.cy, : p.Y] = py.T
    pye[7, p.Y] = pye[8 + p.cy, p.Y + 1] = 1
    out["pye"] = pye
    return out


def tables(p):
    rx = np.kron(np.eye(p.X // 4), RESTRICT)
    rz = np.kron(np.eye(p.Z // 4), RESTRICT)
    ry = np.kron(np.eye(p.Y // 4), RESTRICT)
    px = np.kron(np.eye(p.X // 4), PROLONG)
    pz = np.kron(np.eye(p.Z // 4), PROLONG)
    py = np.kron(np.eye(p.Y // 4), PROLONG)
    sx, sz, sy = sine_table(p.NX), sine_table(p.NZ), sine_table(p.NY)
    out = {}
    out["rxz"] = np.kron(rx, rz)
    out["ry"] = ry
    padded = np.zeros((p.NY + 16, p.NYp), np.float32)
    padded[8 : 8 + p.NY, : p.NY] = sy
    out["sy"] = padded
    wz = np.zeros((p.cx, p.NZ, p.nz, p.cx, p.cz), np.float32)
    for x in range(p.cx):
        wz[x, :, :, x, :] = sz.reshape(p.NZ, p.nz, p.cz)
    out["wz"] = wz.reshape(p.cx * p.NZ, p.nz * p.lanes)
    wx = np.einsum("bxk,mn->xbmkn", sx.reshape(p.nx, p.cx, p.NX), np.eye(p.modes))
    wx = wx.reshape(p.NX * p.modes, p.NX * p.modes)
    out["wx"], out["wxt"] = wx, wx.T
    szp = np.zeros((p.NZ, p.NZ + 2), np.float32)
    szp[:, 1:-1] = sz
    wzi = np.zeros((p.nz, p.cx, p.NZ, 2 * p.lanes), np.float32)
    for b in range(p.nz):
        for x in range(p.cx):
            wzi[b, x, :, x * p.cz : (x + 1) * p.cz] = sz[:, b * p.cz : (b + 1) * p.cz]
            wzi[b, x, :, p.lanes + x] = szp[:, b * p.cz]
            wzi[b, x, :, p.lanes + p.cx + x] = szp[:, (b + 1) * p.cz + 1]
    out["wzi"] = wzi.reshape(p.nz, p.cx * p.NZ, 2 * p.lanes)
    out["pyt"] = py.T
    pall = np.zeros((p.X * p.Z + 2 * p.Z + 2 * p.X, 2 * p.lanes), np.float32)
    at = p.X * p.Z
    pall[:at, : p.lanes] = np.kron(px, pz)
    col = p.lanes
    for _ in range(2):
        pall[at : at + p.Z, col : col + p.cz] = 3 * pz
        at, col = at + p.Z, col + p.cz
    for _ in range(2):
        pall[at : at + p.X, col : col + p.cx] = 3 * px
        at, col = at + p.X, col + p.cx
    out["pall"] = np.concatenate([pall, np.tile(pz, (1, 2 * p.cx))])
    pyh = np.zeros((2, p.lanes, p.Y), np.float32)
    spread = np.repeat(px.T, p.cz, axis=0)
    for side in range(2):
        pyh[side, :, side : 2 * p.X : 2] = 3 * spread
    out["pyh"] = pyh.reshape(2 * p.lanes, p.Y)
    if p.staged:
        out.update(staged_tables(p, sx, sz, py))
    out = {key: jnp.asarray(value.astype(BF16)) for key, value in out.items()}
    if p.staged:
        lam = spectrum_values(p.NX)[None, :, None] + spectrum_values(p.NZ).reshape(-1, 1, LOW)
        out["lam_xz"] = jnp.asarray(lam.reshape(-1, 1).astype(np.float32))
        out["lam_y"] = jnp.asarray(spectrum_values(p.NY).reshape(1, -1).astype(np.float32))
        return out
    lam = spectrum_values(p.NX)[None, :, None] + spectrum_values(p.NZ)[:, None, None]
    out["lamxz"] = jnp.asarray(np.broadcast_to(lam, (p.NZ, p.NX, p.modes)).reshape(p.NZ, -1).astype(np.float32))
    lamy = np.zeros(p.NYp)
    lamy[: p.NY] = spectrum_values(p.NY)
    lamy = np.broadcast_to(lamy.reshape(p.n, 1, 1, p.modes), (p.n, 1, p.NX, p.modes))
    out["lamy"] = jnp.asarray(lamy.reshape(p.n, 1, -1).astype(np.float32))
    return out


def iota(shape, dim):
    return lax.broadcasted_iota(jnp.int32, shape, dim)


def dot(a, b, dims=((1,), (0,))):
    return lax.dot_general(a, b, (dims, ((), ())), preferred_element_type=F32)


def halves(value):
    high = value.astype(BF16)
    return high, (value - high.astype(F32)).astype(BF16)


def dot_wide_right(table, value, dims=((1,), (0,))):
    axis = 1 - dims[1][0]
    count = value.shape[axis]
    both = dot(table, jnp.concatenate(halves(value), axis=axis), dims)
    return both[:, :count] + both[:, count:]


def dot_wide_left(value, table, dims=((1,), (0,))):
    high, low = halves(value)
    return dot(high, table, dims) + dot(low, table, dims)


def roll(value, shift, axis):
    size = value.shape[axis]
    shift = shift % size
    return value if shift == 0 else pltpu.roll(value, shift, axis)


def lookup(classes, coef_ref, row):
    total = jnp.zeros_like(classes)
    for k in range(coef_ref.shape[1]):
        total = jnp.where(classes == k + 1.0, coef_ref[row, k], total)
    return total


def col_faces(get, p):
    lane = iota((p.Z, p.Y), 1) // 2
    total = jnp.zeros((p.Z, p.Y), F32)
    for i in range(p.X):
        total = jnp.where(lane == i, roll(get(i), 2 * i + 1, 1), total)
    return total


def swap_lanes(value):
    even = iota(value.shape, 1) % 2 == 0
    return jnp.where(even, roll(value, -1, 1), roll(value, 1, 1))


def shifted(value, axis, before, after):
    size = value.shape[axis]
    at = iota(value.shape, axis)
    low = jnp.where(at == 0, before, roll(value, 1, axis))
    high = jnp.where(at == size - 1, after, roll(value, -1, axis))
    return low, high


def plane_weights(kap, row_m, row_p, col_m, col_p):
    up, down = shifted(kap, 0, row_m, row_p)
    left, right = shifted(kap, 1, col_m, col_p)
    row, lane = iota(kap.shape, 0) % 4, iota(kap.shape, 1) % 4
    return (
        jnp.where(row == 0, kap + up, kap),
        jnp.where(row == 3, kap + down, kap),
        jnp.where(lane == 0, kap + left, kap),
        jnp.where(lane == 3, kap + right, kap),
    )


KAP, WZM, WZP, WYM, WYP, BASE, BETA, DAMP = range(8)
QUANTITIES = DAMP + 3


class Brick:
    def __init__(self, p, cst_ref, kap_xm, kap_xp):
        self.p, self.cst, self.kap_xm, self.kap_xp = p, cst_ref, kap_xm, kap_xp

    def of(self, quantity, i):
        return self.cst[quantity, i // 4]

    def x_weights(self, i):
        kap = self.of(KAP, i)
        low = high = kap
        if i % 4 == 0:
            low = kap + (self.of(KAP, i - 1) if i else self.kap_xm)
        if i % 4 == 3:
            high = kap + (self.of(KAP, i + 1) if i + 1 < self.p.X else self.kap_xp)
        return low, high

    def diagonal(self, i):
        low, high = self.x_weights(i)
        return self.of(BASE, i) + (low + high)

    def damp(self, i):
        return self.cst[DAMP + (0 if i % 4 == 0 else 2 if i % 4 == 3 else 1), i // 4]

    def neighbours(self, i, get, halo=None):
        p, v = self.p, get(i)
        low, high = self.x_weights(i)
        total = jnp.zeros_like(v)
        if i:
            total = total + low * get(i - 1)
        elif halo is not None:
            total = total + low * halo[0]
        if i + 1 < p.X:
            total = total + high * get(i + 1)
        elif halo is not None:
            total = total + high * halo[1]
        if halo is None:
            ends = (0.0, 0.0, 0.0, 0.0)
        else:
            side = self.y_ends(halo[4], i)
            ends = (halo[2][i : i + 1], halo[3][i : i + 1], side, side)
        up, down = shifted(v, 0, ends[0], ends[1])
        left, right = shifted(v, 1, ends[2], ends[3])
        total = total + self.of(WZM, i) * up + self.of(WZP, i) * down
        return total + self.of(WYM, i) * left + self.of(WYP, i) * right

    def y_ends(self, yh, i):
        return roll(swap_lanes(yh), self.p.Y - 1 - 2 * i, 1)

    def from_halo(self, i, halo):
        p = self.p
        row, lane = iota((p.Z, p.Y), 0), iota((p.Z, p.Y), 1)
        side = self.y_ends(halo[4], i)
        total = jnp.where(row == 0, self.of(WZM, i) * halo[2][i : i + 1], 0.0)
        total = jnp.where(row == p.Z - 1, self.of(WZP, i) * halo[3][i : i + 1], total)
        total = total + jnp.where(lane == 0, self.of(WYM, i) * side, 0.0)
        total = total + jnp.where(lane == p.Y - 1, self.of(WYP, i) * side, 0.0)
        if i == 0:
            total = total + self.x_weights(i)[0] * halo[0]
        if i == p.X - 1:
            total = total + self.x_weights(i)[1] * halo[1]
        return total


def residual_plane(brick, i, get, halo, f):
    v = get(i)
    return f - brick.diagonal(i) * v + brick.neighbours(i, get, halo) - brick.of(BETA, i) * v * v * v


def put_rows(ref, stride, offset, n, rows):
    height = -(-rows.shape[0] // n)
    if rows.shape[0] < height * n:
        rows = jnp.concatenate([rows, jnp.zeros((height * n - rows.shape[0], rows.shape[1]), F32)], axis=0)
    for k in range(height):
        ref[pl.ds(offset + k, n, stride=stride), :] = rows[k * n : (k + 1) * n]


def get_rows(ref, stride, offset, n, count):
    height = -(-count // n)
    parts = [ref[pl.ds(offset + k, n, stride=stride), :] for k in range(height)]
    value = parts[0] if height == 1 else jnp.concatenate(parts, axis=0)
    return value[:count]


class Bounds:
    def __init__(self, p):
        self.uxm, self.uxp = (0, p.Z), (p.Z, p.Z)
        self.uzm, self.uzp = (2 * p.Z, p.X), (2 * p.Z + p.X, p.X)
        self.uy = (2 * p.Z + 2 * p.X, p.Z)
        self.count = 3 * p.Z + 2 * p.X


def read(ref, span):
    return ref[span[0] : span[0] + span[1], :]


def write_bounds(ref, b, values):
    for span, value in zip((b.uxm, b.uxp, b.uzm, b.uzp, b.uy), values):
        ref[span[0] : span[0] + span[1], :] = value


def read_bounds(ref, b):
    return tuple(read(ref, span) for span in (b.uxm, b.uxp, b.uzm, b.uzp, b.uy))


def advance(p, brick, get, residual, rxz, ry, s_ref, r_scr, z_scr, z2_scr):
    X, Z = p.X, p.Z
    for i in range(X):
        r = residual(i)
        r_scr[i * Z : (i + 1) * Z, :] = r
        z_scr[i] = r * brick.damp(i)
    z1 = lambda i: z_scr[i]
    coarse = dot_wide_right(rxz[...], r_scr[...])
    coarse = dot_wide_right(ry[...], coarse, ((1,), (1,))) * (1.0 / 216.0)
    for i in range(X):
        v = z1(i)
        smooth = (2.0 - DAMPING) * v + brick.damp(i) * brick.neighbours(i, z1)
        z2_scr[i] = smooth
        s_ref[i] = get(i) + smooth
    return coarse.astype(BF16)


def start_cycle(p, brick, get, residual, classes, rxz, ry, sy, s_ref, z1b_ref, go_ref, r_scr, z_scr, z2_scr, go_scr):
    X, Z, n = p.X, p.Z, p.n
    coarse = advance(p, brick, get, residual, rxz, ry, s_ref, r_scr, z_scr, z2_scr)
    z1 = lambda i: z_scr[i]
    rows = sy[pl.ds(pl.multiple_of(lax.axis_index("by") * p.cy + 8, 8), p.cy), :]
    part = dot(rows.T, coarse)
    for j in range(n):
        go_scr[j * p.go : j * p.go + p.modes, :] = part[j * p.modes : (j + 1) * p.modes]
    z2 = lambda i: z2_scr[i]
    z1_y, z2_y = col_faces(z1, p), col_faces(z2, p)
    z1_zm, z1_zp = z_scr[:, 0, :], z_scr[:, Z - 1, :]
    write_bounds(z1b_ref, Bounds(p), (z1(0), z1(X - 1), z1_zm, z1_zp, z1_y))
    lane = iota((Z, p.Y), 1)
    sides = jnp.where(lane < 2 * X, z1_y, roll(z2_y, 2 * X, 1))
    edges = [z_scr[0, 0:1, :], z_scr[0, Z - 1 : Z, :], z_scr[X - 1, 0:1, :], z_scr[X - 1, Z - 1 : Z, :]]
    edges += [z1_y[0:1], z1_y[Z - 1 : Z]]
    if classes is None:
        sides = jnp.where(lane < 4 * X, sides, 0.0)
    else:
        cls, cls_y = classes
        sides = jnp.where(lane < 4 * X, sides, roll(cls_y, 4 * X, 1))
        sides = jnp.where(lane < 6 * X, sides, 0.0)
        edges += [cls(0)[0:1], cls(0)[Z - 1 : Z], cls(X - 1)[0:1], cls(X - 1)[Z - 1 : Z]]
        edges += [cls_y[0:1], cls_y[Z - 1 : Z]]
    pieces = (
        jnp.concatenate([z1(0), z2(0)], axis=0),
        jnp.concatenate([z1(X - 1), z2(X - 1)], axis=0),
        jnp.concatenate([z1_zm, z2_scr[:, 0, :]], axis=0),
        jnp.concatenate([z1_zp, z2_scr[:, Z - 1, :]], axis=0),
        sides,
        jnp.concatenate(edges, axis=0),
    )
    for piece, offset in zip(pieces, p.offsets):
        put_rows(go_scr, p.go, p.go_halo + offset, n, piece)
    used = p.go_halo + sum(p.heights)
    for k in range(used, p.go):
        go_scr[pl.ds(k, n, stride=p.go), :] = jnp.zeros((n, p.Y), F32)
    go_ref[...] = go_scr[...].astype(BF16)


def sides_kernel(p, u_ref, y_ref):
    y_ref[...] = col_faces(lambda i: u_ref[i], p)


def pack_kernel(p, index_ref, u_ref, uy_ref, cls_ref, xa_ref, xb_ref, za_ref, zb_ref, y_ref):
    X, Z, Y = p.X, p.Z, p.Y
    spread_z = (iota((Z, Z // 4), 0) // 4 == iota((Z, Z // 4), 1)).astype(BF16)
    spread_y = (iota((Y // 4, Y), 1) // 4 == iota((Y // 4, Y), 0)).astype(BF16)
    for a in range(X // 4):
        element = (index_ref[a] + 1).astype(F32).astype(BF16)
        cls_ref[a] = dot(dot(spread_z, element).astype(BF16), spread_y)
    cls = lambda i: cls_ref[i // 4]

    def face(axis, low, high, a_ref, b_ref, at):
        even = lax.axis_index(axis) % 2 == 0
        count = low.shape[0]
        a_ref[at : at + count, :] = jnp.where(even, high, low)
        b_ref[at : at + count, :] = jnp.where(even, low, high)

    face("bx", u_ref[0], u_ref[X - 1], xa_ref, xb_ref, 0)
    face("bx", cls(0), cls(X - 1), xa_ref, xb_ref, Z)
    rows = lambda z: jnp.concatenate([cls(i)[z : z + 1] for i in range(X)], axis=0)
    face("bz", u_ref[:, 0, :], u_ref[:, Z - 1, :], za_ref, zb_ref, 0)
    face("bz", rows(0), rows(Z - 1), za_ref, zb_ref, X)
    if X < Z:
        za_ref[2 * X :, :] = zb_ref[2 * X :, :] = jnp.zeros((2 * (Z - X), Y), F32)
    y_ref[0:Z, :] = uy_ref[...]
    y_ref[Z : 2 * Z, :] = col_faces(cls, p)


def received(axis, count, a_ref, b_ref):
    at = lax.axis_index(axis)
    even = at % 2 == 0
    a, b = a_ref[...], b_ref[...]
    low = jnp.where(even, b, a)
    high = jnp.where(even, a, b)
    return jnp.where(at > 0, low, 0.0), jnp.where(at < count - 1, high, 0.0)


def prepare_kernel(p, coef, u_ref, f_ref, cls_ref, cst_ref, r_ref):
    for a in range(p.X // 4):
        kap = lookup(cls_ref[a], coef, 0)
        wzm, wzp, wym, wyp = plane_weights(kap, 0.0, 0.0, 0.0, 0.0)
        cst_ref[KAP, a] = kap
        cst_ref[WZM, a] = wzm
        cst_ref[WZP, a] = wzp
        cst_ref[WYM, a] = wym
        cst_ref[WYP, a] = wyp
        cst_ref[BASE, a] = lookup(cls_ref[a], coef, 1) + ((wzm + wzp) + (wym + wyp))
        cst_ref[BETA, a] = lookup(cls_ref[a], coef, 2)
    brick = Brick(p, cst_ref, 0.0, 0.0)
    get = lambda i: u_ref[i]
    for i in range(p.X):
        r_ref[i] = residual_plane(brick, i, get, None, f_ref[i])


def neighbours_in(p, coef, u_ref, r_ref, cst0_ref, xa, xb, za, zb, ya, yb, uhb_ref, clsb_ref, cst_ref):
    X, Z, Y, b = p.X, p.Z, p.Y, Bounds(p)
    xm, xp = received("bx", p.nx, xa, xb)
    zm, zp = (value[: 2 * X] for value in received("bz", p.nz, za, zb))
    ym, yp = received("by", p.ny, ya, yb)
    y = jnp.where(iota(ym.shape, 1) % 2 == 0, ym, yp)
    halo = (xm[:Z], xp[:Z], zm[:X], zp[:X], y[:Z])
    outside = (xm[Z:], xp[Z:], zm[X:], zp[X:], y[Z:])
    write_bounds(uhb_ref, b, halo)
    write_bounds(clsb_ref, b, outside)
    kap_h = tuple(lookup(value, coef, 0) for value in outside)
    row, lane = iota((Z, Y), 0), iota((Z, Y), 1)
    more = []
    for a in range(X // 4):
        i = 4 * a
        ends = (
            (WZM, jnp.where(row == 0, kap_h[2][i : i + 1], 0.0)),
            (WZP, jnp.where(row == Z - 1, kap_h[3][i : i + 1], 0.0)),
            (WYM, jnp.where(lane == 0, kap_h[4][:, 2 * i : 2 * i + 1], 0.0)),
            (WYP, jnp.where(lane == Y - 1, kap_h[4][:, 2 * i + 1 : 2 * i + 2], 0.0)),
        )
        for k, end in ends:
            cst_ref[k, a] = cst0_ref[k, a] + end
        more.append((ends[0][1] + ends[1][1]) + (ends[2][1] + ends[3][1]))
        cst_ref[BASE, a] = cst0_ref[BASE, a] + more[a]
        cst_ref[KAP, a] = cst0_ref[KAP, a]
        cst_ref[BETA, a] = cst0_ref[BETA, a]
    brick = Brick(p, cst_ref, kap_h[0], kap_h[1])
    for a in range(X // 4):
        for k, i in enumerate((4 * a, 4 * a + 1, 4 * a + 3)):
            cst_ref[DAMP + k, a] = DAMPING / brick.diagonal(i)

    def residual(i):
        added = more[i // 4]
        if i == 0:
            added = added + kap_h[0]
        if i == X - 1:
            added = added + kap_h[1]
        return r_ref[i] - added * u_ref[i] + brick.from_halo(i, halo)

    return brick, residual


def first_kernel(p, coef, u_ref, r_ref, cls_ref, cst0_ref, xa, xb, za, zb, ya, yb, rxz, ry, sy,
                 go_ref, s_ref, z1b_ref, uhb_ref, clsb_ref, cst_ref, r_scr, z_scr, z2_scr, go_scr):
    brick, residual = neighbours_in(p, coef, u_ref, r_ref, cst0_ref, xa, xb, za, zb, ya, yb, uhb_ref, clsb_ref, cst_ref)
    cls = lambda i: cls_ref[i // 4]
    start_cycle(p, brick, lambda i: u_ref[i], residual, (cls, col_faces(cls, p)), rxz, ry, sy,
                s_ref, z1b_ref, go_ref, r_scr, z_scr, z2_scr, go_scr)


def owner_kernel(p, coef, in_ref, wz, wx, wxt, wzi, lamxz, lamy, out_ref, in_scr, out_scr):
    n, m, nx, ny, nz = p.n, p.modes, p.nx, p.ny, p.nz
    me = (lax.axis_index("bx") * ny + lax.axis_index("by")) * nz + lax.axis_index("bz")
    in_scr[...] = in_ref[...].astype(F32)
    rows = []
    for bx in range(nx):
        lanes = []
        for bz in range(nz):
            total = None
            for by in range(ny):
                at = ((bx * ny + by) * nz + bz) * p.go
                piece = in_scr[at : at + m, :]
                total = piece if total is None else total + piece
            lanes.append(total)
        rows.append(jnp.concatenate(lanes, axis=1))
    data = jnp.concatenate(rows, axis=0)
    data = dot_wide_right(wz[...], data, ((1,), (1,)))
    data = jnp.concatenate([data[x * p.NZ : (x + 1) * p.NZ] for x in range(p.cx)], axis=1)
    data = dot_wide_left(data, wx[...])
    classes = coef.shape[1]
    kap_mean = sum(coef[0, k] for k in range(classes)) * (1.0 / classes)
    sig_mean = sum(coef[1, k] for k in range(classes)) * (1.0 / classes)
    data = data / (kap_mean * (lamxz[...] + lamy[me]) + sig_mean)
    data = dot_wide_left(data, wxt[...])
    width = nx * m
    data = jnp.concatenate([data[:, x * width : (x + 1) * width] for x in range(p.cx)], axis=0)
    high, low = halves(data)
    high, low = high.T, low.T
    lane = iota((m, p.Y), 1)
    for bz in range(nz):
        back = dot(high, wzi[bz]) + dot(low, wzi[bz])
        core = lambda bx: back[bx * m : (bx + 1) * m, : p.lanes]
        for bx in range(nx):
            ends = roll(back[bx * m : (bx + 1) * m, p.lanes :], 2 * p.cz, 1)
            below = roll(core(bx - 1), p.cz - p.lanes, 1) if bx else jnp.zeros((m, p.lanes), F32)
            above = roll(core(bx + 1), p.cz, 1) if bx + 1 < nx else jnp.zeros((m, p.lanes), F32)
            extra = jnp.where(lane < p.cz, below, jnp.where(lane < 2 * p.cz, above, ends))
            mine = core(bx)
            for by in range(ny):
                at = ((bx * ny + by) * nz + bz) * p.back
                out_scr[at : at + m, :] = mine
                out_scr[at + m : at + 2 * m, :] = extra

    device = iota((n, p.Y), 0)
    at_x, at_y, at_z = device // (ny * nz), (device // nz) % ny, device % nz

    def shift(value, dx, dy, dz):
        value = roll(value, -((dx * ny + dy) * nz + dz), 0)
        for at, step, count in ((at_x, dx, nx), (at_y, dy, ny), (at_z, dz, nz)):
            if step:
                value = jnp.where((at + step >= 0) & (at + step < count), value, 0.0)
        return value

    def take(k):
        return in_scr[pl.ds(p.go_halo + k, n, stride=p.go), :]

    def give(k, value):
        out_scr[pl.ds(p.back_halo + k, n, stride=p.back), :] = value

    for to, source, step in ((0, 1, (-1, 0, 0)), (1, 0, (1, 0, 0)), (2, 3, (0, 0, -1)), (3, 2, (0, 0, 1))):
        for k in range(p.heights[to]):
            give(p.offsets[to] + k, shift(take(p.offsets[source] + k), *step))
    lane = iota((n, p.Y), 1)
    even = lane % 2 == 0
    first, X2 = p.edge_lane, 2 * p.X
    for k in range(p.heights[4]):
        sides = take(p.offsets[4] + k)
        moved = jnp.where(lane < first + 2, roll(sides, first, 1), roll(sides, first + 2 - (X2 - 2), 1))
        moved = jnp.where(lane < first + 4, moved, roll(sides, first + 4 - 2 * X2, 1))
        moved = jnp.where(lane < first + 6, moved, roll(sides, first + 6 - (3 * X2 - 2), 1))
        which = (lane - first) % 4
        corner = jnp.where(
            which < 2,
            jnp.where(even, shift(moved, 1, -1, 0), shift(moved, 1, 1, 0)),
            jnp.where(even, shift(moved, -1, -1, 0), shift(moved, -1, 1, 0)),
        )
        plain = jnp.where(even, shift(sides, 0, -1, 0), shift(sides, 0, 1, 0))
        give(p.offsets[4] + k, jnp.where(lane < first, plain, jnp.where(lane < first + 8, corner, 0.0)))
    edges = take(p.offsets[5])
    kind = me % 6
    moved = jnp.where(even, shift(edges, 0, -1, -1), shift(edges, 0, 1, -1))
    for k, value in (
        (0, lambda: shift(edges, 1, 0, 1)),
        (1, lambda: shift(edges, 1, 0, -1)),
        (2, lambda: shift(edges, -1, 0, 1)),
        (3, lambda: shift(edges, -1, 0, -1)),
        (4, lambda: jnp.where(even, shift(edges, 0, -1, 1), shift(edges, 0, 1, 1))),
    ):
        moved = jnp.where(kind == k, value(), moved)
    give(p.offsets[5], moved)
    used = p.back_halo + sum(p.heights)
    for k in range(used, p.back):
        out_scr[pl.ds(k, n, stride=p.back), :] = jnp.zeros((n, p.Y), F32)
    out_ref[...] = out_scr[...].astype(BF16)


class Arrived:
    def __init__(self, p, ref):
        X, Z = p.X, p.Z
        rows = (2 * Z, 2 * Z, 2 * X, 2 * X, Z, 12)
        xm, xp, zm, zp, sides, edges = (
            get_rows(ref, p.back, p.back_halo + offset, p.n, count) for offset, count in zip(p.offsets, rows)
        )
        self.p, self.ref, self.sides, self.edges = p, ref, sides, edges
        self.z1 = (xm[:Z], xp[:Z], zm[:X], zp[:X], sides)
        self.z2 = (xm[Z:], xp[Z:], zm[X:], zp[X:], roll(sides, -2 * X, 1))

    def xz(self, kind, sx, sz):
        k = 6 * kind + (0 if sx else 2) + (0 if sz else 1)
        return self.edges[k : k + 1]

    def zy(self, kind, sz):
        k = 6 * kind + (4 if sz else 5)
        return self.edges[k : k + 1]

    def xy(self, kind, sx, sy):
        lane = self.p.edge_lane + 4 * kind + (0 if sx else 2) + sy
        return self.sides[:, lane : lane + 1]

    def xy_lanes(self, kind, plain):
        first, X2 = self.p.edge_lane + 4 * kind, 2 * self.p.X
        lane = iota(plain.shape, 1)
        value = jnp.where(lane < X2, plain, roll(self.sides, X2 - first, 1))
        return jnp.where(lane >= self.p.Y - 2, roll(self.sides, self.p.Y - 2 - first - 2, 1), value)


def coarse_rows(p, ref, sy, pyt, pall, pyh):
    n, m = p.n, p.modes
    core = jnp.concatenate([ref[j * p.back : j * p.back + m, :] for j in range(n)], axis=0)
    extra = jnp.concatenate([ref[j * p.back + m : j * p.back + 2 * m, :] for j in range(n)], axis=0)
    modes = jnp.concatenate([core, extra], axis=1).astype(BF16)
    rows = sy[pl.ds(pl.multiple_of(lax.axis_index("by") * p.cy, 8), p.cy + 16), :]
    values = dot(rows, modes).astype(BF16)
    along = dot(values[8 : 8 + p.cy].T, pyt[...])
    count = pall.shape[0] - p.Z
    nodes = dot_wide_right(pall[:count], along) * (1.0 / 27.0)
    weights = pall[count:, : p.lanes].astype(F32)
    ends = [weights * values.astype(F32)[k : k + 1, : p.lanes] for k in (7, 8 + p.cy)]
    side = dot_wide_left(jnp.concatenate(ends, axis=1), pyh[...]) * (1.0 / 27.0)
    return nodes, side


def column(row, count, side):
    shape = (count, row.shape[1])
    pick = iota(shape, 1) == 2 * iota(shape, 0) + side
    return jnp.sum(jnp.where(pick, row, 0.0), axis=1, keepdims=True)


def finish_cycle(p, coef, brick, now, first, s_ref, z1b_ref, uhb_ref, clsb_ref, nodes, side, u_ref):
    X, Z, b = p.X, p.Z, Bounds(p)
    for i in range(X):
        u_ref[i] = s_ref[i] + brick.damp(i) * brick.from_halo(i, now.z1) + nodes[i * Z : (i + 1) * Z]
    old, cls, own = read_bounds(uhb_ref, b), read_bounds(clsb_ref, b), read_bounds(z1b_ref, b)
    kap = lambda value: lookup(value, coef, 0)
    halo = []

    def new(k, weights, toward, others, correction):
        kap_here = kap(cls[k])
        diagonal = lookup(cls[k], coef, 1) + (kap_here + toward) + ((weights[0] + weights[1]) + (weights[2] + weights[3]))
        total = toward * own_faces[k]
        for part in others:
            total = total + part
        value = old[k] + now.z2[k] + (DAMPING / diagonal) * total + correction
        halo.append(jnp.where(cls[k] > 0.5, value, 0.0))

    own_faces = list(own[:4]) + [swap_lanes(own[4])]
    at = X * Z
    for k in range(2):
        kap_here = kap(cls[k])
        row_m, row_p = kap(first.xz(1, k, 0)), kap(first.xz(1, k, 1))
        col_m, col_p = kap(first.xy(1, k, 0)), kap(first.xy(1, k, 1))
        w = plane_weights(kap_here, row_m, row_p, col_m, col_p)
        row, lane = iota((Z, p.Y), 0), iota((Z, p.Y), 1)
        others = (
            jnp.where(row == 0, w[0] * now.xz(0, k, 0), 0.0),
            jnp.where(row == Z - 1, w[1] * now.xz(0, k, 1), 0.0),
            jnp.where(lane == 0, w[2] * now.xy(0, k, 0), 0.0),
            jnp.where(lane == p.Y - 1, w[3] * now.xy(0, k, 1), 0.0),
        )
        toward = kap_here + brick.of(KAP, 0 if k == 0 else X - 1)
        new(k, w, toward, others, nodes[at : at + Z])
        at += Z
    for k in range(2):
        kap_here = kap(cls[2 + k])
        row_m, row_p = kap(first.xz(1, 0, k)), kap(first.xz(1, 1, k))
        col_m, col_p = (kap(column(first.zy(1, k), X, side_y)) for side_y in range(2))
        w = plane_weights(kap_here, row_m, row_p, col_m, col_p)
        row, lane = iota((X, p.Y), 0), iota((X, p.Y), 1)
        others = (
            jnp.where(row == 0, w[0] * now.xz(0, 0, k), 0.0),
            jnp.where(row == X - 1, w[1] * now.xz(0, 1, k), 0.0),
            jnp.where(lane == 0, w[2] * column(now.zy(0, k), X, 0), 0.0),
            jnp.where(lane == p.Y - 1, w[3] * column(now.zy(0, k), X, 1), 0.0),
        )
        z = 0 if k == 0 else Z - 1
        mine = jnp.concatenate([brick.of(KAP, i)[z : z + 1] for i in range(X)], axis=0)
        new(2 + k, w, kap_here + mine, others, nodes[at : at + X])
        at += X
    wide = kap(first.xy_lanes(1, cls[4]))
    z1_wide = now.xy_lanes(0, now.z1[4])
    row_m, row_p = kap(first.zy(1, 0)), kap(first.zy(1, 1))
    up, down = shifted(wide, 0, row_m, row_p)
    left, right = roll(wide, 2, 1), roll(wide, -2, 1)
    row, lane = iota((Z, p.Y), 0), iota((Z, p.Y), 1)
    w = (
        jnp.where(row % 4 == 0, wide + up, wide),
        jnp.where(row % 4 == 3, wide + down, wide),
        jnp.where((lane // 2) % 4 == 0, wide + left, wide),
        jnp.where((lane // 2) % 4 == 3, wide + right, wide),
    )
    others = (
        jnp.where(row == 0, w[0] * now.zy(0, 0), 0.0),
        jnp.where(row == Z - 1, w[1] * now.zy(0, 1), 0.0),
        jnp.where(lane // 2 == 0, w[2] * roll(z1_wide, 2, 1), 0.0),
        jnp.where(lane // 2 == X - 1, w[3] * roll(z1_wide, -2, 1), 0.0),
    )
    mine = swap_lanes(col_faces(lambda i: brick.of(KAP, i), p))
    new(4, w, wide + mine, others, side)
    return tuple(halo)


def middle_kernel(p, coef, in_ref, f_ref, s_ref, z1b_ref, uhb_ref, clsb_ref, cst_ref,
                  sy, pyt, pall, pyh, rxz, ry,
                  go_ref, s_out, z1b_out, uhb_out, in_scr, u_scr, r_scr, z_scr, z2_scr, go_scr):
    in_scr[...] = in_ref[...].astype(F32)
    b = Bounds(p)
    outside = read_bounds(clsb_ref, b)
    brick = Brick(p, cst_ref, lookup(outside[0], coef, 0), lookup(outside[1], coef, 0))
    now = Arrived(p, in_scr)
    nodes, side = coarse_rows(p, in_scr, sy, pyt, pall, pyh)
    halo = finish_cycle(p, coef, brick, now, now, s_ref, z1b_ref, uhb_ref, clsb_ref, nodes, side, u_scr)
    write_bounds(uhb_out, b, halo)
    get = lambda i: u_scr[i]
    residual = lambda i: residual_plane(brick, i, get, halo, f_ref[i])
    start_cycle(p, brick, get, residual, None, rxz, ry, sy,
                s_out, z1b_out, go_ref, r_scr, z_scr, z2_scr, go_scr)


def last_kernel(p, coef, in_ref, first_ref, f_ref, s_ref, z1b_ref, uhb_ref, clsb_ref, cst_ref,
                sy, pyt, pall, pyh, u_out, r_out, in_scr, first_scr):
    in_scr[...] = in_ref[...].astype(F32)
    first_scr[...] = first_ref[...].astype(F32)
    outside = read_bounds(clsb_ref, Bounds(p))
    brick = Brick(p, cst_ref, lookup(outside[0], coef, 0), lookup(outside[1], coef, 0))
    now, first = Arrived(p, in_scr), Arrived(p, first_scr)
    nodes, side = coarse_rows(p, in_scr, sy, pyt, pall, pyh)
    halo = finish_cycle(p, coef, brick, now, first, s_ref, z1b_ref, uhb_ref, clsb_ref, nodes, side, u_out)
    for i in range(p.X):
        r_out[i] = residual_plane(brick, i, lambda k: u_out[k], halo, f_ref[i])


class Sends:
    def __init__(self, p):
        X, Z = p.X, p.Z
        self.first = p.cy + Z // 2
        self.x_face, self.z_face = p.NY, p.NY
        self.x_rows = p.NY + 2 * Z + Z // 2
        self.z_rows = p.NY + 2 * X + 16
        self.xz_rows = p.NY + 16
        self.second = 2 * p.cx * p.NZ * p.NY // p.Y
        self.corner = self.second + 2 * Z + Z // 2
        self.last = self.corner + 16
        self.faces = 4 * Z + 4 * X


def pick(condition, a, b):
    return jnp.where(condition, a, b)


def fold(value):
    count, lanes = value.shape
    low, high = value[: count // 2], value[count // 2 :]
    return jnp.where(iota(low.shape, 1) < lanes // 2, low, roll(high, lanes // 2, 1)).astype(BF16)


def unfold(value):
    value = value.astype(F32)
    return jnp.concatenate([value, roll(value, value.shape[1] // 2, 1)], axis=0)


def go_on(p, brick, residual, rxz, ry, a_ref, z_ref, r_scr):
    X, Z = p.X, p.Z
    lane = iota((Z, p.Y), 1) // 4
    sides = jnp.zeros((Z, p.Y), F32)
    for i in range(X):
        r = residual(i)
        r_scr[i * Z : (i + 1) * Z, :] = r
        step = r * brick.damp(i)
        z_ref[i] = step
        sides = jnp.where(lane == i, roll(step, 4 * i + 2, 1), sides)
    coarse = dot_wide_right(rxz[...], r_scr[...])
    coarse = dot_wide_right(ry[...], coarse, ((1,), (1,))) * (1.0 / 216.0)
    a_ref[0 : p.cy, :] = coarse.astype(BF16)
    a_ref[p.cy :, :] = fold(sides)


def smooth_kernel(p, u_ref, z_ref, cst_ref, s_ref, z1b_ref, faces_ref, z2_scr):
    X, Z = p.X, p.Z
    brick = Brick(p, cst_ref, 0.0, 0.0)
    z1, z2 = (lambda i: z_ref[i]), (lambda i: z2_scr[i])
    for i in range(X):
        smooth = (2.0 - DAMPING) * z1(i) + brick.damp(i) * brick.neighbours(i, z1)
        z2_scr[i] = smooth
        s_ref[i] = u_ref[i] + smooth
    z_rows = (z_ref[:, 0, :], z_ref[:, Z - 1, :], z2_scr[:, 0, :], z2_scr[:, Z - 1, :])
    write_bounds(z1b_ref, Bounds(p), (z1(0), z1(X - 1), z_rows[0], z_rows[1], col_faces(z1, p)))
    for k, plane in enumerate((z1(0), z1(X - 1), z2(0), z2(X - 1))):
        faces_ref[k * Z : (k + 1) * Z, :] = plane.astype(BF16)
    for k, rows in enumerate(z_rows):
        faces_ref[4 * Z + k * X : 4 * Z + (k + 1) * X, :] = rows.astype(BF16)


def face_x(p, faces_ref, high):
    X, Z = p.X, p.Z
    return tuple(pick(high, faces_ref[(k + 1) * Z : (k + 2) * Z, :], faces_ref[k * Z : (k + 1) * Z, :]) for k in (0, 2))


def face_z(p, faces_ref, high):
    X, at = p.X, 4 * p.Z
    return tuple(
        pick(high, faces_ref[at + (k + 1) * X : at + (k + 2) * X, :], faces_ref[at + k * X : at + (k + 1) * X, :]) for k in (0, 2)
    )


def pad_rows(rows, count):
    rows = [row.astype(F32) for row in rows]
    return jnp.concatenate(rows + [jnp.zeros((count - len(rows), rows[0].shape[1]), F32)], axis=0).astype(BF16)


def y_block(p, sides, cls_y):
    lane = iota(sides.shape, 1)
    return jnp.where(lane < 2 * p.X, sides, roll(cls_y, 2 * p.X, 1))


def distances(count):
    return tuple(range(1, count))


def after_first(p, *refs):
    ny = p.ny
    buffers, (faces_ref, clsb_ref, cls_ref, sy, x_ref, z_ref, xz_ref, sides_ref, all_scr) = refs[:ny], refs[ny:]
    X, Z, sends, b = p.X, p.Z, Sends(p), Bounds(p)
    bx, by, bz = (lax.axis_index(axis) for axis in AXES)
    low = high = jnp.zeros((Z, p.Y), F32)
    for d, buffer in zip((0,) + distances(ny), buffers):
        other = by ^ d
        all_scr[pl.ds(pl.multiple_of(other * p.cy, 16), p.cy), :] = buffer[0 : p.cy, :]
        if d and d & (d + 1) == 0:
            value = unfold(buffer[p.cy :, :])
            low = pick(other == by - 1, value, low)
            high = pick(other == by + 1, value, high)
    to, source = iota((p.Y, p.Y), 1), iota((p.Y, p.Y), 0)
    place = (to % (2 * X)) // 2 * 4 + jnp.where(to < 2 * X, 1 + to % 2, 3 * (to % 2))
    order = ((source == place) & (to < 4 * X)).astype(BF16)
    both = dot(jnp.concatenate([low, high], axis=0).astype(BF16), order)
    sides = jnp.where(iota((Z, p.Y), 1) % 2 == 0, both[:Z], both[Z:])
    sides_ref[...] = sides
    modes = dot(sy[8 : 8 + p.NY, :], all_scr[...]).astype(BF16)
    cls_y = read(clsb_ref, b.uy)
    odd, up = bx % 2 == 1, bz == 0
    for ref in (x_ref, z_ref, xz_ref):
        ref[0 : p.NY, :] = modes
    at = p.NY
    z1, z2 = face_x(p, faces_ref, odd)
    x_ref[at : at + Z, :] = z1
    x_ref[at + Z : at + 2 * Z, :] = z2
    x_ref[at + 2 * Z :, :] = fold(y_block(p, sides, cls_y))
    z1, z2 = face_z(p, faces_ref, up)
    z_ref[at : at + X, :] = z1
    z_ref[at + X : at + 2 * X, :] = z2
    z_ref[at + 2 * X : at + 2 * X + 16, :] = pad_rows(
        [pick(up, value[Z - 1 : Z], value[0:1]) for value in (sides, cls_y)], 16
    )
    z1 = z1.astype(F32)
    cls = pick(odd, cls_ref[X // 4 - 1], cls_ref[0])
    xz_ref[at : at + 16, :] = pad_rows(
        [pick(odd, z1[X - 1 : X], z1[0:1]), pick(up, cls[Z - 1 : Z], cls[0:1])], 16
    )


def after_second(p, own_ref, x_in, z_in, xz_in, faces_ref, clsb_ref, sides_ref, wzt, out_ref):
    X, Z, Y, sends, b = p.X, p.Z, p.Y, Sends(p), Bounds(p)
    bx, bz = lax.axis_index("bx"), lax.axis_index("bz")
    odd, up = bx % 2 == 1, bz == 0
    at = 0
    for one, two in ((own_ref, z_in), (x_in, xz_in)):
        one, two = one[0 : p.NY, :], two[0 : p.NY, :]
        data = jnp.concatenate([pick(up, one, two), pick(up, two, one)], axis=1)
        data = dot(wzt[...], data, ((1,), (1,))).astype(BF16)
        for k in range(p.NY // Y):
            rows = data.shape[0]
            out_ref[at : at + rows, :] = data[:, k * Y : (k + 1) * Y]
            at += rows
    z1, z2 = face_x(p, faces_ref, jnp.logical_not(odd))
    out_ref[at : at + Z, :] = z1
    out_ref[at + Z : at + 2 * Z, :] = z2
    out_ref[at + 2 * Z : sends.corner, :] = fold(y_block(p, sides_ref[...], read(clsb_ref, b.uy)))
    beyond = z_in[p.NY : p.NY + X, :].astype(F32)
    classes = pick(up, read(clsb_ref, b.uzp), read(clsb_ref, b.uzm))
    out_ref[sends.corner :, :] = pad_rows(
        [pick(odd, value[0:1], value[X - 1 : X]) for value in (beyond, classes)], 16
    )


class Beyond:
    def __init__(self, p):
        X, Z = p.X, p.Z
        self.cross = 0
        self.core = Z
        self.z = 6 * Z
        self.y = 6 * Z + 4 * X
        self.kap = 10 * Z + 4 * X
        self.count = self.kap + Bounds(p).count


def rows_at(ref, at, count):
    return ref[at : at + count, :]


def beyond_kernel(p, coef, s_ref, z1b_ref, uhb_ref, clsb_ref, cls_ref, cst_ref, sides_ref, x_in, z_in, xz_in, s_out, out_ref):
    X, Z, Y, b, to = p.X, p.Z, p.Y, Bounds(p), Beyond(p)
    bx, bz = lax.axis_index("bx"), lax.axis_index("bz")
    odd, up = bx % 2 == 1, bz == 0
    some = (bx > 0) & (bx < p.nx - 1)
    kaps, sigs = lookup(clsb_ref[...], coef, 0), lookup(clsb_ref[...], coef, 1)
    out_ref[to.kap :, :] = kaps
    part = lambda value, span: value[span[0] : span[0] + span[1]]
    x_part = lambda value, high: pick(high, part(value, b.uxp), part(value, b.uxm))
    z_part = lambda value: pick(up, part(value, b.uzp), part(value, b.uzm))
    z1b, uhb = z1b_ref[...], uhb_ref[...]
    across = lambda at, count: pick(some, x_in[p.NY + at : p.NY + at + count, :].astype(F32), 0.0)
    x_z1, x_z2, block = across(0, Z), across(Z, Z), unfold(across(2 * Z, Z // 2))
    corner = pick(some, xz_in[p.NY : p.NY + 16, :].astype(F32), 0.0)
    corner_z1, corner_kap = corner[0:1], lookup(corner[1:2], coef, 0)
    z_z1, z_z2 = (z_in[p.NY + k * X : p.NY + (k + 1) * X, :].astype(F32) for k in range(2))
    z_rows = z_in[p.NY + 2 * X : p.NY + 2 * X + 16, :].astype(F32)
    zy_z1, zy_kap = z_rows[0:1], lookup(z_rows[1:2], coef, 0)
    block_kap = lookup(block, coef, 0)
    sides = sides_ref[...]
    brick = Brick(p, cst_ref, part(kaps, b.uxm), part(kaps, b.uxp))
    halo = (pick(odd, 0.0, x_z1), pick(odd, x_z1, 0.0), pick(up, 0.0, z_z1), pick(up, z_z1, 0.0), sides)
    for i in range(X):
        s_out[i] = s_ref[i] + brick.damp(i) * brick.from_halo(i, halo)
    row, lane = iota((Z, Y), 0), iota((Z, Y), 1)
    face = lambda high: pick(high, brick.of(KAP, X - 1), brick.of(KAP, 0))

    k, sigma = x_part(kaps, odd), x_part(sigs, odd)
    toward = k + face(odd)
    X2 = 2 * X
    ends = lambda value, first: [pick(odd, value[:, first + c : first + c + 1], value[:, first + X2 - 2 + c : first + X2 - 1 + c]) for c in (0, 1)]
    col_kap, col_z1 = ends(block_kap, X2), ends(block, 0)
    w = plane_weights(k, pick(up, 0.0, corner_kap), pick(up, corner_kap, 0.0), col_kap[0], col_kap[1])
    total = toward * x_part(z1b, odd)
    total = total + jnp.where(row == pick(up, Z - 1, 0), pick(up, w[1], w[0]) * corner_z1, 0.0)
    total = total + jnp.where(lane == 0, w[2] * col_z1[0], 0.0) + jnp.where(lane == Y - 1, w[3] * col_z1[1], 0.0)
    diagonal = sigma + (k + toward) + ((w[0] + w[1]) + (w[2] + w[3]))
    value = x_part(uhb, odd) + x_z2 + (DAMPING / diagonal) * total
    out_ref[to.cross : to.cross + Z, :] = jnp.where(k > 0.0, value, 0.0)

    other = jnp.logical_not(odd)
    k, sigma = x_part(kaps, other), x_part(sigs, other)
    toward = k + face(other)
    for j, value in enumerate((k, toward, sigma + (k + toward), x_part(z1b, other), x_part(uhb, other))):
        out_ref[to.core + j * Z : to.core + (j + 1) * Z, :] = value

    k, sigma = z_part(kaps), z_part(sigs)
    own = jnp.concatenate([pick(up, cst_ref[KAP, i // 4, Z - 1 : Z, :], cst_ref[KAP, i // 4, 0:1, :]) for i in range(X)], axis=0)
    toward = k + own
    col_kap, col_z1 = ([column(value, X, c) for c in (0, 1)] for value in (zy_kap, zy_z1))
    w = plane_weights(k, pick(odd, 0.0, corner_kap), pick(odd, corner_kap, 0.0), col_kap[0], col_kap[1])
    zrow, zlane = iota((X, Y), 0), iota((X, Y), 1)
    total = toward * z_part(z1b)
    total = total + jnp.where(zrow == pick(odd, X - 1, 0), pick(odd, w[1], w[0]) * corner_z1, 0.0)
    total = total + jnp.where(zlane == 0, w[2] * col_z1[0], 0.0) + jnp.where(zlane == Y - 1, w[3] * col_z1[1], 0.0)
    diagonal = sigma + (k + toward) + ((w[0] + w[1]) + (w[2] + w[3]))
    for j, value in enumerate((z_part(uhb) + z_z2, total, diagonal, k)):
        out_ref[to.z + j * X : to.z + (j + 1) * X, :] = value

    k, sigma = part(kaps, b.uy), part(sigs, b.uy)
    toward = k + swap_lanes(col_faces(lambda i: brick.of(KAP, i), p))
    reach = lambda value, shift: pick(odd, roll(value, X2 + shift, 1), roll(value, Y - X2 + shift, 1))
    begin = pick(odd, X2, Y - 2)
    far = (lane >= begin) & (lane < begin + 2)
    wide = jnp.where(far, reach(block_kap, -X2), jnp.where(lane < X2, k, 0.0))
    wide_z1 = jnp.where(far, reach(block, 0), jnp.where(lane < X2, sides, 0.0))
    above, below = shifted(wide, 0, pick(up, 0.0, zy_kap), pick(up, zy_kap, 0.0))
    left, right = roll(wide, 2, 1), roll(wide, -2, 1)
    place = lane // 2
    w = (
        jnp.where(row % 4 == 0, wide + above, wide),
        jnp.where(row % 4 == 3, wide + below, wide),
        jnp.where(place % 4 == 0, wide + left, wide),
        jnp.where(place % 4 == 3, wide + right, wide),
    )
    above, below = shifted(wide_z1, 0, pick(up, 0.0, zy_z1), pick(up, zy_z1, 0.0))
    total = toward * swap_lanes(part(z1b, b.uy)) + k * roll(sides, -X2, 1)
    total = total + w[0] * above + w[1] * below + w[2] * roll(wide_z1, 2, 1) + w[3] * roll(wide_z1, -2, 1)
    diagonal = sigma + (k + toward) + ((w[0] + w[1]) + (w[2] + w[3]))
    for j, value in enumerate((part(uhb, b.uy) + (2.0 - DAMPING) * sides, total, diagonal, k)):
        out_ref[to.y + j * Z : to.y + (j + 1) * Z, :] = value


def last_halo(p, coef, beyond_ref, last_in):
    X, Z, Y, to = p.X, p.Z, p.Y, Beyond(p)
    bx, bz = lax.axis_index("bx"), lax.axis_index("bz")
    odd, up = bx % 2 == 1, bz == 0
    start, end, X2 = Sends(p).second, Sends(p).corner, 2 * X
    z1, z2 = (last_in[start + k * Z : start + (k + 1) * Z, :].astype(F32) for k in range(2))
    block = unfold(last_in[start + 2 * Z : end, :])
    corner = last_in[end : end + 16, :].astype(F32)
    corner_z1, corner_kap = corner[0:1], lookup(corner[1:2], coef, 0)
    block_kap = lookup(block, coef, 0)
    row, lane = iota((Z, Y), 0), iota((Z, Y), 1)

    k, toward, diagonal, own, old = (rows_at(beyond_ref, to.core + j * Z, Z) for j in range(5))
    ends = lambda value, first: [pick(odd, value[:, first + X2 - 2 + c : first + X2 - 1 + c], value[:, first + c : first + c + 1]) for c in (0, 1)]
    col_kap, col_z1 = ends(block_kap, X2), ends(block, 0)
    w = plane_weights(k, pick(up, 0.0, corner_kap), pick(up, corner_kap, 0.0), col_kap[0], col_kap[1])
    total = toward * own
    total = total + jnp.where(row == pick(up, Z - 1, 0), pick(up, w[1], w[0]) * corner_z1, 0.0)
    total = total + jnp.where(lane == 0, w[2] * col_z1[0], 0.0) + jnp.where(lane == Y - 1, w[3] * col_z1[1], 0.0)
    diagonal = diagonal + ((w[0] + w[1]) + (w[2] + w[3]))
    core = (k, old + z2 + (DAMPING / diagonal) * total)
    value, total, diagonal, k = (rows_at(beyond_ref, to.z + j * X, X) for j in range(4))
    edge = iota((X, Y), 0) == pick(odd, 0, X - 1)
    total = total + jnp.where(edge, (k + corner_kap) * corner_z1, 0.0)
    diagonal = diagonal + jnp.where(edge, corner_kap, 0.0)
    z = (k, value + (DAMPING / diagonal) * total)

    value, total, diagonal, k = (rows_at(beyond_ref, to.y + j * Z, Z) for j in range(4))
    begin = pick(odd, 0, X2 - 2)
    edge = (lane >= begin) & (lane < begin + 2)
    reach = lambda value, shift: pick(odd, roll(value, 2 - X2 + shift, 1), roll(value, X2 - 2 + shift, 1))
    edge_kap = reach(block_kap, -X2)
    total = total + jnp.where(edge, (k + edge_kap) * reach(block, 0), 0.0)
    diagonal = diagonal + jnp.where(edge, edge_kap, 0.0)
    return z1, core, z, (k, value + (DAMPING / diagonal) * total)


def finish_staged(p, brick, s_ref, beyond_ref, parts, nodes, side, u_ref):
    X, Z, to = p.X, p.Z, Beyond(p)
    bx, bz = lax.axis_index("bx"), lax.axis_index("bz")
    odd, up = bx % 2 == 1, bz == 0
    some = (bx > 0) & (bx < p.nx - 1)
    z1, core, z, y = parts
    for i in range(X):
        value = s_ref[i] + nodes[i * Z : (i + 1) * Z]
        if i in (0, X - 1):
            weight = brick.x_weights(i)[0 if i == 0 else 1]
            here = odd if i == 0 else jnp.logical_not(odd)
            value = value + brick.damp(i) * (weight * pick(here, z1, 0.0))
        u_ref[i] = value
    at = X * Z
    below, above = nodes[at : at + Z], nodes[at + Z : at + 2 * Z]
    core = jnp.where(core[0] > 0.0, core[1] + pick(odd, below, above), 0.0)
    cross = pick(some, rows_at(beyond_ref, to.cross, Z) + pick(odd, above, below), 0.0)
    at += 2 * Z
    z = jnp.where(z[0] > 0.0, z[1] + pick(up, nodes[at + X : at + 2 * X], nodes[at : at + X]), 0.0)
    y = jnp.where(y[0] > 0.0, y[1] + side, 0.0)
    return pick(odd, core, cross), pick(odd, cross, core), pick(up, 0.0, z), pick(up, z, 0.0), y


def coarse_staged(p, own_ref, last_in, inverse, kx, kxi, zi, along_y, pall, pyh):
    Y, NY = p.Y, p.NY
    bx, bz = lax.axis_index("bx"), lax.axis_index("bz")
    rows, step, count = p.cx * p.NZ, p.cx * LOW, p.NX * LOW
    back = kxi[pl.ds(pl.multiple_of(bx * step, 16), step + 2 * LOW), :]
    table = kx[bx]
    parts = []
    for h in range(p.NZ // LOW):
        lines = []
        for ref in (own_ref, last_in):
            for block in range(2):
                at = [(block * (NY // Y) + k) * rows + h * step for k in range(NY // Y)]
                lines.append(jnp.concatenate([ref[i : i + step, :] for i in at], axis=1))
        parts.append(dot(table, jnp.concatenate(lines, axis=0)))
    parts = [(value * inverse[h * count : (h + 1) * count, :]).astype(BF16) for h, value in enumerate(parts)]
    values = dot(back, jnp.concatenate(parts, axis=1)).astype(BF16)
    values = jnp.concatenate([values[:, h * NY : (h + 1) * NY] for h in range(len(parts))], axis=0)
    values = dot(zi[bz], values).astype(BF16)
    values = dot(jnp.concatenate([values, values], axis=1), along_y[...])
    count = pall.shape[0] - p.Z
    nodes = dot_wide_right(pall[:count, : p.lanes + p.extra], values[:, :Y]) * (1.0 / 27.0)
    ends = values[: p.lanes, Y:]
    spread = ends[:, 0:1] * pyh[: p.lanes].astype(F32) + ends[:, 1:2] * pyh[p.lanes :].astype(F32)
    side = dot_wide_right(pall[count:, : p.lanes], spread) * (1.0 / 27.0)
    return nodes, side


def inverse_kernel(p, coef, lam_xz, lam_y, sy, pye, out_ref, along_ref):
    classes = coef.shape[1]
    kap_mean = sum(coef[0, k] for k in range(classes)) * (1.0 / classes)
    sig_mean = sum(coef[1, k] for k in range(classes)) * (1.0 / classes)
    step = p.NX * LOW
    for h in range(p.NZ // LOW):
        lam = lam_xz[h * step : (h + 1) * step, :] + lam_y[...]
        out_ref[h * step : (h + 1) * step, :] = 1.0 / (kap_mean * lam + sig_mean)
    rows = sy[pl.ds(pl.multiple_of(lax.axis_index("by") * p.cy, 16), p.cy + 16), :]
    high, low = halves(dot(rows.T, pye[...]))
    along_ref[: p.NY, :] = high
    along_ref[p.NY :, :] = low


def first_staged(p, coef, u_ref, r_ref, cls_ref, cst0_ref, xa, xb, za, zb, ya, yb, rxz, ry,
                 a_ref, z_ref, uhb_ref, clsb_ref, cst_ref, r_scr):
    brick, residual = neighbours_in(p, coef, u_ref, r_ref, cst0_ref, xa, xb, za, zb, ya, yb, uhb_ref, clsb_ref, cst_ref)
    go_on(p, brick, residual, rxz, ry, a_ref, z_ref, r_scr)


def correct(p, coef, s_ref, beyond_ref, cst_ref, own, last_in, inverse, kx, kxi, zi, along_y, pall, pyh, u_ref):
    b, at = Bounds(p), Beyond(p).kap
    brick = Brick(p, cst_ref, rows_at(beyond_ref, at + b.uxm[0], p.Z), rows_at(beyond_ref, at + b.uxp[0], p.Z))
    parts = last_halo(p, coef, beyond_ref, last_in)
    nodes, side = coarse_staged(p, own, last_in, inverse, kx, kxi, zi, along_y, pall, pyh)
    return brick, finish_staged(p, brick, s_ref, beyond_ref, parts, nodes, side, u_ref)


def middle_staged(p, coef, f_ref, s_ref, beyond_ref, cst_ref, own, last_in, inverse, kx, kxi, zi, along_y, pall, pyh, rxz, ry,
                  a_ref, z_ref, uhb_out, u_out, r_scr):
    brick, halo = correct(p, coef, s_ref, beyond_ref, cst_ref, own, last_in, inverse, kx, kxi, zi, along_y, pall, pyh, u_out)
    write_bounds(uhb_out, Bounds(p), halo)
    residual = lambda i: residual_plane(brick, i, lambda k: u_out[k], halo, f_ref[i])
    go_on(p, brick, residual, rxz, ry, a_ref, z_ref, r_scr)


def last_staged(p, coef, f_ref, s_ref, beyond_ref, cst_ref, own, last_in, inverse, kx, kxi, zi, along_y, pall, pyh,
                u_out, r_out, u_scr, r_scr, sems):
    brick, halo = correct(p, coef, s_ref, beyond_ref, cst_ref, own, last_in, inverse, kx, kxi, zi, along_y, pall, pyh, u_scr)
    copies = [pltpu.make_async_copy(u_scr, u_out, sems.at[0])]
    copies[0].start()
    chunk = p.X // 4
    for k in range(4):
        for i in range(k * chunk, (k + 1) * chunk):
            r_scr[i] = residual_plane(brick, i, lambda j: u_scr[j], halo, f_ref[i])
        part = pl.ds(k * chunk, chunk)
        copies.append(pltpu.make_async_copy(r_scr.at[part], r_out.at[part], sems.at[k + 1]))
        copies[-1].start()
    for copy in copies:
        copy.wait()


def call(kernel, p, name, coef, inputs, outputs, scratch, us=2, out_space=pltpu.VMEM):
    smem = [pl.BlockSpec(memory_space=pltpu.SMEM)] if coef is not None else []
    args = ([coef] if coef is not None else []) + list(inputs)
    return pl.pallas_call(
        functools.partial(kernel, p),
        out_shape=[jax.ShapeDtypeStruct(shape, dtype) for shape, dtype in outputs],
        in_specs=smem + [pl.BlockSpec(memory_space=pltpu.VMEM)] * len(inputs),
        out_specs=[pl.BlockSpec(memory_space=out_space)] * len(outputs),
        scratch_shapes=[pltpu.VMEM(shape, F32) if isinstance(shape, tuple) else shape for shape in scratch],
        compiler_params=pltpu.CompilerParams(vmem_limit_bytes=VMEM_LIMIT),
        cost_estimate=pl.CostEstimate(flops=0, bytes_accessed=us * 3_600_000, transcendentals=0),
        name=name,
    )(*args)


def swaps(axis, count, a, b, near=None):
    if count == 1:
        return a, b
    assert count % 2 == 0
    first = lax.ppermute(a, axis, [(i, i ^ 1) for i in range(count)])
    if count == 2:
        return first, first
    other = lambda i: (i + 1 if i % 2 else i - 1) % count
    if near is None:
        return first, lax.ppermute(b, axis, [(i, other(i)) for i in range(count)])
    name, size = near
    pairs = []
    for k in range(size):
        for i in range(count):
            to = (k ^ 1, i) if i in (0, count - 1) else (k, other(i))
            pairs.append((k * count + i, to[0] * count + to[1]))
    return first, lax.ppermute(b, (name, axis), pairs)


def body(forcing, start, element_class_index, class_coef):
    p = Plan(start.shape, *(lax.axis_size(axis) for axis in AXES))
    t = tables(p)
    X, Z, Y, n = p.X, p.Z, p.Y, p.n
    bounds = Bounds(p).count
    block, flat, cst = (X, Z, Y), (X * Z, Y), (DAMP, X // 4, Z, Y)
    (uy,) = call(sides_kernel, p, "start_sides", None, (start,), [((Z, Y), F32)], [], us=20)
    cls, xa, xb, za, zb, yf = call(
        pack_kernel, p, "pack_faces", None, (element_class_index, start, uy),
        [((X // 4, Z, Y), F32)] + [((2 * Z, Y), F32)] * 2 + [((2 * max(X, Z), Y), F32)] * 2 + [((2 * Z, Y), F32)], [], us=20,
    )
    xa, xb = swaps("bx", p.nx, xa, xb)
    za, zb = swaps("bz", p.nz, za, zb)
    ya, yb = swaps("by", p.ny, yf, yf, ("bx", p.nx) if p.nx % 2 == 0 else None)
    go_shape, back_shape = (n * p.go, Y), (n * p.back, Y)
    starting = [flat, block, block, go_shape]
    rxz, ry, sy = t["rxz"], t["ry"], t["sy"]
    cst0, r0 = call(prepare_kernel, p, "prepare", class_coef, (start, forcing, cls), [(cst, F32), (block, F32)], [], us=6)
    if p.staged:
        return staged_cycles(p, t, class_coef, forcing, cls, start, r0, cst0, (xa, xb, za, zb, ya, yb))
    go, s, z1b, uhb, clsb, coefs = call(
        first_kernel, p, "first_residual", class_coef,
        (start, r0, cls, cst0, xa, xb, za, zb, ya, yb, rxz, ry, sy),
        [(go_shape, BF16), (block, F32), ((bounds, Y), F32), ((bounds, Y), F32), ((bounds, Y), F32), ((QUANTITIES,) + cst[1:], F32)],
        starting,
    )
    prolong = (sy, t["pyt"], t["pall"], t["pyh"])
    first = None
    for cycle in range(CYCLES):
        came = lax.all_to_all(go, AXES, split_axis=0, concat_axis=0, tiled=True)
        (out,) = call(
            owner_kernel, p, "owned_modes", class_coef,
            (came, t["wz"], t["wx"], t["wxt"], t["wzi"], t["lamxz"], t["lamy"]),
            [(back_shape, BF16)], [go_shape, back_shape],
        )
        back = lax.all_to_all(out, AXES, split_axis=0, concat_axis=0, tiled=True)
        if cycle + 1 < CYCLES:
            assert first is None
            first = back
            go, s, z1b, uhb = call(
                middle_kernel, p, "next_residual", class_coef,
                (back, forcing, s, z1b, uhb, clsb, coefs) + prolong + (rxz, ry),
                [(go_shape, BF16), (block, F32), ((bounds, Y), F32), ((bounds, Y), F32)],
                [back_shape, block] + starting,
            )
        else:
            return tuple(call(
                last_kernel, p, "last_residual", class_coef,
                (back, first, forcing, s, z1b, uhb, clsb, coefs) + prolong,
                [(block, F32), (block, F32)], [back_shape, back_shape],
            ))


def staged_cycles(p, t, class_coef, forcing, cls, u, r0, cst0, faces_in):
    X, Z, Y = p.X, p.Z, p.Y
    sends, bounds = Sends(p), (Bounds(p).count, Y)
    block, flat = (X, Z, Y), (X * Z, Y)
    out = [((sends.first, Y), BF16), (block, F32), (bounds, F32)]
    inverse, along_y = call(
        inverse_kernel, p, "inverse_spectrum", class_coef, (t["lam_xz"], t["lam_y"], t["sy"], t["pye"]),
        [((p.NZ * p.NX, p.NY), F32), ((2 * p.NY, 2 * Y), BF16)], [],
    )
    a, z1, uhb, clsb, coefs = call(
        first_staged, p, "first_residual", class_coef, (u, r0, cls, cst0) + faces_in + (t["rxz"], t["ry"]),
        out + [(bounds, F32), ((QUANTITIES,) + cst0.shape[1:], F32)], [flat],
    )
    pairs = lambda count, d: [(i, i ^ d) for i in range(count)]
    for cycle in range(CYCLES):
        came = [a] + [lax.ppermute(a, "by", pairs(p.ny, d)) for d in distances(p.ny)]
        s, z1b, faces = call(
            smooth_kernel, p, "smooth", None, (u, z1, coefs),
            [(block, F32), (bounds, F32), ((sends.faces, Y), BF16)], [block],
        )
        x, z, xz, sides = call(
            after_first, p, "y_modes", None, (*came, faces, clsb, cls, t["sy"]),
            [((rows, Y), BF16) for rows in (sends.x_rows, sends.z_rows, sends.xz_rows)] + [((Z, Y), F32)],
            [pltpu.VMEM((p.NY, Y), BF16)],
        )
        plane, across = p.nx * p.nz, (p.nx - 1) * p.nz
        x_in = lax.ppermute(x, ("bx", "bz"), pairs(plane, across))
        z_in = lax.ppermute(z, ("bx", "bz"), pairs(plane, 1))
        xz_in = lax.ppermute(xz, ("bx", "bz"), pairs(plane, across + 1))
        if cycle == 0:
            x_in, inverse, along_y = lax.optimization_barrier((x_in, inverse, along_y))
            back = (inverse, t["kx"], t["kxi"], t["zi"], along_y, t["pall"], t["pyh"])
        (own,) = call(
            after_second, p, "z_modes", None, (x, x_in, z_in, xz_in, faces, clsb, sides, t["wzt"]),
            [((sends.last, Y), BF16)], [],
        )
        last_in = lax.ppermute(own, "bx", pairs(p.nx, 1))
        s, beyond = call(
            beyond_kernel, p, "beyond", class_coef, (s, z1b, uhb, clsb, cls, coefs, sides, x_in, z_in, xz_in),
            [(block, F32), ((Beyond(p).count, Y), F32)], [],
        )
        inputs = (forcing, s, beyond, coefs, own, last_in) + back
        if cycle + 1 < CYCLES:
            a, z1, uhb, u = call(
                middle_staged, p, "next_residual", class_coef, inputs + (t["rxz"], t["ry"]), out + [(block, F32)], [flat]
            )
        else:
            return tuple(call(
                last_staged, p, "last_residual", class_coef, inputs, [(block, F32), (block, F32)],
                [block, block, pltpu.SemaphoreType.DMA((5,))], out_space=pl.ANY,
            ))


def solution(mesh):
    spec = P("bx", "bz", "by")
    return jax.shard_map(body, mesh=mesh, in_specs=(spec, spec, spec, P()), out_specs=(spec, spec), check_vma=False)
```

```python
import functools
import math

import jax
import jax.numpy as jnp
import numpy as np
from jax import lax
from jax.experimental import pallas as pl
from jax.experimental.pallas import tpu as pltpu
from jax.sharding import PartitionSpec as P

CYCLES = 2
DAMPING = 0.6666666666666666
F32 = jnp.float32
BF16 = jnp.bfloat16
AXES = ("bx", "by", "bz")
VMEM_LIMIT = 32 * 1024 * 1024


def up_to(value, multiple):
    return -(-value // multiple) * multiple


class Plan:
    def __init__(self, shape, nx, ny, nz):
        self.X, self.Z, self.Y = shape
        self.nx, self.ny, self.nz = nx, ny, nz
        self.n = nx * ny * nz
        self.cx, self.cz, self.cy = self.X // 2, self.Z // 2, self.Y // 2
        self.NX, self.NZ, self.NY = self.cx * nx, self.cz * nz, self.cy * ny
        self.modes = -(-self.NY // self.n)
        self.NYp = self.modes * self.n
        self.lanes = self.cx * self.cz
        rows = (2 * self.Z, 2 * self.Z, 2 * self.X, 2 * self.X, self.Z, 12)
        self.heights = [-(-r // self.n) for r in rows]
        self.offsets = [sum(self.heights[:i]) for i in range(6)]
        halo = sum(self.heights)
        self.go_halo = self.modes
        self.go = up_to(self.modes + halo, 8)
        self.back_halo = 2 * self.modes
        self.back = up_to(2 * self.modes + halo, 8)
        self.edge_lane = 6 * self.X
        self.extra = 2 * self.cz + 2 * self.cx
        self.staged = nx == 4 and nz == 2 and ny & (ny - 1) == 0 and self.NZ % LOW == 0 and 8 * self.X <= self.Y
        assert self.lanes <= self.Y and self.extra <= self.lanes and self.edge_lane + 8 <= self.Y
        assert self.heights[5] == 1


def sine_table(count):
    index_one = np.arange(1, count + 1, dtype=np.int32)
    product = (index_one[:, None] * index_one[None, :]).astype(np.float32)
    value = np.sin(product * np.float32(math.pi / (count + 1)))
    return (value * np.float32(math.sqrt(2.0 / (count + 1)))).astype(BF16).astype(np.float32)


def spectrum_values(count):
    return 2.0 - 2.0 * np.cos(np.arange(1, count + 1) * (math.pi / (count + 1)))


RESTRICT = np.array([[3, 2, 1, 0], [0, 1, 2, 3]], np.float32)
PROLONG = np.array([[3, 0], [2, 1], [1, 2], [0, 3]], np.float32)


LOW = 8


def staged_tables(p, sx, sz, py):
    high, eye = p.NZ // LOW, np.eye(LOW)
    out = {}
    wzt = np.zeros((high, p.cx, LOW, p.nz, p.cx, p.cz), np.float32)
    for x in range(p.cx):
        wzt[:, x, :, :, x, :] = sz.reshape(high, LOW, p.nz, p.cz)
    out["wzt"] = wzt.reshape(p.cx * p.NZ, p.nz * p.lanes)
    blocks = sx.reshape(p.NX, p.nx, p.cx)
    order = lambda b: [b, b ^ 3, b ^ 1, b ^ 2]
    out["kx"] = np.stack([np.kron(blocks[:, order(b)].reshape(p.NX, p.NX), eye) for b in range(p.nx)])
    sxp = np.zeros((p.NX + 2, p.NX), np.float32)
    sxp[1:-1] = sx
    out["kxi"] = np.kron(sxp, eye)
    szp = np.zeros((p.NZ + 2, p.NZ), np.float32)
    szp[1:-1] = sz
    zi = np.zeros((p.nz, p.lanes + p.extra, high, p.cx + 2, LOW), np.float32)
    for b in range(p.nz):
        mine = szp[b * p.cz + 1 : (b + 1) * p.cz + 1].reshape(p.cz, high, LOW)
        for x in range(p.cx):
            zi[b, x * p.cz : (x + 1) * p.cz, :, x + 1, :] = mine
            zi[b, p.lanes + 2 * p.cz + x, :, x + 1, :] = szp[b * p.cz].reshape(high, LOW)
            zi[b, p.lanes + 2 * p.cz + p.cx + x, :, x + 1, :] = szp[(b + 1) * p.cz + 1].reshape(high, LOW)
        zi[b, p.lanes : p.lanes + p.cz, :, 0, :] = mine
        zi[b, p.lanes + p.cz : p.lanes + 2 * p.cz, :, p.cx + 1, :] = mine
    out["zi"] = zi.reshape(p.nz, p.lanes + p.extra, -1)
    pye = np.zeros((p.cy + 16, 2 * p.Y), np.float32)
    pye[8 : 8 + p.cy, : p.Y] = py.T
    pye[7, p.Y] = pye[8 + p.cy, p.Y + 1] = 1
    out["pye"] = pye
    return out


def tables(p):
    rx = np.kron(np.eye(p.X // 4), RESTRICT)
    rz = np.kron(np.eye(p.Z // 4), RESTRICT)
    ry = np.kron(np.eye(p.Y // 4), RESTRICT)
    px = np.kron(np.eye(p.X // 4), PROLONG)
    pz = np.kron(np.eye(p.Z // 4), PROLONG)
    py = np.kron(np.eye(p.Y // 4), PROLONG)
    sx, sz, sy = sine_table(p.NX), sine_table(p.NZ), sine_table(p.NY)
    out = {}
    out["rxz"] = np.kron(rx, rz)
    out["ry"] = ry
    padded = np.zeros((p.NY + 16, p.NYp), np.float32)
    padded[8 : 8 + p.NY, : p.NY] = sy
    out["sy"] = padded
    wz = np.zeros((p.cx, p.NZ, p.nz, p.cx, p.cz), np.float32)
    for x in range(p.cx):
        wz[x, :, :, x, :] = sz.reshape(p.NZ, p.nz, p.cz)
    out["wz"] = wz.reshape(p.cx * p.NZ, p.nz * p.lanes)
    wx = np.einsum("bxk,mn->xbmkn", sx.reshape(p.nx, p.cx, p.NX), np.eye(p.modes))
    wx = wx.reshape(p.NX * p.modes, p.NX * p.modes)
    out["wx"], out["wxt"] = wx, wx.T
    szp = np.zeros((p.NZ, p.NZ + 2), np.float32)
    szp[:, 1:-1] = sz
    wzi = np.zeros((p.nz, p.cx, p.NZ, 2 * p.lanes), np.float32)
    for b in range(p.nz):
        for x in range(p.cx):
            wzi[b, x, :, x * p.cz : (x + 1) * p.cz] = sz[:, b * p.cz : (b + 1) * p.cz]
            wzi[b, x, :, p.lanes + x] = szp[:, b * p.cz]
            wzi[b, x, :, p.lanes + p.cx + x] = szp[:, (b + 1) * p.cz + 1]
    out["wzi"] = wzi.reshape(p.nz, p.cx * p.NZ, 2 * p.lanes)
    out["pyt"] = py.T
    pall = np.zeros((p.X * p.Z + 2 * p.Z + 2 * p.X, 2 * p.lanes), np.float32)
    at = p.X * p.Z
    pall[:at, : p.lanes] = np.kron(px, pz)
    col = p.lanes
    for _ in range(2):
        pall[at : at + p.Z, col : col + p.cz] = 3 * pz
        at, col = at + p.Z, col + p.cz
    for _ in range(2):
        pall[at : at + p.X, col : col + p.cx] = 3 * px
        at, col = at + p.X, col + p.cx
    out["pall"] = np.concatenate([pall, np.tile(pz, (1, 2 * p.cx))])
    pyh = np.zeros((2, p.lanes, p.Y), np.float32)
    spread = np.repeat(px.T, p.cz, axis=0)
    for side in range(2):
        pyh[side, :, side : 2 * p.X : 2] = 3 * spread
    out["pyh"] = pyh.reshape(2 * p.lanes, p.Y)
    if p.staged:
        out.update(staged_tables(p, sx, sz, py))
    out = {key: jnp.asarray(value.astype(BF16)) for key, value in out.items()}
    if p.staged:
        lam = spectrum_values(p.NX)[None, :, None] + spectrum_values(p.NZ).reshape(-1, 1, LOW)
        out["lam_xz"] = jnp.asarray(lam.reshape(-1, 1).astype(np.float32))
        out["lam_y"] = jnp.asarray(spectrum_values(p.NY).reshape(1, -1).astype(np.float32))
        return out
    lam = spectrum_values(p.NX)[None, :, None] + spectrum_values(p.NZ)[:, None, None]
    out["lamxz"] = jnp.asarray(np.broadcast_to(lam, (p.NZ, p.NX, p.modes)).reshape(p.NZ, -1).astype(np.float32))
    lamy = np.zeros(p.NYp)
    lamy[: p.NY] = spectrum_values(p.NY)
    lamy = np.broadcast_to(lamy.reshape(p.n, 1, 1, p.modes), (p.n, 1, p.NX, p.modes))
    out["lamy"] = jnp.asarray(lamy.reshape(p.n, 1, -1).astype(np.float32))
    return out


def iota(shape, dim):
    return lax.broadcasted_iota(jnp.int32, shape, dim)


def dot(a, b, dims=((1,), (0,))):
    return lax.dot_general(a, b, (dims, ((), ())), preferred_element_type=F32)


def halves(value):
    high = value.astype(BF16)
    return high, (value - high.astype(F32)).astype(BF16)


def dot_wide_right(table, value, dims=((1,), (0,))):
    axis = 1 - dims[1][0]
    count = value.shape[axis]
    both = dot(table, jnp.concatenate(halves(value), axis=axis), dims)
    return both[:, :count] + both[:, count:]


def dot_wide_left(value, table, dims=((1,), (0,))):
    high, low = halves(value)
    return dot(high, table, dims) + dot(low, table, dims)


def roll(value, shift, axis):
    size = value.shape[axis]
    shift = shift % size
    return value if shift == 0 else pltpu.roll(value, shift, axis)


def lookup(classes, coef_ref, row):
    total = jnp.zeros_like(classes)
    for k in range(coef_ref.shape[1]):
        total = jnp.where(classes == k + 1.0, coef_ref[row, k], total)
    return total


def col_faces(get, p):
    lane = iota((p.Z, p.Y), 1) // 2
    total = jnp.zeros((p.Z, p.Y), F32)
    for i in range(p.X):
        total = jnp.where(lane == i, roll(get(i), 2 * i + 1, 1), total)
    return total


def swap_lanes(value):
    even = iota(value.shape, 1) % 2 == 0
    return jnp.where(even, roll(value, -1, 1), roll(value, 1, 1))


def shifted(value, axis, before, after):
    size = value.shape[axis]
    at = iota(value.shape, axis)
    low = jnp.where(at == 0, before, roll(value, 1, axis))
    high = jnp.where(at == size - 1, after, roll(value, -1, axis))
    return low, high


def plane_weights(kap, row_m, row_p, col_m, col_p):
    up, down = shifted(kap, 0, row_m, row_p)
    left, right = shifted(kap, 1, col_m, col_p)
    row, lane = iota(kap.shape, 0) % 4, iota(kap.shape, 1) % 4
    return (
        jnp.where(row == 0, kap + up, kap),
        jnp.where(row == 3, kap + down, kap),
        jnp.where(lane == 0, kap + left, kap),
        jnp.where(lane == 3, kap + right, kap),
    )


KAP, WZM, WZP, WYM, WYP, BASE, BETA, DAMP = range(8)
QUANTITIES = DAMP + 3


class Brick:
    def __init__(self, p, cst_ref, kap_xm, kap_xp):
        self.p, self.cst, self.kap_xm, self.kap_xp = p, cst_ref, kap_xm, kap_xp

    def of(self, quantity, i):
        return self.cst[quantity, i // 4]

    def x_weights(self, i):
        kap = self.of(KAP, i)
        low = high = kap
        if i % 4 == 0:
            low = kap + (self.of(KAP, i - 1) if i else self.kap_xm)
        if i % 4 == 3:
            high = kap + (self.of(KAP, i + 1) if i + 1 < self.p.X else self.kap_xp)
        return low, high

    def diagonal(self, i):
        low, high = self.x_weights(i)
        return self.of(BASE, i) + (low + high)

    def damp(self, i):
        return self.cst[DAMP + (0 if i % 4 == 0 else 2 if i % 4 == 3 else 1), i // 4]

    def neighbours(self, i, get, halo=None):
        p, v = self.p, get(i)
        low, high = self.x_weights(i)
        total = jnp.zeros_like(v)
        if i:
            total = total + low * get(i - 1)
        elif halo is not None:
            total = total + low * halo[0]
        if i + 1 < p.X:
            total = total + high * get(i + 1)
        elif halo is not None:
            total = total + high * halo[1]
        if halo is None:
            ends = (0.0, 0.0, 0.0, 0.0)
        else:
            side = self.y_ends(halo[4], i)
            ends = (halo[2][i : i + 1], halo[3][i : i + 1], side, side)
        up, down = shifted(v, 0, ends[0], ends[1])
        left, right = shifted(v, 1, ends[2], ends[3])
        total = total + self.of(WZM, i) * up + self.of(WZP, i) * down
        return total + self.of(WYM, i) * left + self.of(WYP, i) * right

    def y_ends(self, yh, i):
        return roll(swap_lanes(yh), self.p.Y - 1 - 2 * i, 1)

    def from_halo(self, i, halo):
        p = self.p
        row, lane = iota((p.Z, p.Y), 0), iota((p.Z, p.Y), 1)
        side = self.y_ends(halo[4], i)
        total = jnp.where(row == 0, self.of(WZM, i) * halo[2][i : i + 1], 0.0)
        total = jnp.where(row == p.Z - 1, self.of(WZP, i) * halo[3][i : i + 1], total)
        total = total + jnp.where(lane == 0, self.of(WYM, i) * side, 0.0)
        total = total + jnp.where(lane == p.Y - 1, self.of(WYP, i) * side, 0.0)
        if i == 0:
            total = total + self.x_weights(i)[0] * halo[0]
        if i == p.X - 1:
            total = total + self.x_weights(i)[1] * halo[1]
        return total


def residual_plane(brick, i, get, halo, f):
    v = get(i)
    return f - brick.diagonal(i) * v + brick.neighbours(i, get, halo) - brick.of(BETA, i) * v * v * v


def put_rows(ref, stride, offset, n, rows):
    height = -(-rows.shape[0] // n)
    if rows.shape[0] < height * n:
        rows = jnp.concatenate([rows, jnp.zeros((height * n - rows.shape[0], rows.shape[1]), F32)], axis=0)
    for k in range(height):
        ref[pl.ds(offset + k, n, stride=stride), :] = rows[k * n : (k + 1) * n]


def get_rows(ref, stride, offset, n, count):
    height = -(-count // n)
    parts = [ref[pl.ds(offset + k, n, stride=stride), :] for k in range(height)]
    value = parts[0] if height == 1 else jnp.concatenate(parts, axis=0)
    return value[:count]


class Bounds:
    def __init__(self, p):
        self.uxm, self.uxp = (0, p.Z), (p.Z, p.Z)
        self.uzm, self.uzp = (2 * p.Z, p.X), (2 * p.Z + p.X, p.X)
        self.uy = (2 * p.Z + 2 * p.X, p.Z)
        self.count = 3 * p.Z + 2 * p.X


def read(ref, span):
    return ref[span[0] : span[0] + span[1], :]


def write_bounds(ref, b, values):
    for span, value in zip((b.uxm, b.uxp, b.uzm, b.uzp, b.uy), values):
        ref[span[0] : span[0] + span[1], :] = value


def read_bounds(ref, b):
    return tuple(read(ref, span) for span in (b.uxm, b.uxp, b.uzm, b.uzp, b.uy))


def advance(p, brick, get, residual, rxz, ry, s_ref, r_scr, z_scr, z2_scr):
    X, Z = p.X, p.Z
    for i in range(X):
        r = residual(i)
        r_scr[i * Z : (i + 1) * Z, :] = r
        z_scr[i] = r * brick.damp(i)
    z1 = lambda i: z_scr[i]
    coarse = dot_wide_right(rxz[...], r_scr[...])
    coarse = dot_wide_right(ry[...], coarse, ((1,), (1,))) * (1.0 / 216.0)
    for i in range(X):
        v = z1(i)
        smooth = (2.0 - DAMPING) * v + brick.damp(i) * brick.neighbours(i, z1)
        z2_scr[i] = smooth
        s_ref[i] = get(i) + smooth
    return coarse.astype(BF16)


def start_cycle(p, brick, get, residual, classes, rxz, ry, sy, s_ref, z1b_ref, go_ref, r_scr, z_scr, z2_scr, go_scr):
    X, Z, n = p.X, p.Z, p.n
    coarse = advance(p, brick, get, residual, rxz, ry, s_ref, r_scr, z_scr, z2_scr)
    z1 = lambda i: z_scr[i]
    rows = sy[pl.ds(pl.multiple_of(lax.axis_index("by") * p.cy + 8, 8), p.cy), :]
    part = dot(rows.T, coarse)
    for j in range(n):
        go_scr[j * p.go : j * p.go + p.modes, :] = part[j * p.modes : (j + 1) * p.modes]
    z2 = lambda i: z2_scr[i]
    z1_y, z2_y = col_faces(z1, p), col_faces(z2, p)
    z1_zm, z1_zp = z_scr[:, 0, :], z_scr[:, Z - 1, :]
    write_bounds(z1b_ref, Bounds(p), (z1(0), z1(X - 1), z1_zm, z1_zp, z1_y))
    lane = iota((Z, p.Y), 1)
    sides = jnp.where(lane < 2 * X, z1_y, roll(z2_y, 2 * X, 1))
    edges = [z_scr[0, 0:1, :], z_scr[0, Z - 1 : Z, :], z_scr[X - 1, 0:1, :], z_scr[X - 1, Z - 1 : Z, :]]
    edges += [z1_y[0:1], z1_y[Z - 1 : Z]]
    if classes is None:
        sides = jnp.where(lane < 4 * X, sides, 0.0)
    else:
        cls, cls_y = classes
        sides = jnp.where(lane < 4 * X, sides, roll(cls_y, 4 * X, 1))
        sides = jnp.where(lane < 6 * X, sides, 0.0)
        edges += [cls(0)[0:1], cls(0)[Z - 1 : Z], cls(X - 1)[0:1], cls(X - 1)[Z - 1 : Z]]
        edges += [cls_y[0:1], cls_y[Z - 1 : Z]]
    pieces = (
        jnp.concatenate([z1(0), z2(0)], axis=0),
        jnp.concatenate([z1(X - 1), z2(X - 1)], axis=0),
        jnp.concatenate([z1_zm, z2_scr[:, 0, :]], axis=0),
        jnp.concatenate([z1_zp, z2_scr[:, Z - 1, :]], axis=0),
        sides,
        jnp.concatenate(edges, axis=0),
    )
    for piece, offset in zip(pieces, p.offsets):
        put_rows(go_scr, p.go, p.go_halo + offset, n, piece)
    used = p.go_halo + sum(p.heights)
    for k in range(used, p.go):
        go_scr[pl.ds(k, n, stride=p.go), :] = jnp.zeros((n, p.Y), F32)
    go_ref[...] = go_scr[...].astype(BF16)


def sides_kernel(p, u_ref, y_ref):
    y_ref[...] = col_faces(lambda i: u_ref[i], p)


def pack_kernel(p, index_ref, u_ref, uy_ref, cls_ref, xa_ref, xb_ref, za_ref, zb_ref, y_ref):
    X, Z, Y = p.X, p.Z, p.Y
    spread_z = (iota((Z, Z // 4), 0) // 4 == iota((Z, Z // 4), 1)).astype(BF16)
    spread_y = (iota((Y // 4, Y), 1) // 4 == iota((Y // 4, Y), 0)).astype(BF16)
    for a in range(X // 4):
        element = (index_ref[a] + 1).astype(F32).astype(BF16)
        cls_ref[a] = dot(dot(spread_z, element).astype(BF16), spread_y)
    cls = lambda i: cls_ref[i // 4]

    def face(axis, low, high, a_ref, b_ref, at):
        even = lax.axis_index(axis) % 2 == 0
        count = low.shape[0]
        a_ref[at : at + count, :] = jnp.where(even, high, low)
        b_ref[at : at + count, :] = jnp.where(even, low, high)

    face("bx", u_ref[0], u_ref[X - 1], xa_ref, xb_ref, 0)
    face("bx", cls(0), cls(X - 1), xa_ref, xb_ref, Z)
    rows = lambda z: jnp.concatenate([cls(i)[z : z + 1] for i in range(X)], axis=0)
    face("bz", u_ref[:, 0, :], u_ref[:, Z - 1, :], za_ref, zb_ref, 0)
    face("bz", rows(0), rows(Z - 1), za_ref, zb_ref, X)
    if X < Z:
        za_ref[2 * X :, :] = zb_ref[2 * X :, :] = jnp.zeros((2 * (Z - X), Y), F32)
    y_ref[0:Z, :] = uy_ref[...]
    y_ref[Z : 2 * Z, :] = col_faces(cls, p)


def received(axis, count, a_ref, b_ref):
    at = lax.axis_index(axis)
    even = at % 2 == 0
    a, b = a_ref[...], b_ref[...]
    low = jnp.where(even, b, a)
    high = jnp.where(even, a, b)
    return jnp.where(at > 0, low, 0.0), jnp.where(at < count - 1, high, 0.0)


def prepare_kernel(p, coef, u_ref, f_ref, cls_ref, cst_ref, r_ref):
    for a in range(p.X // 4):
        kap = lookup(cls_ref[a], coef, 0)
        wzm, wzp, wym, wyp = plane_weights(kap, 0.0, 0.0, 0.0, 0.0)
        cst_ref[KAP, a] = kap
        cst_ref[WZM, a] = wzm
        cst_ref[WZP, a] = wzp
        cst_ref[WYM, a] = wym
        cst_ref[WYP, a] = wyp
        cst_ref[BASE, a] = lookup(cls_ref[a], coef, 1) + ((wzm + wzp) + (wym + wyp))
        cst_ref[BETA, a] = lookup(cls_ref[a], coef, 2)
    brick = Brick(p, cst_ref, 0.0, 0.0)
    get = lambda i: u_ref[i]
    for i in range(p.X):
        r_ref[i] = residual_plane(brick, i, get, None, f_ref[i])


def neighbours_in(p, coef, u_ref, r_ref, cst0_ref, xa, xb, za, zb, ya, yb, uhb_ref, clsb_ref, cst_ref):
    X, Z, Y, b = p.X, p.Z, p.Y, Bounds(p)
    xm, xp = received("bx", p.nx, xa, xb)
    zm, zp = (value[: 2 * X] for value in received("bz", p.nz, za, zb))
    ym, yp = received("by", p.ny, ya, yb)
    y = jnp.where(iota(ym.shape, 1) % 2 == 0, ym, yp)
    halo = (xm[:Z], xp[:Z], zm[:X], zp[:X], y[:Z])
    outside = (xm[Z:], xp[Z:], zm[X:], zp[X:], y[Z:])
    write_bounds(uhb_ref, b, halo)
    write_bounds(clsb_ref, b, outside)
    kap_h = tuple(lookup(value, coef, 0) for value in outside)
    row, lane = iota((Z, Y), 0), iota((Z, Y), 1)
    more = []
    for a in range(X // 4):
        i = 4 * a
        ends = (
            (WZM, jnp.where(row == 0, kap_h[2][i : i + 1], 0.0)),
            (WZP, jnp.where(row == Z - 1, kap_h[3][i : i + 1], 0.0)),
            (WYM, jnp.where(lane == 0, kap_h[4][:, 2 * i : 2 * i + 1], 0.0)),
            (WYP, jnp.where(lane == Y - 1, kap_h[4][:, 2 * i + 1 : 2 * i + 2], 0.0)),
        )
        for k, end in ends:
            cst_ref[k, a] = cst0_ref[k, a] + end
        more.append((ends[0][1] + ends[1][1]) + (ends[2][1] + ends[3][1]))
        cst_ref[BASE, a] = cst0_ref[BASE, a] + more[a]
        cst_ref[KAP, a] = cst0_ref[KAP, a]
        cst_ref[BETA, a] = cst0_ref[BETA, a]
    brick = Brick(p, cst_ref, kap_h[0], kap_h[1])
    for a in range(X // 4):
        for k, i in enumerate((4 * a, 4 * a + 1, 4 * a + 3)):
            cst_ref[DAMP + k, a] = DAMPING / brick.diagonal(i)

    def residual(i):
        added = more[i // 4]
        if i == 0:
            added = added + kap_h[0]
        if i == X - 1:
            added = added + kap_h[1]
        return r_ref[i] - added * u_ref[i] + brick.from_halo(i, halo)

    return brick, residual


def first_kernel(p, coef, u_ref, r_ref, cls_ref, cst0_ref, xa, xb, za, zb, ya, yb, rxz, ry, sy,
                 go_ref, s_ref, z1b_ref, uhb_ref, clsb_ref, cst_ref, r_scr, z_scr, z2_scr, go_scr):
    brick, residual = neighbours_in(p, coef, u_ref, r_ref, cst0_ref, xa, xb, za, zb, ya, yb, uhb_ref, clsb_ref, cst_ref)
    cls = lambda i: cls_ref[i // 4]
    start_cycle(p, brick, lambda i: u_ref[i], residual, (cls, col_faces(cls, p)), rxz, ry, sy,
                s_ref, z1b_ref, go_ref, r_scr, z_scr, z2_scr, go_scr)


def owner_kernel(p, coef, in_ref, wz, wx, wxt, wzi, lamxz, lamy, out_ref, in_scr, out_scr):
    n, m, nx, ny, nz = p.n, p.modes, p.nx, p.ny, p.nz
    me = (lax.axis_index("bx") * ny + lax.axis_index("by")) * nz + lax.axis_index("bz")
    in_scr[...] = in_ref[...].astype(F32)
    rows = []
    for bx in range(nx):
        lanes = []
        for bz in range(nz):
            total = None
            for by in range(ny):
                at = ((bx * ny + by) * nz + bz) * p.go
                piece = in_scr[at : at + m, :]
                total = piece if total is None else total + piece
            lanes.append(total)
        rows.append(jnp.concatenate(lanes, axis=1))
    data = jnp.concatenate(rows, axis=0)
    data = dot_wide_right(wz[...], data, ((1,), (1,)))
    data = jnp.concatenate([data[x * p.NZ : (x + 1) * p.NZ] for x in range(p.cx)], axis=1)
    data = dot_wide_left(data, wx[...])
    classes = coef.shape[1]
    kap_mean = sum(coef[0, k] for k in range(classes)) * (1.0 / classes)
    sig_mean = sum(coef[1, k] for k in range(classes)) * (1.0 / classes)
    data = data / (kap_mean * (lamxz[...] + lamy[me]) + sig_mean)
    data = dot_wide_left(data, wxt[...])
    width = nx * m
    data = jnp.concatenate([data[:, x * width : (x + 1) * width] for x in range(p.cx)], axis=0)
    high, low = halves(data)
    high, low = high.T, low.T
    lane = iota((m, p.Y), 1)
    for bz in range(nz):
        back = dot(high, wzi[bz]) + dot(low, wzi[bz])
        core = lambda bx: back[bx * m : (bx + 1) * m, : p.lanes]
        for bx in range(nx):
            ends = roll(back[bx * m : (bx + 1) * m, p.lanes :], 2 * p.cz, 1)
            below = roll(core(bx - 1), p.cz - p.lanes, 1) if bx else jnp.zeros((m, p.lanes), F32)
            above = roll(core(bx + 1), p.cz, 1) if bx + 1 < nx else jnp.zeros((m, p.lanes), F32)
            extra = jnp.where(lane < p.cz, below, jnp.where(lane < 2 * p.cz, above, ends))
            mine = core(bx)
            for by in range(ny):
                at = ((bx * ny + by) * nz + bz) * p.back
                out_scr[at : at + m, :] = mine
                out_scr[at + m : at + 2 * m, :] = extra

    device = iota((n, p.Y), 0)
    at_x, at_y, at_z = device // (ny * nz), (device // nz) % ny, device % nz

    def shift(value, dx, dy, dz):
        value = roll(value, -((dx * ny + dy) * nz + dz), 0)
        for at, step, count in ((at_x, dx, nx), (at_y, dy, ny), (at_z, dz, nz)):
            if step:
                value = jnp.where((at + step >= 0) & (at + step < count), value, 0.0)
        return value

    def take(k):
        return in_scr[pl.ds(p.go_halo + k, n, stride=p.go), :]

    def give(k, value):
        out_scr[pl.ds(p.back_halo + k, n, stride=p.back), :] = value

    for to, source, step in ((0, 1, (-1, 0, 0)), (1, 0, (1, 0, 0)), (2, 3, (0, 0, -1)), (3, 2, (0, 0, 1))):
        for k in range(p.heights[to]):
            give(p.offsets[to] + k, shift(take(p.offsets[source] + k), *step))
    lane = iota((n, p.Y), 1)
    even = lane % 2 == 0
    first, X2 = p.edge_lane, 2 * p.X
    for k in range(p.heights[4]):
        sides = take(p.offsets[4] + k)
        moved = jnp.where(lane < first + 2, roll(sides, first, 1), roll(sides, first + 2 - (X2 - 2), 1))
        moved = jnp.where(lane < first + 4, moved, roll(sides, first + 4 - 2 * X2, 1))
        moved = jnp.where(lane < first + 6, moved, roll(sides, first + 6 - (3 * X2 - 2), 1))
        which = (lane - first) % 4
        corner = jnp.where(
            which < 2,
            jnp.where(even, shift(moved, 1, -1, 0), shift(moved, 1, 1, 0)),
            jnp.where(even, shift(moved, -1, -1, 0), shift(moved, -1, 1, 0)),
        )
        plain = jnp.where(even, shift(sides, 0, -1, 0), shift(sides, 0, 1, 0))
        give(p.offsets[4] + k, jnp.where(lane < first, plain, jnp.where(lane < first + 8, corner, 0.0)))
    edges = take(p.offsets[5])
    kind = me % 6
    moved = jnp.where(even, shift(edges, 0, -1, -1), shift(edges, 0, 1, -1))
    for k, value in (
        (0, lambda: shift(edges, 1, 0, 1)),
        (1, lambda: shift(edges, 1, 0, -1)),
        (2, lambda: shift(edges, -1, 0, 1)),
        (3, lambda: shift(edges, -1, 0, -1)),
        (4, lambda: jnp.where(even, shift(edges, 0, -1, 1), shift(edges, 0, 1, 1))),
    ):
        moved = jnp.where(kind == k, value(), moved)
    give(p.offsets[5], moved)
    used = p.back_halo + sum(p.heights)
    for k in range(used, p.back):
        out_scr[pl.ds(k, n, stride=p.back), :] = jnp.zeros((n, p.Y), F32)
    out_ref[...] = out_scr[...].astype(BF16)


class Arrived:
    def __init__(self, p, ref):
        X, Z = p.X, p.Z
        rows = (2 * Z, 2 * Z, 2 * X, 2 * X, Z, 12)
        xm, xp, zm, zp, sides, edges = (
            get_rows(ref, p.back, p.back_halo + offset, p.n, count) for offset, count in zip(p.offsets, rows)
        )
        self.p, self.ref, self.sides, self.edges = p, ref, sides, edges
        self.z1 = (xm[:Z], xp[:Z], zm[:X], zp[:X], sides)
        self.z2 = (xm[Z:], xp[Z:], zm[X:], zp[X:], roll(sides, -2 * X, 1))

    def xz(self, kind, sx, sz):
        k = 6 * kind + (0 if sx else 2) + (0 if sz else 1)
        return self.edges[k : k + 1]

    def zy(self, kind, sz):
        k = 6 * kind + (4 if sz else 5)
        return self.edges[k : k + 1]

    def xy(self, kind, sx, sy):
        lane = self.p.edge_lane + 4 * kind + (0 if sx else 2) + sy
        return self.sides[:, lane : lane + 1]

    def xy_lanes(self, kind, plain):
        first, X2 = self.p.edge_lane + 4 * kind, 2 * self.p.X
        lane = iota(plain.shape, 1)
        value = jnp.where(lane < X2, plain, roll(self.sides, X2 - first, 1))
        return jnp.where(lane >= self.p.Y - 2, roll(self.sides, self.p.Y - 2 - first - 2, 1), value)


def coarse_rows(p, ref, sy, pyt, pall, pyh):
    n, m = p.n, p.modes
    core = jnp.concatenate([ref[j * p.back : j * p.back + m, :] for j in range(n)], axis=0)
    extra = jnp.concatenate([ref[j * p.back + m : j * p.back + 2 * m, :] for j in range(n)], axis=0)
    modes = jnp.concatenate([core, extra], axis=1).astype(BF16)
    rows = sy[pl.ds(pl.multiple_of(lax.axis_index("by") * p.cy, 8), p.cy + 16), :]
    values = dot(rows, modes).astype(BF16)
    along = dot(values[8 : 8 + p.cy].T, pyt[...])
    count = pall.shape[0] - p.Z
    nodes = dot_wide_right(pall[:count], along) * (1.0 / 27.0)
    weights = pall[count:, : p.lanes].astype(F32)
    ends = [weights * values.astype(F32)[k : k + 1, : p.lanes] for k in (7, 8 + p.cy)]
    side = dot_wide_left(jnp.concatenate(ends, axis=1), pyh[...]) * (1.0 / 27.0)
    return nodes, side


def column(row, count, side):
    shape = (count, row.shape[1])
    pick = iota(shape, 1) == 2 * iota(shape, 0) + side
    return jnp.sum(jnp.where(pick, row, 0.0), axis=1, keepdims=True)


def finish_cycle(p, coef, brick, now, first, s_ref, z1b_ref, uhb_ref, clsb_ref, nodes, side, u_ref):
    X, Z, b = p.X, p.Z, Bounds(p)
    for i in range(X):
        u_ref[i] = s_ref[i] + brick.damp(i) * brick.from_halo(i, now.z1) + nodes[i * Z : (i + 1) * Z]
    old, cls, own = read_bounds(uhb_ref, b), read_bounds(clsb_ref, b), read_bounds(z1b_ref, b)
    kap = lambda value: lookup(value, coef, 0)
    halo = []

    def new(k, weights, toward, others, correction):
        kap_here = kap(cls[k])
        diagonal = lookup(cls[k], coef, 1) + (kap_here + toward) + ((weights[0] + weights[1]) + (weights[2] + weights[3]))
        total = toward * own_faces[k]
        for part in others:
            total = total + part
        value = old[k] + now.z2[k] + (DAMPING / diagonal) * total + correction
        halo.append(jnp.where(cls[k] > 0.5, value, 0.0))

    own_faces = list(own[:4]) + [swap_lanes(own[4])]
    at = X * Z
    for k in range(2):
        kap_here = kap(cls[k])
        row_m, row_p = kap(first.xz(1, k, 0)), kap(first.xz(1, k, 1))
        col_m, col_p = kap(first.xy(1, k, 0)), kap(first.xy(1, k, 1))
        w = plane_weights(kap_here, row_m, row_p, col_m, col_p)
        row, lane = iota((Z, p.Y), 0), iota((Z, p.Y), 1)
        others = (
            jnp.where(row == 0, w[0] * now.xz(0, k, 0), 0.0),
            jnp.where(row == Z - 1, w[1] * now.xz(0, k, 1), 0.0),
            jnp.where(lane == 0, w[2] * now.xy(0, k, 0), 0.0),
            jnp.where(lane == p.Y - 1, w[3] * now.xy(0, k, 1), 0.0),
        )
        toward = kap_here + brick.of(KAP, 0 if k == 0 else X - 1)
        new(k, w, toward, others, nodes[at : at + Z])
        at += Z
    for k in range(2):
        kap_here = kap(cls[2 + k])
        row_m, row_p = kap(first.xz(1, 0, k)), kap(first.xz(1, 1, k))
        col_m, col_p = (kap(column(first.zy(1, k), X, side_y)) for side_y in range(2))
        w = plane_weights(kap_here, row_m, row_p, col_m, col_p)
        row, lane = iota((X, p.Y), 0), iota((X, p.Y), 1)
        others = (
            jnp.where(row == 0, w[0] * now.xz(0, 0, k), 0.0),
            jnp.where(row == X - 1, w[1] * now.xz(0, 1, k), 0.0),
            jnp.where(lane == 0, w[2] * column(now.zy(0, k), X, 0), 0.0),
            jnp.where(lane == p.Y - 1, w[3] * column(now.zy(0, k), X, 1), 0.0),
        )
        z = 0 if k == 0 else Z - 1
        mine = jnp.concatenate([brick.of(KAP, i)[z : z + 1] for i in range(X)], axis=0)
        new(2 + k, w, kap_here + mine, others, nodes[at : at + X])
        at += X
    wide = kap(first.xy_lanes(1, cls[4]))
    z1_wide = now.xy_lanes(0, now.z1[4])
    row_m, row_p = kap(first.zy(1, 0)), kap(first.zy(1, 1))
    up, down = shifted(wide, 0, row_m, row_p)
    left, right = roll(wide, 2, 1), roll(wide, -2, 1)
    row, lane = iota((Z, p.Y), 0), iota((Z, p.Y), 1)
    w = (
        jnp.where(row % 4 == 0, wide + up, wide),
        jnp.where(row % 4 == 3, wide + down, wide),
        jnp.where((lane // 2) % 4 == 0, wide + left, wide),
        jnp.where((lane // 2) % 4 == 3, wide + right, wide),
    )
    others = (
        jnp.where(row == 0, w[0] * now.zy(0, 0), 0.0),
        jnp.where(row == Z - 1, w[1] * now.zy(0, 1), 0.0),
        jnp.where(lane // 2 == 0, w[2] * roll(z1_wide, 2, 1), 0.0),
        jnp.where(lane // 2 == X - 1, w[3] * roll(z1_wide, -2, 1), 0.0),
    )
    mine = swap_lanes(col_faces(lambda i: brick.of(KAP, i), p))
    new(4, w, wide + mine, others, side)
    return tuple(halo)


def middle_kernel(p, coef, in_ref, f_ref, s_ref, z1b_ref, uhb_ref, clsb_ref, cst_ref,
                  sy, pyt, pall, pyh, rxz, ry,
                  go_ref, s_out, z1b_out, uhb_out, in_scr, u_scr, r_scr, z_scr, z2_scr, go_scr):
    in_scr[...] = in_ref[...].astype(F32)
    b = Bounds(p)
    outside = read_bounds(clsb_ref, b)
    brick = Brick(p, cst_ref, lookup(outside[0], coef, 0), lookup(outside[1], coef, 0))
    now = Arrived(p, in_scr)
    nodes, side = coarse_rows(p, in_scr, sy, pyt, pall, pyh)
    halo = finish_cycle(p, coef, brick, now, now, s_ref, z1b_ref, uhb_ref, clsb_ref, nodes, side, u_scr)
    write_bounds(uhb_out, b, halo)
    get = lambda i: u_scr[i]
    residual = lambda i: residual_plane(brick, i, get, halo, f_ref[i])
    start_cycle(p, brick, get, residual, None, rxz, ry, sy,
                s_out, z1b_out, go_ref, r_scr, z_scr, z2_scr, go_scr)


def last_kernel(p, coef, in_ref, first_ref, f_ref, s_ref, z1b_ref, uhb_ref, clsb_ref, cst_ref,
                sy, pyt, pall, pyh, u_out, r_out, in_scr, first_scr):
    in_scr[...] = in_ref[...].astype(F32)
    first_scr[...] = first_ref[...].astype(F32)
    outside = read_bounds(clsb_ref, Bounds(p))
    brick = Brick(p, cst_ref, lookup(outside[0], coef, 0), lookup(outside[1], coef, 0))
    now, first = Arrived(p, in_scr), Arrived(p, first_scr)
    nodes, side = coarse_rows(p, in_scr, sy, pyt, pall, pyh)
    halo = finish_cycle(p, coef, brick, now, first, s_ref, z1b_ref, uhb_ref, clsb_ref, nodes, side, u_out)
    for i in range(p.X):
        r_out[i] = residual_plane(brick, i, lambda k: u_out[k], halo, f_ref[i])


class Sends:
    def __init__(self, p):
        X, Z = p.X, p.Z
        self.first = p.cy + Z // 2
        self.x_face, self.z_face = p.NY, p.NY
        self.x_rows = p.NY + 2 * Z + Z // 2
        self.z_rows = p.NY + 2 * X + 16
        self.xz_rows = p.NY + 16
        self.second = 2 * p.cx * p.NZ * p.NY // p.Y
        self.corner = self.second + 2 * Z + Z // 2
        self.last = self.corner + 16
        self.faces = 4 * Z + 4 * X


def pick(condition, a, b):
    return jnp.where(condition, a, b)


def fold(value):
    count, lanes = value.shape
    low, high = value[: count // 2], value[count // 2 :]
    return jnp.where(iota(low.shape, 1) < lanes // 2, low, roll(high, lanes // 2, 1)).astype(BF16)


def unfold(value):
    value = value.astype(F32)
    return jnp.concatenate([value, roll(value, value.shape[1] // 2, 1)], axis=0)


def go_on(p, brick, residual, rxz, ry, a_ref, z_ref, r_scr):
    X, Z = p.X, p.Z
    lane = iota((Z, p.Y), 1) // 4
    sides = jnp.zeros((Z, p.Y), F32)
    for i in range(X):
        r = residual(i)
        r_scr[i * Z : (i + 1) * Z, :] = r
        step = r * brick.damp(i)
        z_ref[i] = step
        sides = jnp.where(lane == i, roll(step, 4 * i + 2, 1), sides)
    coarse = dot_wide_right(rxz[...], r_scr[...])
    coarse = dot_wide_right(ry[...], coarse, ((1,), (1,))) * (1.0 / 216.0)
    a_ref[0 : p.cy, :] = coarse.astype(BF16)
    a_ref[p.cy :, :] = fold(sides)


def smooth_kernel(p, u_ref, z_ref, cst_ref, s_ref, z1b_ref, faces_ref, z2_scr):
    X, Z = p.X, p.Z
    brick = Brick(p, cst_ref, 0.0, 0.0)
    z1, z2 = (lambda i: z_ref[i]), (lambda i: z2_scr[i])
    for i in range(X):
        smooth = (2.0 - DAMPING) * z1(i) + brick.damp(i) * brick.neighbours(i, z1)
        z2_scr[i] = smooth
        s_ref[i] = u_ref[i] + smooth
    z_rows = (z_ref[:, 0, :], z_ref[:, Z - 1, :], z2_scr[:, 0, :], z2_scr[:, Z - 1, :])
    write_bounds(z1b_ref, Bounds(p), (z1(0), z1(X - 1), z_rows[0], z_rows[1], col_faces(z1, p)))
    for k, plane in enumerate((z1(0), z1(X - 1), z2(0), z2(X - 1))):
        faces_ref[k * Z : (k + 1) * Z, :] = plane.astype(BF16)
    for k, rows in enumerate(z_rows):
        faces_ref[4 * Z + k * X : 4 * Z + (k + 1) * X, :] = rows.astype(BF16)


def face_x(p, faces_ref, high):
    X, Z = p.X, p.Z
    return tuple(pick(high, faces_ref[(k + 1) * Z : (k + 2) * Z, :], faces_ref[k * Z : (k + 1) * Z, :]) for k in (0, 2))


def face_z(p, faces_ref, high):
    X, at = p.X, 4 * p.Z
    return tuple(
        pick(high, faces_ref[at + (k + 1) * X : at + (k + 2) * X, :], faces_ref[at + k * X : at + (k + 1) * X, :]) for k in (0, 2)
    )


def pad_rows(rows, count):
    rows = [row.astype(F32) for row in rows]
    return jnp.concatenate(rows + [jnp.zeros((count - len(rows), rows[0].shape[1]), F32)], axis=0).astype(BF16)


def y_block(p, sides, cls_y):
    lane = iota(sides.shape, 1)
    return jnp.where(lane < 2 * p.X, sides, roll(cls_y, 2 * p.X, 1))


def distances(count):
    return tuple(range(1, count))


def after_first(p, *refs):
    ny = p.ny
    buffers, (faces_ref, clsb_ref, cls_ref, sy, x_ref, z_ref, xz_ref, sides_ref, all_scr) = refs[:ny], refs[ny:]
    X, Z, sends, b = p.X, p.Z, Sends(p), Bounds(p)
    bx, by, bz = (lax.axis_index(axis) for axis in AXES)
    low = high = jnp.zeros((Z, p.Y), F32)
    for d, buffer in zip((0,) + distances(ny), buffers):
        other = by ^ d
        all_scr[pl.ds(pl.multiple_of(other * p.cy, 16), p.cy), :] = buffer[0 : p.cy, :]
        if d and d & (d + 1) == 0:
            value = unfold(buffer[p.cy :, :])
            low = pick(other == by - 1, value, low)
            high = pick(other == by + 1, value, high)
    to, source = iota((p.Y, p.Y), 1), iota((p.Y, p.Y), 0)
    place = (to % (2 * X)) // 2 * 4 + jnp.where(to < 2 * X, 1 + to % 2, 3 * (to % 2))
    order = ((source == place) & (to < 4 * X)).astype(BF16)
    both = dot(jnp.concatenate([low, high], axis=0).astype(BF16), order)
    sides = jnp.where(iota((Z, p.Y), 1) % 2 == 0, both[:Z], both[Z:])
    sides_ref[...] = sides
    modes = dot(sy[8 : 8 + p.NY, :], all_scr[...]).astype(BF16)
    cls_y = read(clsb_ref, b.uy)
    odd, up = bx % 2 == 1, bz == 0
    for ref in (x_ref, z_ref, xz_ref):
        ref[0 : p.NY, :] = modes
    at = p.NY
    z1, z2 = face_x(p, faces_ref, odd)
    x_ref[at : at + Z, :] = z1
    x_ref[at + Z : at + 2 * Z, :] = z2
    x_ref[at + 2 * Z :, :] = fold(y_block(p, sides, cls_y))
    z1, z2 = face_z(p, faces_ref, up)
    z_ref[at : at + X, :] = z1
    z_ref[at + X : at + 2 * X, :] = z2
    z_ref[at + 2 * X : at + 2 * X + 16, :] = pad_rows(
        [pick(up, value[Z - 1 : Z], value[0:1]) for value in (sides, cls_y)], 16
    )
    z1 = z1.astype(F32)
    cls = pick(odd, cls_ref[X // 4 - 1], cls_ref[0])
    xz_ref[at : at + 16, :] = pad_rows(
        [pick(odd, z1[X - 1 : X], z1[0:1]), pick(up, cls[Z - 1 : Z], cls[0:1])], 16
    )


def after_second(p, own_ref, x_in, z_in, xz_in, faces_ref, clsb_ref, sides_ref, wzt, out_ref):
    X, Z, Y, sends, b = p.X, p.Z, p.Y, Sends(p), Bounds(p)
    bx, bz = lax.axis_index("bx"), lax.axis_index("bz")
    odd, up = bx % 2 == 1, bz == 0
    at = 0
    for one, two in ((own_ref, z_in), (x_in, xz_in)):
        one, two = one[0 : p.NY, :], two[0 : p.NY, :]
        data = jnp.concatenate([pick(up, one, two), pick(up, two, one)], axis=1)
        data = dot(wzt[...], data, ((1,), (1,))).astype(BF16)
        for k in range(p.NY // Y):
            rows = data.shape[0]
            out_ref[at : at + rows, :] = data[:, k * Y : (k + 1) * Y]
            at += rows
    z1, z2 = face_x(p, faces_ref, jnp.logical_not(odd))
    out_ref[at : at + Z, :] = z1
    out_ref[at + Z : at + 2 * Z, :] = z2
    out_ref[at + 2 * Z : sends.corner, :] = fold(y_block(p, sides_ref[...], read(clsb_ref, b.uy)))
    beyond = z_in[p.NY : p.NY + X, :].astype(F32)
    classes = pick(up, read(clsb_ref, b.uzp), read(clsb_ref, b.uzm))
    out_ref[sends.corner :, :] = pad_rows(
        [pick(odd, value[0:1], value[X - 1 : X]) for value in (beyond, classes)], 16
    )


class Beyond:
    def __init__(self, p):
        X, Z = p.X, p.Z
        self.cross = 0
        self.core = Z
        self.z = 6 * Z
        self.y = 6 * Z + 4 * X
        self.kap = 10 * Z + 4 * X
        self.count = self.kap + Bounds(p).count


def rows_at(ref, at, count):
    return ref[at : at + count, :]


def beyond_kernel(p, coef, s_ref, z1b_ref, uhb_ref, clsb_ref, cls_ref, cst_ref, sides_ref, x_in, z_in, xz_in, s_out, out_ref):
    X, Z, Y, b, to = p.X, p.Z, p.Y, Bounds(p), Beyond(p)
    bx, bz = lax.axis_index("bx"), lax.axis_index("bz")
    odd, up = bx % 2 == 1, bz == 0
    some = (bx > 0) & (bx < p.nx - 1)
    kaps, sigs = lookup(clsb_ref[...], coef, 0), lookup(clsb_ref[...], coef, 1)
    out_ref[to.kap :, :] = kaps
    part = lambda value, span: value[span[0] : span[0] + span[1]]
    x_part = lambda value, high: pick(high, part(value, b.uxp), part(value, b.uxm))
    z_part = lambda value: pick(up, part(value, b.uzp), part(value, b.uzm))
    z1b, uhb = z1b_ref[...], uhb_ref[...]
    across = lambda at, count: pick(some, x_in[p.NY + at : p.NY + at + count, :].astype(F32), 0.0)
    x_z1, x_z2, block = across(0, Z), across(Z, Z), unfold(across(2 * Z, Z // 2))
    corner = pick(some, xz_in[p.NY : p.NY + 16, :].astype(F32), 0.0)
    corner_z1, corner_kap = corner[0:1], lookup(corner[1:2], coef, 0)
    z_z1, z_z2 = (z_in[p.NY + k * X : p.NY + (k + 1) * X, :].astype(F32) for k in range(2))
    z_rows = z_in[p.NY + 2 * X : p.NY + 2 * X + 16, :].astype(F32)
    zy_z1, zy_kap = z_rows[0:1], lookup(z_rows[1:2], coef, 0)
    block_kap = lookup(block, coef, 0)
    sides = sides_ref[...]
    brick = Brick(p, cst_ref, part(kaps, b.uxm), part(kaps, b.uxp))
    halo = (pick(odd, 0.0, x_z1), pick(odd, x_z1, 0.0), pick(up, 0.0, z_z1), pick(up, z_z1, 0.0), sides)
    for i in range(X):
        s_out[i] = s_ref[i] + brick.damp(i) * brick.from_halo(i, halo)
    row, lane = iota((Z, Y), 0), iota((Z, Y), 1)
    face = lambda high: pick(high, brick.of(KAP, X - 1), brick.of(KAP, 0))

    k, sigma = x_part(kaps, odd), x_part(sigs, odd)
    toward = k + face(odd)
    X2 = 2 * X
    ends = lambda value, first: [pick(odd, value[:, first + c : first + c + 1], value[:, first + X2 - 2 + c : first + X2 - 1 + c]) for c in (0, 1)]
    col_kap, col_z1 = ends(block_kap, X2), ends(block, 0)
    w = plane_weights(k, pick(up, 0.0, corner_kap), pick(up, corner_kap, 0.0), col_kap[0], col_kap[1])
    total = toward * x_part(z1b, odd)
    total = total + jnp.where(row == pick(up, Z - 1, 0), pick(up, w[1], w[0]) * corner_z1, 0.0)
    total = total + jnp.where(lane == 0, w[2] * col_z1[0], 0.0) + jnp.where(lane == Y - 1, w[3] * col_z1[1], 0.0)
    diagonal = sigma + (k + toward) + ((w[0] + w[1]) + (w[2] + w[3]))
    value = x_part(uhb, odd) + x_z2 + (DAMPING / diagonal) * total
    out_ref[to.cross : to.cross + Z, :] = jnp.where(k > 0.0, value, 0.0)

    other = jnp.logical_not(odd)
    k, sigma = x_part(kaps, other), x_part(sigs, other)
    toward = k + face(other)
    for j, value in enumerate((k, toward, sigma + (k + toward), x_part(z1b, other), x_part(uhb, other))):
        out_ref[to.core + j * Z : to.core + (j + 1) * Z, :] = value

    k, sigma = z_part(kaps), z_part(sigs)
    own = jnp.concatenate([pick(up, cst_ref[KAP, i // 4, Z - 1 : Z, :], cst_ref[KAP, i // 4, 0:1, :]) for i in range(X)], axis=0)
    toward = k + own
    col_kap, col_z1 = ([column(value, X, c) for c in (0, 1)] for value in (zy_kap, zy_z1))
    w = plane_weights(k, pick(odd, 0.0, corner_kap), pick(odd, corner_kap, 0.0), col_kap[0], col_kap[1])
    zrow, zlane = iota((X, Y), 0), iota((X, Y), 1)
    total = toward * z_part(z1b)
    total = total + jnp.where(zrow == pick(odd, X - 1, 0), pick(odd, w[1], w[0]) * corner_z1, 0.0)
    total = total + jnp.where(zlane == 0, w[2] * col_z1[0], 0.0) + jnp.where(zlane == Y - 1, w[3] * col_z1[1], 0.0)
    diagonal = sigma + (k + toward) + ((w[0] + w[1]) + (w[2] + w[3]))
    for j, value in enumerate((z_part(uhb) + z_z2, total, diagonal, k)):
        out_ref[to.z + j * X : to.z + (j + 1) * X, :] = value

    k, sigma = part(kaps, b.uy), part(sigs, b.uy)
    toward = k + swap_lanes(col_faces(lambda i: brick.of(KAP, i), p))
    reach = lambda value, shift: pick(odd, roll(value, X2 + shift, 1), roll(value, Y - X2 + shift, 1))
    begin = pick(odd, X2, Y - 2)
    far = (lane >= begin) & (lane < begin + 2)
    wide = jnp.where(far, reach(block_kap, -X2), jnp.where(lane < X2, k, 0.0))
    wide_z1 = jnp.where(far, reach(block, 0), jnp.where(lane < X2, sides, 0.0))
    above, below = shifted(wide, 0, pick(up, 0.0, zy_kap), pick(up, zy_kap, 0.0))
    left, right = roll(wide, 2, 1), roll(wide, -2, 1)
    place = lane // 2
    w = (
        jnp.where(row % 4 == 0, wide + above, wide),
        jnp.where(row % 4 == 3, wide + below, wide),
        jnp.where(place % 4 == 0, wide + left, wide),
        jnp.where(place % 4 == 3, wide + right, wide),
    )
    above, below = shifted(wide_z1, 0, pick(up, 0.0, zy_z1), pick(up, zy_z1, 0.0))
    total = toward * swap_lanes(part(z1b, b.uy)) + k * roll(sides, -X2, 1)
    total = total + w[0] * above + w[1] * below + w[2] * roll(wide_z1, 2, 1) + w[3] * roll(wide_z1, -2, 1)
    diagonal = sigma + (k + toward) + ((w[0] + w[1]) + (w[2] + w[3]))
    for j, value in enumerate((part(uhb, b.uy) + (2.0 - DAMPING) * sides, total, diagonal, k)):
        out_ref[to.y + j * Z : to.y + (j + 1) * Z, :] = value


def last_halo(p, coef, beyond_ref, last_in):
    X, Z, Y, to = p.X, p.Z, p.Y, Beyond(p)
    bx, bz = lax.axis_index("bx"), lax.axis_index("bz")
    odd, up = bx % 2 == 1, bz == 0
    start, end, X2 = Sends(p).second, Sends(p).corner, 2 * X
    z1, z2 = (last_in[start + k * Z : start + (k + 1) * Z, :].astype(F32) for k in range(2))
    block = unfold(last_in[start + 2 * Z : end, :])
    corner = last_in[end : end + 16, :].astype(F32)
    corner_z1, corner_kap = corner[0:1], lookup(corner[1:2], coef, 0)
    block_kap = lookup(block, coef, 0)
    row, lane = iota((Z, Y), 0), iota((Z, Y), 1)

    k, toward, diagonal, own, old = (rows_at(beyond_ref, to.core + j * Z, Z) for j in range(5))
    ends = lambda value, first: [pick(odd, value[:, first + X2 - 2 + c : first + X2 - 1 + c], value[:, first + c : first + c + 1]) for c in (0, 1)]
    col_kap, col_z1 = ends(block_kap, X2), ends(block, 0)
    w = plane_weights(k, pick(up, 0.0, corner_kap), pick(up, corner_kap, 0.0), col_kap[0], col_kap[1])
    total = toward * own
    total = total + jnp.where(row == pick(up, Z - 1, 0), pick(up, w[1], w[0]) * corner_z1, 0.0)
    total = total + jnp.where(lane == 0, w[2] * col_z1[0], 0.0) + jnp.where(lane == Y - 1, w[3] * col_z1[1], 0.0)
    diagonal = diagonal + ((w[0] + w[1]) + (w[2] + w[3]))
    core = (k, old + z2 + (DAMPING / diagonal) * total)
    value, total, diagonal, k = (rows_at(beyond_ref, to.z + j * X, X) for j in range(4))
    edge = iota((X, Y), 0) == pick(odd, 0, X - 1)
    total = total + jnp.where(edge, (k + corner_kap) * corner_z1, 0.0)
    diagonal = diagonal + jnp.where(edge, corner_kap, 0.0)
    z = (k, value + (DAMPING / diagonal) * total)

    value, total, diagonal, k = (rows_at(beyond_ref, to.y + j * Z, Z) for j in range(4))
    begin = pick(odd, 0, X2 - 2)
    edge = (lane >= begin) & (lane < begin + 2)
    reach = lambda value, shift: pick(odd, roll(value, 2 - X2 + shift, 1), roll(value, X2 - 2 + shift, 1))
    edge_kap = reach(block_kap, -X2)
    total = total + jnp.where(edge, (k + edge_kap) * reach(block, 0), 0.0)
    diagonal = diagonal + jnp.where(edge, edge_kap, 0.0)
    return z1, core, z, (k, value + (DAMPING / diagonal) * total)


def finish_staged(p, brick, s_ref, beyond_ref, parts, nodes, side, u_ref):
    X, Z, to = p.X, p.Z, Beyond(p)
    bx, bz = lax.axis_index("bx"), lax.axis_index("bz")
    odd, up = bx % 2 == 1, bz == 0
    some = (bx > 0) & (bx < p.nx - 1)
    z1, core, z, y = parts
    for i in range(X):
        value = s_ref[i] + nodes[i * Z : (i + 1) * Z]
        if i in (0, X - 1):
            weight = brick.x_weights(i)[0 if i == 0 else 1]
            here = odd if i == 0 else jnp.logical_not(odd)
            value = value + brick.damp(i) * (weight * pick(here, z1, 0.0))
        u_ref[i] = value
    at = X * Z
    below, above = nodes[at : at + Z], nodes[at + Z : at + 2 * Z]
    core = jnp.where(core[0] > 0.0, core[1] + pick(odd, below, above), 0.0)
    cross = pick(some, rows_at(beyond_ref, to.cross, Z) + pick(odd, above, below), 0.0)
    at += 2 * Z
    z = jnp.where(z[0] > 0.0, z[1] + pick(up, nodes[at + X : at + 2 * X], nodes[at : at + X]), 0.0)
    y = jnp.where(y[0] > 0.0, y[1] + side, 0.0)
    return pick(odd, core, cross), pick(odd, cross, core), pick(up, 0.0, z), pick(up, z, 0.0), y


def coarse_staged(p, own_ref, last_in, inverse, kx, kxi, zi, sy, pye, pall, pyh):
    Y, NY = p.Y, p.NY
    bx, bz = lax.axis_index("bx"), lax.axis_index("bz")
    rows, step, count = p.cx * p.NZ, p.cx * LOW, p.NX * LOW
    back = kxi[pl.ds(pl.multiple_of(bx * step, 16), step + 2 * LOW), :]
    table = kx[bx]
    parts = []
    for h in range(p.NZ // LOW):
        lines = []
        for ref in (own_ref, last_in):
            for block in range(2):
                at = [(block * (NY // Y) + k) * rows + h * step for k in range(NY // Y)]
                lines.append(jnp.concatenate([ref[i : i + step, :] for i in at], axis=1))
        parts.append(dot(table, jnp.concatenate(lines, axis=0)))
    parts = [(value * inverse[h * count : (h + 1) * count, :]).astype(BF16) for h, value in enumerate(parts)]
    values = dot(back, jnp.concatenate(parts, axis=1)).astype(BF16)
    values = jnp.concatenate([values[:, h * NY : (h + 1) * NY] for h in range(len(parts))], axis=0)
    values = dot(zi[bz], values).astype(BF16)
    table = sy[pl.ds(pl.multiple_of(lax.axis_index("by") * p.cy, 16), p.cy + 16), :]
    values = dot(dot(values, table, ((1,), (1,))).astype(BF16), pye[...])
    count = pall.shape[0] - p.Z
    nodes = dot_wide_right(pall[:count, : p.lanes + p.extra], values[:, :Y]) * (1.0 / 27.0)
    ends = values[: p.lanes, Y:]
    spread = ends[:, 0:1] * pyh[: p.lanes].astype(F32) + ends[:, 1:2] * pyh[p.lanes :].astype(F32)
    side = dot_wide_right(pall[count:, : p.lanes], spread) * (1.0 / 27.0)
    return nodes, side


def inverse_kernel(p, coef, lam_xz, lam_y, out_ref):
    classes = coef.shape[1]
    kap_mean = sum(coef[0, k] for k in range(classes)) * (1.0 / classes)
    sig_mean = sum(coef[1, k] for k in range(classes)) * (1.0 / classes)
    step = p.NX * LOW
    for h in range(p.NZ // LOW):
        lam = lam_xz[h * step : (h + 1) * step, :] + lam_y[...]
        out_ref[h * step : (h + 1) * step, :] = 1.0 / (kap_mean * lam + sig_mean)


def first_staged(p, coef, u_ref, r_ref, cls_ref, cst0_ref, xa, xb, za, zb, ya, yb, rxz, ry,
                 a_ref, z_ref, uhb_ref, clsb_ref, cst_ref, r_scr):
    brick, residual = neighbours_in(p, coef, u_ref, r_ref, cst0_ref, xa, xb, za, zb, ya, yb, uhb_ref, clsb_ref, cst_ref)
    go_on(p, brick, residual, rxz, ry, a_ref, z_ref, r_scr)


def correct(p, coef, s_ref, beyond_ref, cst_ref, own, last_in, inverse, kx, kxi, zi, sy, pye, pall, pyh, u_ref):
    b, at = Bounds(p), Beyond(p).kap
    brick = Brick(p, cst_ref, rows_at(beyond_ref, at + b.uxm[0], p.Z), rows_at(beyond_ref, at + b.uxp[0], p.Z))
    parts = last_halo(p, coef, beyond_ref, last_in)
    nodes, side = coarse_staged(p, own, last_in, inverse, kx, kxi, zi, sy, pye, pall, pyh)
    return brick, finish_staged(p, brick, s_ref, beyond_ref, parts, nodes, side, u_ref)


def middle_staged(p, coef, f_ref, s_ref, beyond_ref, cst_ref, own, last_in, inverse, kx, kxi, zi, sy, pye, pall, pyh, rxz, ry,
                  a_ref, z_ref, uhb_out, u_out, r_scr):
    brick, halo = correct(p, coef, s_ref, beyond_ref, cst_ref, own, last_in, inverse, kx, kxi, zi, sy, pye, pall, pyh, u_out)
    write_bounds(uhb_out, Bounds(p), halo)
    residual = lambda i: residual_plane(brick, i, lambda k: u_out[k], halo, f_ref[i])
    go_on(p, brick, residual, rxz, ry, a_ref, z_ref, r_scr)


def last_staged(p, coef, f_ref, s_ref, beyond_ref, cst_ref, own, last_in, inverse, kx, kxi, zi, sy, pye, pall, pyh,
                u_out, r_out, u_scr, r_scr, sems):
    brick, halo = correct(p, coef, s_ref, beyond_ref, cst_ref, own, last_in, inverse, kx, kxi, zi, sy, pye, pall, pyh, u_scr)
    copies = [pltpu.make_async_copy(u_scr, u_out, sems.at[0])]
    copies[0].start()
    chunk = p.X // 4
    for k in range(4):
        for i in range(k * chunk, (k + 1) * chunk):
            r_scr[i] = residual_plane(brick, i, lambda j: u_scr[j], halo, f_ref[i])
        part = pl.ds(k * chunk, chunk)
        copies.append(pltpu.make_async_copy(r_scr.at[part], r_out.at[part], sems.at[k + 1]))
        copies[-1].start()
    for copy in copies:
        copy.wait()


def call(kernel, p, name, coef, inputs, outputs, scratch, us=2, out_space=pltpu.VMEM):
    smem = [pl.BlockSpec(memory_space=pltpu.SMEM)] if coef is not None else []
    args = ([coef] if coef is not None else []) + list(inputs)
    return pl.pallas_call(
        functools.partial(kernel, p),
        out_shape=[jax.ShapeDtypeStruct(shape, dtype) for shape, dtype in outputs],
        in_specs=smem + [pl.BlockSpec(memory_space=pltpu.VMEM)] * len(inputs),
        out_specs=[pl.BlockSpec(memory_space=out_space)] * len(outputs),
        scratch_shapes=[pltpu.VMEM(shape, F32) if isinstance(shape, tuple) else shape for shape in scratch],
        compiler_params=pltpu.CompilerParams(vmem_limit_bytes=VMEM_LIMIT),
        cost_estimate=pl.CostEstimate(flops=0, bytes_accessed=us * 3_600_000, transcendentals=0),
        name=name,
    )(*args)


def swaps(axis, count, a, b, near=None):
    if count == 1:
        return a, b
    assert count % 2 == 0
    first = lax.ppermute(a, axis, [(i, i ^ 1) for i in range(count)])
    if count == 2:
        return first, first
    other = lambda i: (i + 1 if i % 2 else i - 1) % count
    if near is None:
        return first, lax.ppermute(b, axis, [(i, other(i)) for i in range(count)])
    name, size = near
    pairs = []
    for k in range(size):
        for i in range(count):
            to = (k ^ 1, i) if i in (0, count - 1) else (k, other(i))
            pairs.append((k * count + i, to[0] * count + to[1]))
    return first, lax.ppermute(b, (name, axis), pairs)


def body(forcing, start, element_class_index, class_coef):
    p = Plan(start.shape, *(lax.axis_size(axis) for axis in AXES))
    t = tables(p)
    X, Z, Y, n = p.X, p.Z, p.Y, p.n
    bounds = Bounds(p).count
    block, flat, cst = (X, Z, Y), (X * Z, Y), (DAMP, X // 4, Z, Y)
    (uy,) = call(sides_kernel, p, "start_sides", None, (start,), [((Z, Y), F32)], [], us=20)
    cls, xa, xb, za, zb, yf = call(
        pack_kernel, p, "pack_faces", None, (element_class_index, start, uy),
        [((X // 4, Z, Y), F32)] + [((2 * Z, Y), F32)] * 2 + [((2 * max(X, Z), Y), F32)] * 2 + [((2 * Z, Y), F32)], [], us=20,
    )
    xa, xb = swaps("bx", p.nx, xa, xb)
    za, zb = swaps("bz", p.nz, za, zb)
    ya, yb = swaps("by", p.ny, yf, yf, ("bx", p.nx) if p.nx % 2 == 0 else None)
    go_shape, back_shape = (n * p.go, Y), (n * p.back, Y)
    starting = [flat, block, block, go_shape]
    rxz, ry, sy = t["rxz"], t["ry"], t["sy"]
    cst0, r0 = call(prepare_kernel, p, "prepare", class_coef, (start, forcing, cls), [(cst, F32), (block, F32)], [], us=6)
    if p.staged:
        return staged_cycles(p, t, class_coef, forcing, cls, start, r0, cst0, (xa, xb, za, zb, ya, yb))
    go, s, z1b, uhb, clsb, coefs = call(
        first_kernel, p, "first_residual", class_coef,
        (start, r0, cls, cst0, xa, xb, za, zb, ya, yb, rxz, ry, sy),
        [(go_shape, BF16), (block, F32), ((bounds, Y), F32), ((bounds, Y), F32), ((bounds, Y), F32), ((QUANTITIES,) + cst[1:], F32)],
        starting,
    )
    prolong = (sy, t["pyt"], t["pall"], t["pyh"])
    first = None
    for cycle in range(CYCLES):
        came = lax.all_to_all(go, AXES, split_axis=0, concat_axis=0, tiled=True)
        (out,) = call(
            owner_kernel, p, "owned_modes", class_coef,
            (came, t["wz"], t["wx"], t["wxt"], t["wzi"], t["lamxz"], t["lamy"]),
            [(back_shape, BF16)], [go_shape, back_shape],
        )
        back = lax.all_to_all(out, AXES, split_axis=0, concat_axis=0, tiled=True)
        if cycle + 1 < CYCLES:
            assert first is None
            first = back
            go, s, z1b, uhb = call(
                middle_kernel, p, "next_residual", class_coef,
                (back, forcing, s, z1b, uhb, clsb, coefs) + prolong + (rxz, ry),
                [(go_shape, BF16), (block, F32), ((bounds, Y), F32), ((bounds, Y), F32)],
                [back_shape, block] + starting,
            )
        else:
            return tuple(call(
                last_kernel, p, "last_residual", class_coef,
                (back, first, forcing, s, z1b, uhb, clsb, coefs) + prolong,
                [(block, F32), (block, F32)], [back_shape, back_shape],
            ))


def staged_cycles(p, t, class_coef, forcing, cls, u, r0, cst0, faces_in):
    X, Z, Y = p.X, p.Z, p.Y
    sends, bounds = Sends(p), (Bounds(p).count, Y)
    block, flat = (X, Z, Y), (X * Z, Y)
    out = [((sends.first, Y), BF16), (block, F32), (bounds, F32)]
    (inverse,) = call(
        inverse_kernel, p, "inverse_spectrum", class_coef, (t["lam_xz"], t["lam_y"]), [((p.NZ * p.NX, p.NY), F32)], []
    )
    a, z1, uhb, clsb, coefs = call(
        first_staged, p, "first_residual", class_coef, (u, r0, cls, cst0) + faces_in + (t["rxz"], t["ry"]),
        out + [(bounds, F32), ((QUANTITIES,) + cst0.shape[1:], F32)], [flat],
    )
    pairs = lambda count, d: [(i, i ^ d) for i in range(count)]
    for cycle in range(CYCLES):
        came = [a] + [lax.ppermute(a, "by", pairs(p.ny, d)) for d in distances(p.ny)]
        s, z1b, faces = call(
            smooth_kernel, p, "smooth", None, (u, z1, coefs),
            [(block, F32), (bounds, F32), ((sends.faces, Y), BF16)], [block],
        )
        x, z, xz, sides = call(
            after_first, p, "y_modes", None, (*came, faces, clsb, cls, t["sy"]),
            [((rows, Y), BF16) for rows in (sends.x_rows, sends.z_rows, sends.xz_rows)] + [((Z, Y), F32)],
            [pltpu.VMEM((p.NY, Y), BF16)],
        )
        plane, across = p.nx * p.nz, (p.nx - 1) * p.nz
        x_in = lax.ppermute(x, ("bx", "bz"), pairs(plane, across))
        z_in = lax.ppermute(z, ("bx", "bz"), pairs(plane, 1))
        xz_in = lax.ppermute(xz, ("bx", "bz"), pairs(plane, across + 1))
        if cycle == 0:
            x_in, inverse = lax.optimization_barrier((x_in, inverse))
            back = (inverse,) + tuple(t[key] for key in ("kx", "kxi", "zi", "sy", "pye", "pall", "pyh"))
        (own,) = call(
            after_second, p, "z_modes", None, (x, x_in, z_in, xz_in, faces, clsb, sides, t["wzt"]),
            [((sends.last, Y), BF16)], [],
        )
        last_in = lax.ppermute(own, "bx", pairs(p.nx, 1))
        s, beyond = call(
            beyond_kernel, p, "beyond", class_coef, (s, z1b, uhb, clsb, cls, coefs, sides, x_in, z_in, xz_in),
            [(block, F32), ((Beyond(p).count, Y), F32)], [],
        )
        inputs = (forcing, s, beyond, coefs, own, last_in) + back
        if cycle + 1 < CYCLES:
            a, z1, uhb, u = call(
                middle_staged, p, "next_residual", class_coef, inputs + (t["rxz"], t["ry"]), out + [(block, F32)], [flat]
            )
        else:
            return tuple(call(
                last_staged, p, "last_residual", class_coef, inputs, [(block, F32), (block, F32)],
                [block, block, pltpu.SemaphoreType.DMA((5,))], out_space=pl.ANY,
            ))


def solution(mesh):
    spec = P("bx", "bz", "by")
    return jax.shard_map(body, mesh=mesh, in_specs=(spec, spec, spec, P()), out_specs=(spec, spec), check_vma=False)
```
